32 devices in a mesh: freq: 4 (over z), dom: 8 (over y, x, core).
Axes of the slice: x: 2, y: 2, z: 4, core: 2. Of those that a mesh axis runs over, the one named last changes fastest.
Arguments:
- angular: float32 [8], P('freq'), may hold values from 0.5 to 4
- stiffness: float32 [8, 36, 1024], P('dom'), as said below
- mass_matrix: float32 [8, 36, 1024], P('dom'), as said below
- conductivity: float32 [8, 1024], P('dom'), may hold values from 0.3 to 3
- element_edges: int32 [8, 6, 1024], P('dom'), may hold values from 0 to 1279
- live_slots: int32 [8, 1024], P('dom'), may hold values from 0 to 1, as said below
- adjoint_source: float32 [8, 2, 8, 1280], P('freq', None, 'dom'), may hold values from -6 to 6
- forward_field: float32 [8, 2, 8, 1280], P('freq', None, 'dom'), may hold values from -6 to 6
- neighbour_map: int32 [8, 256], P('dom'), may hold values from 0 to 255, each once within a row
Outputs:
- gradient: float32 [8, 1024], P('dom')
- updated_conductivity: float32 [8, 1024], P('dom')
The draws below stay inside these ranges and needn't reach their ends.
Inputs may be any that keep to these rules, and one draw needn't show every extreme that they name: `live_slots`: in each partition the live slots come first; at least half of the 1024 slots are live, and some partition has all slots live. `neighbour_map`: each row is a permutation of the rim slots; row 0 is not used. `stiffness`: each element matrix is symmetric with a strictly dominant positive diagonal. `mass_matrix`: each element matrix is symmetric with a strictly dominant positive diagonal.
All inputs are finite; a program needn't handle non-finite values.
Results may differ from the reference program's by a relative error of at most 0.0003.
Values sent between devices are 32-bit elements; how exact they have to be, the bound alone decides.
No kernel may reach another device: no remote copies, remote signals or barrier semaphores. Data moves between devices by JAX's collectives and lax.ppermute only.
A program may use at most 64 MiB of HBM per device.

```python
import math
import jax
import jax.numpy as jnp
from jax import lax

ELEMS = 1024
EDGES = 1280
IFACE = 256
NPOL = 2
ITERS = 3
FREQS = 8
PARTS_SIZE = 8


def symmetric_blocks(key, diag_lo, diag_hi, spread):
    upper = jax.random.uniform(key, (PARTS_SIZE, 6, 6, ELEMS), jnp.float32, -spread, spread)
    upper = 0.5 * (upper + jnp.swapaxes(upper, 1, 2))
    diagonal = jax.random.uniform(jax.random.fold_in(key, 1), (PARTS_SIZE, 6, ELEMS), jnp.float32, diag_lo, diag_hi)
    identity = (jnp.arange(6)[:, None] == jnp.arange(6)[None, :]).astype(jnp.float32)[None, :, :, None]
    blocks = upper * (1.0 - identity) + identity * diagonal[:, :, None, :]
    return blocks.reshape(PARTS_SIZE, 36, ELEMS)


def draw_stiffness(key, part):
    return symmetric_blocks(jax.random.fold_in(key, 11), 1.8, 2.6, 0.35)


def draw_mass_matrix(key, part):
    return symmetric_blocks(jax.random.fold_in(key, 23), 1.0, 1.5, 0.2)


def draw_live_slots(key, part):
    counts = jax.random.randint(jax.random.fold_in(key, 31), (PARTS_SIZE,), ELEMS // 2, ELEMS + 1)
    chosen = jax.random.randint(jax.random.fold_in(key, 37), (), 0, PARTS_SIZE)
    counts = jnp.where(jnp.arange(PARTS_SIZE) == chosen, ELEMS, counts)
    return (jnp.arange(ELEMS)[None, :] < counts[:, None]).astype(jnp.int32)


def place_ends(values, key, least, largest):
    dims = values.shape
    spot = [jax.random.randint(jax.random.fold_in(key, axis), (), 0, dims[axis]) for axis in range(len(dims))]
    values = values.at[tuple(spot)].set(least)
    longest = dims.index(max(dims))
    spot[longest] = (spot[longest] + 1) % dims[longest]
    return values.at[tuple(spot)].set(largest)


def shard_levels(stream_key, extent, cuts, least, high):
    def one(axis_at, shards_of):
        steps = jax.random.uniform(jax.random.fold_in(jax.random.fold_in(stream_key, 6), axis_at), (shards_of,), jnp.float32, least / len(cuts), high / len(cuts))
        return jnp.repeat(jnp.exp(steps), extent[axis_at] // shards_of).reshape((-1,) + (1,) * (len(extent) - axis_at - 1))

    gain = one(*cuts[0])
    for cut in cuts[1:]:
        gain = gain * one(*cut)
    return gain


def scatter_about(key, shape, scale, bound, shards=(), kind=jnp.bfloat16):
    entries = jax.random.normal(key, shape, jnp.float32) * scale
    if len(shards) > 0:
        entries = shard_levels(key, shape, shards, -0.22, 0.18) * entries
    return jnp.clip(entries, min=-bound, max=bound).astype(kind)


def setup_inputs(seed: int = 0) -> dict:
    key_list = jax.random.split(jax.random.key(seed), 10)
    angular = jnp.clip(jnp.exp(math.log(4.0) - 2.0794415 * jax.random.uniform(key_list[0], (FREQS,), jnp.float32) ** shard_levels(key_list[0], (FREQS,), ((0, 4),), -0.2, 0.2)), 0.5, 4.0)
    stiffness = draw_stiffness(jax.random.fold_in(key_list[9], 71), 0)
    mass_matrix = draw_mass_matrix(jax.random.fold_in(key_list[9], 71), 0)
    conductivity = jnp.clip(jnp.exp(math.log(3.0) - 2.3025851 * jax.random.uniform(key_list[3], (PARTS_SIZE, ELEMS), jnp.float32) ** shard_levels(key_list[3], (PARTS_SIZE, ELEMS), ((0, 8),), -0.2, 0.2)), 0.3, 3.0)
    element_edges = place_ends(jax.random.randint(key_list[4], (PARTS_SIZE, 6, ELEMS), 0, EDGES), jax.random.fold_in(key_list[4], 1), 0, EDGES - 1).astype(jnp.int32)
    live_slots = draw_live_slots(jax.random.fold_in(key_list[9], 71), 0)
    adjoint_source = scatter_about(key_list[6], (FREQS, NPOL, PARTS_SIZE, EDGES), 1.0, 6.0, ((0, 4), (2, 8)), jnp.float32)
    forward_field = scatter_about(key_list[7], (FREQS, NPOL, PARTS_SIZE, EDGES), 1.0, 6.0, ((0, 4), (2, 8)), jnp.float32)
    neighbour_map = jax.vmap(lambda own: jax.random.permutation(own, IFACE))(jax.random.split(key_list[8], PARTS_SIZE)).reshape((PARTS_SIZE, IFACE)).astype(jnp.int32)
    return dict(angular=angular, stiffness=stiffness, mass_matrix=mass_matrix, conductivity=conductivity, element_edges=element_edges, live_slots=live_slots, adjoint_source=adjoint_source, forward_field=forward_field, neighbour_map=neighbour_map)


def element_blocks(angular, stiffness, mass_matrix, conductivity, live_slots):
    weights = live_slots.astype(jnp.float32)
    shifted = angular[:, None, None] * (conductivity * weights)[None, None, :]
    return stiffness[None] * weights[None, None, :] + shifted * mass_matrix[None]


def pick_edges(vector_in, edge_ids):
    groups = vector_in.shape[0]
    polars = vector_in.shape[1]
    return vector_in[:, :, edge_ids.reshape(-1)].reshape(groups, polars, 6, -1)


def element_apply(blocks, vector_in, edge_ids):
    picked = pick_edges(vector_in, edge_ids)
    stacked = []
    for i in range(6):
        running = blocks[:, None, 6 * i, :] * picked[:, :, 0, :]
        for j in range(1, 6):
            running = running + blocks[:, None, 6 * i + j, :] * picked[:, :, j, :]
        stacked.append(running)
    return jnp.stack(stacked, axis=2)


def scatter_edges(values, edge_ids, edge_count):
    flat_values = values.reshape(values.shape[0], values.shape[1], -1)
    flat_index = edge_ids.reshape(-1)

    def single(row_values):
        return jax.ops.segment_sum(row_values, flat_index, num_segments=edge_count)

    return jax.vmap(jax.vmap(single))(flat_values)


def element_gradient(angular, mass_matrix, live_slots, adjoint, forward_local, edge_ids):
    applied = element_apply(mass_matrix[None], forward_local, edge_ids)
    picked = pick_edges(adjoint, edge_ids)
    inner_terms = jnp.sum(picked * applied, axis=(1, 2))
    return -jnp.sum(angular[:, None] * inner_terms, axis=0) * live_slots.astype(jnp.float32)


def assemble(vectors, neighbour_map):
    lower_rim = vectors[..., :IFACE]
    upper_rim = vectors[..., EDGES - IFACE:]
    arranged = jax.vmap(lambda rim, order: jnp.zeros_like(rim).at[..., order].set(rim))(lower_rim, neighbour_map)
    previous = jnp.concatenate([jnp.zeros_like(upper_rim[:1]), upper_rim[:-1]], axis=0)
    from_below = jax.vmap(lambda rim, order: jnp.take(rim, order, axis=-1))(previous, neighbour_map)
    from_above = jnp.concatenate([arranged[1:], jnp.zeros_like(arranged[:1])], axis=0)
    middle = vectors[..., IFACE:EDGES - IFACE]
    return jnp.concatenate([lower_rim + from_below, middle, upper_rim + from_above], axis=-1)


def reference(angular, stiffness, mass_matrix, conductivity, element_edges, live_slots, adjoint_source, forward_field, neighbour_map):
    source_parts = jnp.transpose(adjoint_source, (2, 0, 1, 3))
    forward_parts = jnp.transpose(forward_field, (2, 0, 1, 3))
    positions = jnp.arange(EDGES)[None, :]
    part_ids = jnp.arange(PARTS_SIZE)[:, None]
    owned = jnp.where((positions < IFACE) & (part_ids > 0), 0.0, 1.0).astype(jnp.float32)

    def apply_all(vector_parts):
        def one_part(inputs):
            vector_in, stiff_part, mass_part, cond_part, edges_part, live_part = inputs
            blocks = element_blocks(angular, stiff_part, mass_part, cond_part, live_part)
            return scatter_edges(element_apply(blocks, vector_in, edges_part), edges_part, EDGES)

        local = lax.map(one_part, (vector_parts, stiffness, mass_matrix, conductivity, element_edges, live_slots))
        return assemble(local, neighbour_map)

    def inner(first, second):
        return jnp.sum(first * second * owned[:, None, None, :], axis=(0, 3))

    rhs = assemble(source_parts, neighbour_map)
    adjoint = jnp.zeros_like(rhs)
    residual = rhs
    direction = rhs
    norm_now = inner(residual, residual)
    for step in range(ITERS):
        image = apply_all(direction)
        alpha = (norm_now / inner(direction, image))[None, :, :, None]
        adjoint = adjoint + alpha * direction
        residual = residual - alpha * image
        norm_next = inner(residual, residual)
        direction = residual + (norm_next / norm_now)[None, :, :, None] * direction
        norm_now = norm_next

    def grad_part(inputs):
        adjoint_part, forward_part, mass_part, live_part, edges_part = inputs
        return element_gradient(angular, mass_part, live_part, adjoint_part, forward_part, edges_part)

    gradient = lax.map(grad_part, (adjoint, forward_parts, mass_matrix, live_slots, element_edges))
    updated = conductivity * jnp.exp(-0.5 * jnp.tanh(gradient))
    return gradient, updated
```

```python
import functools

import jax
import jax.numpy as jnp
from jax import lax
from jax.experimental import pallas as pl
from jax.experimental.pallas import tpu as pltpu
from jax.sharding import PartitionSpec as P

LANES = 128
SIDE = 6
VMEM = pl.BlockSpec(memory_space=pltpu.VMEM)
SMEM = pl.BlockSpec(memory_space=pltpu.SMEM)

PICK_LANES = lax.GatherDimensionNumbers(
    offset_dims=(),
    collapsed_slice_dims=(1,),
    start_index_map=(1,),
    operand_batching_dims=(0,),
    start_indices_batching_dims=(0,),
)


def pick_lanes(block, lanes):
    return lax.gather(
        block,
        lanes[..., None],
        PICK_LANES,
        (1, 1),
        mode=lax.GatherScatterMode.PROMISE_IN_BOUNDS,
    )


def pick_wide(chunks, index):
    lanes = index & (LANES - 1)
    high = index >> 7
    level = [pick_lanes(chunk, lanes) for chunk in chunks]
    bit = 0
    while len(level) > 1:
        odd = (high >> bit) & 1 == 1
        level = [
            jnp.where(odd, level[t + 1], level[t]) if t + 1 < len(level) else level[t]
            for t in range(0, len(level), 2)
        ]
        bit += 1
    return level[0]


def row_ids(rows):
    return lax.broadcasted_iota(jnp.int32, (rows, LANES), 0)


def lane_ids(rows):
    return lax.broadcasted_iota(jnp.int32, (rows, LANES), 1)


def spread(row, rows):
    return jnp.broadcast_to(row, (rows, row.shape[-1]))


def cut(ref, start=0):
    return [ref[:, c : c + LANES] for c in range(start, ref.shape[-1], LANES)]


def swap_halves(block):
    return pltpu.roll(block, block.shape[0] // 2, 0)


def doubled(block):
    half = block.shape[0] // 2
    return jnp.where(row_ids(2 * half) < half, block, swap_halves(block))


def row_weights(angular_ref, rows, polars):
    ids = row_ids(rows)
    out = jnp.zeros((rows, LANES), jnp.float32)
    for f in range(angular_ref.shape[0]):
        for base in (0, rows // 2):
            here = (ids >= base + f * polars) & (ids < base + (f + 1) * polars)
            out = jnp.where(here, angular_ref[f], out)
    return out


def lane_sum(block):
    return jnp.broadcast_to(jnp.sum(block, axis=1, keepdims=True), block.shape)


def product(chunks, rate, inverse_scale, weights, edges, stiffness, mass, sigma, live, tables):
    rows = chunks[0].shape[0]
    half = rows // 2
    count = len(chunks)
    lower_half = row_ids(rows) < half
    slots = stiffness.shape[-1]

    def body(s, quad):
        here = pl.ds(pl.multiple_of(s * LANES, LANES), LANES)
        index = [spread(edges[pl.ds(j, 1), here], rows) for j in range(SIDE)]
        picked = [pick_wide(chunks, index[j]) for j in range(SIDE)]
        shift = weights * spread(sigma[:, here], rows)
        alive = spread(live[:, here], rows).astype(jnp.float32) * inverse_scale
        for i in range(SIDE):
            stiff = None
            heavy = None
            for j in range(SIDE):
                entry = pl.ds(SIDE * i + j, 1)
                one = spread(stiffness[entry, here], rows) * picked[j]
                two = spread(mass[entry, here], rows) * picked[j]
                stiff = one if stiff is None else stiff + one
                heavy = two if heavy is None else heavy + two
            value = (stiff + shift * heavy) * alive
            quad = quad + picked[i] * value
            if tables is None:
                continue
            values, places = tables
            coarse = value.astype(jnp.bfloat16).astype(jnp.float32)
            both = jnp.where(lower_half, coarse, value - coarse)
            high = index[i] >> 7
            column = pl.ds(pl.multiple_of(i * slots + s * LANES, LANES), LANES)
            for h in range(0, count, 2):
                block = [jnp.where(high == h + t, both, 0.0) for t in range(2)]
                values[rows * h : rows * (h + 2), column] = jnp.concatenate(
                    block, axis=0
                ).astype(jnp.bfloat16)
            lanes = spread(index[i][:1] & (LANES - 1), LANES)
            places[:, column] = jnp.where(lanes == row_ids(LANES), 1.0, 0.0).astype(
                jnp.bfloat16
            )
        return quad

    quad = lax.fori_loop(0, slots // LANES, body, jnp.zeros((rows, LANES), jnp.float32))
    if tables is None:
        return None, quad
    values, places = tables
    total = lax.dot_general(
        values[...],
        places[...],
        (((1,), (1,)), ((), ())),
        preferred_element_type=jnp.float32,
    )
    out = []
    for h in range(count):
        piece = total[rows * h : rows * (h + 1)]
        out.append(piece + swap_halves(piece))
    return out, quad


def joined(own, from_prior, from_above, order, inverse):
    rim = len(from_prior)
    lower = [own[c] + pick_wide(from_prior, order[c]) for c in range(rim)]
    upper = [own[len(own) - rim + c] + pick_wide(from_above, inverse[c]) for c in range(rim)]
    return lower + own[rim : len(own) - rim] + upper


def squares(chunks, rim, has_prior):
    total = None
    for c, chunk in enumerate(chunks):
        term = chunk * chunk
        if c < rim:
            term = term * (1.0 - has_prior)
        total = term if total is None else total + term
    return total


def put_lane(block, lane, value):
    return jnp.where(lane_ids(block.shape[0]) == lane, value, block)


def put_chunks(ref, chunks):
    for c, chunk in enumerate(chunks):
        ref[:, c * LANES : (c + 1) * LANES] = chunk


def first_stage(
    polars,
    angular,
    source,
    order_ref,
    prior_ref,
    above_ref,
    stiffness,
    mass,
    sigma,
    edges,
    live,
    field_ref,
    image_ref,
    lower_ref,
    upper_ref,
    inverse_ref,
    sums_ref,
    values,
    places,
):
    groups = source.shape[0]
    rows = 2 * groups
    ids = row_ids(rows)
    weights = row_weights(angular, rows, polars)

    peak = None
    for i in range(SIDE):
        entry = pl.ds((SIDE + 1) * i, 1)
        for f in range(angular.shape[0]):
            size = stiffness[entry, :] + angular[f] * sigma[...] * mass[entry, :]
            peak = size if peak is None else jnp.maximum(peak, size)
    peak = spread(peak * live[...].astype(jnp.float32), rows)
    scale = peak[:, :LANES]
    for c in range(LANES, peak.shape[-1], LANES):
        scale = jnp.maximum(scale, peak[:, c : c + LANES])
    scale = jnp.broadcast_to(jnp.max(scale, axis=1, keepdims=True), (rows, LANES))

    rim = order_ref.shape[-1]
    order = [spread(piece, rows) for piece in cut(order_ref)]
    above_order = spread(above_ref[groups : groups + 1, :], rim)
    slot = lax.broadcasted_iota(jnp.int32, (rim, rim), 0).astype(jnp.float32)
    match = jnp.where(above_order == slot, 1.0, 0.0).astype(jnp.bfloat16)
    numbers = lax.broadcasted_iota(jnp.int32, (2 * rows, rim), 1).astype(jnp.bfloat16)
    inverse = lax.dot_general(
        numbers, match, (((1,), (1,)), ((), ())), preferred_element_type=jnp.float32
    )[:rows].astype(jnp.int32)
    inverse_ref[...] = inverse
    inverse = [inverse[:, c : c + LANES] for c in range(0, rim, LANES)]

    own = [jnp.concatenate([piece, piece], axis=0) for piece in cut(source)]
    prior = cut(prior_ref)
    has_prior = spread(prior[0][groups : groups + 1], rows)
    field = joined(
        own, [doubled(x) for x in prior], [doubled(x) for x in cut(above_ref)], order, inverse
    )
    put_chunks(field_ref, field)
    image, quad = product(
        field,
        None,
        1.0 / scale,
        weights,
        edges,
        stiffness,
        mass,
        sigma,
        live,
        (values, places),
    )
    put_chunks(image_ref, image)
    count = rim // LANES
    first = ids < groups
    put_chunks(lower_ref, [jnp.where(first, x, scale) for x in image[:count]])
    put_chunks(upper_ref, [jnp.where(first, x, scale) for x in image[len(image) - count :]])
    sums = jnp.zeros((rows, LANES), jnp.float32)
    sums = put_lane(sums, 0, lane_sum(squares(field, count, has_prior)))
    sums = put_lane(sums, 1, lane_sum(quad))
    sums_ref[...] = jnp.where(first, sums, scale)


def later_stage(
    polars,
    step,
    last,
    angular,
    image_in,
    order_ref,
    inverse_ref,
    prior_ref,
    above_ref,
    sums_in,
    stiffness,
    mass,
    sigma,
    edges,
    live,
    field_ref,
    sums_ref,
    *rest,
):
    rows = image_in.shape[0]
    groups = rows // 2
    first = row_ids(rows) < groups
    weights = row_weights(angular, rows, polars)
    sums = sums_in[...]
    scale = jnp.where(first, swap_halves(sums), sums)
    inverse_scale = 1.0 / scale
    rim = order_ref.shape[-1]
    count = rim // LANES
    order = [spread(piece, rows) for piece in cut(order_ref)]
    inverse = cut(inverse_ref)

    def rescaled(block):
        ratio = swap_halves(block) * inverse_scale
        for _ in range(step):
            block = block * ratio
        return doubled(block)

    prior = cut(prior_ref)
    has_prior = jnp.where(first, swap_halves(prior[0]), prior[0])
    has_prior = jnp.where(has_prior > 0.0, 1.0, 0.0)
    field = joined(
        cut(image_in),
        [rescaled(x) for x in prior],
        [rescaled(x) for x in cut(above_ref)],
        order,
        inverse,
    )
    put_chunks(field_ref, field)
    image, quad = product(
        field,
        None,
        inverse_scale,
        weights,
        edges,
        stiffness,
        mass,
        sigma,
        live,
        None if last else (rest[4 - 1], rest[4]),
    )
    fresh = put_lane(sums, 2 * step, lane_sum(squares(field, count, has_prior)))
    fresh = put_lane(fresh, 2 * step + 1, lane_sum(quad))
    sums_ref[...] = jnp.where(first, fresh, scale)
    if not last:
        image_ref, lower_ref, upper_ref = rest[:3]
        put_chunks(image_ref, image)
        put_chunks(lower_ref, [jnp.where(first, x, scale) for x in image[:count]])
        put_chunks(upper_ref, [jnp.where(first, x, scale) for x in image[len(image) - count :]])


def gradient_stage(
    polars,
    angular,
    everyone,
    sums_in,
    field0,
    field1,
    field2,
    forward,
    mass,
    edges,
    live,
    term_ref,
):
    rows = field0.shape[0]
    groups = rows // 2
    first = row_ids(rows) < groups
    weights = jnp.where(first, row_weights(angular, rows, polars), 0.0)

    def scale_of(block):
        return jnp.where(first, swap_halves(block), block)

    parts = [everyone[q] for q in range(everyone.shape[0])]
    scales = [scale_of(block) for block in parts]
    top = functools.reduce(jnp.maximum, scales)
    lanes = lane_ids(rows)
    total = None
    for block, scale in zip(parts, scales):
        ratio = scale / top
        power = jnp.ones_like(ratio)
        factor = jnp.ones_like(ratio)
        for k in range(1, 6):
            power = power * ratio
            factor = jnp.where(lanes == k, power, factor)
        term = block * factor
        total = term if total is None else total + term
    m = [jnp.broadcast_to(total[:, k : k + 1], (rows, LANES)) for k in range(6)]
    l1 = m[2] / m[1]
    l2 = m[3] / m[1]
    d2 = m[3] - l1 * m[2]
    cross = m[4] - l2 * m[2]
    l3 = cross / d2
    d3 = m[5] - l2 * m[3] - l3 * cross
    y1 = m[1] - l1 * m[0]
    y2 = m[2] - l2 * m[0] - l3 * y1
    c2 = y2 / d3
    c1 = y1 / d2 - l3 * c2
    c0 = m[0] / m[1] - l1 * c1 - l2 * c2
    mine = scale_of(sums_in[...]) / top
    c0 = c0 / top
    c1 = c1 * mine / top
    c2 = c2 * mine * mine / top

    stacked = []
    for a, b, c, u in zip(cut(field0), cut(field1), cut(field2), cut(forward)):
        adjoint = c0 * a + c1 * b + c2 * c
        stacked.append(jnp.where(first, adjoint, jnp.concatenate([u, u], axis=0)))

    def body(s, carry):
        here = pl.ds(pl.multiple_of(s * LANES, LANES), LANES)
        picked = [
            pick_wide(stacked, spread(edges[pl.ds(j, 1), here], rows)) for j in range(SIDE)
        ]
        total = jnp.zeros((rows, LANES), jnp.float32)
        for i in range(SIDE):
            heavy = None
            for j in range(SIDE):
                one = spread(mass[pl.ds(SIDE * i + j, 1), here], rows) * picked[j]
                heavy = one if heavy is None else heavy + one
            total = total + picked[i] * swap_halves(heavy)
        term = jnp.sum(total * weights, axis=0, keepdims=True)
        term_ref[:, here] = -term * live[:, here].astype(jnp.float32)
        return carry

    lax.fori_loop(0, edges.shape[-1] // LANES, body, 0)


def call(kernel, arguments, outs, scratch=()):
    specs = [SMEM] + [VMEM] * (len(arguments) - 1)
    return pl.pallas_call(
        kernel,
        out_shape=outs,
        in_specs=specs,
        out_specs=jax.tree.map(lambda _: VMEM, outs),
        scratch_shapes=list(scratch),
        compiler_params=pltpu.CompilerParams(vmem_limit_bytes=24 * 1024 * 1024),
    )(*arguments)


def pass_along(block, distance):
    devices = range(lax.axis_size("dom"))
    route = [(i - distance, i) for i in devices if i - distance in devices]
    return lax.ppermute(block, "dom", route)


def gather_all(block, axis):
    size = lax.axis_size(axis)
    copies = jnp.broadcast_to(block[None], (size, *block.shape))
    return lax.all_to_all(copies, axis, 0, 0)


def local(
    angular,
    stiffness,
    mass_matrix,
    conductivity,
    element_edges,
    live_slots,
    adjoint_source,
    forward_field,
    neighbour_map,
):
    polars = adjoint_source.shape[1]
    groups = adjoint_source.shape[0] * polars
    rows = 2 * groups
    edge_count = adjoint_source.shape[-1]
    rim = neighbour_map.shape[-1]
    slots = element_edges.shape[-1]
    stiff, mass, edges = stiffness[0], mass_matrix[0], element_edges[0]
    source = adjoint_source.reshape(groups, edge_count)
    forward = forward_field.reshape(groups, edge_count)

    def shape(*dims, kind=jnp.float32):
        return jax.ShapeDtypeStruct(dims, kind)

    tables = (
        pltpu.VMEM((rows * edge_count // LANES, SIDE * slots), jnp.bfloat16),
        pltpu.VMEM((LANES, SIDE * slots), jnp.bfloat16),
    )
    elements = (stiff, mass, conductivity, edges, live_slots)
    field_shape, rim_shape = shape(rows, edge_count), shape(rows, rim)
    sums_shape = shape(rows, LANES)

    filler = jnp.ones((rows - groups - 1, rim), jnp.float32)
    down = jnp.concatenate([source[:, :rim], neighbour_map.astype(jnp.float32), filler], axis=0)
    up = jnp.concatenate(
        [source[:, edge_count - rim :], jnp.ones((rows - groups, rim), jnp.float32)], axis=0
    )
    above, prior = pass_along(down, -1), pass_along(up, 1)
    field0, image, lower, upper, inverse, sums = call(
        functools.partial(first_stage, polars),
        (angular, source, neighbour_map, prior, above, *elements),
        [
            field_shape,
            field_shape,
            rim_shape,
            rim_shape,
            shape(rows, rim, kind=jnp.int32),
            sums_shape,
        ],
        tables,
    )
    above, prior = pass_along(lower, -1), pass_along(upper, 1)
    field1, sums, image, lower, upper = call(
        functools.partial(later_stage, polars, 1, False),
        (angular, image, neighbour_map, inverse, prior, above, sums, *elements),
        [field_shape, sums_shape, field_shape, rim_shape, rim_shape],
        tables,
    )
    above, prior = pass_along(lower, -1), pass_along(upper, 1)
    field2, sums = call(
        functools.partial(later_stage, polars, 2, True),
        (angular, image, neighbour_map, inverse, prior, above, sums, *elements),
        [field_shape, sums_shape],
    )
    term = call(
        functools.partial(gradient_stage, polars),
        (
            angular,
            gather_all(sums, "dom"),
            sums,
            field0,
            field1,
            field2,
            forward,
            mass,
            edges,
            live_slots,
        ),
        shape(1, slots),
    )
    gradient = jnp.sum(gather_all(term, "freq"), axis=0)
    updated = conductivity * jnp.exp(-0.5 * jnp.tanh(gradient))
    return gradient, updated


def solution(mesh):
    return jax.shard_map(
        local,
        mesh=mesh,
        in_specs=(
            P("freq"),
            P("dom", None, None),
            P("dom", None, None),
            P("dom", None),
            P("dom", None, None),
            P("dom", None),
            P("freq", None, "dom", None),
            P("freq", None, "dom", None),
            P("dom", None),
        ),
        out_specs=(P("dom", None), P("dom", None)),
        check_vma=False,
    )
```

```python
import functools

import jax
import jax.numpy as jnp
from jax import lax
from jax.experimental import pallas as pl
from jax.experimental.pallas import tpu as pltpu
from jax.sharding import PartitionSpec as P

LANES = 128
SUBLANES = 8
SIDE = 6
VMEM = pl.BlockSpec(memory_space=pltpu.VMEM)
SMEM = pl.BlockSpec(memory_space=pltpu.SMEM)

PICK_LANES = lax.GatherDimensionNumbers(
    offset_dims=(),
    collapsed_slice_dims=(1,),
    start_index_map=(1,),
    operand_batching_dims=(0,),
    start_indices_batching_dims=(0,),
)


def pick_lanes(block, lanes):
    return lax.gather(
        block,
        lanes[..., None],
        PICK_LANES,
        (1, 1),
        mode=lax.GatherScatterMode.PROMISE_IN_BOUNDS,
    )


def pick_wide(chunks, index):
    lanes = index & (LANES - 1)
    high = index >> 7
    level = [pick_lanes(chunk, lanes) for chunk in chunks]
    bit = 0
    while len(level) > 1:
        odd = (high >> bit) & 1 == 1
        level = [
            jnp.where(odd, level[t + 1], level[t]) if t + 1 < len(level) else level[t]
            for t in range(0, len(level), 2)
        ]
        bit += 1
    return level[0]


def row_ids(rows):
    return lax.broadcasted_iota(jnp.int32, (rows, LANES), 0)


def lane_ids(rows):
    return lax.broadcasted_iota(jnp.int32, (rows, LANES), 1)


def spread(row, rows):
    return jnp.broadcast_to(row, (rows, row.shape[-1]))


def cut(ref):
    return [ref[:, c : c + LANES] for c in range(0, ref.shape[-1], LANES)]


def swap_halves(block):
    return pltpu.roll(block, block.shape[0] // 2, 0)


def doubled(block):
    half = block.shape[0] // 2
    return jnp.where(row_ids(2 * half) < half, block, swap_halves(block))


def lane_sum(block):
    return jnp.broadcast_to(jnp.sum(block, axis=1, keepdims=True), block.shape)


def put_lane(block, lane, value):
    return jnp.where(lane_ids(block.shape[0]) == lane, value, block)


def put_chunks(ref, chunks):
    for c, chunk in enumerate(chunks):
        ref[:, c * LANES : (c + 1) * LANES] = chunk


def is_even():
    return lax.rem(lax.axis_index("dom"), 2) == 0


def put_rims(across_ref, beside_ref, lower, upper):
    even = is_even()
    for c, (low, high) in enumerate(zip(lower, upper)):
        here = slice(c * LANES, (c + 1) * LANES)
        across_ref[:, here] = jnp.where(even, low, high)
        beside_ref[:, here] = jnp.where(even, high, low)


def take_rims(across_ref, beside_ref):
    even = is_even()
    pairs = list(zip(cut(across_ref), cut(beside_ref)))
    prior = [jnp.where(even, a, b) for a, b in pairs]
    above = [jnp.where(even, b, a) for a, b in pairs]
    return prior, above


def picks_of(rows_of_group, edges):
    chunks = [spread(row, edges.shape[1]) for row in rows_of_group]
    return [pick_wide(chunks, edges[j]) for j in range(SIDE)]


def group_rows(ref, g):
    return [ref[g : g + 1, c : c + LANES] for c in range(0, ref.shape[-1], LANES)]


def times_block(entries, base, picked):
    out = []
    for i in range(SIDE):
        total = None
        for j in range(SIDE):
            one = entries[base + SIDE * i + j] * picked[j]
            total = one if total is None else total + one
        out.append(total)
    return out


def weighted_sum(left, right):
    total = None
    for a, b in zip(left, right):
        total = a * b if total is None else total + a * b
    return total


def scatter(pieces, edges, places, count):
    depth = SIDE * edges.shape[1]
    rows = pieces.shape[0] // depth
    slots = edges.shape[1] * LANES
    total = None
    for i in range(SIDE):
        columns = []
        for s in range(edges.shape[1]):
            both = pieces[pl.ds(i * edges.shape[1] + s, rows, stride=depth), :]
            high = spread(edges[i, s : s + 1, :] >> 7, rows)
            stacked = [jnp.where(high == h, both, 0.0) for h in range(count)]
            columns.append(jnp.concatenate(stacked, axis=0).astype(jnp.bfloat16))
        part = lax.dot_general(
            jnp.concatenate(columns, axis=1),
            places[:, i * slots : (i + 1) * slots],
            (((1,), (1,)), ((), ())),
            preferred_element_type=jnp.float32,
        )
        total = part if total is None else total + part
    out = []
    for h in range(count):
        piece = total[rows * h : rows * (h + 1)]
        out.append(piece + swap_halves(piece))
    return out


def joined(own, from_prior, from_above, order, inverse):
    rim = len(from_prior)
    lower = [own[c] + pick_wide(from_prior, order[c]) for c in range(rim)]
    upper = [own[len(own) - rim + c] + pick_wide(from_above, inverse[c]) for c in range(rim)]
    return lower + own[rim : len(own) - rim] + upper


def squares(chunks, rim, has_prior):
    total = None
    for c, chunk in enumerate(chunks):
        term = chunk * chunk
        if c < rim:
            term = term * (1.0 - has_prior)
        total = term if total is None else total + term
    return total


def rims_stage(source, order_ref, across_ref, beside_ref, stacked_ref):
    groups = source.shape[0]
    rows = stacked_ref.shape[0]
    first = row_ids(rows) < groups
    chunks = []
    for c in range(0, source.shape[-1], LANES):
        piece = [source[g, :, c : c + LANES] for g in range(groups)]
        chunks.append(jnp.concatenate(piece + piece, axis=0))
    put_chunks(stacked_ref, chunks)
    order = [spread(piece.astype(jnp.float32), rows) for piece in cut(order_ref)]
    count = len(order)
    lower = [jnp.where(first, x, o) for x, o in zip(chunks[:count], order)]
    upper = [jnp.where(first, x, 1.0) for x in chunks[len(chunks) - count :]]
    put_rims(across_ref, beside_ref, lower, upper)


def table_stage(
    angular, stiffness, mass, sigma, live, edges, places_ref, blocks_ref, scale_ref
):
    rows = edges.shape[1]
    alive = live[...].astype(jnp.float32)
    weight = sigma[...]
    freqs = angular.shape[0]
    peak = None
    for i in range(SIDE):
        for f in range(freqs):
            entry = (SIDE + 1) * i
            size = stiffness[entry] + angular[f] * weight * mass[entry]
            peak = size if peak is None else jnp.maximum(peak, size)
    peak = jnp.max(peak * alive, axis=1, keepdims=True)
    scale = jnp.broadcast_to(jnp.max(peak, axis=0, keepdims=True), scale_ref.shape)
    scale_ref[...] = scale
    alive = alive / scale[:1, :1]
    for entry in range(SIDE * SIDE):
        stiff = stiffness[entry] * alive
        heavy = mass[entry] * (weight * alive)
        for f in range(freqs):
            blocks_ref[f * SIDE * SIDE + entry] = stiff + angular[f] * heavy
    numbers = row_ids(LANES)

    def body(i, carry):
        for s in range(rows):
            lanes = spread(edges[i, s : s + 1, :] & (LANES - 1), LANES)
            column = pl.ds(pl.multiple_of((i * rows + s) * LANES, LANES), LANES)
            places_ref[:, column] = jnp.where(lanes == numbers, 1.0, 0.0).astype(jnp.bfloat16)
        return carry

    lax.fori_loop(0, SIDE, body, 0)


def apply_all(field_ref, blocks, edges, polars, groups, pieces, visit):
    rows = field_ref.shape[0]
    depth = SIDE * edges.shape[1]
    forms = jnp.zeros((rows, LANES), jnp.float32)
    for g in range(groups):
        picked = picks_of(group_rows(field_ref, g), edges)
        visit(g, picked)
        values = times_block(blocks, (g // polars) * SIDE * SIDE, picked)
        form = jnp.sum(weighted_sum(picked, values), axis=0, keepdims=True)
        forms = jnp.where(row_ids(rows) == g, spread(form, rows), forms)
        if pieces is None:
            continue
        for i, value in enumerate(values):
            coarse = value.astype(jnp.bfloat16).astype(jnp.float32)
            for part, piece in enumerate((coarse, value - coarse)):
                at = (part * groups + g) * depth + i * edges.shape[1]
                pieces[at : at + edges.shape[1], :] = piece
    return lane_sum(forms)


def first_stage(
    polars,
    source,
    order_ref,
    across_in,
    beside_in,
    scale_in,
    blocks,
    edges,
    places,
    picks_ref,
    image_ref,
    across_ref,
    beside_ref,
    inverse_ref,
    sums_ref,
    field_ref,
    pieces,
):
    rows = source.shape[0]
    groups = rows // 2
    first = row_ids(rows) < groups
    scale = scale_in[...]
    prior, above = take_rims(across_in, beside_in)

    rim = order_ref.shape[-1]
    order = [spread(piece, rows) for piece in cut(order_ref)]
    above_order = spread(
        jnp.concatenate([x[groups : groups + 1] for x in above], axis=1), rim
    )
    slot = lax.broadcasted_iota(jnp.int32, (rim, rim), 0).astype(jnp.float32)
    match = jnp.where(above_order == slot, 1.0, 0.0).astype(jnp.bfloat16)
    numbers = lax.broadcasted_iota(jnp.int32, (2 * rows, rim), 1).astype(jnp.bfloat16)
    inverse = lax.dot_general(
        numbers, match, (((1,), (1,)), ((), ())), preferred_element_type=jnp.float32
    )[:rows].astype(jnp.int32)
    inverse_ref[...] = inverse
    inverse = [inverse[:, c : c + LANES] for c in range(0, rim, LANES)]

    has_prior = spread(prior[0][groups : groups + 1], rows)
    field = joined(
        cut(source), [doubled(x) for x in prior], [doubled(x) for x in above], order, inverse
    )
    put_chunks(field_ref, field)

    def visit(g, picked):
        for j in range(SIDE):
            picks_ref[g * SIDE + j] = picked[j]

    forms = apply_all(field_ref, blocks, edges, polars, groups, pieces, visit)
    image = scatter(pieces, edges, places, len(field))
    put_chunks(image_ref, image)
    count = rim // LANES
    put_rims(
        across_ref,
        beside_ref,
        [jnp.where(first, x, scale) for x in image[:count]],
        [jnp.where(first, x, scale) for x in image[len(image) - count :]],
    )
    sums = jnp.zeros((rows, LANES), jnp.float32)
    sums = put_lane(sums, 0, lane_sum(squares(field, count, has_prior)))
    sums = put_lane(sums, 1, forms)
    sums_ref[...] = jnp.where(first, sums, scale)


def later_stage(
    polars,
    step,
    last,
    image_in,
    order_ref,
    inverse_ref,
    across_in,
    beside_in,
    sums_in,
    blocks,
    edges,
    heavy,
    *rest,
):
    if last:
        terms_ref, sums_ref, field_ref = rest
        pieces = None
    else:
        places, terms_ref, sums_ref, image_ref, across_ref, beside_ref, field_ref, pieces = rest
    rows = image_in.shape[0]
    groups = rows // 2
    first = row_ids(rows) < groups
    sums = sums_in[...]
    scale = jnp.where(first, swap_halves(sums), sums)
    inverse_scale = 1.0 / scale
    rim = order_ref.shape[-1]
    count = rim // LANES
    order = [spread(piece, rows) for piece in cut(order_ref)]
    inverse = cut(inverse_ref)

    def rescaled(block):
        ratio = swap_halves(block) * inverse_scale
        for _ in range(step):
            block = block * ratio
        return doubled(block)

    prior, above = take_rims(across_in, beside_in)
    has_prior = jnp.where(first, swap_halves(prior[0]), prior[0])
    has_prior = jnp.where(has_prior > 0.0, 1.0, 0.0)
    field = joined(
        cut(image_in),
        [rescaled(x) for x in prior],
        [rescaled(x) for x in above],
        order,
        inverse,
    )
    put_chunks(field_ref, field)

    def visit(g, picked):
        terms_ref[g] = weighted_sum(picked, [heavy[g * SIDE + i] for i in range(SIDE)])

    forms = apply_all(field_ref, blocks, edges, polars, groups, pieces, visit)
    fresh = put_lane(sums, 2 * step, lane_sum(squares(field, count, has_prior)))
    fresh = put_lane(fresh, 2 * step + 1, forms)
    sums_ref[...] = jnp.where(first, fresh, scale)
    if not last:
        image = scatter(pieces, edges, places, len(field))
        put_chunks(image_ref, image)
        put_rims(
            across_ref,
            beside_ref,
            [jnp.where(first, x, scale) for x in image[:count]],
            [jnp.where(first, x, scale) for x in image[len(image) - count :]],
        )


def forward_stage(polars, angular, forward, mass, live, edges, picks, heavy_ref, terms_ref):
    dead = -live[...].astype(jnp.float32)
    for g in range(forward.shape[0]):
        rows = [forward[g, :, c : c + LANES] for c in range(0, forward.shape[-1], LANES)]
        values = times_block(mass, 0, picks_of(rows, edges))
        factor = dead * angular[g // polars]
        values = [factor * value for value in values]
        for i in range(SIDE):
            heavy_ref[g * SIDE + i] = values[i]
        terms_ref[g] = weighted_sum(values, [picks[g * SIDE + i] for i in range(SIDE)])


def combine_stage(everyone, sums_in, terms0, terms1, terms2, out_ref):
    rows = sums_in.shape[0]
    groups = rows // 2
    first = row_ids(rows) < groups

    def scale_of(block):
        return jnp.where(first, swap_halves(block), block)

    parts = [everyone[q] for q in range(everyone.shape[0])]
    scales = [scale_of(block) for block in parts]
    top = functools.reduce(jnp.maximum, scales)
    lanes = lane_ids(rows)
    inverse_top = 1.0 / top
    total = None
    for block, scale in zip(parts, scales):
        ratio = scale * inverse_top
        power = jnp.ones_like(ratio)
        factor = jnp.ones_like(ratio)
        for k in range(1, 6):
            power = power * ratio
            factor = jnp.where(lanes == k, power, factor)
        term = block * factor
        total = term if total is None else total + term
    m = [jnp.broadcast_to(total[:, k : k + 1], (rows, LANES)) for k in range(6)]
    l1 = m[2] / m[1]
    l2 = m[3] / m[1]
    d2 = m[3] - l1 * m[2]
    cross = m[4] - l2 * m[2]
    l3 = cross / d2
    d3 = m[5] - l2 * m[3] - l3 * cross
    y1 = m[1] - l1 * m[0]
    y2 = m[2] - l2 * m[0] - l3 * y1
    c2 = y2 / d3
    c1 = y1 / d2 - l3 * c2
    c0 = m[0] / m[1] - l1 * c1 - l2 * c2
    mine = scale_of(sums_in[...]) * inverse_top
    c0 = c0 * inverse_top
    c1 = c1 * mine * inverse_top
    c2 = c2 * mine * mine * inverse_top
    out = None
    for terms, c in ((terms0, c0), (terms1, c1), (terms2, c2)):
        for g in range(groups):
            one = terms[g] * spread(c[g : g + 1], out_ref.shape[0])
            out = one if out is None else out + one
    out_ref[...] = out


def call(kernel, arguments, outs, scratch=(), scalars=0, cost=0):
    return pl.pallas_call(
        kernel,
        out_shape=outs,
        in_specs=[SMEM] * scalars + [VMEM] * (len(arguments) - scalars),
        out_specs=jax.tree.map(lambda _: VMEM, outs),
        scratch_shapes=list(scratch),
        cost_estimate=pl.CostEstimate(flops=cost, bytes_accessed=cost, transcendentals=0),
        compiler_params=pltpu.CompilerParams(vmem_limit_bytes=16 * 1024 * 1024),
    )(*arguments)


def swap(block, axis, offset):
    size = lax.axis_size(axis)
    route = []
    for low in range(offset, size - 1, 2):
        route += [(low, low + 1), (low + 1, low)]
    return lax.ppermute(block, axis, route)


def gather_all(block, axis):
    size = lax.axis_size(axis)
    copies = jnp.broadcast_to(block[None], (size, *block.shape))
    return lax.all_to_all(copies, axis, 0, 0)


def sum_over(block, axis):
    size = lax.axis_size(axis)
    if size & (size - 1):
        return jnp.sum(gather_all(block, axis), axis=0)
    step = 1
    while step < size:
        block = block + lax.ppermute(block, axis, [(i, i ^ step) for i in range(size)])
        step *= 2
    return block


def local(
    angular,
    stiffness,
    mass_matrix,
    conductivity,
    element_edges,
    live_slots,
    adjoint_source,
    forward_field,
    neighbour_map,
):
    freqs = angular.shape[0]
    polars = adjoint_source.shape[1]
    groups = freqs * polars
    rows = 2 * groups
    edge_count = adjoint_source.shape[-1]
    rim = neighbour_map.shape[-1]
    slots = element_edges.shape[-1]
    tall = slots // LANES
    stiff = stiffness.reshape(SIDE * SIDE, tall, LANES)
    mass = mass_matrix.reshape(SIDE * SIDE, tall, LANES)
    edges = element_edges.reshape(SIDE, tall, LANES)
    sigma = conductivity.reshape(tall, LANES)
    live = live_slots.reshape(tall, LANES)
    source = adjoint_source.reshape(groups, 1, edge_count)
    forward = forward_field.reshape(groups, 1, edge_count)

    def shape(*dims, kind=jnp.float32):
        return jax.ShapeDtypeStruct(dims, kind)

    field_shape, rim_shape = shape(rows, edge_count), shape(rows, rim)
    sums_shape, terms_shape = shape(rows, LANES), shape(groups, tall, LANES)
    picks_shape = shape(groups * SIDE, tall, LANES)
    field_room = pltpu.VMEM((rows, edge_count), jnp.float32)
    piece_room = pltpu.VMEM((rows * SIDE * tall, LANES), jnp.float32)

    across, beside, source = call(
        rims_stage, (source, neighbour_map), [rim_shape, rim_shape, field_shape]
    )
    across, beside = swap(across, "dom", 1), swap(beside, "dom", 0)
    places, blocks, scale = call(
        table_stage,
        (angular, stiff, mass, sigma, live, edges),
        [
            shape(LANES, SIDE * slots, kind=jnp.bfloat16),
            shape(freqs * SIDE * SIDE, tall, LANES),
            sums_shape,
        ],
        scalars=1,
        cost=4_000_000,
    )
    picks, image, across, beside, inverse, sums = call(
        functools.partial(first_stage, polars),
        (source, neighbour_map, across, beside, scale, blocks, edges, places),
        [
            picks_shape,
            field_shape,
            rim_shape,
            rim_shape,
            shape(rows, rim, kind=jnp.int32),
            sums_shape,
        ],
        (field_room, piece_room),
    )
    across, beside = swap(across, "dom", 1), swap(beside, "dom", 0)
    heavy, terms0 = call(
        functools.partial(forward_stage, polars),
        (angular, forward, mass, live, edges, picks),
        [picks_shape, terms_shape],
        scalars=1,
        cost=4_000_000,
    )
    terms1, sums, image, across, beside = call(
        functools.partial(later_stage, polars, 1, False),
        (image, neighbour_map, inverse, across, beside, sums, blocks, edges, heavy, places),
        [terms_shape, sums_shape, field_shape, rim_shape, rim_shape],
        (field_room, piece_room),
    )
    across, beside = swap(across, "dom", 1), swap(beside, "dom", 0)
    terms2, sums = call(
        functools.partial(later_stage, polars, 2, True),
        (image, neighbour_map, inverse, across, beside, sums, blocks, edges, heavy),
        [terms_shape, sums_shape],
        (field_room,),
    )
    term = call(
        combine_stage,
        (gather_all(sums, "dom"), sums, terms0, terms1, terms2),
        shape(tall, LANES),
    )
    gradient = sum_over(term, "freq").reshape(1, slots)
    updated = conductivity * jnp.exp(-0.5 * jnp.tanh(gradient))
    return gradient, updated


def solution(mesh):
    return jax.shard_map(
        local,
        mesh=mesh,
        in_specs=(
            P("freq"),
            P("dom", None, None),
            P("dom", None, None),
            P("dom", None),
            P("dom", None, None),
            P("dom", None),
            P("freq", None, "dom", None),
            P("freq", None, "dom", None),
            P("dom", None),
        ),
        out_specs=(P("dom", None), P("dom", None)),
        check_vma=False,
    )
```

```python
import functools

import jax
import jax.numpy as jnp
from jax import lax
from jax.experimental import pallas as pl
from jax.experimental.pallas import tpu as pltpu
from jax.sharding import PartitionSpec as P

LANES = 128
SUBLANES = 8
SIDE = 6
VMEM = pl.BlockSpec(memory_space=pltpu.VMEM)
HBM = pl.BlockSpec(memory_space=pltpu.HBM)

PICK_LANES = lax.GatherDimensionNumbers(
    offset_dims=(),
    collapsed_slice_dims=(1,),
    start_index_map=(1,),
    operand_batching_dims=(0,),
    start_indices_batching_dims=(0,),
)


def pick_lanes(block, lanes):
    return lax.gather(
        block,
        lanes[..., None],
        PICK_LANES,
        (1, 1),
        mode=lax.GatherScatterMode.PROMISE_IN_BOUNDS,
    )


def pick_wide(chunks, index):
    lanes = index & (LANES - 1)
    high = index >> 7
    level = [pick_lanes(chunk, lanes) for chunk in chunks]
    bit = 0
    while len(level) > 1:
        odd = (high >> bit) & 1 == 1
        level = [
            jnp.where(odd, level[t + 1], level[t]) if t + 1 < len(level) else level[t]
            for t in range(0, len(level), 2)
        ]
        bit += 1
    return level[0]


def row_ids(rows):
    return lax.broadcasted_iota(jnp.int32, (rows, LANES), 0)


def lane_ids(rows):
    return lax.broadcasted_iota(jnp.int32, (rows, LANES), 1)


def spread(row, rows):
    return jnp.broadcast_to(row, (rows, row.shape[-1]))


def cut(ref):
    return [ref[:, c : c + LANES] for c in range(0, ref.shape[-1], LANES)]


def swap_halves(block):
    return pltpu.roll(block, block.shape[0] // 2, 0)


def doubled(block):
    half = block.shape[0] // 2
    return jnp.where(row_ids(2 * half) < half, block, swap_halves(block))


def lane_sum(block):
    return jnp.broadcast_to(jnp.sum(block, axis=1, keepdims=True), block.shape)


def put_lane(block, lane, value):
    return jnp.where(lane_ids(block.shape[0]) == lane, value, block)


def put_chunks(ref, chunks):
    for c, chunk in enumerate(chunks):
        ref[:, c * LANES : (c + 1) * LANES] = chunk


def is_even():
    return lax.rem(lax.axis_index("dom"), 2) == 0


def put_rims(across_ref, beside_ref, lower, upper):
    even = is_even()
    for c, (low, high) in enumerate(zip(lower, upper)):
        here = slice(c * LANES, (c + 1) * LANES)
        across_ref[:, here] = jnp.where(even, low, high)
        beside_ref[:, here] = jnp.where(even, high, low)


def take_rims(across_ref, beside_ref):
    even = is_even()
    pairs = list(zip(cut(across_ref), cut(beside_ref)))
    prior = [jnp.where(even, a, b) for a, b in pairs]
    above = [jnp.where(even, b, a) for a, b in pairs]
    return prior, above


def picks_of(rows_of_group, edges):
    chunks = [spread(row, edges.shape[1]) for row in rows_of_group]
    return [pick_wide(chunks, edges[j]) for j in range(SIDE)]


def group_rows(ref, g):
    return [ref[g : g + 1, c : c + LANES] for c in range(0, ref.shape[-1], LANES)]


def times_block(entries, base, picked):
    out = []
    for i in range(SIDE):
        total = None
        for j in range(SIDE):
            one = entries[base + SIDE * i + j] * picked[j]
            total = one if total is None else total + one
        out.append(total)
    return out


def weighted_sum(left, right):
    total = None
    for a, b in zip(left, right):
        total = a * b if total is None else total + a * b
    return total


def scatter(pieces, edges, places, count):
    depth = SIDE * edges.shape[1]
    rows = pieces.shape[0] // depth
    slots = edges.shape[1] * LANES
    total = None
    for i in range(SIDE):
        columns = []
        for s in range(edges.shape[1]):
            both = pieces[pl.ds(i * edges.shape[1] + s, rows, stride=depth), :]
            high = spread(edges[i, s : s + 1, :] >> 7, rows)
            stacked = [jnp.where(high == h, both, 0.0) for h in range(count)]
            columns.append(jnp.concatenate(stacked, axis=0).astype(jnp.bfloat16))
        part = lax.dot_general(
            jnp.concatenate(columns, axis=1),
            places[:, i * slots : (i + 1) * slots],
            (((1,), (1,)), ((), ())),
            preferred_element_type=jnp.float32,
        )
        total = part if total is None else total + part
    out = []
    for h in range(count):
        piece = total[rows * h : rows * (h + 1)]
        out.append(piece + swap_halves(piece))
    return out


def joined(own, from_prior, from_above, order, inverse):
    rim = len(from_prior)
    lower = [own[c] + pick_wide(from_prior, order[c]) for c in range(rim)]
    upper = [own[len(own) - rim + c] + pick_wide(from_above, inverse[c]) for c in range(rim)]
    return lower + own[rim : len(own) - rim] + upper


def squares(chunks, rim, has_prior):
    total = None
    for c, chunk in enumerate(chunks):
        term = chunk * chunk
        if c < rim:
            term = term * (1.0 - has_prior)
        total = term if total is None else total + term
    return total


def load_stage(
    angular_in,
    source_in,
    order_in,
    stiffness_in,
    mass_in,
    sigma_in,
    live_in,
    edges_in,
    forward_in,
    across_ref,
    beside_ref,
    stacked_ref,
    order_ref,
    rates_ref,
    stiffness_ref,
    mass_ref,
    sigma_ref,
    live_ref,
    edges_ref,
    forward_ref,
    angular,
    source,
    order,
    arrived,
):
    routes = (
        (source_in, source),
        (order_in, order),
        (angular_in, angular),
        (edges_in, edges_ref),
        (stiffness_in, stiffness_ref),
        (mass_in, mass_ref),
        (sigma_in, sigma_ref),
        (live_in, live_ref),
        (forward_in, forward_ref),
    )
    copies = [
        pltpu.make_async_copy(here, there, arrived.at[n])
        for n, (here, there) in enumerate(routes)
    ]
    for copy in copies:
        copy.start()
    for copy in copies[:2]:
        copy.wait()
    groups = source.shape[0]
    rows = stacked_ref.shape[0]
    first = row_ids(rows) < groups
    chunks = []
    for c in range(0, source.shape[-1], LANES):
        piece = [source[g, :, c : c + LANES] for g in range(groups)]
        chunks.append(jnp.concatenate(piece + piece, axis=0))
    put_chunks(stacked_ref, chunks)
    order_ref[...] = spread(order[...], rows)
    numbers = [x.astype(jnp.float32) for x in cut(order_ref)]
    count = len(numbers)
    lower = [jnp.where(first, x, o) for x, o in zip(chunks[:count], numbers)]
    upper = [jnp.where(first, x, 1.0) for x in chunks[len(chunks) - count :]]
    put_rims(across_ref, beside_ref, lower, upper)
    for copy in copies[2:]:
        copy.wait()
    for f in range(angular.shape[0]):
        rates_ref[f] = jnp.full(rates_ref.shape[1:], angular[f], jnp.float32)


def table_stage(
    rates, stiffness, mass, sigma, live, edges, places_ref, blocks_ref, scale_ref
):
    rows = edges.shape[1]
    alive = live[...].astype(jnp.float32)
    weight = sigma[...]
    freqs = rates.shape[0]
    peak = None
    for i in range(SIDE):
        for f in range(freqs):
            entry = (SIDE + 1) * i
            size = stiffness[entry] + rates[f] * weight * mass[entry]
            peak = size if peak is None else jnp.maximum(peak, size)
    peak = jnp.max(peak * alive, axis=1, keepdims=True)
    scale = jnp.broadcast_to(jnp.max(peak, axis=0, keepdims=True), scale_ref.shape)
    scale_ref[...] = scale
    alive = alive / scale[:1, :1]
    for entry in range(SIDE * SIDE):
        stiff = stiffness[entry] * alive
        heavy = mass[entry] * (weight * alive)
        for f in range(freqs):
            blocks_ref[f * SIDE * SIDE + entry] = stiff + rates[f] * heavy
    numbers = row_ids(LANES)

    def body(i, carry):
        for s in range(rows):
            lanes = spread(edges[i, s : s + 1, :] & (LANES - 1), LANES)
            column = pl.ds(pl.multiple_of((i * rows + s) * LANES, LANES), LANES)
            places_ref[:, column] = jnp.where(lanes == numbers, 1.0, 0.0).astype(jnp.bfloat16)
        return carry

    lax.fori_loop(0, SIDE, body, 0)


def apply_all(field_ref, blocks, edges, polars, groups, pieces, visit):
    rows = field_ref.shape[0]
    depth = SIDE * edges.shape[1]
    forms = jnp.zeros((rows, LANES), jnp.float32)
    for g in range(groups):
        picked = picks_of(group_rows(field_ref, g), edges)
        visit(g, picked)
        values = times_block(blocks, (g // polars) * SIDE * SIDE, picked)
        form = jnp.sum(weighted_sum(picked, values), axis=0, keepdims=True)
        forms = jnp.where(row_ids(rows) == g, spread(form, rows), forms)
        if pieces is None:
            continue
        for i, value in enumerate(values):
            coarse = value.astype(jnp.bfloat16).astype(jnp.float32)
            for part, piece in enumerate((coarse, value - coarse)):
                at = (part * groups + g) * depth + i * edges.shape[1]
                pieces[at : at + edges.shape[1], :] = piece
    return lane_sum(forms)


def first_stage(
    polars,
    source,
    order_ref,
    across_in,
    beside_in,
    scale_in,
    blocks,
    edges,
    places,
    picks_ref,
    image_ref,
    across_ref,
    beside_ref,
    inverse_ref,
    sums_ref,
    field_ref,
    pieces,
):
    rows = source.shape[0]
    groups = rows // 2
    first = row_ids(rows) < groups
    scale = scale_in[...]
    prior, above = take_rims(across_in, beside_in)

    rim = order_ref.shape[-1]
    order = cut(order_ref)
    above_order = spread(
        jnp.concatenate([x[groups : groups + 1] for x in above], axis=1), rim
    )
    slot = lax.broadcasted_iota(jnp.int32, (rim, rim), 0).astype(jnp.float32)
    match = jnp.where(above_order == slot, 1.0, 0.0).astype(jnp.bfloat16)
    numbers = lax.broadcasted_iota(jnp.int32, (2 * rows, rim), 1).astype(jnp.bfloat16)
    inverse = lax.dot_general(
        numbers, match, (((1,), (1,)), ((), ())), preferred_element_type=jnp.float32
    )[:rows].astype(jnp.int32)
    inverse_ref[...] = inverse
    inverse = [inverse[:, c : c + LANES] for c in range(0, rim, LANES)]

    has_prior = spread(prior[0][groups : groups + 1], rows)
    field = joined(
        cut(source), [doubled(x) for x in prior], [doubled(x) for x in above], order, inverse
    )
    put_chunks(field_ref, field)

    def visit(g, picked):
        for j in range(SIDE):
            picks_ref[g * SIDE + j] = picked[j]

    forms = apply_all(field_ref, blocks, edges, polars, groups, pieces, visit)
    image = scatter(pieces, edges, places, len(field))
    put_chunks(image_ref, image)
    count = rim // LANES
    put_rims(
        across_ref,
        beside_ref,
        [jnp.where(first, x, scale) for x in image[:count]],
        [jnp.where(first, x, scale) for x in image[len(image) - count :]],
    )
    sums = jnp.zeros((rows, LANES), jnp.float32)
    sums = put_lane(sums, 0, lane_sum(squares(field, count, has_prior)))
    sums = put_lane(sums, 1, forms)
    sums_ref[...] = jnp.where(first, sums, scale)


def later_stage(
    polars,
    step,
    last,
    image_in,
    order_ref,
    inverse_ref,
    across_in,
    beside_in,
    sums_in,
    blocks,
    edges,
    heavy,
    *rest,
):
    if last:
        terms_ref, sums_ref, field_ref = rest
        pieces = None
    else:
        places, terms_ref, sums_ref, image_ref, across_ref, beside_ref, field_ref, pieces = rest
    rows = image_in.shape[0]
    groups = rows // 2
    first = row_ids(rows) < groups
    sums = sums_in[...]
    scale = jnp.where(first, swap_halves(sums), sums)
    inverse_scale = 1.0 / scale
    rim = order_ref.shape[-1]
    count = rim // LANES
    order = cut(order_ref)
    inverse = cut(inverse_ref)

    def rescaled(block):
        ratio = swap_halves(block) * inverse_scale
        for _ in range(step):
            block = block * ratio
        return doubled(block)

    prior, above = take_rims(across_in, beside_in)
    has_prior = jnp.where(first, swap_halves(prior[0]), prior[0])
    has_prior = jnp.where(has_prior > 0.0, 1.0, 0.0)
    field = joined(
        cut(image_in),
        [rescaled(x) for x in prior],
        [rescaled(x) for x in above],
        order,
        inverse,
    )
    put_chunks(field_ref, field)

    def visit(g, picked):
        terms_ref[g] = weighted_sum(picked, [heavy[g * SIDE + i] for i in range(SIDE)])

    forms = apply_all(field_ref, blocks, edges, polars, groups, pieces, visit)
    fresh = put_lane(sums, 2 * step, lane_sum(squares(field, count, has_prior)))
    fresh = put_lane(fresh, 2 * step + 1, forms)
    sums_ref[...] = jnp.where(first, fresh, scale)
    if not last:
        image = scatter(pieces, edges, places, len(field))
        put_chunks(image_ref, image)
        put_rims(
            across_ref,
            beside_ref,
            [jnp.where(first, x, scale) for x in image[:count]],
            [jnp.where(first, x, scale) for x in image[len(image) - count :]],
        )


def forward_stage(polars, rates, forward, mass, live, edges, picks, heavy_ref, terms_ref):
    dead = -live[...].astype(jnp.float32)
    for g in range(forward.shape[0]):
        rows = [forward[g, :, c : c + LANES] for c in range(0, forward.shape[-1], LANES)]
        values = times_block(mass, 0, picks_of(rows, edges))
        factor = dead * rates[g // polars]
        values = [factor * value for value in values]
        for i in range(SIDE):
            heavy_ref[g * SIDE + i] = values[i]
        terms_ref[g] = weighted_sum(values, [picks[g * SIDE + i] for i in range(SIDE)])


def combine_stage(everyone, sums_in, terms0, terms1, terms2, out_ref):
    rows = sums_in.shape[0]
    groups = rows // 2
    first = row_ids(rows) < groups

    def scale_of(block):
        return jnp.where(first, swap_halves(block), block)

    parts = [everyone[q] for q in range(everyone.shape[0])]
    scales = [scale_of(block) for block in parts]
    top = functools.reduce(jnp.maximum, scales)
    lanes = lane_ids(rows)
    inverse_top = 1.0 / top
    total = None
    for block, scale in zip(parts, scales):
        ratio = scale * inverse_top
        power = jnp.ones_like(ratio)
        factor = jnp.ones_like(ratio)
        for k in range(1, 6):
            power = power * ratio
            factor = jnp.where(lanes == k, power, factor)
        term = block * factor
        total = term if total is None else total + term
    m = [jnp.broadcast_to(total[:, k : k + 1], (rows, LANES)) for k in range(6)]
    l1 = m[2] / m[1]
    l2 = m[3] / m[1]
    d2 = m[3] - l1 * m[2]
    cross = m[4] - l2 * m[2]
    l3 = cross / d2
    d3 = m[5] - l2 * m[3] - l3 * cross
    y1 = m[1] - l1 * m[0]
    y2 = m[2] - l2 * m[0] - l3 * y1
    c2 = y2 / d3
    c1 = y1 / d2 - l3 * c2
    c0 = m[0] / m[1] - l1 * c1 - l2 * c2
    mine = scale_of(sums_in[...]) * inverse_top
    c0 = c0 * inverse_top
    c1 = c1 * mine * inverse_top
    c2 = c2 * mine * mine * inverse_top
    out = None
    for terms, c in ((terms0, c0), (terms1, c1), (terms2, c2)):
        for g in range(groups):
            one = terms[g] * spread(c[g : g + 1], out_ref.shape[0])
            out = one if out is None else out + one
    out_ref[...] = out


def call(kernel, arguments, outs, scratch=(), space=VMEM, cost=0):
    return pl.pallas_call(
        kernel,
        out_shape=outs,
        in_specs=[space] * len(arguments),
        out_specs=jax.tree.map(lambda _: VMEM, outs),
        scratch_shapes=list(scratch),
        cost_estimate=pl.CostEstimate(flops=cost, bytes_accessed=cost, transcendentals=0),
        compiler_params=pltpu.CompilerParams(vmem_limit_bytes=16 * 1024 * 1024),
    )(*arguments)


def swap(block, axis, offset):
    size = lax.axis_size(axis)
    route = []
    for low in range(offset, size - 1, 2):
        route += [(low, low + 1), (low + 1, low)]
    return lax.ppermute(block, axis, route)


def gather_all(block, axis):
    size = lax.axis_size(axis)
    copies = jnp.broadcast_to(block[None], (size, *block.shape))
    return lax.all_to_all(copies, axis, 0, 0)


def sum_over(block, axis):
    size = lax.axis_size(axis)
    if size & (size - 1):
        return jnp.sum(gather_all(block, axis), axis=0)
    step = 1
    while step < size:
        block = block + lax.ppermute(block, axis, [(i, i ^ step) for i in range(size)])
        step *= 2
    return block


def local(
    angular,
    stiffness,
    mass_matrix,
    conductivity,
    element_edges,
    live_slots,
    adjoint_source,
    forward_field,
    neighbour_map,
):
    freqs = angular.shape[0]
    polars = adjoint_source.shape[1]
    groups = freqs * polars
    rows = 2 * groups
    edge_count = adjoint_source.shape[-1]
    rim = neighbour_map.shape[-1]
    slots = element_edges.shape[-1]
    tall = slots // LANES
    stiff = stiffness.reshape(SIDE * SIDE, tall, LANES)
    mass = mass_matrix.reshape(SIDE * SIDE, tall, LANES)
    edges = element_edges.reshape(SIDE, tall, LANES)
    sigma = conductivity.reshape(tall, LANES)
    live = live_slots.reshape(tall, LANES)
    source = adjoint_source.reshape(groups, 1, edge_count)
    forward = forward_field.reshape(groups, 1, edge_count)

    def shape(*dims, kind=jnp.float32):
        return jax.ShapeDtypeStruct(dims, kind)

    field_shape, rim_shape = shape(rows, edge_count), shape(rows, rim)
    sums_shape, terms_shape = shape(rows, LANES), shape(groups, tall, LANES)
    picks_shape = shape(groups * SIDE, tall, LANES)
    field_room = pltpu.VMEM((rows, edge_count), jnp.float32)
    piece_room = pltpu.VMEM((rows * SIDE * tall, LANES), jnp.float32)

    arguments = (
        angular,
        source,
        neighbour_map,
        stiff,
        mass,
        sigma,
        live,
        edges,
        forward,
    )
    arguments = [pltpu.with_memory_space_constraint(x, pltpu.HBM) for x in arguments]
    kept = [jax.ShapeDtypeStruct(x.shape, x.dtype) for x in arguments[3:]]
    across, beside, source, order, rates, stiff, mass, sigma, live, edges, forward = call(
        load_stage,
        arguments,
        [
            rim_shape,
            rim_shape,
            field_shape,
            shape(rows, rim, kind=jnp.int32),
            shape(freqs, tall, LANES),
            *kept,
        ],
        (
            pltpu.SMEM(angular.shape, angular.dtype),
            pltpu.VMEM(source.shape, source.dtype),
            pltpu.VMEM(neighbour_map.shape, neighbour_map.dtype),
            pltpu.SemaphoreType.DMA((len(arguments),)),
        ),
        space=HBM,
    )
    across, beside = swap(across, "dom", 1), swap(beside, "dom", 0)
    places, blocks, scale = call(
        table_stage,
        (rates, stiff, mass, sigma, live, edges),
        [
            shape(LANES, SIDE * slots, kind=jnp.bfloat16),
            shape(freqs * SIDE * SIDE, tall, LANES),
            sums_shape,
        ],
        cost=4_000_000,
    )
    picks, image, across, beside, inverse, sums = call(
        functools.partial(first_stage, polars),
        (source, order, across, beside, scale, blocks, edges, places),
        [
            picks_shape,
            field_shape,
            rim_shape,
            rim_shape,
            shape(rows, rim, kind=jnp.int32),
            sums_shape,
        ],
        (field_room, piece_room),
    )
    across, beside = swap(across, "dom", 1), swap(beside, "dom", 0)
    heavy, terms0 = call(
        functools.partial(forward_stage, polars),
        (rates, forward, mass, live, edges, picks),
        [picks_shape, terms_shape],
        cost=4_000_000,
    )
    terms1, sums, image, across, beside = call(
        functools.partial(later_stage, polars, 1, False),
        (image, order, inverse, across, beside, sums, blocks, edges, heavy, places),
        [terms_shape, sums_shape, field_shape, rim_shape, rim_shape],
        (field_room, piece_room),
    )
    across, beside = swap(across, "dom", 1), swap(beside, "dom", 0)
    terms2, sums = call(
        functools.partial(later_stage, polars, 2, True),
        (image, order, inverse, across, beside, sums, blocks, edges, heavy),
        [terms_shape, sums_shape],
        (field_room,),
    )
    term = call(
        combine_stage,
        (gather_all(sums, "dom"), sums, terms0, terms1, terms2),
        shape(tall, LANES),
    )
    gradient = sum_over(term, "freq").reshape(1, slots)
    updated = sigma.reshape(1, slots) * jnp.exp(-0.5 * jnp.tanh(gradient))
    return gradient, updated


def solution(mesh):
    return jax.shard_map(
        local,
        mesh=mesh,
        in_specs=(
            P("freq"),
            P("dom", None, None),
            P("dom", None, None),
            P("dom", None),
            P("dom", None, None),
            P("dom", None),
            P("freq", None, "dom", None),
            P("freq", None, "dom", None),
            P("dom", None),
        ),
        out_specs=(P("dom", None), P("dom", None)),
        check_vma=False,
    )
```

```python
import functools

import jax
import jax.numpy as jnp
from jax import lax
from jax.experimental import pallas as pl
from jax.experimental.pallas import tpu as pltpu
from jax.sharding import PartitionSpec as P

LANES = 128
SUBLANES = 8
SIDE = 6
VMEM = pl.BlockSpec(memory_space=pltpu.VMEM)
HBM = pl.BlockSpec(memory_space=pltpu.HBM)

PICK_LANES = lax.GatherDimensionNumbers(
    offset_dims=(),
    collapsed_slice_dims=(1,),
    start_index_map=(1,),
    operand_batching_dims=(0,),
    start_indices_batching_dims=(0,),
)


def pick_lanes(block, lanes):
    return lax.gather(
        block,
        lanes[..., None],
        PICK_LANES,
        (1, 1),
        mode=lax.GatherScatterMode.PROMISE_IN_BOUNDS,
    )


def pick_wide(chunks, index):
    lanes = index & (LANES - 1)
    high = index >> 7
    level = [pick_lanes(chunk, lanes) for chunk in chunks]
    bit = 0
    while len(level) > 1:
        odd = (high >> bit) & 1 == 1
        level = [
            jnp.where(odd, level[t + 1], level[t]) if t + 1 < len(level) else level[t]
            for t in range(0, len(level), 2)
        ]
        bit += 1
    return level[0]


def row_ids(rows):
    return lax.broadcasted_iota(jnp.int32, (rows, LANES), 0)


def lane_ids(rows):
    return lax.broadcasted_iota(jnp.int32, (rows, LANES), 1)


def spread(row, rows):
    return jnp.broadcast_to(row, (rows, row.shape[-1]))


def cut(ref):
    return [ref[:, c : c + LANES] for c in range(0, ref.shape[-1], LANES)]


def swap_halves(block):
    return pltpu.roll(block, block.shape[0] // 2, 0)


def doubled(block):
    half = block.shape[0] // 2
    return jnp.where(row_ids(2 * half) < half, block, swap_halves(block))


def lane_sum(block):
    return jnp.broadcast_to(jnp.sum(block, axis=1, keepdims=True), block.shape)


def put_lane(block, lane, value):
    return jnp.where(lane_ids(block.shape[0]) == lane, value, block)


def put_chunks(ref, chunks):
    for c, chunk in enumerate(chunks):
        ref[:, c * LANES : (c + 1) * LANES] = chunk


def is_even():
    return lax.rem(lax.axis_index("dom"), 2) == 0


def put_rims(across_ref, beside_ref, lower, upper):
    even = is_even()
    for c, (low, high) in enumerate(zip(lower, upper)):
        here = slice(c * LANES, (c + 1) * LANES)
        across_ref[:, here] = jnp.where(even, low, high)
        beside_ref[:, here] = jnp.where(even, high, low)


def take_rims(across_ref, beside_ref):
    even = is_even()
    pairs = list(zip(cut(across_ref), cut(beside_ref)))
    prior = [jnp.where(even, a, b) for a, b in pairs]
    above = [jnp.where(even, b, a) for a, b in pairs]
    return prior, above


def picks_of(rows_of_group, edges):
    chunks = [spread(row, edges.shape[1]) for row in rows_of_group]
    return [pick_wide(chunks, edges[j]) for j in range(SIDE)]


def group_rows(ref, g):
    return [ref[g : g + 1, c : c + LANES] for c in range(0, ref.shape[-1], LANES)]


def times_block(entries, base, picked):
    out = []
    for i in range(SIDE):
        total = None
        for j in range(SIDE):
            one = entries[base + SIDE * i + j] * picked[j]
            total = one if total is None else total + one
        out.append(total)
    return out


def weighted_sum(left, right):
    total = None
    for a, b in zip(left, right):
        total = a * b if total is None else total + a * b
    return total


def scatter(pieces, edges, places, count):
    depth = SIDE * edges.shape[1]
    rows = pieces.shape[0] // depth
    slots = edges.shape[1] * LANES
    total = None
    for i in range(SIDE):
        columns = []
        for s in range(edges.shape[1]):
            both = pieces[pl.ds(i * edges.shape[1] + s, rows, stride=depth), :]
            high = spread(edges[i, s : s + 1, :] >> 7, rows)
            stacked = [jnp.where(high == h, both, 0.0) for h in range(count)]
            columns.append(jnp.concatenate(stacked, axis=0).astype(jnp.bfloat16))
        part = lax.dot_general(
            jnp.concatenate(columns, axis=1),
            places[:, i * slots : (i + 1) * slots],
            (((1,), (1,)), ((), ())),
            preferred_element_type=jnp.float32,
        )
        total = part if total is None else total + part
    out = []
    for h in range(count):
        piece = total[rows * h : rows * (h + 1)]
        out.append(piece + swap_halves(piece))
    return out


def joined(own, from_prior, from_above, order, inverse):
    rim = len(from_prior)
    lower = [own[c] + pick_wide(from_prior, order[c]) for c in range(rim)]
    upper = [own[len(own) - rim + c] + pick_wide(from_above, inverse[c]) for c in range(rim)]
    return lower + own[rim : len(own) - rim] + upper


def squares(chunks, rim, has_prior):
    total = None
    for c, chunk in enumerate(chunks):
        term = chunk * chunk
        if c < rim:
            term = term * (1.0 - has_prior)
        total = term if total is None else total + term
    return total


def load_stage(
    angular_in,
    source_in,
    order_in,
    stiffness_in,
    mass_in,
    sigma_in,
    live_in,
    edges_in,
    forward_in,
    across_ref,
    beside_ref,
    stacked_ref,
    order_ref,
    rates_ref,
    stiffness_ref,
    mass_ref,
    sigma_ref,
    live_ref,
    edges_ref,
    forward_ref,
    angular,
    source,
    order,
    arrived,
):
    routes = (
        (source_in, source),
        (order_in, order),
        (angular_in, angular),
        (edges_in, edges_ref),
        (stiffness_in, stiffness_ref),
        (mass_in, mass_ref),
        (sigma_in, sigma_ref),
        (live_in, live_ref),
        (forward_in, forward_ref),
    )
    copies = [
        pltpu.make_async_copy(here, there, arrived.at[n])
        for n, (here, there) in enumerate(routes)
    ]
    for copy in copies:
        copy.start()
    for copy in copies[:2]:
        copy.wait()
    groups = source.shape[0]
    rows = stacked_ref.shape[0]
    first = row_ids(rows) < groups
    chunks = []
    for c in range(0, source.shape[-1], LANES):
        piece = [source[g, :, c : c + LANES] for g in range(groups)]
        chunks.append(jnp.concatenate(piece + piece, axis=0))
    put_chunks(stacked_ref, chunks)
    order_ref[...] = spread(order[...], rows)
    numbers = [x.astype(jnp.float32) for x in cut(order_ref)]
    count = len(numbers)
    lower = [jnp.where(first, x, o) for x, o in zip(chunks[:count], numbers)]
    upper = [jnp.where(first, x, 1.0) for x in chunks[len(chunks) - count :]]
    put_rims(across_ref, beside_ref, lower, upper)
    for copy in copies[2:]:
        copy.wait()
    for f in range(angular.shape[0]):
        rates_ref[f] = jnp.full(rates_ref.shape[1:], angular[f], jnp.float32)


def table_stage(
    rates, stiffness, mass, sigma, live, edges, places_ref, blocks_ref, scale_ref
):
    rows = edges.shape[1]
    alive = live[...].astype(jnp.float32)
    weight = sigma[...]
    freqs = rates.shape[0]
    peak = None
    for i in range(SIDE):
        for f in range(freqs):
            entry = (SIDE + 1) * i
            size = stiffness[entry] + rates[f] * weight * mass[entry]
            peak = size if peak is None else jnp.maximum(peak, size)
    peak = jnp.max(peak * alive, axis=1, keepdims=True)
    scale = jnp.broadcast_to(jnp.max(peak, axis=0, keepdims=True), scale_ref.shape)
    scale_ref[...] = scale
    alive = alive / scale[:1, :1]
    for entry in range(SIDE * SIDE):
        stiff = stiffness[entry] * alive
        heavy = mass[entry] * (weight * alive)
        for f in range(freqs):
            blocks_ref[f * SIDE * SIDE + entry] = stiff + rates[f] * heavy
    numbers = row_ids(LANES)

    def body(i, carry):
        for s in range(rows):
            lanes = spread(edges[i, s : s + 1, :] & (LANES - 1), LANES)
            column = pl.ds(pl.multiple_of((i * rows + s) * LANES, LANES), LANES)
            places_ref[:, column] = jnp.where(lanes == numbers, 1.0, 0.0).astype(jnp.bfloat16)
        return carry

    lax.fori_loop(0, SIDE, body, 0)


def apply_all(field_ref, blocks, edges, polars, groups, pieces, visit):
    rows = field_ref.shape[0]
    depth = SIDE * edges.shape[1]
    forms = jnp.zeros((rows, LANES), jnp.float32)
    for g in range(groups):
        picked = picks_of(group_rows(field_ref, g), edges)
        visit(g, picked)
        values = times_block(blocks, (g // polars) * SIDE * SIDE, picked)
        form = jnp.sum(weighted_sum(picked, values), axis=0, keepdims=True)
        forms = jnp.where(row_ids(rows) == g, spread(form, rows), forms)
        if pieces is None:
            continue
        for i, value in enumerate(values):
            coarse = value.astype(jnp.bfloat16).astype(jnp.float32)
            for part, piece in enumerate((coarse, value - coarse)):
                at = (part * groups + g) * depth + i * edges.shape[1]
                pieces[at : at + edges.shape[1], :] = piece
    return lane_sum(forms)


def first_stage(
    polars,
    source,
    order_ref,
    across_in,
    beside_in,
    scale_in,
    blocks,
    edges,
    places,
    picks_ref,
    image_ref,
    across_ref,
    beside_ref,
    inverse_ref,
    sums_ref,
    field_ref,
    pieces,
):
    rows = source.shape[0]
    groups = rows // 2
    first = row_ids(rows) < groups
    scale = scale_in[...]
    prior, above = take_rims(across_in, beside_in)

    rim = order_ref.shape[-1]
    order = cut(order_ref)
    above_order = spread(
        jnp.concatenate([x[groups : groups + 1] for x in above], axis=1), rim
    )
    slot = lax.broadcasted_iota(jnp.int32, (rim, rim), 0).astype(jnp.float32)
    match = jnp.where(above_order == slot, 1.0, 0.0).astype(jnp.bfloat16)
    numbers = lax.broadcasted_iota(jnp.int32, (2 * rows, rim), 1).astype(jnp.bfloat16)
    inverse = lax.dot_general(
        numbers, match, (((1,), (1,)), ((), ())), preferred_element_type=jnp.float32
    )[:rows].astype(jnp.int32)
    inverse_ref[...] = inverse
    inverse = [inverse[:, c : c + LANES] for c in range(0, rim, LANES)]

    has_prior = spread(prior[0][groups : groups + 1], rows)
    field = joined(
        cut(source), [doubled(x) for x in prior], [doubled(x) for x in above], order, inverse
    )
    put_chunks(field_ref, field)

    def visit(g, picked):
        for j in range(SIDE):
            picks_ref[g * SIDE + j] = picked[j]

    forms = apply_all(field_ref, blocks, edges, polars, groups, pieces, visit)
    image = scatter(pieces, edges, places, len(field))
    put_chunks(image_ref, image)
    count = rim // LANES
    put_rims(
        across_ref,
        beside_ref,
        [jnp.where(first, x, scale) for x in image[:count]],
        [jnp.where(first, x, scale) for x in image[len(image) - count :]],
    )
    sums = jnp.zeros((rows, LANES), jnp.float32)
    sums = put_lane(sums, 0, lane_sum(squares(field, count, has_prior)))
    sums = put_lane(sums, 1, forms)
    sums_ref[...] = jnp.where(first, sums, scale)


def later_stage(
    polars,
    step,
    last,
    image_in,
    order_ref,
    inverse_ref,
    across_in,
    beside_in,
    sums_in,
    blocks,
    edges,
    heavy,
    *rest,
):
    if last:
        terms_ref, sums_ref, field_ref = rest
        pieces = None
    else:
        places, terms_ref, sums_ref, image_ref, across_ref, beside_ref, field_ref, pieces = rest
    rows = image_in.shape[0]
    groups = rows // 2
    first = row_ids(rows) < groups
    sums = sums_in[...]
    scale = jnp.where(first, swap_halves(sums), sums)
    inverse_scale = 1.0 / scale
    rim = order_ref.shape[-1]
    count = rim // LANES
    order = cut(order_ref)
    inverse = cut(inverse_ref)

    def rescaled(block):
        ratio = swap_halves(block) * inverse_scale
        for _ in range(step):
            block = block * ratio
        return doubled(block)

    prior, above = take_rims(across_in, beside_in)
    has_prior = jnp.where(first, swap_halves(prior[0]), prior[0])
    has_prior = jnp.where(has_prior > 0.0, 1.0, 0.0)
    field = joined(
        cut(image_in),
        [rescaled(x) for x in prior],
        [rescaled(x) for x in above],
        order,
        inverse,
    )
    put_chunks(field_ref, field)

    def visit(g, picked):
        terms_ref[g] = weighted_sum(picked, [heavy[g * SIDE + i] for i in range(SIDE)])

    forms = apply_all(field_ref, blocks, edges, polars, groups, pieces, visit)
    fresh = put_lane(sums, 2 * step, lane_sum(squares(field, count, has_prior)))
    fresh = put_lane(fresh, 2 * step + 1, forms)
    sums_ref[...] = jnp.where(first, fresh, scale)
    if not last:
        image = scatter(pieces, edges, places, len(field))
        put_chunks(image_ref, image)
        put_rims(
            across_ref,
            beside_ref,
            [jnp.where(first, x, scale) for x in image[:count]],
            [jnp.where(first, x, scale) for x in image[len(image) - count :]],
        )


def forward_stage(polars, rates, forward, mass, live, edges, picks, heavy_ref, terms_ref):
    dead = -live[...].astype(jnp.float32)
    for g in range(forward.shape[0]):
        rows = [forward[g, :, c : c + LANES] for c in range(0, forward.shape[-1], LANES)]
        values = times_block(mass, 0, picks_of(rows, edges))
        factor = dead * rates[g // polars]
        values = [factor * value for value in values]
        for i in range(SIDE):
            heavy_ref[g * SIDE + i] = values[i]
        terms_ref[g] = weighted_sum(values, [picks[g * SIDE + i] for i in range(SIDE)])


def combine_stage(everyone, sums_in, terms0, terms1, terms2, out_ref):
    rows = sums_in.shape[0]
    groups = rows // 2
    first = row_ids(rows) < groups

    def scale_of(block):
        return jnp.where(first, swap_halves(block), block)

    parts = [everyone[q] for q in range(everyone.shape[0])]
    scales = [scale_of(block) for block in parts]
    top = functools.reduce(jnp.maximum, scales)
    lanes = lane_ids(rows)
    inverse_top = 1.0 / top
    total = None
    for block, scale in zip(parts, scales):
        ratio = scale * inverse_top
        power = jnp.ones_like(ratio)
        factor = jnp.ones_like(ratio)
        for k in range(1, 6):
            power = power * ratio
            factor = jnp.where(lanes == k, power, factor)
        term = block * factor
        total = term if total is None else total + term
    m = [jnp.broadcast_to(total[:, k : k + 1], (rows, LANES)) for k in range(6)]
    l1 = m[2] / m[1]
    l2 = m[3] / m[1]
    d2 = m[3] - l1 * m[2]
    cross = m[4] - l2 * m[2]
    l3 = cross / d2
    d3 = m[5] - l2 * m[3] - l3 * cross
    y1 = m[1] - l1 * m[0]
    y2 = m[2] - l2 * m[0] - l3 * y1
    c2 = y2 / d3
    c1 = y1 / d2 - l3 * c2
    c0 = m[0] / m[1] - l1 * c1 - l2 * c2
    mine = scale_of(sums_in[...]) * inverse_top
    c0 = c0 * inverse_top
    c1 = c1 * mine * inverse_top
    c2 = c2 * mine * mine * inverse_top
    out = None
    for terms, c in ((terms0, c0), (terms1, c1), (terms2, c2)):
        for g in range(groups):
            one = terms[g] * spread(c[g : g + 1], out_ref.shape[0])
            out = one if out is None else out + one
    out_ref[...] = out


def call(kernel, arguments, outs, scratch=(), space=VMEM, cost=0):
    return pl.pallas_call(
        kernel,
        out_shape=outs,
        in_specs=[space] * len(arguments),
        out_specs=jax.tree.map(lambda _: VMEM, outs),
        scratch_shapes=list(scratch),
        cost_estimate=pl.CostEstimate(flops=cost, bytes_accessed=cost, transcendentals=0),
        compiler_params=pltpu.CompilerParams(vmem_limit_bytes=16 * 1024 * 1024),
    )(*arguments)


def swap(block, axis, offset):
    size = lax.axis_size(axis)
    route = []
    for low in range(offset, size - 1, 2):
        route += [(low, low + 1), (low + 1, low)]
    return lax.ppermute(block, axis, route)


def sum_over(block, axis):
    return jnp.sum(lax.all_gather(block, axis), axis=0)


def local(
    angular,
    stiffness,
    mass_matrix,
    conductivity,
    element_edges,
    live_slots,
    adjoint_source,
    forward_field,
    neighbour_map,
):
    freqs = angular.shape[0]
    polars = adjoint_source.shape[1]
    groups = freqs * polars
    rows = 2 * groups
    edge_count = adjoint_source.shape[-1]
    rim = neighbour_map.shape[-1]
    slots = element_edges.shape[-1]
    tall = slots // LANES
    stiff = stiffness.reshape(SIDE * SIDE, tall, LANES)
    mass = mass_matrix.reshape(SIDE * SIDE, tall, LANES)
    edges = element_edges.reshape(SIDE, tall, LANES)
    sigma = conductivity.reshape(tall, LANES)
    live = live_slots.reshape(tall, LANES)
    source = adjoint_source.reshape(groups, 1, edge_count)
    forward = forward_field.reshape(groups, 1, edge_count)

    def shape(*dims, kind=jnp.float32):
        return jax.ShapeDtypeStruct(dims, kind)

    field_shape, rim_shape = shape(rows, edge_count), shape(rows, rim)
    sums_shape, terms_shape = shape(rows, LANES), shape(groups, tall, LANES)
    picks_shape = shape(groups * SIDE, tall, LANES)
    field_room = pltpu.VMEM((rows, edge_count), jnp.float32)
    piece_room = pltpu.VMEM((rows * SIDE * tall, LANES), jnp.float32)

    arguments = (
        angular,
        source,
        neighbour_map,
        stiff,
        mass,
        sigma,
        live,
        edges,
        forward,
    )
    arguments = [pltpu.with_memory_space_constraint(x, pltpu.HBM) for x in arguments]
    kept = [jax.ShapeDtypeStruct(x.shape, x.dtype) for x in arguments[3:]]
    across, beside, source, order, rates, stiff, mass, sigma, live, edges, forward = call(
        load_stage,
        arguments,
        [
            rim_shape,
            rim_shape,
            field_shape,
            shape(rows, rim, kind=jnp.int32),
            shape(freqs, tall, LANES),
            *kept,
        ],
        (
            pltpu.SMEM(angular.shape, angular.dtype),
            pltpu.VMEM(source.shape, source.dtype),
            pltpu.VMEM(neighbour_map.shape, neighbour_map.dtype),
            pltpu.SemaphoreType.DMA((len(arguments),)),
        ),
        space=HBM,
    )
    across, beside = swap(across, "dom", 1), swap(beside, "dom", 0)
    places, blocks, scale = call(
        table_stage,
        (rates, stiff, mass, sigma, live, edges),
        [
            shape(LANES, SIDE * slots, kind=jnp.bfloat16),
            shape(freqs * SIDE * SIDE, tall, LANES),
            sums_shape,
        ],
        cost=4_000_000,
    )
    picks, image, across, beside, inverse, sums = call(
        functools.partial(first_stage, polars),
        (source, order, across, beside, scale, blocks, edges, places),
        [
            picks_shape,
            field_shape,
            rim_shape,
            rim_shape,
            shape(rows, rim, kind=jnp.int32),
            sums_shape,
        ],
        (field_room, piece_room),
    )
    across, beside = swap(across, "dom", 1), swap(beside, "dom", 0)
    heavy, terms0 = call(
        functools.partial(forward_stage, polars),
        (rates, forward, mass, live, edges, picks),
        [picks_shape, terms_shape],
        cost=4_000_000,
    )
    terms1, sums, image, across, beside = call(
        functools.partial(later_stage, polars, 1, False),
        (image, order, inverse, across, beside, sums, blocks, edges, heavy, places),
        [terms_shape, sums_shape, field_shape, rim_shape, rim_shape],
        (field_room, piece_room),
    )
    across, beside = swap(across, "dom", 1), swap(beside, "dom", 0)
    terms2, sums = call(
        functools.partial(later_stage, polars, 2, True),
        (image, order, inverse, across, beside, sums, blocks, edges, heavy),
        [terms_shape, sums_shape],
        (field_room,),
    )
    term = call(
        combine_stage,
        (lax.all_gather(sums, "dom"), sums, terms0, terms1, terms2),
        shape(tall, LANES),
    )
    gradient = sum_over(term, "freq").reshape(1, slots)
    updated = sigma.reshape(1, slots) * jnp.exp(-0.5 * jnp.tanh(gradient))
    return gradient, updated


def solution(mesh):
    return jax.shard_map(
        local,
        mesh=mesh,
        in_specs=(
            P("freq"),
            P("dom", None, None),
            P("dom", None, None),
            P("dom", None),
            P("dom", None, None),
            P("dom", None),
            P("freq", None, "dom", None),
            P("freq", None, "dom", None),
            P("dom", None),
        ),
        out_specs=(P("dom", None), P("dom", None)),
        check_vma=False,
    )
```

```python
import functools

import jax
import jax.numpy as jnp
from jax import lax
from jax.experimental import pallas as pl
from jax.experimental.pallas import tpu as pltpu
from jax.sharding import PartitionSpec as P

LANES = 128
SUBLANES = 8
SIDE = 6
VMEM = pl.BlockSpec(memory_space=pltpu.VMEM)
HBM = pl.BlockSpec(memory_space=pltpu.HBM)

PICK_LANES = lax.GatherDimensionNumbers(
    offset_dims=(),
    collapsed_slice_dims=(1,),
    start_index_map=(1,),
    operand_batching_dims=(0,),
    start_indices_batching_dims=(0,),
)


def pick_lanes(block, lanes):
    return lax.gather(
        block,
        lanes[..., None],
        PICK_LANES,
        (1, 1),
        mode=lax.GatherScatterMode.PROMISE_IN_BOUNDS,
    )


def pick_wide(chunks, index):
    lanes = index & (LANES - 1)
    high = index >> 7
    level = [pick_lanes(chunk, lanes) for chunk in chunks]
    bit = 0
    while len(level) > 1:
        odd = (high >> bit) & 1 == 1
        level = [
            jnp.where(odd, level[t + 1], level[t]) if t + 1 < len(level) else level[t]
            for t in range(0, len(level), 2)
        ]
        bit += 1
    return level[0]


def row_ids(rows):
    return lax.broadcasted_iota(jnp.int32, (rows, LANES), 0)


def lane_ids(rows):
    return lax.broadcasted_iota(jnp.int32, (rows, LANES), 1)


def spread(row, rows):
    return jnp.broadcast_to(row, (rows, row.shape[-1]))


def cut(ref):
    return [ref[:, c : c + LANES] for c in range(0, ref.shape[-1], LANES)]


def swap_halves(block):
    return pltpu.roll(block, block.shape[0] // 2, 0)


def doubled(block):
    half = block.shape[0] // 2
    return jnp.where(row_ids(2 * half) < half, block, swap_halves(block))


def lane_sum(block):
    return jnp.broadcast_to(jnp.sum(block, axis=1, keepdims=True), block.shape)


def put_lane(block, lane, value):
    return jnp.where(lane_ids(block.shape[0]) == lane, value, block)


def put_chunks(ref, chunks):
    for c, chunk in enumerate(chunks):
        ref[:, c * LANES : (c + 1) * LANES] = chunk


def is_even():
    device = lax.axis_index("dom")
    return lax.rem(device + 1 + device // 2, 2) == 0


def put_rims(across_ref, beside_ref, lower, upper):
    even = is_even()
    for c, (low, high) in enumerate(zip(lower, upper)):
        here = slice(c * LANES, (c + 1) * LANES)
        across_ref[:, here] = jnp.where(even, low, high)
        beside_ref[:, here] = jnp.where(even, high, low)


def take_rims(across_ref, beside_ref):
    even = is_even()
    pairs = list(zip(cut(across_ref), cut(beside_ref)))
    prior = [jnp.where(even, a, b) for a, b in pairs]
    above = [jnp.where(even, b, a) for a, b in pairs]
    return prior, above


def picks_of(rows_of_group, edges):
    chunks = [spread(row, edges.shape[1]) for row in rows_of_group]
    return [pick_wide(chunks, edges[j]) for j in range(SIDE)]


def group_rows(ref, g):
    return [ref[g : g + 1, c : c + LANES] for c in range(0, ref.shape[-1], LANES)]


def times_block(entries, base, picked):
    out = []
    for i in range(SIDE):
        total = None
        for j in range(SIDE):
            one = entries[base + SIDE * i + j] * picked[j]
            total = one if total is None else total + one
        out.append(total)
    return out


def weighted_sum(left, right):
    total = None
    for a, b in zip(left, right):
        total = a * b if total is None else total + a * b
    return total


def scatter(pieces, edges, places, count):
    depth = SIDE * edges.shape[1]
    rows = pieces.shape[0] // depth
    slots = edges.shape[1] * LANES
    total = None
    for i in range(SIDE):
        columns = []
        for s in range(edges.shape[1]):
            both = pieces[pl.ds(i * edges.shape[1] + s, rows, stride=depth), :]
            high = spread(edges[i, s : s + 1, :] >> 7, rows)
            stacked = [jnp.where(high == h, both, 0.0) for h in range(count)]
            columns.append(jnp.concatenate(stacked, axis=0).astype(jnp.bfloat16))
        part = lax.dot_general(
            jnp.concatenate(columns, axis=1),
            places[:, i * slots : (i + 1) * slots],
            (((1,), (1,)), ((), ())),
            preferred_element_type=jnp.float32,
        )
        total = part if total is None else total + part
    out = []
    for h in range(count):
        piece = total[rows * h : rows * (h + 1)]
        out.append(piece + swap_halves(piece))
    return out


def joined(own, from_prior, from_above, order, inverse):
    rim = len(from_prior)
    lower = [own[c] + pick_wide(from_prior, order[c]) for c in range(rim)]
    upper = [own[len(own) - rim + c] + pick_wide(from_above, inverse[c]) for c in range(rim)]
    return lower + own[rim : len(own) - rim] + upper


def squares(chunks, rim, has_prior):
    total = None
    for c, chunk in enumerate(chunks):
        term = chunk * chunk
        if c < rim:
            term = term * (1.0 - has_prior)
        total = term if total is None else total + term
    return total


def start_copies(routes, arrived):
    copies = [
        pltpu.make_async_copy(here, there, arrived.at[n])
        for n, (here, there) in enumerate(routes)
    ]
    for copy in copies:
        copy.start()
    return copies


def load_stage(
    source_in,
    order_in,
    angular_in,
    stiffness_in,
    mass_in,
    edges_in,
    sigma_in,
    live_in,
    forward_in,
    source_ref,
    parcel_ref,
    sigma_ref,
    rates_ref,
    order,
    angular,
    edges,
    live,
    arrived,
):
    count = source_in.shape[0]
    tall = sigma_ref.shape[0]
    matrix = stiffness_in.shape[0]
    base = 2 * matrix
    copies = start_copies(
        (
            (source_in, source_ref.at[pl.ds(0, count)]),
            (order_in, order),
            (edges_in, edges),
            (sigma_in, sigma_ref),
            (live_in, live),
            (angular_in, angular),
            (stiffness_in, parcel_ref.at[pl.ds(0, matrix)]),
            (mass_in, parcel_ref.at[pl.ds(matrix, matrix)]),
            (forward_in, parcel_ref.at[pl.ds(base + (SIDE + 2) * tall, forward_in.shape[0])]),
        ),
        arrived,
    )
    for copy in copies:
        copy.wait()
    for c, piece in enumerate(cut(order)):
        at = count + c * SUBLANES
        source_ref[at : at + SUBLANES, :] = spread(piece.astype(jnp.float32), SUBLANES)
    parcel_ref[base : base + SIDE * tall, :] = edges[...].astype(jnp.float32)
    base += SIDE * tall
    parcel_ref[base : base + tall, :] = sigma_ref[...]
    parcel_ref[base + tall : base + 2 * tall, :] = live[...].astype(jnp.float32)
    for f in range(angular.shape[0]):
        rates_ref[f] = jnp.full(rates_ref.shape[1:], angular[f], jnp.float32)


class Elements:
    def __init__(self, parcel, tall):
        self.parcel, self.tall = parcel, tall

    def __getitem__(self, entry):
        return self.parcel[entry * self.tall : (entry + 1) * self.tall, :]

    def stiffness(self, entry):
        return self[entry]

    def mass(self, entry):
        return self[SIDE * SIDE + entry]

    def edges(self, j):
        return self[2 * SIDE * SIDE + j].astype(jnp.int32)

    def sigma(self):
        return self[2 * SIDE * SIDE + SIDE]

    def live(self):
        return self[2 * SIDE * SIDE + SIDE + 1]

    def forward(self, row):
        at = (2 * SIDE * SIDE + SIDE + 2) * self.tall + row
        return self.parcel[at : at + 1, :]


def rims_stage(groups, parcel, across_ref, beside_ref, stacked_ref, order_ref):
    rows = 2 * groups
    count = stacked_ref.shape[-1] // LANES
    first = row_ids(rows) < groups
    chunks = []
    for c in range(count):
        piece = [parcel[g * count + c : g * count + c + 1, :] for g in range(groups)]
        chunks.append(jnp.concatenate(piece + piece, axis=0))
    put_chunks(stacked_ref, chunks)
    rim = order_ref.shape[-1] // LANES
    numbers = []
    for c in range(rim):
        at = groups * count + c * SUBLANES
        numbers.append(spread(parcel[at : at + 1, :], rows))
    put_chunks(order_ref, [x.astype(jnp.int32) for x in numbers])
    lower = [jnp.where(first, x, o) for x, o in zip(chunks[:rim], numbers)]
    upper = [jnp.where(first, x, 1.0) for x in chunks[count - rim :]]
    put_rims(across_ref, beside_ref, lower, upper)


def table_stage(rates, parcel, places_ref, blocks_ref, scale_ref, edges_ref):
    rows = edges_ref.shape[1]
    elements = Elements(parcel, rows)
    alive = elements.live()
    weight = elements.sigma()
    freqs = rates.shape[0]
    peak = None
    for i in range(SIDE):
        entry = (SIDE + 1) * i
        for f in range(freqs):
            size = elements.stiffness(entry) + rates[f] * weight * elements.mass(entry)
            peak = size if peak is None else jnp.maximum(peak, size)
    peak = jnp.max(peak * alive, axis=1, keepdims=True)
    scale = jnp.broadcast_to(jnp.max(peak, axis=0, keepdims=True), scale_ref.shape)
    scale_ref[...] = scale
    alive = alive / scale[:1, :1]
    for entry in range(SIDE * SIDE):
        stiff = elements.stiffness(entry) * alive
        heavy = elements.mass(entry) * (weight * alive)
        for f in range(freqs):
            blocks_ref[f * SIDE * SIDE + entry] = stiff + rates[f] * heavy
    for j in range(SIDE):
        edges_ref[j] = elements.edges(j)
    numbers = row_ids(LANES)

    def body(i, carry):
        for s in range(rows):
            lanes = spread(edges_ref[i, s : s + 1, :] & (LANES - 1), LANES)
            column = pl.ds(pl.multiple_of((i * rows + s) * LANES, LANES), LANES)
            places_ref[:, column] = jnp.where(lanes == numbers, 1.0, 0.0).astype(jnp.bfloat16)
        return carry

    lax.fori_loop(0, SIDE, body, 0)


def apply_all(field_ref, blocks, edges, polars, groups, pieces, visit):
    rows = field_ref.shape[0]
    depth = SIDE * edges.shape[1]
    forms = jnp.zeros((rows, LANES), jnp.float32)
    for g in range(groups):
        picked = picks_of(group_rows(field_ref, g), edges)
        visit(g, picked)
        values = times_block(blocks, (g // polars) * SIDE * SIDE, picked)
        form = jnp.sum(weighted_sum(picked, values), axis=0, keepdims=True)
        forms = jnp.where(row_ids(rows) == g, spread(form, rows), forms)
        if pieces is None:
            continue
        for i, value in enumerate(values):
            coarse = value.astype(jnp.bfloat16).astype(jnp.float32)
            for part, piece in enumerate((coarse, value - coarse)):
                at = (part * groups + g) * depth + i * edges.shape[1]
                pieces[at : at + edges.shape[1], :] = piece
    return lane_sum(forms)


def first_stage(
    polars,
    source,
    order_ref,
    across_in,
    beside_in,
    scale_in,
    blocks,
    edges,
    places,
    picks_ref,
    image_ref,
    across_ref,
    beside_ref,
    inverse_ref,
    sums_ref,
    field_ref,
    pieces,
):
    rows = source.shape[0]
    groups = rows // 2
    first = row_ids(rows) < groups
    scale = scale_in[...]
    prior, above = take_rims(across_in, beside_in)

    rim = order_ref.shape[-1]
    order = cut(order_ref)
    above_order = spread(
        jnp.concatenate([x[groups : groups + 1] for x in above], axis=1), rim
    )
    slot = lax.broadcasted_iota(jnp.int32, (rim, rim), 0).astype(jnp.float32)
    match = jnp.where(above_order == slot, 1.0, 0.0).astype(jnp.bfloat16)
    numbers = lax.broadcasted_iota(jnp.int32, (2 * rows, rim), 1).astype(jnp.bfloat16)
    inverse = lax.dot_general(
        numbers, match, (((1,), (1,)), ((), ())), preferred_element_type=jnp.float32
    )[:rows].astype(jnp.int32)
    inverse_ref[...] = inverse
    inverse = [inverse[:, c : c + LANES] for c in range(0, rim, LANES)]

    has_prior = spread(prior[0][groups : groups + 1], rows)
    field = joined(
        cut(source), [doubled(x) for x in prior], [doubled(x) for x in above], order, inverse
    )
    put_chunks(field_ref, field)

    def visit(g, picked):
        for j in range(SIDE):
            picks_ref[g * SIDE + j] = picked[j]

    forms = apply_all(field_ref, blocks, edges, polars, groups, pieces, visit)
    image = scatter(pieces, edges, places, len(field))
    put_chunks(image_ref, image)
    count = rim // LANES
    put_rims(
        across_ref,
        beside_ref,
        [jnp.where(first, x, scale) for x in image[:count]],
        [jnp.where(first, x, scale) for x in image[len(image) - count :]],
    )
    sums = jnp.zeros((rows, LANES), jnp.float32)
    sums = put_lane(sums, 0, lane_sum(squares(field, count, has_prior)))
    sums = put_lane(sums, 1, forms)
    sums_ref[...] = jnp.where(first, sums, scale)


def later_stage(
    polars,
    step,
    last,
    image_in,
    order_ref,
    inverse_ref,
    across_in,
    beside_in,
    sums_in,
    blocks,
    edges,
    heavy,
    *rest,
):
    if last:
        terms0, terms1, terms_ref, sums_ref, field_ref = rest
        pieces = None
        groups = terms0.shape[0]
        terms_ref[groups : 2 * groups] = terms0[...]
        terms_ref[2 * groups : 3 * groups] = terms1[...]
    else:
        places, terms_ref, sums_ref, image_ref, across_ref, beside_ref, field_ref, pieces = rest
    rows = image_in.shape[0]
    groups = rows // 2
    first = row_ids(rows) < groups
    sums = sums_in[...]
    scale = jnp.where(first, swap_halves(sums), sums)
    inverse_scale = 1.0 / scale
    rim = order_ref.shape[-1]
    count = rim // LANES
    order = cut(order_ref)
    inverse = cut(inverse_ref)

    def rescaled(block):
        ratio = swap_halves(block) * inverse_scale
        for _ in range(step):
            block = block * ratio
        return doubled(block)

    prior, above = take_rims(across_in, beside_in)
    has_prior = jnp.where(first, swap_halves(prior[0]), prior[0])
    has_prior = jnp.where(has_prior > 0.0, 1.0, 0.0)
    field = joined(
        cut(image_in),
        [rescaled(x) for x in prior],
        [rescaled(x) for x in above],
        order,
        inverse,
    )
    put_chunks(field_ref, field)

    def visit(g, picked):
        terms_ref[g] = weighted_sum(picked, [heavy[g * SIDE + i] for i in range(SIDE)])

    forms = apply_all(field_ref, blocks, edges, polars, groups, pieces, visit)
    fresh = put_lane(sums, 2 * step, lane_sum(squares(field, count, has_prior)))
    fresh = put_lane(fresh, 2 * step + 1, forms)
    sums_ref[...] = jnp.where(first, fresh, scale)
    if last:
        terms_ref[3 * groups] = scale
    else:
        image = scatter(pieces, edges, places, len(field))
        put_chunks(image_ref, image)
        put_rims(
            across_ref,
            beside_ref,
            [jnp.where(first, x, scale) for x in image[:count]],
            [jnp.where(first, x, scale) for x in image[len(image) - count :]],
        )


def forward_stage(polars, rates, parcel, edges, picks, heavy_ref, terms_ref):
    groups = terms_ref.shape[0]
    elements = Elements(parcel, edges.shape[1])
    mass = [elements.mass(entry) for entry in range(SIDE * SIDE)]
    dead = -elements.live()
    count = (parcel.shape[0] - (2 * SIDE * SIDE + SIDE + 2) * edges.shape[1]) // groups
    for g in range(groups):
        rows = [elements.forward(g * count + c) for c in range(count)]
        values = times_block(mass, 0, picks_of(rows, edges))
        factor = dead * rates[g // polars]
        values = [factor * value for value in values]
        for i in range(SIDE):
            heavy_ref[g * SIDE + i] = values[i]
        terms_ref[g] = weighted_sum(values, [picks[g * SIDE + i] for i in range(SIDE)])


def combine_stage(everyone, terms, out_ref):
    rows = everyone.shape[1]
    groups = rows // 2
    first = row_ids(rows) < groups

    def scale_of(block):
        return jnp.where(first, swap_halves(block), block)

    parts = [everyone[q] for q in range(everyone.shape[0])]
    scales = [scale_of(block) for block in parts]
    top = functools.reduce(jnp.maximum, scales)
    lanes = lane_ids(rows)
    inverse_top = 1.0 / top
    total = None
    for block, scale in zip(parts, scales):
        ratio = scale * inverse_top
        power = jnp.ones_like(ratio)
        factor = jnp.ones_like(ratio)
        for k in range(1, 6):
            power = power * ratio
            factor = jnp.where(lanes == k, power, factor)
        term = block * factor
        total = term if total is None else total + term
    m = [jnp.broadcast_to(total[:, k : k + 1], (rows, LANES)) for k in range(6)]
    l1 = m[2] / m[1]
    l2 = m[3] / m[1]
    d2 = m[3] - l1 * m[2]
    cross = m[4] - l2 * m[2]
    l3 = cross / d2
    d3 = m[5] - l2 * m[3] - l3 * cross
    y1 = m[1] - l1 * m[0]
    y2 = m[2] - l2 * m[0] - l3 * y1
    c2 = y2 / d3
    c1 = y1 / d2 - l3 * c2
    c0 = m[0] / m[1] - l1 * c1 - l2 * c2
    mine = terms[3 * groups] * inverse_top
    c0 = c0 * inverse_top
    c1 = c1 * mine * inverse_top
    c2 = c2 * mine * mine * inverse_top
    out = None
    for place, c in enumerate((c2, c0, c1)):
        for g in range(groups):
            one = terms[place * groups + g] * spread(c[g : g + 1], out_ref.shape[0])
            out = one if out is None else out + one
    out_ref[...] = out


def call(kernel, arguments, outs, scratch=(), space=VMEM, cost=0):
    return pl.pallas_call(
        kernel,
        out_shape=outs,
        in_specs=[space] * len(arguments),
        out_specs=jax.tree.map(lambda _: VMEM, outs),
        scratch_shapes=list(scratch),
        cost_estimate=pl.CostEstimate(flops=cost, bytes_accessed=cost, transcendentals=0),
        compiler_params=pltpu.CompilerParams(vmem_limit_bytes=16 * 1024 * 1024),
    )(*arguments)


def device_of(partition):
    return partition ^ 1 if partition // 2 % 2 == 0 else partition


def swap(block, offset):
    route = []
    for low in range(offset, lax.axis_size("dom") - 1, 2):
        pair = device_of(low), device_of(low + 1)
        route += [pair, pair[::-1]]
    return lax.ppermute(block, "dom", route)


def trade(block):
    return lax.ppermute(block, "dom", [(i, device_of(i)) for i in range(lax.axis_size("dom"))])


def gather_all(block, axis):
    size = lax.axis_size(axis)
    copies = jnp.broadcast_to(block[None], (size, *block.shape))
    return lax.all_to_all(copies, axis, 0, 0)


def sum_over(block, axis):
    size = lax.axis_size(axis)
    if size & (size - 1):
        return jnp.sum(gather_all(block, axis), axis=0)
    step = 1
    while step < size:
        block = block + lax.ppermute(block, axis, [(i, i ^ step) for i in range(size)])
        step *= 2
    return block


def local(
    angular,
    stiffness,
    mass_matrix,
    conductivity,
    element_edges,
    live_slots,
    adjoint_source,
    forward_field,
    neighbour_map,
):
    freqs = angular.shape[0]
    polars = adjoint_source.shape[1]
    groups = freqs * polars
    rows = 2 * groups
    edge_count = adjoint_source.shape[-1]
    rim = neighbour_map.shape[-1]
    slots = element_edges.shape[-1]
    tall = slots // LANES
    matrix = SIDE * SIDE * tall
    stiff = stiffness.reshape(matrix, LANES)
    mass = mass_matrix.reshape(matrix, LANES)
    edges = element_edges.reshape(SIDE * tall, LANES)
    sigma = conductivity.reshape(tall, LANES)
    live = live_slots.reshape(tall, LANES)
    source = adjoint_source.reshape(-1, LANES)
    forward = forward_field.reshape(-1, LANES)

    def shape(*dims, kind=jnp.float32):
        return jax.ShapeDtypeStruct(dims, kind)

    field_shape, rim_shape = shape(rows, edge_count), shape(rows, rim)
    sums_shape, terms_shape = shape(rows, LANES), shape(groups, tall, LANES)
    picks_shape = shape(groups * SIDE, tall, LANES)
    field_room = pltpu.VMEM((rows, edge_count), jnp.float32)
    piece_room = pltpu.VMEM((rows * SIDE * tall, LANES), jnp.float32)

    arguments = (source, neighbour_map, angular, stiff, mass, edges, sigma, live, forward)
    parcel, elements, sigma, rates = call(
        load_stage,
        [pltpu.with_memory_space_constraint(x, pltpu.HBM) for x in arguments],
        [
            shape(source.shape[0] + rim // LANES * SUBLANES, LANES),
            shape(2 * matrix + (SIDE + 2) * tall + forward.shape[0], LANES),
            shape(tall, LANES),
            shape(freqs, tall, LANES),
        ],
        (
            pltpu.VMEM(neighbour_map.shape, neighbour_map.dtype),
            pltpu.SMEM(angular.shape, angular.dtype),
            pltpu.VMEM(edges.shape, edges.dtype),
            pltpu.VMEM(live.shape, live.dtype),
            pltpu.SemaphoreType.DMA((len(arguments),)),
        ),
        space=HBM,
    )
    parcel = trade(parcel)
    elements = trade(elements)
    across, beside, source, order = call(
        functools.partial(rims_stage, groups),
        (parcel,),
        [rim_shape, rim_shape, field_shape, shape(rows, rim, kind=jnp.int32)],
    )
    across, beside = swap(across, 1), swap(beside, 0)
    places, blocks, scale, edges = call(
        table_stage,
        (rates, elements),
        [
            shape(LANES, SIDE * slots, kind=jnp.bfloat16),
            shape(freqs * SIDE * SIDE, tall, LANES),
            sums_shape,
            shape(SIDE, tall, LANES, kind=jnp.int32),
        ],
        cost=4_000_000,
    )
    picks, image, across, beside, inverse, sums = call(
        functools.partial(first_stage, polars),
        (source, order, across, beside, scale, blocks, edges, places),
        [
            picks_shape,
            field_shape,
            rim_shape,
            rim_shape,
            shape(rows, rim, kind=jnp.int32),
            sums_shape,
        ],
        (field_room, piece_room),
    )
    across, beside = swap(across, 1), swap(beside, 0)
    heavy, terms0 = call(
        functools.partial(forward_stage, polars),
        (rates, elements, edges, picks),
        [picks_shape, terms_shape],
        cost=4_000_000,
    )
    terms1, sums, image, across, beside = call(
        functools.partial(later_stage, polars, 1, False),
        (image, order, inverse, across, beside, sums, blocks, edges, heavy, places),
        [terms_shape, sums_shape, field_shape, rim_shape, rim_shape],
        (field_room, piece_room),
    )
    across, beside = swap(across, 1), swap(beside, 0)
    terms, sums = call(
        functools.partial(later_stage, polars, 2, True),
        (image, order, inverse, across, beside, sums, blocks, edges, heavy, terms0, terms1),
        [shape(3 * groups + 1, tall, LANES), sums_shape],
        (field_room,),
    )
    term = call(
        combine_stage,
        (gather_all(sums, "dom"), trade(terms)),
        shape(tall, LANES),
    )
    gradient = sum_over(term, "freq").reshape(1, slots)
    updated = sigma.reshape(1, slots) * jnp.exp(-0.5 * jnp.tanh(gradient))
    return gradient, updated


def solution(mesh):
    return jax.shard_map(
        local,
        mesh=mesh,
        in_specs=(
            P("freq"),
            P("dom", None, None),
            P("dom", None, None),
            P("dom", None),
            P("dom", None, None),
            P("dom", None),
            P("freq", None, "dom", None),
            P("freq", None, "dom", None),
            P("dom", None),
        ),
        out_specs=(P("dom", None), P("dom", None)),
        check_vma=False,
    )
```

```python
import functools

import jax
import jax.numpy as jnp
from jax import lax
from jax.experimental import pallas as pl
from jax.experimental.pallas import tpu as pltpu
from jax.sharding import PartitionSpec as P

LANES = 128
SUBLANES = 8
SIDE = 6
VMEM = pl.BlockSpec(memory_space=pltpu.VMEM)
HBM = pl.BlockSpec(memory_space=pltpu.HBM)

PICK_LANES = lax.GatherDimensionNumbers(
    offset_dims=(),
    collapsed_slice_dims=(1,),
    start_index_map=(1,),
    operand_batching_dims=(0,),
    start_indices_batching_dims=(0,),
)


def pick_lanes(block, lanes):
    return lax.gather(
        block,
        lanes[..., None],
        PICK_LANES,
        (1, 1),
        mode=lax.GatherScatterMode.PROMISE_IN_BOUNDS,
    )


def pick_wide(chunks, index):
    lanes = index & (LANES - 1)
    high = index >> 7
    level = [pick_lanes(chunk, lanes) for chunk in chunks]
    bit = 0
    while len(level) > 1:
        odd = (high >> bit) & 1 == 1
        level = [
            jnp.where(odd, level[t + 1], level[t]) if t + 1 < len(level) else level[t]
            for t in range(0, len(level), 2)
        ]
        bit += 1
    return level[0]


def row_ids(rows):
    return lax.broadcasted_iota(jnp.int32, (rows, LANES), 0)


def lane_ids(rows):
    return lax.broadcasted_iota(jnp.int32, (rows, LANES), 1)


def spread(row, rows):
    return jnp.broadcast_to(row, (rows, row.shape[-1]))


def cut(ref):
    return [ref[:, c : c + LANES] for c in range(0, ref.shape[-1], LANES)]


def swap_halves(block):
    return pltpu.roll(block, block.shape[0] // 2, 0)


def doubled(block):
    half = block.shape[0] // 2
    return jnp.where(row_ids(2 * half) < half, block, swap_halves(block))


def lane_sum(block):
    return jnp.broadcast_to(jnp.sum(block, axis=1, keepdims=True), block.shape)


def put_lane(block, lane, value):
    return jnp.where(lane_ids(block.shape[0]) == lane, value, block)


def put_chunks(ref, chunks):
    for c, chunk in enumerate(chunks):
        ref[:, c * LANES : (c + 1) * LANES] = chunk


def is_even():
    return lax.rem(lax.axis_index("dom"), 2) == 0


def put_rims(across_ref, beside_ref, lower, upper):
    even = is_even()
    for c, (low, high) in enumerate(zip(lower, upper)):
        here = slice(c * LANES, (c + 1) * LANES)
        across_ref[:, here] = jnp.where(even, low, high)
        beside_ref[:, here] = jnp.where(even, high, low)


def take_rims(across_ref, beside_ref):
    even = is_even()
    pairs = list(zip(cut(across_ref), cut(beside_ref)))
    prior = [jnp.where(even, a, b) for a, b in pairs]
    above = [jnp.where(even, b, a) for a, b in pairs]
    return prior, above


def picks_of(rows_of_group, edges):
    chunks = [spread(row, edges.shape[1]) for row in rows_of_group]
    return [pick_wide(chunks, edges[j]) for j in range(SIDE)]


def group_rows(ref, g):
    return [ref[g : g + 1, c : c + LANES] for c in range(0, ref.shape[-1], LANES)]


def times_block(entries, base, picked):
    out = []
    for i in range(SIDE):
        total = None
        for j in range(SIDE):
            one = entries[base + SIDE * i + j] * picked[j]
            total = one if total is None else total + one
        out.append(total)
    return out


def weighted_sum(left, right):
    total = None
    for a, b in zip(left, right):
        total = a * b if total is None else total + a * b
    return total


def scatter(pieces, edges, places, count):
    depth = SIDE * edges.shape[1]
    rows = pieces.shape[0] // depth
    slots = edges.shape[1] * LANES
    total = None
    for i in range(SIDE):
        columns = []
        for s in range(edges.shape[1]):
            both = pieces[pl.ds(i * edges.shape[1] + s, rows, stride=depth), :]
            high = spread(edges[i, s : s + 1, :] >> 7, rows)
            stacked = [jnp.where(high == h, both, 0.0) for h in range(count)]
            columns.append(jnp.concatenate(stacked, axis=0).astype(jnp.bfloat16))
        part = lax.dot_general(
            jnp.concatenate(columns, axis=1),
            places[:, i * slots : (i + 1) * slots],
            (((1,), (1,)), ((), ())),
            preferred_element_type=jnp.float32,
        )
        total = part if total is None else total + part
    out = []
    for h in range(count):
        piece = total[rows * h : rows * (h + 1)]
        out.append(piece + swap_halves(piece))
    return out


def joined(own, from_prior, from_above, order, inverse):
    rim = len(from_prior)
    lower = [own[c] + pick_wide(from_prior, order[c]) for c in range(rim)]
    upper = [own[len(own) - rim + c] + pick_wide(from_above, inverse[c]) for c in range(rim)]
    return lower + own[rim : len(own) - rim] + upper


def squares(chunks, rim, has_prior):
    total = None
    for c, chunk in enumerate(chunks):
        term = chunk * chunk
        if c < rim:
            term = term * (1.0 - has_prior)
        total = term if total is None else total + term
    return total


def start_copies(routes, arrived):
    copies = [
        pltpu.make_async_copy(here, there, arrived.at[n])
        for n, (here, there) in enumerate(routes)
    ]
    for copy in copies:
        copy.start()
    return copies


def rims_stage(
    source_in, order_in, across_ref, beside_ref, stacked_ref, order_ref, source, order, arrived
):
    for copy in start_copies(((source_in, source), (order_in, order)), arrived):
        copy.wait()
    groups = source.shape[0]
    rows = stacked_ref.shape[0]
    first = row_ids(rows) < groups
    chunks = []
    for c in range(0, source.shape[-1], LANES):
        piece = [source[g, :, c : c + LANES] for g in range(groups)]
        chunks.append(jnp.concatenate(piece + piece, axis=0))
    put_chunks(stacked_ref, chunks)
    order_ref[...] = spread(order[...], rows)
    numbers = [x.astype(jnp.float32) for x in cut(order_ref)]
    count = len(numbers)
    lower = [jnp.where(first, x, o) for x, o in zip(chunks[:count], numbers)]
    upper = [jnp.where(first, x, 1.0) for x in chunks[len(chunks) - count :]]
    put_rims(across_ref, beside_ref, lower, upper)


def table_stage(
    angular_in,
    stiffness_in,
    mass_in,
    sigma_in,
    live_in,
    edges_in,
    forward_in,
    places_ref,
    blocks_ref,
    scale_ref,
    rates,
    mass,
    sigma,
    live,
    edges,
    forward_ref,
    angular,
    stiffness,
    arrived,
):
    copies = start_copies(
        (
            (edges_in, edges),
            (angular_in, angular),
            (sigma_in, sigma),
            (live_in, live),
            (stiffness_in, stiffness),
            (mass_in, mass),
            (forward_in, forward_ref),
        ),
        arrived,
    )
    copies[0].wait()
    numbers = row_ids(LANES)
    rows = edges.shape[1]

    def body(i, carry):
        for s in range(rows):
            lanes = spread(edges[i, s : s + 1, :] & (LANES - 1), LANES)
            column = pl.ds(pl.multiple_of((i * rows + s) * LANES, LANES), LANES)
            places_ref[:, column] = jnp.where(lanes == numbers, 1.0, 0.0).astype(jnp.bfloat16)
        return carry

    lax.fori_loop(0, SIDE, body, 0)
    for copy in copies[1:]:
        copy.wait()
    for f in range(angular.shape[0]):
        rates[f] = jnp.full(rates.shape[1:], angular[f], jnp.float32)
    alive = live[...].astype(jnp.float32)
    weight = sigma[...]
    freqs = rates.shape[0]
    peak = None
    for i in range(SIDE):
        for f in range(freqs):
            entry = (SIDE + 1) * i
            size = stiffness[entry] + rates[f] * weight * mass[entry]
            peak = size if peak is None else jnp.maximum(peak, size)
    peak = jnp.max(peak * alive, axis=1, keepdims=True)
    scale = jnp.broadcast_to(jnp.max(peak, axis=0, keepdims=True), scale_ref.shape)
    scale_ref[...] = scale
    alive = alive / scale[:1, :1]
    for entry in range(SIDE * SIDE):
        stiff = stiffness[entry] * alive
        heavy = mass[entry] * (weight * alive)
        for f in range(freqs):
            blocks_ref[f * SIDE * SIDE + entry] = stiff + rates[f] * heavy


def apply_all(field_ref, blocks, edges, polars, groups, pieces, visit):
    rows = field_ref.shape[0]
    depth = SIDE * edges.shape[1]
    forms = jnp.zeros((rows, LANES), jnp.float32)
    for g in range(groups):
        picked = picks_of(group_rows(field_ref, g), edges)
        visit(g, picked)
        values = times_block(blocks, (g // polars) * SIDE * SIDE, picked)
        form = jnp.sum(weighted_sum(picked, values), axis=0, keepdims=True)
        forms = jnp.where(row_ids(rows) == g, spread(form, rows), forms)
        if pieces is None:
            continue
        for i, value in enumerate(values):
            coarse = value.astype(jnp.bfloat16).astype(jnp.float32)
            for part, piece in enumerate((coarse, value - coarse)):
                at = (part * groups + g) * depth + i * edges.shape[1]
                pieces[at : at + edges.shape[1], :] = piece
    return lane_sum(forms)


def first_stage(
    polars,
    source,
    order_ref,
    across_in,
    beside_in,
    scale_in,
    blocks,
    edges,
    places,
    picks_ref,
    image_ref,
    across_ref,
    beside_ref,
    inverse_ref,
    sums_ref,
    field_ref,
    pieces,
):
    rows = source.shape[0]
    groups = rows // 2
    first = row_ids(rows) < groups
    scale = scale_in[...]
    prior, above = take_rims(across_in, beside_in)

    rim = order_ref.shape[-1]
    order = cut(order_ref)
    above_order = spread(
        jnp.concatenate([x[groups : groups + 1] for x in above], axis=1), rim
    )
    slot = lax.broadcasted_iota(jnp.int32, (rim, rim), 0).astype(jnp.float32)
    match = jnp.where(above_order == slot, 1.0, 0.0).astype(jnp.bfloat16)
    numbers = lax.broadcasted_iota(jnp.int32, (2 * rows, rim), 1).astype(jnp.bfloat16)
    inverse = lax.dot_general(
        numbers, match, (((1,), (1,)), ((), ())), preferred_element_type=jnp.float32
    )[:rows].astype(jnp.int32)
    inverse_ref[...] = inverse
    inverse = [inverse[:, c : c + LANES] for c in range(0, rim, LANES)]

    has_prior = spread(prior[0][groups : groups + 1], rows)
    field = joined(
        cut(source), [doubled(x) for x in prior], [doubled(x) for x in above], order, inverse
    )
    put_chunks(field_ref, field)

    def visit(g, picked):
        for j in range(SIDE):
            picks_ref[g * SIDE + j] = picked[j]

    forms = apply_all(field_ref, blocks, edges, polars, groups, pieces, visit)
    image = scatter(pieces, edges, places, len(field))
    put_chunks(image_ref, image)
    count = rim // LANES
    put_rims(
        across_ref,
        beside_ref,
        [jnp.where(first, x, scale) for x in image[:count]],
        [jnp.where(first, x, scale) for x in image[len(image) - count :]],
    )
    sums = jnp.zeros((rows, LANES), jnp.float32)
    sums = put_lane(sums, 0, lane_sum(squares(field, count, has_prior)))
    sums = put_lane(sums, 1, forms)
    sums_ref[...] = jnp.where(first, sums, scale)


def later_stage(
    polars,
    step,
    last,
    image_in,
    order_ref,
    inverse_ref,
    across_in,
    beside_in,
    sums_in,
    blocks,
    edges,
    heavy,
    *rest,
):
    if last:
        terms_ref, sums_ref, field_ref = rest
        pieces = None
    else:
        places, terms_ref, sums_ref, image_ref, across_ref, beside_ref, field_ref, pieces = rest
    rows = image_in.shape[0]
    groups = rows // 2
    first = row_ids(rows) < groups
    sums = sums_in[...]
    scale = jnp.where(first, swap_halves(sums), sums)
    inverse_scale = 1.0 / scale
    rim = order_ref.shape[-1]
    count = rim // LANES
    order = cut(order_ref)
    inverse = cut(inverse_ref)

    def rescaled(block):
        ratio = swap_halves(block) * inverse_scale
        for _ in range(step):
            block = block * ratio
        return doubled(block)

    prior, above = take_rims(across_in, beside_in)
    has_prior = jnp.where(first, swap_halves(prior[0]), prior[0])
    has_prior = jnp.where(has_prior > 0.0, 1.0, 0.0)
    field = joined(
        cut(image_in),
        [rescaled(x) for x in prior],
        [rescaled(x) for x in above],
        order,
        inverse,
    )
    put_chunks(field_ref, field)

    def visit(g, picked):
        terms_ref[g] = weighted_sum(picked, [heavy[g * SIDE + i] for i in range(SIDE)])

    forms = apply_all(field_ref, blocks, edges, polars, groups, pieces, visit)
    fresh = put_lane(sums, 2 * step, lane_sum(squares(field, count, has_prior)))
    fresh = put_lane(fresh, 2 * step + 1, forms)
    sums_ref[...] = jnp.where(first, fresh, scale)
    if not last:
        image = scatter(pieces, edges, places, len(field))
        put_chunks(image_ref, image)
        put_rims(
            across_ref,
            beside_ref,
            [jnp.where(first, x, scale) for x in image[:count]],
            [jnp.where(first, x, scale) for x in image[len(image) - count :]],
        )


def forward_stage(polars, rates, forward, mass, live, edges, picks, heavy_ref, terms_ref):
    dead = -live[...].astype(jnp.float32)
    for g in range(forward.shape[0]):
        rows = [forward[g, :, c : c + LANES] for c in range(0, forward.shape[-1], LANES)]
        values = times_block(mass, 0, picks_of(rows, edges))
        factor = dead * rates[g // polars]
        values = [factor * value for value in values]
        for i in range(SIDE):
            heavy_ref[g * SIDE + i] = values[i]
        terms_ref[g] = weighted_sum(values, [picks[g * SIDE + i] for i in range(SIDE)])


def combine_stage(everyone, sums_in, terms0, terms1, terms2, out_ref):
    rows = sums_in.shape[0]
    groups = rows // 2
    first = row_ids(rows) < groups

    def scale_of(block):
        return jnp.where(first, swap_halves(block), block)

    parts = [everyone[q] for q in range(everyone.shape[0])]
    scales = [scale_of(block) for block in parts]
    top = functools.reduce(jnp.maximum, scales)
    lanes = lane_ids(rows)
    inverse_top = 1.0 / top
    total = None
    for block, scale in zip(parts, scales):
        ratio = scale * inverse_top
        power = jnp.ones_like(ratio)
        factor = jnp.ones_like(ratio)
        for k in range(1, 6):
            power = power * ratio
            factor = jnp.where(lanes == k, power, factor)
        term = block * factor
        total = term if total is None else total + term
    m = [jnp.broadcast_to(total[:, k : k + 1], (rows, LANES)) for k in range(6)]
    l1 = m[2] / m[1]
    l2 = m[3] / m[1]
    d2 = m[3] - l1 * m[2]
    cross = m[4] - l2 * m[2]
    l3 = cross / d2
    d3 = m[5] - l2 * m[3] - l3 * cross
    y1 = m[1] - l1 * m[0]
    y2 = m[2] - l2 * m[0] - l3 * y1
    c2 = y2 / d3
    c1 = y1 / d2 - l3 * c2
    c0 = m[0] / m[1] - l1 * c1 - l2 * c2
    mine = scale_of(sums_in[...]) * inverse_top
    c0 = c0 * inverse_top
    c1 = c1 * mine * inverse_top
    c2 = c2 * mine * mine * inverse_top
    out = None
    for terms, c in ((terms0, c0), (terms1, c1), (terms2, c2)):
        for g in range(groups):
            one = terms[g] * spread(c[g : g + 1], out_ref.shape[0])
            out = one if out is None else out + one
    out_ref[...] = out


def pinned(*arguments):
    return [pltpu.with_memory_space_constraint(x, pltpu.HBM) for x in arguments]


def call(kernel, arguments, outs, scratch=(), space=VMEM, cost=0):
    return pl.pallas_call(
        kernel,
        out_shape=outs,
        in_specs=[space] * len(arguments),
        out_specs=jax.tree.map(lambda _: VMEM, outs),
        scratch_shapes=list(scratch),
        cost_estimate=pl.CostEstimate(flops=cost, bytes_accessed=cost, transcendentals=0),
        compiler_params=pltpu.CompilerParams(vmem_limit_bytes=16 * 1024 * 1024),
    )(*arguments)


def swap(block, axis, offset):
    size = lax.axis_size(axis)
    route = []
    for low in range(offset, size - 1, 2):
        route += [(low, low + 1), (low + 1, low)]
    return lax.ppermute(block, axis, route)


def gather_all(block, axis):
    size = lax.axis_size(axis)
    copies = jnp.broadcast_to(block[None], (size, *block.shape))
    return lax.all_to_all(copies, axis, 0, 0)


def sum_over(block, axis):
    size = lax.axis_size(axis)
    if size & (size - 1):
        return jnp.sum(gather_all(block, axis), axis=0)
    near = min(size, 4)
    parts = [block] + [None] * (near - 1)
    for step in reversed(range(1, near)):
        parts[step] = lax.ppermute(block, axis, [(i, i ^ step) for i in range(size)])
    while len(parts) > 1:
        parts = [a + b for a, b in zip(parts[::2], parts[1::2])]
    block = parts[0]
    step = near
    while step < size:
        block = block + lax.ppermute(block, axis, [(i, i ^ step) for i in range(size)])
        step *= 2
    return block


def local(
    angular,
    stiffness,
    mass_matrix,
    conductivity,
    element_edges,
    live_slots,
    adjoint_source,
    forward_field,
    neighbour_map,
):
    freqs = angular.shape[0]
    polars = adjoint_source.shape[1]
    groups = freqs * polars
    rows = 2 * groups
    edge_count = adjoint_source.shape[-1]
    rim = neighbour_map.shape[-1]
    slots = element_edges.shape[-1]
    tall = slots // LANES
    stiff = stiffness.reshape(SIDE * SIDE, tall, LANES)
    mass = mass_matrix.reshape(SIDE * SIDE, tall, LANES)
    edges = element_edges.reshape(SIDE, tall, LANES)
    sigma = conductivity.reshape(tall, LANES)
    live = live_slots.reshape(tall, LANES)
    source = adjoint_source.reshape(groups, 1, edge_count)
    forward = forward_field.reshape(groups, 1, edge_count)

    def shape(*dims, kind=jnp.float32):
        return jax.ShapeDtypeStruct(dims, kind)

    field_shape, rim_shape = shape(rows, edge_count), shape(rows, rim)
    sums_shape, terms_shape = shape(rows, LANES), shape(groups, tall, LANES)
    picks_shape = shape(groups * SIDE, tall, LANES)
    field_room = pltpu.VMEM((rows, edge_count), jnp.float32)
    piece_room = pltpu.VMEM((rows * SIDE * tall, LANES), jnp.float32)

    across, beside, source, order = call(
        rims_stage,
        pinned(source, neighbour_map),
        [rim_shape, rim_shape, field_shape, shape(rows, rim, kind=jnp.int32)],
        (
            pltpu.VMEM(source.shape, source.dtype),
            pltpu.VMEM(neighbour_map.shape, neighbour_map.dtype),
            pltpu.SemaphoreType.DMA((2,)),
        ),
        space=HBM,
    )
    across, beside = swap(across, "dom", 1), swap(beside, "dom", 0)
    kept = [jax.ShapeDtypeStruct(x.shape, x.dtype) for x in (mass, sigma, live, edges, forward)]
    places, blocks, scale, rates, mass, sigma, live, edges, forward = call(
        table_stage,
        pinned(angular, stiff, mass, sigma, live, edges, forward),
        [
            shape(LANES, SIDE * slots, kind=jnp.bfloat16),
            shape(freqs * SIDE * SIDE, tall, LANES),
            sums_shape,
            shape(freqs, tall, LANES),
            *kept,
        ],
        (
            pltpu.SMEM(angular.shape, angular.dtype),
            pltpu.VMEM(stiff.shape, stiff.dtype),
            pltpu.SemaphoreType.DMA((7,)),
        ),
        space=HBM,
        cost=4_000_000,
    )
    picks, image, across, beside, inverse, sums = call(
        functools.partial(first_stage, polars),
        (source, order, across, beside, scale, blocks, edges, places),
        [
            picks_shape,
            field_shape,
            rim_shape,
            rim_shape,
            shape(rows, rim, kind=jnp.int32),
            sums_shape,
        ],
        (field_room, piece_room),
    )
    across, beside = swap(across, "dom", 1), swap(beside, "dom", 0)
    heavy, terms0 = call(
        functools.partial(forward_stage, polars),
        (rates, forward, mass, live, edges, picks),
        [picks_shape, terms_shape],
        cost=4_000_000,
    )
    terms1, sums, image, across, beside = call(
        functools.partial(later_stage, polars, 1, False),
        (image, order, inverse, across, beside, sums, blocks, edges, heavy, places),
        [terms_shape, sums_shape, field_shape, rim_shape, rim_shape],
        (field_room, piece_room),
    )
    across, beside = swap(across, "dom", 1), swap(beside, "dom", 0)
    terms2, sums = call(
        functools.partial(later_stage, polars, 2, True),
        (image, order, inverse, across, beside, sums, blocks, edges, heavy),
        [terms_shape, sums_shape],
        (field_room,),
    )
    term = call(
        combine_stage,
        (gather_all(sums, "dom"), sums, terms0, terms1, terms2),
        shape(tall, LANES),
    )
    gradient = sum_over(term, "freq").reshape(1, slots)
    updated = sigma.reshape(1, slots) * jnp.exp(-0.5 * jnp.tanh(gradient))
    return gradient, updated


def solution(mesh):
    return jax.shard_map(
        local,
        mesh=mesh,
        in_specs=(
            P("freq"),
            P("dom", None, None),
            P("dom", None, None),
            P("dom", None),
            P("dom", None, None),
            P("dom", None),
            P("freq", None, "dom", None),
            P("freq", None, "dom", None),
            P("dom", None),
        ),
        out_specs=(P("dom", None), P("dom", None)),
        check_vma=False,
    )
```

```python
import functools

import jax
import jax.numpy as jnp
from jax import lax
from jax.experimental import pallas as pl
from jax.experimental.pallas import tpu as pltpu
from jax.sharding import PartitionSpec as P

LANES = 128
SUBLANES = 8
SIDE = 6
VMEM = pl.BlockSpec(memory_space=pltpu.VMEM)
HBM = pl.BlockSpec(memory_space=pltpu.HBM)

PICK_LANES = lax.GatherDimensionNumbers(
    offset_dims=(),
    collapsed_slice_dims=(1,),
    start_index_map=(1,),
    operand_batching_dims=(0,),
    start_indices_batching_dims=(0,),
)


def pick_lanes(block, lanes):
    return lax.gather(
        block,
        lanes[..., None],
        PICK_LANES,
        (1, 1),
        mode=lax.GatherScatterMode.PROMISE_IN_BOUNDS,
    )


def pick_wide(chunks, index):
    lanes = index & (LANES - 1)
    high = index >> 7
    level = [pick_lanes(chunk, lanes) for chunk in chunks]
    bit = 0
    while len(level) > 1:
        odd = (high >> bit) & 1 == 1
        level = [
            jnp.where(odd, level[t + 1], level[t]) if t + 1 < len(level) else level[t]
            for t in range(0, len(level), 2)
        ]
        bit += 1
    return level[0]


def row_ids(rows):
    return lax.broadcasted_iota(jnp.int32, (rows, LANES), 0)


def lane_ids(rows):
    return lax.broadcasted_iota(jnp.int32, (rows, LANES), 1)


def spread(row, rows):
    return jnp.broadcast_to(row, (rows, row.shape[-1]))


def cut(ref):
    return [ref[:, c : c + LANES] for c in range(0, ref.shape[-1], LANES)]


def swap_halves(block):
    return pltpu.roll(block, block.shape[0] // 2, 0)


def doubled(block):
    half = block.shape[0] // 2
    return jnp.where(row_ids(2 * half) < half, block, swap_halves(block))


def lane_sum(block):
    return jnp.broadcast_to(jnp.sum(block, axis=1, keepdims=True), block.shape)


def put_lane(block, lane, value):
    return jnp.where(lane_ids(block.shape[0]) == lane, value, block)


def put_chunks(ref, chunks):
    for c, chunk in enumerate(chunks):
        ref[:, c * LANES : (c + 1) * LANES] = chunk


def is_even():
    return lax.rem(lax.axis_index("dom"), 2) == 0


def put_rims(across_ref, beside_ref, lower, upper):
    even = is_even()
    for c, (low, high) in enumerate(zip(lower, upper)):
        here = slice(c * LANES, (c + 1) * LANES)
        across_ref[:, here] = jnp.where(even, low, high)
        beside_ref[:, here] = jnp.where(even, high, low)


def take_rims(across_ref, beside_ref):
    even = is_even()
    pairs = list(zip(cut(across_ref), cut(beside_ref)))
    prior = [jnp.where(even, a, b) for a, b in pairs]
    above = [jnp.where(even, b, a) for a, b in pairs]
    return prior, above


def picks_of(rows_of_group, edges):
    chunks = [spread(row, edges.shape[1]) for row in rows_of_group]
    return [pick_wide(chunks, edges[j]) for j in range(SIDE)]


def group_rows(ref, g):
    return [ref[g : g + 1, c : c + LANES] for c in range(0, ref.shape[-1], LANES)]


def times_block(entries, base, picked):
    out = []
    for i in range(SIDE):
        total = None
        for j in range(SIDE):
            one = entries[base + SIDE * i + j] * picked[j]
            total = one if total is None else total + one
        out.append(total)
    return out


def weighted_sum(left, right):
    total = None
    for a, b in zip(left, right):
        total = a * b if total is None else total + a * b
    return total


def scatter(pieces, edges, places, heights):
    depth = SIDE * edges.shape[1]
    rows = pieces.shape[0] // depth
    slots = edges.shape[1] * LANES
    total = None
    for i in range(SIDE):
        columns = []
        for s in range(edges.shape[1]):
            both = pieces[pl.ds(i * edges.shape[1] + s, rows, stride=depth), :]
            high = spread(edges[i, s : s + 1, :] >> 7, rows)
            stacked = [jnp.where(high == h, both, 0.0) for h in heights]
            columns.append(jnp.concatenate(stacked, axis=0).astype(jnp.bfloat16))
        part = lax.dot_general(
            jnp.concatenate(columns, axis=1),
            places[:, i * slots : (i + 1) * slots],
            (((1,), (1,)), ((), ())),
            preferred_element_type=jnp.float32,
        )
        total = part if total is None else total + part
    out = []
    for n in range(len(heights)):
        piece = total[rows * n : rows * (n + 1)]
        out.append(piece + swap_halves(piece))
    return out


def rim_heights(edge_count, rim):
    count = edge_count // LANES
    return [*range(rim), *range(count - rim, count)], list(range(rim, count - rim))


def corrections(from_prior, from_above, order, inverse):
    lower = [pick_wide(from_prior, index) for index in order]
    return lower + [pick_wide(from_above, index) for index in inverse]


def corrected(own, delta):
    rim = len(delta) // 2
    lower = [a + b for a, b in zip(own[:rim], delta[:rim])]
    upper = [a + b for a, b in zip(own[len(own) - rim :], delta[rim:])]
    return lower + own[rim : len(own) - rim] + upper


def squares(chunks, rim, has_prior):
    total = None
    for c, chunk in enumerate(chunks):
        term = chunk * chunk
        if c < rim:
            term = term * (1.0 - has_prior)
        total = term if total is None else total + term
    return total


def start_copies(routes, arrived):
    copies = [
        pltpu.make_async_copy(here, there, arrived.at[n])
        for n, (here, there) in enumerate(routes)
    ]
    for copy in copies:
        copy.start()
    return copies


def rims_stage(
    source_in, order_in, across_ref, beside_ref, stacked_ref, order_ref, source, order, arrived
):
    for copy in start_copies(((source_in, source), (order_in, order)), arrived):
        copy.wait()
    groups = source.shape[0]
    rows = stacked_ref.shape[0]
    first = row_ids(rows) < groups
    chunks = []
    for c in range(0, source.shape[-1], LANES):
        piece = [source[g, :, c : c + LANES] for g in range(groups)]
        chunks.append(jnp.concatenate(piece + piece, axis=0))
    put_chunks(stacked_ref, chunks)
    order_ref[...] = spread(order[...], rows)
    numbers = [x.astype(jnp.float32) for x in cut(order_ref)]
    count = len(numbers)
    lower = [jnp.where(first, x, o) for x, o in zip(chunks[:count], numbers)]
    upper = [jnp.where(first, x, 1.0) for x in chunks[len(chunks) - count :]]
    put_rims(across_ref, beside_ref, lower, upper)


def table_stage(
    angular_in,
    stiffness_in,
    mass_in,
    sigma_in,
    live_in,
    edges_in,
    forward_in,
    source,
    places_ref,
    blocks_ref,
    scale_ref,
    picks_ref,
    rates,
    mass,
    sigma,
    live,
    edges,
    forward_ref,
    angular,
    stiffness,
    arrived,
):
    copies = start_copies(
        (
            (edges_in, edges),
            (angular_in, angular),
            (sigma_in, sigma),
            (live_in, live),
            (stiffness_in, stiffness),
            (mass_in, mass),
            (forward_in, forward_ref),
        ),
        arrived,
    )
    copies[0].wait()
    numbers = row_ids(LANES)
    rows = edges.shape[1]

    def body(i, carry):
        for s in range(rows):
            lanes = spread(edges[i, s : s + 1, :] & (LANES - 1), LANES)
            column = pl.ds(pl.multiple_of((i * rows + s) * LANES, LANES), LANES)
            places_ref[:, column] = jnp.where(lanes == numbers, 1.0, 0.0).astype(jnp.bfloat16)
        return carry

    lax.fori_loop(0, SIDE, body, 0)
    put_picks(picks_ref, source, edges, scale_ref.shape[0] // 2)
    for copy in copies[1:]:
        copy.wait()
    for f in range(angular.shape[0]):
        rates[f] = jnp.full(rates.shape[1:], angular[f], jnp.float32)
    alive = live[...].astype(jnp.float32)
    weight = sigma[...]
    freqs = rates.shape[0]
    peak = None
    for i in range(SIDE):
        for f in range(freqs):
            entry = (SIDE + 1) * i
            size = stiffness[entry] + rates[f] * weight * mass[entry]
            peak = size if peak is None else jnp.maximum(peak, size)
    peak = jnp.max(peak * alive, axis=1, keepdims=True)
    scale = jnp.broadcast_to(jnp.max(peak, axis=0, keepdims=True), scale_ref.shape)
    scale_ref[...] = scale
    alive = alive / scale[:1, :1]
    for entry in range(SIDE * SIDE):
        stiff = stiffness[entry] * alive
        heavy = mass[entry] * (weight * alive)
        for f in range(freqs):
            blocks_ref[f * SIDE * SIDE + entry] = stiff + rates[f] * heavy


def put_picks(picks_ref, field, edges, groups):
    for g in range(groups):
        for j, value in enumerate(picks_of(group_rows(field, g), edges)):
            picks_ref[g * SIDE + j] = value


def pick_rims(rows, index, edge_count):
    rim = len(rows) // 2
    start = edge_count - rim * LANES
    lower = pick_wide([spread(row, index.shape[0]) for row in rows[:rim]], index)
    upper = pick_wide([spread(row, index.shape[0]) for row in rows[rim:]], index - start)
    lower = jnp.where(index < rim * LANES, lower, 0.0)
    return lower + jnp.where(index >= start, upper, 0.0)


def apply_all(delta_ref, own_picks, blocks, edges, polars, edge_count, pieces, visit):
    rows = delta_ref.shape[0]
    groups = rows // 2
    depth = SIDE * edges.shape[1]
    forms = jnp.zeros((rows, LANES), jnp.float32)
    for g in range(groups):
        delta = group_rows(delta_ref, g)
        picked = [
            own_picks[g * SIDE + j] + pick_rims(delta, edges[j], edge_count)
            for j in range(SIDE)
        ]
        visit(g, picked)
        values = times_block(blocks, (g // polars) * SIDE * SIDE, picked)
        form = jnp.sum(weighted_sum(picked, values), axis=0, keepdims=True)
        forms = jnp.where(row_ids(rows) == g, spread(form, rows), forms)
        if pieces is None:
            continue
        for i, value in enumerate(values):
            coarse = value.astype(jnp.bfloat16).astype(jnp.float32)
            for part, piece in enumerate((coarse, value - coarse)):
                at = (part * groups + g) * depth + i * edges.shape[1]
                pieces[at : at + edges.shape[1], :] = piece
    return forms


def invert(above, groups, rows):
    above_order = jnp.concatenate([x[groups : groups + 1] for x in above], axis=1)
    rim = above_order.shape[1]
    slot = lax.broadcasted_iota(jnp.int32, (rim, rim), 0).astype(jnp.float32)
    match = jnp.where(spread(above_order, rim) == slot, 1.0, 0.0).astype(jnp.bfloat16)
    numbers = lax.broadcasted_iota(jnp.int32, (2 * rows, rim), 1).astype(jnp.bfloat16)
    inverse = lax.dot_general(
        numbers, match, (((1,), (1,)), ((), ())), preferred_element_type=jnp.float32
    )
    return inverse[:rows].astype(jnp.int32)


def rescaled(block, inverse_scale, step):
    ratio = swap_halves(block) * inverse_scale
    for _ in range(step):
        block = block * ratio
    return doubled(block)


def front_stage(
    polars,
    step,
    edge_count,
    order_ref,
    across_in,
    beside_in,
    scale_in,
    own_picks,
    blocks,
    edges,
    places,
    *rest,
):
    if step == 0:
        inverse_ref, *rest = rest
    else:
        inverse_in, *rest = rest
    delta_ref, picks_ref, pieces, forms_ref, rims_ref, across_ref, beside_ref = rest
    rows = delta_ref.shape[0]
    groups = rows // 2
    first = row_ids(rows) < groups
    scale = scale_in[...]
    prior, above = take_rims(across_in, beside_in)
    if step == 0:
        inverse_ref[...] = invert(above, groups, rows)
        inverse = cut(inverse_ref)
        prior, above = [doubled(x) for x in prior], [doubled(x) for x in above]
    else:
        inverse = cut(inverse_in)
        inverse_scale = 1.0 / scale
        prior = [rescaled(x, inverse_scale, step) for x in prior]
        above = [rescaled(x, inverse_scale, step) for x in above]
    put_chunks(delta_ref, corrections(prior, above, cut(order_ref), inverse))

    def visit(g, picked):
        for j in range(SIDE):
            picks_ref[g * SIDE + j] = picked[j]

    forms_ref[...] = apply_all(
        delta_ref, own_picks, blocks, edges, polars, edge_count, pieces, visit
    )
    rim = len(prior)
    chunks = scatter(pieces, edges, places, rim_heights(edge_count, rim)[0])
    put_chunks(rims_ref, chunks)
    put_rims(
        across_ref,
        beside_ref,
        [jnp.where(first, x, scale) for x in chunks[:rim]],
        [jnp.where(first, x, scale) for x in chunks[rim:]],
    )


def inner_products(step, sums, own, delta, forms, across_in, beside_in):
    rows = sums.shape[0]
    first = row_ids(rows) < rows // 2
    prior, _ = take_rims(across_in, beside_in)
    has_prior = jnp.where(first, swap_halves(prior[0]), prior[0])
    has_prior = spread(jnp.where(has_prior[:1, :1] > 0.0, 1.0, 0.0), rows)
    field = corrected(own, delta)
    sums = put_lane(sums, 2 * step, lane_sum(squares(field, len(delta) // 2, has_prior)))
    return put_lane(sums, 2 * step + 1, lane_sum(forms))


def back_stage(
    polars,
    step,
    own,
    delta,
    forms,
    across_in,
    beside_in,
    sums_in,
    picks,
    pieces,
    rims,
    edges,
    places,
    *rest,
):
    if step == 0:
        rates, forward, mass, live, heavy, terms_ref, sums_ref, image_ref, picks_ref = rest
    else:
        heavy, terms_ref, sums_ref, image_ref, picks_ref = rest
    rows, edge_count = own.shape
    groups = rows // 2
    rim = rims.shape[-1] // LANES // 2
    outer = cut(rims)
    inner = scatter(pieces, edges, places, rim_heights(edge_count, rim)[1])
    put_chunks(image_ref, outer[:rim] + inner + outer[rim:])
    put_picks(picks_ref, image_ref, edges, groups)
    if step == 0:
        dead = -live[...].astype(jnp.float32)
        for g in range(groups):
            row = [forward[g, :, c : c + LANES] for c in range(0, edge_count, LANES)]
            values = times_block(mass, 0, picks_of(row, edges))
            factor = dead * rates[g // polars]
            for i in range(SIDE):
                heavy[g * SIDE + i] = factor * values[i]
    for g in range(groups):
        side = range(g * SIDE, (g + 1) * SIDE)
        terms_ref[g] = weighted_sum([picks[i] for i in side], [heavy[i] for i in side])
    sums_ref[...] = inner_products(
        step, sums_in[...], cut(own), cut(delta), forms[...], across_in, beside_in
    )


def last_stage(
    polars,
    step,
    own,
    order_ref,
    inverse_in,
    across_in,
    beside_in,
    scale_in,
    sums_in,
    own_picks,
    blocks,
    edges,
    heavy,
    terms_ref,
    sums_ref,
    delta_ref,
):
    rows, edge_count = own.shape
    first = row_ids(rows) < rows // 2
    scale = scale_in[...]
    inverse_scale = 1.0 / scale
    prior, above = take_rims(across_in, beside_in)
    prior = [rescaled(x, inverse_scale, step) for x in prior]
    above = [rescaled(x, inverse_scale, step) for x in above]
    put_chunks(delta_ref, corrections(prior, above, cut(order_ref), cut(inverse_in)))

    def visit(g, picked):
        terms_ref[g] = weighted_sum(picked, [heavy[g * SIDE + i] for i in range(SIDE)])

    forms = apply_all(delta_ref, own_picks, blocks, edges, polars, edge_count, None, visit)
    sums = inner_products(
        step, sums_in[...], cut(own), cut(delta_ref), forms, across_in, beside_in
    )
    sums_ref[...] = jnp.where(first, sums, scale)


def combine_stage(everyone, sums_in, terms0, terms1, terms2, out_ref):
    rows = sums_in.shape[0]
    groups = rows // 2
    first = row_ids(rows) < groups

    def scale_of(block):
        return jnp.where(first, swap_halves(block), block)

    parts = [everyone[q] for q in range(everyone.shape[0])]
    scales = [scale_of(block) for block in parts]
    top = functools.reduce(jnp.maximum, scales)
    lanes = lane_ids(rows)
    inverse_top = 1.0 / top
    total = None
    for block, scale in zip(parts, scales):
        ratio = scale * inverse_top
        power = jnp.ones_like(ratio)
        factor = jnp.ones_like(ratio)
        for k in range(1, 6):
            power = power * ratio
            factor = jnp.where(lanes == k, power, factor)
        term = block * factor
        total = term if total is None else total + term
    m = [jnp.broadcast_to(total[:, k : k + 1], (rows, LANES)) for k in range(6)]
    l1 = m[2] / m[1]
    l2 = m[3] / m[1]
    d2 = m[3] - l1 * m[2]
    cross = m[4] - l2 * m[2]
    l3 = cross / d2
    d3 = m[5] - l2 * m[3] - l3 * cross
    y1 = m[1] - l1 * m[0]
    y2 = m[2] - l2 * m[0] - l3 * y1
    c2 = y2 / d3
    c1 = y1 / d2 - l3 * c2
    c0 = m[0] / m[1] - l1 * c1 - l2 * c2
    mine = scale_of(sums_in[...]) * inverse_top
    c0 = c0 * inverse_top
    c1 = c1 * mine * inverse_top
    c2 = c2 * mine * mine * inverse_top
    out = None
    for terms, c in ((terms0, c0), (terms1, c1), (terms2, c2)):
        for g in range(groups):
            one = terms[g] * spread(c[g : g + 1], out_ref.shape[0])
            out = one if out is None else out + one
    out_ref[...] = out


def pinned(*arguments):
    return [pltpu.with_memory_space_constraint(x, pltpu.HBM) for x in arguments]


def call(kernel, arguments, outs, scratch=(), space=VMEM, cost=0):
    return pl.pallas_call(
        kernel,
        out_shape=outs,
        in_specs=space if isinstance(space, list) else [space] * len(arguments),
        out_specs=jax.tree.map(lambda _: VMEM, outs),
        scratch_shapes=list(scratch),
        cost_estimate=pl.CostEstimate(flops=cost, bytes_accessed=cost, transcendentals=0),
        compiler_params=pltpu.CompilerParams(vmem_limit_bytes=16 * 1024 * 1024),
    )(*arguments)


def swap(block, axis, offset):
    size = lax.axis_size(axis)
    route = []
    for low in range(offset, size - 1, 2):
        route += [(low, low + 1), (low + 1, low)]
    return lax.ppermute(block, axis, route)


def gather_all(block, axis):
    size = lax.axis_size(axis)
    copies = jnp.broadcast_to(block[None], (size, *block.shape))
    return lax.all_to_all(copies, axis, 0, 0)


def sum_over(block, axis):
    size = lax.axis_size(axis)
    if size & (size - 1):
        return jnp.sum(gather_all(block, axis), axis=0)
    near = min(size, 4)
    parts = [block] + [None] * (near - 1)
    for step in reversed(range(1, near)):
        parts[step] = lax.ppermute(block, axis, [(i, i ^ step) for i in range(size)])
    while len(parts) > 1:
        parts = [a + b for a, b in zip(parts[::2], parts[1::2])]
    block = parts[0]
    step = near
    while step < size:
        block = block + lax.ppermute(block, axis, [(i, i ^ step) for i in range(size)])
        step *= 2
    return block


def local(
    angular,
    stiffness,
    mass_matrix,
    conductivity,
    element_edges,
    live_slots,
    adjoint_source,
    forward_field,
    neighbour_map,
):
    freqs = angular.shape[0]
    polars = adjoint_source.shape[1]
    groups = freqs * polars
    rows = 2 * groups
    edge_count = adjoint_source.shape[-1]
    rim = neighbour_map.shape[-1]
    slots = element_edges.shape[-1]
    tall = slots // LANES
    stiff = stiffness.reshape(SIDE * SIDE, tall, LANES)
    mass = mass_matrix.reshape(SIDE * SIDE, tall, LANES)
    edges = element_edges.reshape(SIDE, tall, LANES)
    sigma = conductivity.reshape(tall, LANES)
    live = live_slots.reshape(tall, LANES)
    source = adjoint_source.reshape(groups, 1, edge_count)
    forward = forward_field.reshape(groups, 1, edge_count)

    def shape(*dims, kind=jnp.float32):
        return jax.ShapeDtypeStruct(dims, kind)

    field_shape, rim_shape = shape(rows, edge_count), shape(rows, rim)
    sums_shape, terms_shape = shape(rows, LANES), shape(groups, tall, LANES)
    picks_shape = shape(groups * SIDE, tall, LANES)

    across, beside, source, order = call(
        rims_stage,
        pinned(source, neighbour_map),
        [rim_shape, rim_shape, field_shape, shape(rows, rim, kind=jnp.int32)],
        (
            pltpu.VMEM(source.shape, source.dtype),
            pltpu.VMEM(neighbour_map.shape, neighbour_map.dtype),
            pltpu.SemaphoreType.DMA((2,)),
        ),
        space=HBM,
    )
    across, beside = swap(across, "dom", 1), swap(beside, "dom", 0)
    kept = [jax.ShapeDtypeStruct(x.shape, x.dtype) for x in (mass, sigma, live, edges, forward)]
    places, blocks, scale, picks, rates, mass, sigma, live, edges, forward = call(
        table_stage,
        [*pinned(angular, stiff, mass, sigma, live, edges, forward), source],
        [
            shape(LANES, SIDE * slots, kind=jnp.bfloat16),
            shape(freqs * SIDE * SIDE, tall, LANES),
            sums_shape,
            picks_shape,
            shape(freqs, tall, LANES),
            *kept,
        ],
        (
            pltpu.SMEM(angular.shape, angular.dtype),
            pltpu.VMEM(stiff.shape, stiff.dtype),
            pltpu.SemaphoreType.DMA((7,)),
        ),
        space=[HBM] * 7 + [VMEM],
        cost=4_000_000,
    )
    front_shapes = [
        shape(rows, 2 * rim),
        picks_shape,
        shape(rows * SIDE * tall, LANES),
        sums_shape,
        shape(rows, 2 * rim),
        rim_shape,
        rim_shape,
    ]
    back_shapes = [terms_shape, sums_shape, field_shape, picks_shape]
    own, sums, terms = source, jnp.zeros((rows, LANES), jnp.float32), []
    for step in range(2):
        arrived = (across, beside)
        given = (order, *arrived, scale, picks, blocks, edges, places)
        front = functools.partial(front_stage, polars, step, edge_count)
        if step == 0:
            inverse, *outs = call(
                front, given, [shape(rows, rim, kind=jnp.int32), *front_shapes]
            )
        else:
            outs = call(front, (*given, inverse), front_shapes)
        delta, picks, pieces, forms, rims, across, beside = outs
        across, beside = swap(across, "dom", 1), swap(beside, "dom", 0)
        given = (own, delta, forms, *arrived, sums, picks, pieces, rims, edges, places)
        back = functools.partial(back_stage, polars, step)
        if step == 0:
            heavy, term, sums, own, picks = call(
                back,
                (*given, rates, forward, mass, live),
                [picks_shape, *back_shapes],
                cost=4_000_000,
            )
        else:
            term, sums, own, picks = call(back, (*given, heavy), back_shapes, cost=4_000_000)
        terms.append(term)
    term, sums = call(
        functools.partial(last_stage, polars, 2),
        (own, order, inverse, across, beside, scale, sums, picks, blocks, edges, heavy),
        [terms_shape, sums_shape],
        (pltpu.VMEM((rows, 2 * rim), jnp.float32),),
    )
    terms.append(term)
    term = call(
        combine_stage,
        (gather_all(sums, "dom"), sums, *terms),
        shape(tall, LANES),
    )
    gradient = sum_over(term, "freq").reshape(1, slots)
    updated = sigma.reshape(1, slots) * jnp.exp(-0.5 * jnp.tanh(gradient))
    return gradient, updated


def solution(mesh):
    return jax.shard_map(
        local,
        mesh=mesh,
        in_specs=(
            P("freq"),
            P("dom", None, None),
            P("dom", None, None),
            P("dom", None),
            P("dom", None, None),
            P("dom", None),
            P("freq", None, "dom", None),
            P("freq", None, "dom", None),
            P("dom", None),
        ),
        out_specs=(P("dom", None), P("dom", None)),
        check_vma=False,
    )
```

```python
import functools

import jax
import jax.numpy as jnp
from jax import lax
from jax.experimental import pallas as pl
from jax.experimental.pallas import tpu as pltpu
from jax.sharding import PartitionSpec as P

LANES = 128
SUBLANES = 8
SIDE = 6
MOMENT_LANES = 8
VMEM = pl.BlockSpec(memory_space=pltpu.VMEM)
HBM = pl.BlockSpec(memory_space=pltpu.HBM)

PICK_LANES = lax.GatherDimensionNumbers(
    offset_dims=(),
    collapsed_slice_dims=(1,),
    start_index_map=(1,),
    operand_batching_dims=(0,),
    start_indices_batching_dims=(0,),
)


def pick_lanes(block, lanes):
    return lax.gather(
        block,
        lanes[..., None],
        PICK_LANES,
        (1, 1),
        mode=lax.GatherScatterMode.PROMISE_IN_BOUNDS,
    )


def pick_wide(chunks, index):
    lanes = index & (LANES - 1)
    high = index >> 7
    level = [pick_lanes(chunk, lanes) for chunk in chunks]
    bit = 0
    while len(level) > 1:
        odd = (high >> bit) & 1 == 1
        level = [
            jnp.where(odd, level[t + 1], level[t]) if t + 1 < len(level) else level[t]
            for t in range(0, len(level), 2)
        ]
        bit += 1
    return level[0]


def row_ids(rows):
    return lax.broadcasted_iota(jnp.int32, (rows, LANES), 0)


def lane_ids(rows):
    return lax.broadcasted_iota(jnp.int32, (rows, LANES), 1)


def spread(row, rows):
    return jnp.broadcast_to(row, (rows, row.shape[-1]))


def cut(ref):
    return [ref[:, c : c + LANES] for c in range(0, ref.shape[-1], LANES)]


def swap_halves(block):
    return pltpu.roll(block, block.shape[0] // 2, 0)


def doubled(block):
    half = block.shape[0] // 2
    return jnp.where(row_ids(2 * half) < half, block, swap_halves(block))


def lane_sum(block):
    return jnp.broadcast_to(jnp.sum(block, axis=1, keepdims=True), block.shape)


def put_lane(block, lane, value):
    return jnp.where(lane_ids(block.shape[0]) == lane, value, block)


def put_chunks(ref, chunks):
    for c, chunk in enumerate(chunks):
        ref[:, c * LANES : (c + 1) * LANES] = chunk


def is_even():
    return lax.rem(lax.axis_index("dom"), 2) == 0


def put_rims(across_ref, beside_ref, lower, upper):
    even = is_even()
    for c, (low, high) in enumerate(zip(lower, upper)):
        here = slice(c * LANES, (c + 1) * LANES)
        across_ref[:, here] = jnp.where(even, low, high)
        beside_ref[:, here] = jnp.where(even, high, low)


def take_rims(across_ref, beside_ref):
    even = is_even()
    pairs = list(zip(cut(across_ref), cut(beside_ref)))
    prior = [jnp.where(even, a, b) for a, b in pairs]
    above = [jnp.where(even, b, a) for a, b in pairs]
    return prior, above


def picks_of(rows_of_group, edges):
    chunks = [spread(row, edges.shape[1]) for row in rows_of_group]
    return [pick_wide(chunks, edges[j]) for j in range(SIDE)]


def group_rows(ref, g):
    return [ref[g : g + 1, c : c + LANES] for c in range(0, ref.shape[-1], LANES)]


def times_block(entries, base, picked):
    out = []
    for i in range(SIDE):
        total = None
        for j in range(SIDE):
            one = entries[base + SIDE * i + j] * picked[j]
            total = one if total is None else total + one
        out.append(total)
    return out


def weighted_sum(left, right):
    total = None
    for a, b in zip(left, right):
        total = a * b if total is None else total + a * b
    return total


def scatter(pieces, edges, places, heights):
    depth = SIDE * edges.shape[1]
    rows = pieces.shape[0] // depth
    slots = edges.shape[1] * LANES
    total = None
    for i in range(SIDE):
        columns = []
        for s in range(edges.shape[1]):
            both = pieces[pl.ds(i * edges.shape[1] + s, rows, stride=depth), :]
            high = spread(edges[i, s : s + 1, :] >> 7, rows)
            stacked = [jnp.where(high == h, both, 0.0) for h in heights]
            columns.append(jnp.concatenate(stacked, axis=0).astype(jnp.bfloat16))
        part = lax.dot_general(
            places[:, i * slots : (i + 1) * slots],
            jnp.concatenate(columns, axis=1),
            (((1,), (1,)), ((), ())),
            preferred_element_type=jnp.float32,
        )
        total = part if total is None else total + part
    total = total.T
    out = []
    for n in range(len(heights)):
        piece = total[rows * n : rows * (n + 1)]
        out.append(piece + swap_halves(piece))
    return out


def rim_heights(edge_count, rim):
    count = edge_count // LANES
    return [*range(rim), *range(count - rim, count)], list(range(rim, count - rim))


def corrections(from_prior, from_above, order, inverse):
    lower = [pick_wide(from_prior, index) for index in order]
    return lower + [pick_wide(from_above, index) for index in inverse]


def corrected(own, delta):
    rim = len(delta) // 2
    lower = [a + b for a, b in zip(own[:rim], delta[:rim])]
    upper = [a + b for a, b in zip(own[len(own) - rim :], delta[rim:])]
    return lower + own[rim : len(own) - rim] + upper


def squares(chunks, rim, has_prior):
    total = None
    for c, chunk in enumerate(chunks):
        term = chunk * chunk
        if c < rim:
            term = term * (1.0 - has_prior)
        total = term if total is None else total + term
    return total


def start_copies(routes, arrived):
    copies = [
        pltpu.make_async_copy(here, there, arrived.at[n])
        for n, (here, there) in enumerate(routes)
    ]
    for copy in copies:
        copy.start()
    return copies


def rims_stage(
    source_in, order_in, across_ref, beside_ref, stacked_ref, order_ref, source, order, arrived
):
    for copy in start_copies(((source_in, source), (order_in, order)), arrived):
        copy.wait()
    groups = source.shape[0]
    rows = stacked_ref.shape[0]
    first = row_ids(rows) < groups
    chunks = []
    for c in range(0, source.shape[-1], LANES):
        piece = [source[g, :, c : c + LANES] for g in range(groups)]
        chunks.append(jnp.concatenate(piece + piece, axis=0))
    put_chunks(stacked_ref, chunks)
    order_ref[...] = spread(order[...], rows)
    numbers = [x.astype(jnp.float32) for x in cut(order_ref)]
    count = len(numbers)
    lower = [jnp.where(first, x, o) for x, o in zip(chunks[:count], numbers)]
    upper = [jnp.where(first, x, 1.0) for x in chunks[len(chunks) - count :]]
    put_rims(across_ref, beside_ref, lower, upper)


def table_stage(
    angular_in,
    stiffness_in,
    mass_in,
    sigma_in,
    live_in,
    edges_in,
    forward_in,
    source,
    places_ref,
    blocks_ref,
    scale_ref,
    picks_ref,
    rates,
    mass,
    sigma,
    live,
    edges,
    forward_ref,
    angular,
    stiffness,
    arrived,
):
    copies = start_copies(
        (
            (edges_in, edges),
            (angular_in, angular),
            (sigma_in, sigma),
            (live_in, live),
            (stiffness_in, stiffness),
            (mass_in, mass),
            (forward_in, forward_ref),
        ),
        arrived,
    )
    copies[0].wait()
    numbers = row_ids(LANES)
    rows = edges.shape[1]

    def body(i, carry):
        for s in range(rows):
            lanes = spread(edges[i, s : s + 1, :] & (LANES - 1), LANES)
            column = pl.ds(pl.multiple_of((i * rows + s) * LANES, LANES), LANES)
            places_ref[:, column] = jnp.where(lanes == numbers, 1.0, 0.0).astype(jnp.bfloat16)
        return carry

    lax.fori_loop(0, SIDE, body, 0)
    put_picks(picks_ref, source, edges, scale_ref.shape[0] // 2)
    for copy in copies[1:]:
        copy.wait()
    for f in range(angular.shape[0]):
        rates[f] = jnp.full(rates.shape[1:], angular[f], jnp.float32)
    alive = live[...].astype(jnp.float32)
    weight = sigma[...]
    freqs = rates.shape[0]
    peak = None
    for i in range(SIDE):
        for f in range(freqs):
            entry = (SIDE + 1) * i
            size = stiffness[entry] + rates[f] * weight * mass[entry]
            peak = size if peak is None else jnp.maximum(peak, size)
    peak = jnp.max(peak * alive, axis=1, keepdims=True)
    scale = jnp.broadcast_to(jnp.max(peak, axis=0, keepdims=True), scale_ref.shape)
    scale_ref[...] = scale
    alive = alive / scale[:1, :1]
    for entry in range(SIDE * SIDE):
        stiff = stiffness[entry] * alive
        heavy = mass[entry] * (weight * alive)
        for f in range(freqs):
            blocks_ref[f * SIDE * SIDE + entry] = stiff + rates[f] * heavy


def put_picks(picks_ref, field, edges, groups):
    for g in range(groups):
        for j, value in enumerate(picks_of(group_rows(field, g), edges)):
            picks_ref[g * SIDE + j] = value


def pick_rims(rows, index, edge_count):
    rim = len(rows) // 2
    start = edge_count - rim * LANES
    lower = pick_wide([spread(row, index.shape[0]) for row in rows[:rim]], index)
    upper = pick_wide([spread(row, index.shape[0]) for row in rows[rim:]], index - start)
    lower = jnp.where(index < rim * LANES, lower, 0.0)
    return lower + jnp.where(index >= start, upper, 0.0)


def apply_all(delta_ref, own_picks, blocks, edges, polars, edge_count, pieces, visit):
    rows = delta_ref.shape[0]
    groups = rows // 2
    depth = SIDE * edges.shape[1]
    forms = jnp.zeros((rows, LANES), jnp.float32)
    for g in range(groups):
        delta = group_rows(delta_ref, g)
        picked = [
            own_picks[g * SIDE + j] + pick_rims(delta, edges[j], edge_count)
            for j in range(SIDE)
        ]
        visit(g, picked)
        values = times_block(blocks, (g // polars) * SIDE * SIDE, picked)
        form = jnp.sum(weighted_sum(picked, values), axis=0, keepdims=True)
        forms = jnp.where(row_ids(rows) == g, spread(form, rows), forms)
        if pieces is None:
            continue
        for i, value in enumerate(values):
            coarse = value.astype(jnp.bfloat16).astype(jnp.float32)
            for part, piece in enumerate((coarse, value - coarse)):
                at = (part * groups + g) * depth + i * edges.shape[1]
                pieces[at : at + edges.shape[1], :] = piece
    return forms


def invert(above, groups, rows):
    above_order = jnp.concatenate([x[groups : groups + 1] for x in above], axis=1)
    rim = above_order.shape[1]
    slot = lax.broadcasted_iota(jnp.int32, (rim, rim), 0).astype(jnp.float32)
    match = jnp.where(spread(above_order, rim) == slot, 1.0, 0.0).astype(jnp.bfloat16)
    numbers = lax.broadcasted_iota(jnp.int32, (2 * rows, rim), 1).astype(jnp.bfloat16)
    inverse = lax.dot_general(
        numbers, match, (((1,), (1,)), ((), ())), preferred_element_type=jnp.float32
    )
    return inverse[:rows].astype(jnp.int32)


def rescaled(block, inverse_scale, step):
    ratio = swap_halves(block) * inverse_scale
    for _ in range(step):
        block = block * ratio
    return doubled(block)


def front_stage(
    polars,
    step,
    edge_count,
    order_ref,
    across_in,
    beside_in,
    scale_in,
    own_picks,
    blocks,
    edges,
    places,
    *rest,
):
    if step == 0:
        inverse_ref, *rest = rest
    else:
        inverse_in, *rest = rest
    delta_ref, picks_ref, pieces, forms_ref, rims_ref, across_ref, beside_ref = rest
    rows = delta_ref.shape[0]
    groups = rows // 2
    first = row_ids(rows) < groups
    scale = scale_in[...]
    prior, above = take_rims(across_in, beside_in)
    if step == 0:
        inverse_ref[...] = invert(above, groups, rows)
        inverse = cut(inverse_ref)
        prior, above = [doubled(x) for x in prior], [doubled(x) for x in above]
    else:
        inverse = cut(inverse_in)
        inverse_scale = 1.0 / scale
        prior = [rescaled(x, inverse_scale, step) for x in prior]
        above = [rescaled(x, inverse_scale, step) for x in above]
    put_chunks(delta_ref, corrections(prior, above, cut(order_ref), inverse))

    def visit(g, picked):
        for j in range(SIDE):
            picks_ref[g * SIDE + j] = picked[j]

    forms_ref[...] = apply_all(
        delta_ref, own_picks, blocks, edges, polars, edge_count, pieces, visit
    )
    rim = len(prior)
    chunks = scatter(pieces, edges, places, rim_heights(edge_count, rim)[0])
    put_chunks(rims_ref, chunks)
    put_rims(
        across_ref,
        beside_ref,
        [jnp.where(first, x, scale) for x in chunks[:rim]],
        [jnp.where(first, x, scale) for x in chunks[rim:]],
    )


def inner_products(step, sums, own, delta, forms, across_in, beside_in):
    rows = sums.shape[0]
    first = row_ids(rows) < rows // 2
    prior, _ = take_rims(across_in, beside_in)
    has_prior = jnp.where(first, swap_halves(prior[0]), prior[0])
    has_prior = spread(jnp.where(has_prior[:1, :1] > 0.0, 1.0, 0.0), rows)
    field = corrected(own, delta)
    sums = put_lane(sums, 2 * step, lane_sum(squares(field, len(delta) // 2, has_prior)))
    return put_lane(sums, 2 * step + 1, lane_sum(forms))


def back_stage(
    polars,
    step,
    own,
    delta,
    forms,
    across_in,
    beside_in,
    sums_in,
    picks,
    pieces,
    rims,
    edges,
    places,
    *rest,
):
    if step == 0:
        rates, forward, mass, live, heavy, terms_ref, sums_ref, image_ref, picks_ref = rest
    else:
        heavy, terms_ref, sums_ref, image_ref, picks_ref = rest
    rows, edge_count = own.shape
    groups = rows // 2
    rim = rims.shape[-1] // LANES // 2
    outer = cut(rims)
    inner = scatter(pieces, edges, places, rim_heights(edge_count, rim)[1])
    put_chunks(image_ref, outer[:rim] + inner + outer[rim:])
    put_picks(picks_ref, image_ref, edges, groups)
    if step == 0:
        dead = -live[...].astype(jnp.float32)
        for g in range(groups):
            row = [forward[g, :, c : c + LANES] for c in range(0, edge_count, LANES)]
            values = times_block(mass, 0, picks_of(row, edges))
            factor = dead * rates[g // polars]
            for i in range(SIDE):
                heavy[g * SIDE + i] = factor * values[i]
    for g in range(groups):
        side = range(g * SIDE, (g + 1) * SIDE)
        terms_ref[g] = weighted_sum([picks[i] for i in side], [heavy[i] for i in side])
    sums_ref[...] = inner_products(
        step, sums_in[...], cut(own), cut(delta), forms[...], across_in, beside_in
    )


def last_stage(
    polars,
    step,
    own,
    order_ref,
    inverse_in,
    across_in,
    beside_in,
    scale_in,
    sums_in,
    own_picks,
    blocks,
    edges,
    heavy,
    terms_ref,
    sums_ref,
    delta_ref,
):
    rows, edge_count = own.shape
    scale = scale_in[...]
    inverse_scale = 1.0 / scale
    prior, above = take_rims(across_in, beside_in)
    prior = [rescaled(x, inverse_scale, step) for x in prior]
    above = [rescaled(x, inverse_scale, step) for x in above]
    put_chunks(delta_ref, corrections(prior, above, cut(order_ref), cut(inverse_in)))

    def visit(g, picked):
        terms_ref[g] = weighted_sum(picked, [heavy[g * SIDE + i] for i in range(SIDE)])

    forms = apply_all(delta_ref, own_picks, blocks, edges, polars, edge_count, None, visit)
    sums = inner_products(
        step, sums_in[...], cut(own), cut(delta_ref), forms, across_in, beside_in
    )
    groups = rows // 2
    lanes = lane_ids(rows)
    half = LANES // 2
    packed = scale
    for g in range(groups):
        row = pltpu.roll(spread(sums[g : g + 1], rows), MOMENT_LANES * g, 1)
        here = (lanes >= MOMENT_LANES * g) & (lanes < MOMENT_LANES * (g + 1)) & (lanes < half)
        packed = jnp.where(here, row, packed)
    sums_ref[...] = packed[:1]


def combine_stage(groups, everyone, scale_in, terms0, terms1, terms2, out_ref):
    rows = scale_in.shape[0]
    parts = jnp.concatenate([everyone[q] for q in range(everyone.shape[0])], axis=0)
    scale = pltpu.roll(parts, LANES // 2, 1)
    top = jnp.max(scale, axis=0, keepdims=True)
    ratio = scale / top
    kind = lane_ids(parts.shape[0]) & (MOMENT_LANES - 1)
    power = jnp.ones_like(ratio)
    factor = jnp.ones_like(ratio)
    for k in range(1, 6):
        power = power * ratio
        factor = jnp.where(kind == k, power, factor)
    total = spread(jnp.sum(parts * factor, axis=0, keepdims=True), rows)
    m = [total] + [pltpu.roll(total, LANES - k, 1) for k in range(1, 6)]
    l1 = m[2] / m[1]
    l2 = m[3] / m[1]
    d2 = m[3] - l1 * m[2]
    cross = m[4] - l2 * m[2]
    l3 = cross / d2
    d3 = m[5] - l2 * m[3] - l3 * cross
    y1 = m[1] - l1 * m[0]
    y2 = m[2] - l2 * m[0] - l3 * y1
    c2 = y2 / d3
    c1 = y1 / d2 - l3 * c2
    c0 = m[0] / m[1] - l1 * c1 - l2 * c2
    top = spread(top, rows)
    mine = scale_in[...] / top
    c0 = c0 / top
    c1 = c1 * mine / top
    c2 = c2 * mine * mine / top
    out = None
    for terms, c in ((terms0, c0), (terms1, c1), (terms2, c2)):
        for g in range(groups):
            lane = MOMENT_LANES * g
            one = terms[g] * jnp.broadcast_to(c[:1, lane : lane + 1], out_ref.shape)
            out = one if out is None else out + one
    out_ref[...] = out


def pinned(*arguments):
    return [pltpu.with_memory_space_constraint(x, pltpu.HBM) for x in arguments]


def call(kernel, arguments, outs, scratch=(), space=VMEM, cost=0):
    return pl.pallas_call(
        kernel,
        out_shape=outs,
        in_specs=space if isinstance(space, list) else [space] * len(arguments),
        out_specs=jax.tree.map(lambda _: VMEM, outs),
        scratch_shapes=list(scratch),
        cost_estimate=pl.CostEstimate(flops=cost, bytes_accessed=cost, transcendentals=0),
        compiler_params=pltpu.CompilerParams(vmem_limit_bytes=16 * 1024 * 1024),
    )(*arguments)


def swap(block, axis, offset):
    size = lax.axis_size(axis)
    route = []
    for low in range(offset, size - 1, 2):
        route += [(low, low + 1), (low + 1, low)]
    return lax.ppermute(block, axis, route)


def gather_all(block, axis):
    size = lax.axis_size(axis)
    copies = jnp.broadcast_to(block[None], (size, *block.shape))
    return lax.all_to_all(copies, axis, 0, 0)


def sum_over(block, axis):
    size = lax.axis_size(axis)
    if size & (size - 1):
        return jnp.sum(gather_all(block, axis), axis=0)
    near = min(size, 4)
    parts = [block] + [None] * (near - 1)
    for step in reversed(range(1, near)):
        parts[step] = lax.ppermute(block, axis, [(i, i ^ step) for i in range(size)])
    while len(parts) > 1:
        parts = [a + b for a, b in zip(parts[::2], parts[1::2])]
    block = parts[0]
    step = near
    while step < size:
        block = block + lax.ppermute(block, axis, [(i, i ^ step) for i in range(size)])
        step *= 2
    return block


def local(
    angular,
    stiffness,
    mass_matrix,
    conductivity,
    element_edges,
    live_slots,
    adjoint_source,
    forward_field,
    neighbour_map,
):
    freqs = angular.shape[0]
    polars = adjoint_source.shape[1]
    groups = freqs * polars
    rows = 2 * groups
    edge_count = adjoint_source.shape[-1]
    rim = neighbour_map.shape[-1]
    slots = element_edges.shape[-1]
    tall = slots // LANES
    stiff = stiffness.reshape(SIDE * SIDE, tall, LANES)
    mass = mass_matrix.reshape(SIDE * SIDE, tall, LANES)
    edges = element_edges.reshape(SIDE, tall, LANES)
    sigma = conductivity.reshape(tall, LANES)
    live = live_slots.reshape(tall, LANES)
    source = adjoint_source.reshape(groups, 1, edge_count)
    forward = forward_field.reshape(groups, 1, edge_count)

    def shape(*dims, kind=jnp.float32):
        return jax.ShapeDtypeStruct(dims, kind)

    field_shape, rim_shape = shape(rows, edge_count), shape(rows, rim)
    sums_shape, terms_shape = shape(rows, LANES), shape(groups, tall, LANES)
    picks_shape = shape(groups * SIDE, tall, LANES)

    across, beside, source, order = call(
        rims_stage,
        pinned(source, neighbour_map),
        [rim_shape, rim_shape, field_shape, shape(rows, rim, kind=jnp.int32)],
        (
            pltpu.VMEM(source.shape, source.dtype),
            pltpu.VMEM(neighbour_map.shape, neighbour_map.dtype),
            pltpu.SemaphoreType.DMA((2,)),
        ),
        space=HBM,
    )
    across, beside = swap(across, "dom", 1), swap(beside, "dom", 0)
    kept = [jax.ShapeDtypeStruct(x.shape, x.dtype) for x in (mass, sigma, live, edges, forward)]
    places, blocks, scale, picks, rates, mass, sigma, live, edges, forward = call(
        table_stage,
        [*pinned(angular, stiff, mass, sigma, live, edges, forward), source],
        [
            shape(LANES, SIDE * slots, kind=jnp.bfloat16),
            shape(freqs * SIDE * SIDE, tall, LANES),
            sums_shape,
            picks_shape,
            shape(freqs, tall, LANES),
            *kept,
        ],
        (
            pltpu.SMEM(angular.shape, angular.dtype),
            pltpu.VMEM(stiff.shape, stiff.dtype),
            pltpu.SemaphoreType.DMA((7,)),
        ),
        space=[HBM] * 7 + [VMEM],
        cost=4_000_000,
    )
    front_shapes = [
        shape(rows, 2 * rim),
        picks_shape,
        shape(rows * SIDE * tall, LANES),
        sums_shape,
        shape(rows, 2 * rim),
        rim_shape,
        rim_shape,
    ]
    back_shapes = [terms_shape, sums_shape, field_shape, picks_shape]
    own, sums, terms = source, jnp.zeros((rows, LANES), jnp.float32), []
    for step in range(2):
        arrived = (across, beside)
        given = (order, *arrived, scale, picks, blocks, edges, places)
        front = functools.partial(front_stage, polars, step, edge_count)
        if step == 0:
            inverse, *outs = call(
                front, given, [shape(rows, rim, kind=jnp.int32), *front_shapes]
            )
        else:
            outs = call(front, (*given, inverse), front_shapes)
        delta, picks, pieces, forms, rims, across, beside = outs
        across, beside = swap(across, "dom", 1), swap(beside, "dom", 0)
        given = (own, delta, forms, *arrived, sums, picks, pieces, rims, edges, places)
        back = functools.partial(back_stage, polars, step)
        if step == 0:
            heavy, term, sums, own, picks = call(
                back,
                (*given, rates, forward, mass, live),
                [picks_shape, *back_shapes],
                cost=4_000_000,
            )
        else:
            term, sums, own, picks = call(back, (*given, heavy), back_shapes, cost=4_000_000)
        terms.append(term)
    term, sums = call(
        functools.partial(last_stage, polars, 2),
        (own, order, inverse, across, beside, scale, sums, picks, blocks, edges, heavy),
        [terms_shape, shape(1, LANES)],
        (pltpu.VMEM((rows, 2 * rim), jnp.float32),),
    )
    terms.append(term)
    term = call(
        functools.partial(combine_stage, groups),
        (gather_all(sums, "dom"), scale, *terms),
        shape(tall, LANES),
    )
    gradient = sum_over(term, "freq").reshape(1, slots)
    updated = sigma.reshape(1, slots) * jnp.exp(-0.5 * jnp.tanh(gradient))
    return gradient, updated


def solution(mesh):
    return jax.shard_map(
        local,
        mesh=mesh,
        in_specs=(
            P("freq"),
            P("dom", None, None),
            P("dom", None, None),
            P("dom", None),
            P("dom", None, None),
            P("dom", None),
            P("freq", None, "dom", None),
            P("freq", None, "dom", None),
            P("dom", None),
        ),
        out_specs=(P("dom", None), P("dom", None)),
        check_vma=False,
    )
```

```python
import functools

import jax
import jax.numpy as jnp
from jax import lax
from jax.experimental import pallas as pl
from jax.experimental.pallas import tpu as pltpu
from jax.sharding import PartitionSpec as P

LANES = 128
SUBLANES = 8
SIDE = 6
VMEM = pl.BlockSpec(memory_space=pltpu.VMEM)
HBM = pl.BlockSpec(memory_space=pltpu.HBM)

PICK_LANES = lax.GatherDimensionNumbers(
    offset_dims=(),
    collapsed_slice_dims=(1,),
    start_index_map=(1,),
    operand_batching_dims=(0,),
    start_indices_batching_dims=(0,),
)


def pick_lanes(block, lanes):
    return lax.gather(
        block,
        lanes[..., None],
        PICK_LANES,
        (1, 1),
        mode=lax.GatherScatterMode.PROMISE_IN_BOUNDS,
    )


def pick_wide(chunks, index):
    lanes = index & (LANES - 1)
    high = index >> 7
    level = [pick_lanes(chunk, lanes) for chunk in chunks]
    bit = 0
    while len(level) > 1:
        odd = (high >> bit) & 1 == 1
        level = [
            jnp.where(odd, level[t + 1], level[t]) if t + 1 < len(level) else level[t]
            for t in range(0, len(level), 2)
        ]
        bit += 1
    return level[0]


def row_ids(rows):
    return lax.broadcasted_iota(jnp.int32, (rows, LANES), 0)


def lane_ids(rows):
    return lax.broadcasted_iota(jnp.int32, (rows, LANES), 1)


def spread(row, rows):
    return jnp.broadcast_to(row, (rows, row.shape[-1]))


def cut(ref):
    return [ref[:, c : c + LANES] for c in range(0, ref.shape[-1], LANES)]


def swap_halves(block):
    return pltpu.roll(block, block.shape[0] // 2, 0)


def doubled(block):
    half = block.shape[0] // 2
    return jnp.where(row_ids(2 * half) < half, block, swap_halves(block))


def lane_sum(block):
    return jnp.broadcast_to(jnp.sum(block, axis=1, keepdims=True), block.shape)


def put_lane(block, lane, value):
    return jnp.where(lane_ids(block.shape[0]) == lane, value, block)


def put_chunks(ref, chunks):
    for c, chunk in enumerate(chunks):
        ref[:, c * LANES : (c + 1) * LANES] = chunk


def is_even():
    return lax.rem(lax.axis_index("dom"), 2) == 0


def put_rims(across_ref, beside_ref, lower, upper):
    even = is_even()
    for c, (low, high) in enumerate(zip(lower, upper)):
        here = slice(c * LANES, (c + 1) * LANES)
        across_ref[:, here] = jnp.where(even, low, high)
        beside_ref[:, here] = jnp.where(even, high, low)


def take_rims(across_ref, beside_ref):
    even = is_even()
    pairs = list(zip(cut(across_ref), cut(beside_ref)))
    prior = [jnp.where(even, a, b) for a, b in pairs]
    above = [jnp.where(even, b, a) for a, b in pairs]
    return prior, above


def picks_of(rows_of_group, edges):
    chunks = [spread(row, edges.shape[1]) for row in rows_of_group]
    return [pick_wide(chunks, edges[j]) for j in range(SIDE)]


def group_rows(ref, g):
    return [ref[g : g + 1, c : c + LANES] for c in range(0, ref.shape[-1], LANES)]


def times_block(entries, base, picked):
    out = []
    for i in range(SIDE):
        total = None
        for j in range(SIDE):
            one = entries[base + SIDE * i + j] * picked[j]
            total = one if total is None else total + one
        out.append(total)
    return out


def weighted_sum(left, right):
    total = None
    for a, b in zip(left, right):
        total = a * b if total is None else total + a * b
    return total


def scatter(pieces, edges, places, heights, values):
    depth = SIDE * edges.shape[1]
    rows = pieces.shape[0] // depth
    for i in range(SIDE):
        for s in range(edges.shape[1]):
            at = i * edges.shape[1] + s
            both = pieces[pl.ds(at, rows, stride=depth), :]
            high = spread(edges[i, s : s + 1, :] >> 7, rows)
            stacked = [jnp.where(high == h, both, 0.0) for h in heights]
            values[:, at * LANES : (at + 1) * LANES] = jnp.concatenate(stacked, axis=0).astype(
                jnp.bfloat16
            )
    total = lax.dot_general(
        values[...],
        places[...],
        (((1,), (1,)), ((), ())),
        preferred_element_type=jnp.float32,
    )
    out = []
    for n in range(len(heights)):
        piece = total[rows * n : rows * (n + 1)]
        out.append(piece + swap_halves(piece))
    return out


def rim_heights(edge_count, rim):
    count = edge_count // LANES
    return [*range(rim), *range(count - rim, count)], list(range(rim, count - rim))


def corrections(from_prior, from_above, order, inverse):
    lower = [pick_wide(from_prior, index) for index in order]
    return lower + [pick_wide(from_above, index) for index in inverse]


def corrected(own, delta):
    rim = len(delta) // 2
    lower = [a + b for a, b in zip(own[:rim], delta[:rim])]
    upper = [a + b for a, b in zip(own[len(own) - rim :], delta[rim:])]
    return lower + own[rim : len(own) - rim] + upper


def squares(chunks, rim, has_prior):
    total = None
    for c, chunk in enumerate(chunks):
        term = chunk * chunk
        if c < rim:
            term = term * (1.0 - has_prior)
        total = term if total is None else total + term
    return total


def start_copies(routes, arrived):
    copies = [
        pltpu.make_async_copy(here, there, arrived.at[n])
        for n, (here, there) in enumerate(routes)
    ]
    for copy in copies:
        copy.start()
    return copies


def stacked_chunk(source, at):
    piece = [source[g, :, at : at + LANES] for g in range(source.shape[0])]
    return jnp.concatenate(piece + piece, axis=0)


def rims_stage(source_in, order_in, across_ref, beside_ref, source, order_ref, order, arrived):
    for copy in start_copies(((source_in, source), (order_in, order)), arrived):
        copy.wait()
    rows, rim = order_ref.shape
    first = row_ids(rows) < rows // 2
    order_ref[...] = spread(order[...], rows)
    numbers = [x.astype(jnp.float32) for x in cut(order_ref)]
    lower = [stacked_chunk(source, c) for c in range(0, rim, LANES)]
    start = source.shape[-1] - rim
    upper = [stacked_chunk(source, start + c) for c in range(0, rim, LANES)]
    lower = [jnp.where(first, x, o) for x, o in zip(lower, numbers)]
    upper = [jnp.where(first, x, 1.0) for x in upper]
    put_rims(across_ref, beside_ref, lower, upper)


def table_stage(
    angular_in,
    stiffness_in,
    mass_in,
    sigma_in,
    live_in,
    edges_in,
    forward_in,
    source,
    places_ref,
    blocks_ref,
    scale_ref,
    picks_ref,
    stacked_ref,
    rates,
    mass,
    sigma,
    live,
    edges,
    forward_ref,
    angular,
    stiffness,
    arrived,
):
    copies = start_copies(
        (
            (edges_in, edges),
            (angular_in, angular),
            (sigma_in, sigma),
            (live_in, live),
            (stiffness_in, stiffness),
            (mass_in, mass),
            (forward_in, forward_ref),
        ),
        arrived,
    )
    copies[0].wait()
    numbers = row_ids(LANES)
    rows = edges.shape[1]

    def body(i, carry):
        for s in range(rows):
            lanes = spread(edges[i, s : s + 1, :] & (LANES - 1), LANES)
            column = pl.ds(pl.multiple_of((i * rows + s) * LANES, LANES), LANES)
            places_ref[:, column] = jnp.where(lanes == numbers, 1.0, 0.0).astype(jnp.bfloat16)
        return carry

    lax.fori_loop(0, SIDE, body, 0)
    count = source.shape[-1]
    put_chunks(stacked_ref, [stacked_chunk(source, c) for c in range(0, count, LANES)])
    put_picks(picks_ref, stacked_ref, edges, source.shape[0])
    for copy in copies[1:]:
        copy.wait()
    for f in range(angular.shape[0]):
        rates[f] = jnp.full(rates.shape[1:], angular[f], jnp.float32)
    alive = live[...].astype(jnp.float32)
    weight = sigma[...]
    freqs = rates.shape[0]
    peak = None
    for i in range(SIDE):
        for f in range(freqs):
            entry = (SIDE + 1) * i
            size = stiffness[entry] + rates[f] * weight * mass[entry]
            peak = size if peak is None else jnp.maximum(peak, size)
    peak = jnp.max(peak * alive, axis=1, keepdims=True)
    scale = jnp.broadcast_to(jnp.max(peak, axis=0, keepdims=True), scale_ref.shape)
    scale_ref[...] = scale
    alive = alive / scale[:1, :1]
    for entry in range(SIDE * SIDE):
        stiff = stiffness[entry] * alive
        heavy = mass[entry] * (weight * alive)
        for f in range(freqs):
            blocks_ref[f * SIDE * SIDE + entry] = stiff + rates[f] * heavy


def put_picks(picks_ref, field, edges, groups):
    for g in range(groups):
        for j, value in enumerate(picks_of(group_rows(field, g), edges)):
            picks_ref[g * SIDE + j] = value


def pick_rims(rows, index, edge_count):
    rim = len(rows) // 2
    start = edge_count - rim * LANES
    lower = pick_wide([spread(row, index.shape[0]) for row in rows[:rim]], index)
    upper = pick_wide([spread(row, index.shape[0]) for row in rows[rim:]], index - start)
    lower = jnp.where(index < rim * LANES, lower, 0.0)
    return lower + jnp.where(index >= start, upper, 0.0)


def apply_all(delta_ref, own_picks, blocks, edges, polars, edge_count, pieces, visit):
    rows = delta_ref.shape[0]
    groups = rows // 2
    depth = SIDE * edges.shape[1]
    forms = jnp.zeros((rows, LANES), jnp.float32)
    for g in range(groups):
        delta = group_rows(delta_ref, g)
        picked = [
            own_picks[g * SIDE + j] + pick_rims(delta, edges[j], edge_count)
            for j in range(SIDE)
        ]
        visit(g, picked)
        values = times_block(blocks, (g // polars) * SIDE * SIDE, picked)
        form = jnp.sum(weighted_sum(picked, values), axis=0, keepdims=True)
        forms = jnp.where(row_ids(rows) == g, spread(form, rows), forms)
        if pieces is None:
            continue
        for i, value in enumerate(values):
            coarse = value.astype(jnp.bfloat16).astype(jnp.float32)
            for part, piece in enumerate((coarse, value - coarse)):
                at = (part * groups + g) * depth + i * edges.shape[1]
                pieces[at : at + edges.shape[1], :] = piece
    return forms


def invert(above, groups, rows):
    above_order = jnp.concatenate([x[groups : groups + 1] for x in above], axis=1)
    rim = above_order.shape[1]
    slot = lax.broadcasted_iota(jnp.int32, (rim, rim), 0).astype(jnp.float32)
    match = jnp.where(spread(above_order, rim) == slot, 1.0, 0.0).astype(jnp.bfloat16)
    numbers = lax.broadcasted_iota(jnp.int32, (2 * rows, rim), 1).astype(jnp.bfloat16)
    inverse = lax.dot_general(
        numbers, match, (((1,), (1,)), ((), ())), preferred_element_type=jnp.float32
    )
    return inverse[:rows].astype(jnp.int32)


def rescaled(block, inverse_scale, step):
    ratio = swap_halves(block) * inverse_scale
    for _ in range(step):
        block = block * ratio
    return doubled(block)


def front_stage(
    polars,
    step,
    edge_count,
    order_ref,
    across_in,
    beside_in,
    scale_in,
    own_picks,
    blocks,
    edges,
    places,
    *rest,
):
    if step == 0:
        inverse_ref, *rest = rest
    else:
        inverse_in, *rest = rest
    delta_ref, picks_ref, pieces, forms_ref, rims_ref, across_ref, beside_ref, values = rest
    rows = delta_ref.shape[0]
    groups = rows // 2
    first = row_ids(rows) < groups
    scale = scale_in[...]
    prior, above = take_rims(across_in, beside_in)
    if step == 0:
        inverse_ref[...] = invert(above, groups, rows)
        inverse = cut(inverse_ref)
        prior, above = [doubled(x) for x in prior], [doubled(x) for x in above]
    else:
        inverse = cut(inverse_in)
        inverse_scale = 1.0 / scale
        prior = [rescaled(x, inverse_scale, step) for x in prior]
        above = [rescaled(x, inverse_scale, step) for x in above]
    put_chunks(delta_ref, corrections(prior, above, cut(order_ref), inverse))

    def visit(g, picked):
        for j in range(SIDE):
            picks_ref[g * SIDE + j] = picked[j]

    forms_ref[...] = apply_all(
        delta_ref, own_picks, blocks, edges, polars, edge_count, pieces, visit
    )
    rim = len(prior)
    chunks = scatter(pieces, edges, places, rim_heights(edge_count, rim)[0], values)
    put_chunks(rims_ref, chunks)
    put_rims(
        across_ref,
        beside_ref,
        [jnp.where(first, x, scale) for x in chunks[:rim]],
        [jnp.where(first, x, scale) for x in chunks[rim:]],
    )


def inner_products(step, sums, own, delta, forms, across_in, beside_in):
    rows = sums.shape[0]
    first = row_ids(rows) < rows // 2
    prior, _ = take_rims(across_in, beside_in)
    has_prior = jnp.where(first, swap_halves(prior[0]), prior[0])
    has_prior = spread(jnp.where(has_prior[:1, :1] > 0.0, 1.0, 0.0), rows)
    field = corrected(own, delta)
    sums = put_lane(sums, 2 * step, lane_sum(squares(field, len(delta) // 2, has_prior)))
    return put_lane(sums, 2 * step + 1, lane_sum(forms))


def back_stage(
    polars,
    step,
    own,
    delta,
    forms,
    across_in,
    beside_in,
    sums_in,
    picks,
    pieces,
    rims,
    edges,
    places,
    *rest,
):
    if step == 0:
        rates, forward, mass, live, heavy, terms_ref, sums_ref, image_ref, picks_ref, values = rest
    else:
        heavy, terms_ref, sums_ref, image_ref, picks_ref, values = rest
    rows, edge_count = own.shape
    groups = rows // 2
    rim = rims.shape[-1] // LANES // 2
    outer = cut(rims)
    inner = scatter(pieces, edges, places, rim_heights(edge_count, rim)[1], values)
    put_chunks(image_ref, outer[:rim] + inner + outer[rim:])
    put_picks(picks_ref, image_ref, edges, groups)
    if step == 0:
        dead = -live[...].astype(jnp.float32)
        for g in range(groups):
            row = [forward[g, :, c : c + LANES] for c in range(0, edge_count, LANES)]
            values = times_block(mass, 0, picks_of(row, edges))
            factor = dead * rates[g // polars]
            for i in range(SIDE):
                heavy[g * SIDE + i] = factor * values[i]
    for g in range(groups):
        side = range(g * SIDE, (g + 1) * SIDE)
        terms_ref[g] = weighted_sum([picks[i] for i in side], [heavy[i] for i in side])
    sums_ref[...] = inner_products(
        step, sums_in[...], cut(own), cut(delta), forms[...], across_in, beside_in
    )


def last_stage(
    polars,
    step,
    own,
    order_ref,
    inverse_in,
    across_in,
    beside_in,
    scale_in,
    sums_in,
    own_picks,
    blocks,
    edges,
    heavy,
    terms_ref,
    sums_ref,
    delta_ref,
):
    rows, edge_count = own.shape
    first = row_ids(rows) < rows // 2
    scale = scale_in[...]
    inverse_scale = 1.0 / scale
    prior, above = take_rims(across_in, beside_in)
    prior = [rescaled(x, inverse_scale, step) for x in prior]
    above = [rescaled(x, inverse_scale, step) for x in above]
    put_chunks(delta_ref, corrections(prior, above, cut(order_ref), cut(inverse_in)))

    def visit(g, picked):
        terms_ref[g] = weighted_sum(picked, [heavy[g * SIDE + i] for i in range(SIDE)])

    forms = apply_all(delta_ref, own_picks, blocks, edges, polars, edge_count, None, visit)
    sums = inner_products(
        step, sums_in[...], cut(own), cut(delta_ref), forms, across_in, beside_in
    )
    sums_ref[...] = jnp.where(first, sums, scale)


def combine_stage(everyone, sums_in, terms0, terms1, terms2, out_ref):
    rows = sums_in.shape[0]
    groups = rows // 2
    first = row_ids(rows) < groups

    def scale_of(block):
        return jnp.where(first, swap_halves(block), block)

    parts = [everyone[q] for q in range(everyone.shape[0])]
    scales = [scale_of(block) for block in parts]
    top = functools.reduce(jnp.maximum, scales)
    lanes = lane_ids(rows)
    inverse_top = 1.0 / top
    total = None
    for block, scale in zip(parts, scales):
        ratio = scale * inverse_top
        power = jnp.ones_like(ratio)
        factor = jnp.ones_like(ratio)
        for k in range(1, 6):
            power = power * ratio
            factor = jnp.where(lanes == k, power, factor)
        term = block * factor
        total = term if total is None else total + term
    m = [jnp.broadcast_to(total[:, k : k + 1], (rows, LANES)) for k in range(6)]
    l1 = m[2] / m[1]
    l2 = m[3] / m[1]
    d2 = m[3] - l1 * m[2]
    cross = m[4] - l2 * m[2]
    l3 = cross / d2
    d3 = m[5] - l2 * m[3] - l3 * cross
    y1 = m[1] - l1 * m[0]
    y2 = m[2] - l2 * m[0] - l3 * y1
    c2 = y2 / d3
    c1 = y1 / d2 - l3 * c2
    c0 = m[0] / m[1] - l1 * c1 - l2 * c2
    mine = scale_of(sums_in[...]) * inverse_top
    c0 = c0 * inverse_top
    c1 = c1 * mine * inverse_top
    c2 = c2 * mine * mine * inverse_top
    out = None
    for terms, c in ((terms0, c0), (terms1, c1), (terms2, c2)):
        for g in range(groups):
            one = terms[g] * spread(c[g : g + 1], out_ref.shape[0])
            out = one if out is None else out + one
    out_ref[...] = out


def pinned(*arguments):
    return [pltpu.with_memory_space_constraint(x, pltpu.HBM) for x in arguments]


def call(kernel, arguments, outs, scratch=(), space=VMEM, cost=0):
    return pl.pallas_call(
        kernel,
        out_shape=outs,
        in_specs=space if isinstance(space, list) else [space] * len(arguments),
        out_specs=jax.tree.map(lambda _: VMEM, outs),
        scratch_shapes=list(scratch),
        cost_estimate=pl.CostEstimate(flops=cost, bytes_accessed=cost, transcendentals=0),
        compiler_params=pltpu.CompilerParams(vmem_limit_bytes=16 * 1024 * 1024),
    )(*arguments)


def swap(block, axis, offset):
    size = lax.axis_size(axis)
    route = []
    for low in range(offset, size - 1, 2):
        route += [(low, low + 1), (low + 1, low)]
    return lax.ppermute(block, axis, route)


def gather_all(block, axis):
    size = lax.axis_size(axis)
    copies = jnp.broadcast_to(block[None], (size, *block.shape))
    return lax.all_to_all(copies, axis, 0, 0)


def sum_over(block, axis):
    size = lax.axis_size(axis)
    if size & (size - 1):
        return jnp.sum(gather_all(block, axis), axis=0)
    near = min(size, 4)
    parts = [block] + [None] * (near - 1)
    for step in reversed(range(1, near)):
        parts[step] = lax.ppermute(block, axis, [(i, i ^ step) for i in range(size)])
    while len(parts) > 1:
        parts = [a + b for a, b in zip(parts[::2], parts[1::2])]
    block = parts[0]
    step = near
    while step < size:
        block = block + lax.ppermute(block, axis, [(i, i ^ step) for i in range(size)])
        step *= 2
    return block


def local(
    angular,
    stiffness,
    mass_matrix,
    conductivity,
    element_edges,
    live_slots,
    adjoint_source,
    forward_field,
    neighbour_map,
):
    freqs = angular.shape[0]
    polars = adjoint_source.shape[1]
    groups = freqs * polars
    rows = 2 * groups
    edge_count = adjoint_source.shape[-1]
    rim = neighbour_map.shape[-1]
    slots = element_edges.shape[-1]
    tall = slots // LANES
    stiff = stiffness.reshape(SIDE * SIDE, tall, LANES)
    mass = mass_matrix.reshape(SIDE * SIDE, tall, LANES)
    edges = element_edges.reshape(SIDE, tall, LANES)
    sigma = conductivity.reshape(tall, LANES)
    live = live_slots.reshape(tall, LANES)
    source = adjoint_source.reshape(groups, 1, edge_count)
    forward = forward_field.reshape(groups, 1, edge_count)

    def shape(*dims, kind=jnp.float32):
        return jax.ShapeDtypeStruct(dims, kind)

    field_shape, rim_shape = shape(rows, edge_count), shape(rows, rim)
    sums_shape, terms_shape = shape(rows, LANES), shape(groups, tall, LANES)
    picks_shape = shape(groups * SIDE, tall, LANES)

    across, beside, source, order = call(
        rims_stage,
        pinned(source, neighbour_map),
        [rim_shape, rim_shape, shape(*source.shape), shape(rows, rim, kind=jnp.int32)],
        (
            pltpu.VMEM(neighbour_map.shape, neighbour_map.dtype),
            pltpu.SemaphoreType.DMA((2,)),
        ),
        space=HBM,
    )
    across, beside = swap(across, "dom", 1), swap(beside, "dom", 0)
    kept = [jax.ShapeDtypeStruct(x.shape, x.dtype) for x in (mass, sigma, live, edges, forward)]
    places, blocks, scale, picks, own, rates, mass, sigma, live, edges, forward = call(
        table_stage,
        [*pinned(angular, stiff, mass, sigma, live, edges, forward), source],
        [
            shape(LANES, SIDE * slots, kind=jnp.bfloat16),
            shape(freqs * SIDE * SIDE, tall, LANES),
            sums_shape,
            picks_shape,
            field_shape,
            shape(freqs, tall, LANES),
            *kept,
        ],
        (
            pltpu.SMEM(angular.shape, angular.dtype),
            pltpu.VMEM(stiff.shape, stiff.dtype),
            pltpu.SemaphoreType.DMA((7,)),
        ),
        space=[HBM] * 7 + [VMEM],
        cost=4_000_000,
    )
    front_shapes = [
        shape(rows, 2 * rim),
        picks_shape,
        shape(rows * SIDE * tall, LANES),
        sums_shape,
        shape(rows, 2 * rim),
        rim_shape,
        rim_shape,
    ]
    back_shapes = [terms_shape, sums_shape, field_shape, picks_shape]
    sums, terms = jnp.zeros((rows, LANES), jnp.float32), []
    outer, inner = rim_heights(edge_count, rim // LANES)
    outer = [pltpu.VMEM((rows * len(outer), SIDE * slots), jnp.bfloat16)]
    inner = [pltpu.VMEM((rows * len(inner), SIDE * slots), jnp.bfloat16)]
    for step in range(2):
        arrived = (across, beside)
        given = (order, *arrived, scale, picks, blocks, edges, places)
        front = functools.partial(front_stage, polars, step, edge_count)
        if step == 0:
            inverse, *outs = call(
                front, given, [shape(rows, rim, kind=jnp.int32), *front_shapes], outer
            )
        else:
            outs = call(front, (*given, inverse), front_shapes, outer)
        delta, picks, pieces, forms, rims, across, beside = outs
        across, beside = swap(across, "dom", 1), swap(beside, "dom", 0)
        given = (own, delta, forms, *arrived, sums, picks, pieces, rims, edges, places)
        back = functools.partial(back_stage, polars, step)
        if step == 0:
            heavy, term, sums, own, picks = call(
                back,
                (*given, rates, forward, mass, live),
                [picks_shape, *back_shapes],
                inner,
                cost=4_000_000,
            )
        else:
            term, sums, own, picks = call(back, (*given, heavy), back_shapes, inner, cost=4_000_000)
        terms.append(term)
    term, sums = call(
        functools.partial(last_stage, polars, 2),
        (own, order, inverse, across, beside, scale, sums, picks, blocks, edges, heavy),
        [terms_shape, sums_shape],
        (pltpu.VMEM((rows, 2 * rim), jnp.float32),),
    )
    terms.append(term)
    term = call(
        combine_stage,
        (gather_all(sums, "dom"), sums, *terms),
        shape(tall, LANES),
    )
    gradient = sum_over(term, "freq").reshape(1, slots)
    updated = sigma.reshape(1, slots) * jnp.exp(-0.5 * jnp.tanh(gradient))
    return gradient, updated


def solution(mesh):
    return jax.shard_map(
        local,
        mesh=mesh,
        in_specs=(
            P("freq"),
            P("dom", None, None),
            P("dom", None, None),
            P("dom", None),
            P("dom", None, None),
            P("dom", None),
            P("freq", None, "dom", None),
            P("freq", None, "dom", None),
            P("dom", None),
        ),
        out_specs=(P("dom", None), P("dom", None)),
        check_vma=False,
    )
```

```python
import functools

import jax
import jax.numpy as jnp
from jax import lax
from jax.experimental import pallas as pl
from jax.experimental.pallas import tpu as pltpu
from jax.sharding import PartitionSpec as P

LANES = 128
SUBLANES = 8
SIDE = 6
VMEM = pl.BlockSpec(memory_space=pltpu.VMEM)
HBM = pl.BlockSpec(memory_space=pltpu.HBM)

PICK_LANES = lax.GatherDimensionNumbers(
    offset_dims=(),
    collapsed_slice_dims=(1,),
    start_index_map=(1,),
    operand_batching_dims=(0,),
    start_indices_batching_dims=(0,),
)


def pick_lanes(block, lanes):
    return lax.gather(
        block,
        lanes[..., None],
        PICK_LANES,
        (1, 1),
        mode=lax.GatherScatterMode.PROMISE_IN_BOUNDS,
    )


def pick_wide(chunks, index):
    lanes = index & (LANES - 1)
    high = index >> 7
    level = [pick_lanes(chunk, lanes) for chunk in chunks]
    bit = 0
    while len(level) > 1:
        odd = (high >> bit) & 1 == 1
        level = [
            jnp.where(odd, level[t + 1], level[t]) if t + 1 < len(level) else level[t]
            for t in range(0, len(level), 2)
        ]
        bit += 1
    return level[0]


def row_ids(rows):
    return lax.broadcasted_iota(jnp.int32, (rows, LANES), 0)


def lane_ids(rows):
    return lax.broadcasted_iota(jnp.int32, (rows, LANES), 1)


def spread(row, rows):
    return jnp.broadcast_to(row, (rows, row.shape[-1]))


def cut(ref):
    return [ref[:, c : c + LANES] for c in range(0, ref.shape[-1], LANES)]


def swap_halves(block):
    return pltpu.roll(block, block.shape[0] // 2, 0)


def doubled(block):
    half = block.shape[0] // 2
    return jnp.where(row_ids(2 * half) < half, block, swap_halves(block))


def lane_sum(block):
    return jnp.broadcast_to(jnp.sum(block, axis=1, keepdims=True), block.shape)


def put_lane(block, lane, value):
    return jnp.where(lane_ids(block.shape[0]) == lane, value, block)


def put_chunks(ref, chunks):
    for c, chunk in enumerate(chunks):
        ref[:, c * LANES : (c + 1) * LANES] = chunk


def is_even():
    return lax.rem(lax.axis_index("dom"), 2) == 0


def put_rims(across_ref, beside_ref, lower, upper):
    even = is_even()
    for c, (low, high) in enumerate(zip(lower, upper)):
        here = slice(c * LANES, (c + 1) * LANES)
        across_ref[:, here] = jnp.where(even, low, high)
        beside_ref[:, here] = jnp.where(even, high, low)


def take_rims(across_ref, beside_ref):
    even = is_even()
    pairs = list(zip(cut(across_ref), cut(beside_ref)))
    prior = [jnp.where(even, a, b) for a, b in pairs]
    above = [jnp.where(even, b, a) for a, b in pairs]
    return prior, above


def picks_of(rows_of_group, edges):
    chunks = [spread(row, edges.shape[1]) for row in rows_of_group]
    return [pick_wide(chunks, edges[j]) for j in range(SIDE)]


def group_rows(ref, g):
    return [ref[g : g + 1, c : c + LANES] for c in range(0, ref.shape[-1], LANES)]


def times_block(entries, base, picked):
    out = []
    for i in range(SIDE):
        total = None
        for j in range(SIDE):
            one = entries[base + SIDE * i + j] * picked[j]
            total = one if total is None else total + one
        out.append(total)
    return out


def weighted_sum(left, right):
    total = None
    for a, b in zip(left, right):
        total = a * b if total is None else total + a * b
    return total


def scatter(pieces, edges, places, heights, values):
    depth = SIDE * edges.shape[1]
    rows = pieces.shape[0] // depth
    for i in range(SIDE):
        for s in range(edges.shape[1]):
            at = i * edges.shape[1] + s
            both = pieces[pl.ds(at, rows, stride=depth), :]
            high = spread(edges[i, s : s + 1, :] >> 7, rows)
            stacked = [jnp.where(high == h, both, 0.0) for h in heights]
            values[:, at * LANES : (at + 1) * LANES] = jnp.concatenate(stacked, axis=0).astype(
                jnp.bfloat16
            )
    total = lax.dot_general(
        values[...],
        places[...],
        (((1,), (1,)), ((), ())),
        preferred_element_type=jnp.float32,
    )
    out = []
    for n in range(len(heights)):
        piece = total[rows * n : rows * (n + 1)]
        out.append(piece + swap_halves(piece))
    return out


def rim_heights(edge_count, rim):
    count = edge_count // LANES
    return [*range(rim), *range(count - rim, count)], list(range(rim, count - rim))


def corrections(from_prior, from_above, order, inverse):
    lower = [pick_wide(from_prior, index) for index in order]
    return lower + [pick_wide(from_above, index) for index in inverse]


def corrected(own, delta):
    rim = len(delta) // 2
    lower = [a + b for a, b in zip(own[:rim], delta[:rim])]
    upper = [a + b for a, b in zip(own[len(own) - rim :], delta[rim:])]
    return lower + own[rim : len(own) - rim] + upper


def squares(chunks, rim, has_prior):
    total = None
    for c, chunk in enumerate(chunks):
        term = chunk * chunk
        if c < rim:
            term = term * (1.0 - has_prior)
        total = term if total is None else total + term
    return total


def start_copies(routes, arrived):
    copies = [
        pltpu.make_async_copy(here, there, arrived.at[n])
        for n, (here, there) in enumerate(routes)
    ]
    for copy in copies:
        copy.start()
    return copies


def stacked_chunk(source, at):
    piece = [source[g, :, at : at + LANES] for g in range(source.shape[0])]
    return jnp.concatenate(piece + piece, axis=0)


def rims_stage(source_in, order_in, across_ref, beside_ref, source, order_ref, order, arrived):
    for copy in start_copies(((source_in, source), (order_in, order)), arrived):
        copy.wait()
    rows, rim = order_ref.shape
    first = row_ids(rows) < rows // 2
    order_ref[...] = spread(order[...], rows)
    numbers = [x.astype(jnp.float32) for x in cut(order_ref)]
    lower = [stacked_chunk(source, c) for c in range(0, rim, LANES)]
    start = source.shape[-1] - rim
    upper = [stacked_chunk(source, start + c) for c in range(0, rim, LANES)]
    lower = [jnp.where(first, x, o) for x, o in zip(lower, numbers)]
    upper = [jnp.where(first, x, 1.0) for x in upper]
    put_rims(across_ref, beside_ref, lower, upper)


def table_stage(
    angular_in,
    stiffness_in,
    mass_in,
    sigma_in,
    live_in,
    edges_in,
    forward_in,
    source,
    places_ref,
    blocks_ref,
    scale_ref,
    picks_ref,
    stacked_ref,
    rates,
    mass,
    sigma,
    live,
    edges,
    forward_ref,
    angular,
    stiffness,
    arrived,
):
    copies = start_copies(
        (
            (edges_in, edges),
            (angular_in, angular),
            (sigma_in, sigma),
            (live_in, live),
            (stiffness_in, stiffness),
            (mass_in, mass),
            (forward_in, forward_ref),
        ),
        arrived,
    )
    copies[0].wait()
    numbers = row_ids(LANES)
    rows = edges.shape[1]

    def body(i, carry):
        for s in range(rows):
            lanes = spread(edges[i, s : s + 1, :] & (LANES - 1), LANES)
            column = pl.ds(pl.multiple_of((i * rows + s) * LANES, LANES), LANES)
            places_ref[:, column] = jnp.where(lanes == numbers, 1.0, 0.0).astype(jnp.bfloat16)
        return carry

    lax.fori_loop(0, SIDE, body, 0)
    count = source.shape[-1]
    put_chunks(stacked_ref, [stacked_chunk(source, c) for c in range(0, count, LANES)])
    put_picks(picks_ref, stacked_ref, edges, source.shape[0])
    for copy in copies[1:]:
        copy.wait()
    for f in range(angular.shape[0]):
        rates[f] = jnp.full(rates.shape[1:], angular[f], jnp.float32)
    alive = live[...].astype(jnp.float32)
    weight = sigma[...]
    freqs = rates.shape[0]
    peak = None
    for i in range(SIDE):
        for f in range(freqs):
            entry = (SIDE + 1) * i
            size = stiffness[entry] + rates[f] * weight * mass[entry]
            peak = size if peak is None else jnp.maximum(peak, size)
    peak = jnp.max(peak * alive, axis=1, keepdims=True)
    scale = jnp.broadcast_to(jnp.max(peak, axis=0, keepdims=True), scale_ref.shape)
    scale_ref[...] = scale
    alive = alive / scale[:1, :1]
    for entry in range(SIDE * SIDE):
        stiff = stiffness[entry] * alive
        heavy = mass[entry] * (weight * alive)
        for f in range(freqs):
            blocks_ref[f * SIDE * SIDE + entry] = stiff + rates[f] * heavy


def put_picks(picks_ref, field, edges, groups):
    for g in range(groups):
        for j, value in enumerate(picks_of(group_rows(field, g), edges)):
            picks_ref[g * SIDE + j] = value


def pick_rims(rows, index, edge_count):
    rim = len(rows) // 2
    start = edge_count - rim * LANES
    lower = pick_wide([spread(row, index.shape[0]) for row in rows[:rim]], index)
    upper = pick_wide([spread(row, index.shape[0]) for row in rows[rim:]], index - start)
    lower = jnp.where(index < rim * LANES, lower, 0.0)
    return lower + jnp.where(index >= start, upper, 0.0)


def apply_all(delta_ref, own_picks, blocks, edges, polars, edge_count, pieces, visit):
    rows = delta_ref.shape[0]
    groups = rows // 2
    depth = SIDE * edges.shape[1]
    forms = jnp.zeros((rows, LANES), jnp.float32)
    for g in range(groups):
        delta = group_rows(delta_ref, g)
        picked = [
            own_picks[g * SIDE + j] + pick_rims(delta, edges[j], edge_count)
            for j in range(SIDE)
        ]
        visit(g, picked)
        values = times_block(blocks, (g // polars) * SIDE * SIDE, picked)
        form = jnp.sum(weighted_sum(picked, values), axis=0, keepdims=True)
        forms = jnp.where(row_ids(rows) == g, spread(form, rows), forms)
        if pieces is None:
            continue
        for i, value in enumerate(values):
            coarse = value.astype(jnp.bfloat16).astype(jnp.float32)
            for part, piece in enumerate((coarse, value - coarse)):
                at = (part * groups + g) * depth + i * edges.shape[1]
                pieces[at : at + edges.shape[1], :] = piece
    return forms


def invert(above, groups, rows):
    above_order = jnp.concatenate([x[groups : groups + 1] for x in above], axis=1)
    rim = above_order.shape[1]
    slot = lax.broadcasted_iota(jnp.int32, (rim, rim), 0).astype(jnp.float32)
    match = jnp.where(spread(above_order, rim) == slot, 1.0, 0.0).astype(jnp.bfloat16)
    numbers = lax.broadcasted_iota(jnp.int32, (2 * rows, rim), 1).astype(jnp.bfloat16)
    inverse = lax.dot_general(
        numbers, match, (((1,), (1,)), ((), ())), preferred_element_type=jnp.float32
    )
    return inverse[:rows].astype(jnp.int32)


def rescaled(block, inverse_scale, step):
    ratio = swap_halves(block) * inverse_scale
    for _ in range(step):
        block = block * ratio
    return doubled(block)


def front_stage(
    polars,
    step,
    edge_count,
    order_ref,
    across_in,
    beside_in,
    scale_in,
    own_picks,
    blocks,
    edges,
    places,
    *rest,
):
    if step == 0:
        inverse_ref, *rest = rest
    else:
        inverse_in, *rest = rest
    delta_ref, picks_ref, pieces, forms_ref, rims_ref, across_ref, beside_ref, values = rest
    rows = delta_ref.shape[0]
    groups = rows // 2
    first = row_ids(rows) < groups
    scale = scale_in[...]
    prior, above = take_rims(across_in, beside_in)
    if step == 0:
        inverse_ref[...] = invert(above, groups, rows)
        inverse = cut(inverse_ref)
        prior, above = [doubled(x) for x in prior], [doubled(x) for x in above]
    else:
        inverse = cut(inverse_in)
        inverse_scale = 1.0 / scale
        prior = [rescaled(x, inverse_scale, step) for x in prior]
        above = [rescaled(x, inverse_scale, step) for x in above]
    put_chunks(delta_ref, corrections(prior, above, cut(order_ref), inverse))

    def visit(g, picked):
        for j in range(SIDE):
            picks_ref[g * SIDE + j] = picked[j]

    forms_ref[...] = apply_all(
        delta_ref, own_picks, blocks, edges, polars, edge_count, pieces, visit
    )
    rim = len(prior)
    chunks = scatter(pieces, edges, places, rim_heights(edge_count, rim)[0], values)
    put_chunks(rims_ref, chunks)
    put_rims(
        across_ref,
        beside_ref,
        [jnp.where(first, x, scale) for x in chunks[:rim]],
        [jnp.where(first, x, scale) for x in chunks[rim:]],
    )


def inner_products(step, sums, own, delta, forms, across_in, beside_in):
    rows = sums.shape[0]
    first = row_ids(rows) < rows // 2
    prior, _ = take_rims(across_in, beside_in)
    has_prior = jnp.where(first, swap_halves(prior[0]), prior[0])
    has_prior = spread(jnp.where(has_prior[:1, :1] > 0.0, 1.0, 0.0), rows)
    field = corrected(own, delta)
    sums = put_lane(sums, 2 * step, lane_sum(squares(field, len(delta) // 2, has_prior)))
    return put_lane(sums, 2 * step + 1, lane_sum(forms))


def back_stage(
    polars,
    step,
    own,
    delta,
    forms,
    across_in,
    beside_in,
    sums_in,
    picks,
    pieces,
    rims,
    edges,
    places,
    *rest,
):
    if step == 0:
        rates, forward, mass, live, heavy, terms_ref, sums_ref, image_ref, picks_ref, values = rest
    else:
        heavy, terms_ref, sums_ref, image_ref, picks_ref, values = rest
    rows, edge_count = own.shape
    groups = rows // 2
    rim = rims.shape[-1] // LANES // 2
    outer = cut(rims)
    inner = scatter(pieces, edges, places, rim_heights(edge_count, rim)[1], values)
    put_chunks(image_ref, outer[:rim] + inner + outer[rim:])
    put_picks(picks_ref, image_ref, edges, groups)
    if step == 0:
        dead = -live[...].astype(jnp.float32)
        for g in range(groups):
            row = [forward[g, :, c : c + LANES] for c in range(0, edge_count, LANES)]
            values = times_block(mass, 0, picks_of(row, edges))
            factor = dead * rates[g // polars]
            for i in range(SIDE):
                heavy[g * SIDE + i] = factor * values[i]
    for g in range(groups):
        side = range(g * SIDE, (g + 1) * SIDE)
        terms_ref[g] = weighted_sum([picks[i] for i in side], [heavy[i] for i in side])
    sums_ref[...] = inner_products(
        step, sums_in[...], cut(own), cut(delta), forms[...], across_in, beside_in
    )


def last_stage(
    polars,
    step,
    own,
    order_ref,
    inverse_in,
    across_in,
    beside_in,
    scale_in,
    sums_in,
    own_picks,
    blocks,
    edges,
    heavy,
    terms_ref,
    sums_ref,
    delta_ref,
):
    rows, edge_count = own.shape
    first = row_ids(rows) < rows // 2
    scale = scale_in[...]
    inverse_scale = 1.0 / scale
    prior, above = take_rims(across_in, beside_in)
    prior = [rescaled(x, inverse_scale, step) for x in prior]
    above = [rescaled(x, inverse_scale, step) for x in above]
    put_chunks(delta_ref, corrections(prior, above, cut(order_ref), cut(inverse_in)))

    def visit(g, picked):
        terms_ref[g] = weighted_sum(picked, [heavy[g * SIDE + i] for i in range(SIDE)])

    forms = apply_all(delta_ref, own_picks, blocks, edges, polars, edge_count, None, visit)
    sums = inner_products(
        step, sums_in[...], cut(own), cut(delta_ref), forms, across_in, beside_in
    )
    sums_ref[...] = jnp.where(first, sums, scale)


def combine_stage(everyone, sums_in, terms0, terms1, terms2, out_ref):
    rows = sums_in.shape[0]
    groups = rows // 2
    first = row_ids(rows) < groups

    def scale_of(block):
        return jnp.where(first, swap_halves(block), block)

    parts = [everyone[q] for q in range(everyone.shape[0])]
    scales = [scale_of(block) for block in parts]
    top = functools.reduce(jnp.maximum, scales)
    lanes = lane_ids(rows)
    inverse_top = 1.0 / top
    total = None
    for block, scale in zip(parts, scales):
        ratio = scale * inverse_top
        power = jnp.ones_like(ratio)
        factor = jnp.ones_like(ratio)
        for k in range(1, 6):
            power = power * ratio
            factor = jnp.where(lanes == k, power, factor)
        term = block * factor
        total = term if total is None else total + term
    m = [jnp.broadcast_to(total[:, k : k + 1], (rows, LANES)) for k in range(6)]
    l1 = m[2] / m[1]
    l2 = m[3] / m[1]
    d2 = m[3] - l1 * m[2]
    cross = m[4] - l2 * m[2]
    l3 = cross / d2
    d3 = m[5] - l2 * m[3] - l3 * cross
    y1 = m[1] - l1 * m[0]
    y2 = m[2] - l2 * m[0] - l3 * y1
    c2 = y2 / d3
    c1 = y1 / d2 - l3 * c2
    c0 = m[0] / m[1] - l1 * c1 - l2 * c2
    mine = scale_of(sums_in[...]) * inverse_top
    c0 = c0 * inverse_top
    c1 = c1 * mine * inverse_top
    c2 = c2 * mine * mine * inverse_top
    out = None
    for terms, c in ((terms0, c0), (terms1, c1), (terms2, c2)):
        for g in range(groups):
            one = terms[g] * spread(c[g : g + 1], out_ref.shape[0])
            out = one if out is None else out + one
    out_ref[...] = out


def pinned(*arguments):
    return [pltpu.with_memory_space_constraint(x, pltpu.HBM) for x in arguments]


def call(kernel, arguments, outs, scratch=(), space=VMEM, cost=0):
    return pl.pallas_call(
        kernel,
        out_shape=outs,
        in_specs=space if isinstance(space, list) else [space] * len(arguments),
        out_specs=jax.tree.map(lambda _: VMEM, outs),
        scratch_shapes=list(scratch),
        cost_estimate=pl.CostEstimate(flops=cost, bytes_accessed=cost, transcendentals=0),
        compiler_params=pltpu.CompilerParams(vmem_limit_bytes=16 * 1024 * 1024),
    )(*arguments)


def swap(block, axis, offset):
    size = lax.axis_size(axis)
    route = []
    for low in range(offset, size - 1, 2):
        route += [(low, low + 1), (low + 1, low)]
    return lax.ppermute(block, axis, route)


def gather_all(block, axis):
    size = lax.axis_size(axis)
    copies = jnp.broadcast_to(block[None], (size, *block.shape))
    return lax.all_to_all(copies, axis, 0, 0)


def sum_over(block, axis):
    size = lax.axis_size(axis)
    if size & (size - 1):
        return jnp.sum(gather_all(block, axis), axis=0)
    step = size // 2
    while step > 0:
        block = block + lax.ppermute(block, axis, [(i, i ^ step) for i in range(size)])
        step //= 2
    return block


def local(
    angular,
    stiffness,
    mass_matrix,
    conductivity,
    element_edges,
    live_slots,
    adjoint_source,
    forward_field,
    neighbour_map,
):
    freqs = angular.shape[0]
    polars = adjoint_source.shape[1]
    groups = freqs * polars
    rows = 2 * groups
    edge_count = adjoint_source.shape[-1]
    rim = neighbour_map.shape[-1]
    slots = element_edges.shape[-1]
    tall = slots // LANES
    stiff = stiffness.reshape(SIDE * SIDE, tall, LANES)
    mass = mass_matrix.reshape(SIDE * SIDE, tall, LANES)
    edges = element_edges.reshape(SIDE, tall, LANES)
    sigma = conductivity.reshape(tall, LANES)
    live = live_slots.reshape(tall, LANES)
    source = adjoint_source.reshape(groups, 1, edge_count)
    forward = forward_field.reshape(groups, 1, edge_count)

    def shape(*dims, kind=jnp.float32):
        return jax.ShapeDtypeStruct(dims, kind)

    field_shape, rim_shape = shape(rows, edge_count), shape(rows, rim)
    sums_shape, terms_shape = shape(rows, LANES), shape(groups, tall, LANES)
    picks_shape = shape(groups * SIDE, tall, LANES)

    across, beside, source, order = call(
        rims_stage,
        pinned(source, neighbour_map),
        [rim_shape, rim_shape, shape(*source.shape), shape(rows, rim, kind=jnp.int32)],
        (
            pltpu.VMEM(neighbour_map.shape, neighbour_map.dtype),
            pltpu.SemaphoreType.DMA((2,)),
        ),
        space=HBM,
    )
    across, beside = swap(across, "dom", 1), swap(beside, "dom", 0)
    kept = [jax.ShapeDtypeStruct(x.shape, x.dtype) for x in (mass, sigma, live, edges, forward)]
    places, blocks, scale, picks, own, rates, mass, sigma, live, edges, forward = call(
        table_stage,
        [*pinned(angular, stiff, mass, sigma, live, edges, forward), source],
        [
            shape(LANES, SIDE * slots, kind=jnp.bfloat16),
            shape(freqs * SIDE * SIDE, tall, LANES),
            sums_shape,
            picks_shape,
            field_shape,
            shape(freqs, tall, LANES),
            *kept,
        ],
        (
            pltpu.SMEM(angular.shape, angular.dtype),
            pltpu.VMEM(stiff.shape, stiff.dtype),
            pltpu.SemaphoreType.DMA((7,)),
        ),
        space=[HBM] * 7 + [VMEM],
        cost=4_000_000,
    )
    front_shapes = [
        shape(rows, 2 * rim),
        picks_shape,
        shape(rows * SIDE * tall, LANES),
        sums_shape,
        shape(rows, 2 * rim),
        rim_shape,
        rim_shape,
    ]
    back_shapes = [terms_shape, sums_shape, field_shape, picks_shape]
    sums, terms = jnp.zeros((rows, LANES), jnp.float32), []
    outer, inner = rim_heights(edge_count, rim // LANES)
    outer = [pltpu.VMEM((rows * len(outer), SIDE * slots), jnp.bfloat16)]
    inner = [pltpu.VMEM((rows * len(inner), SIDE * slots), jnp.bfloat16)]
    for step in range(2):
        arrived = (across, beside)
        given = (order, *arrived, scale, picks, blocks, edges, places)
        front = functools.partial(front_stage, polars, step, edge_count)
        if step == 0:
            inverse, *outs = call(
                front, given, [shape(rows, rim, kind=jnp.int32), *front_shapes], outer
            )
        else:
            outs = call(front, (*given, inverse), front_shapes, outer)
        delta, picks, pieces, forms, rims, across, beside = outs
        across, beside = swap(across, "dom", 1), swap(beside, "dom", 0)
        given = (own, delta, forms, *arrived, sums, picks, pieces, rims, edges, places)
        back = functools.partial(back_stage, polars, step)
        if step == 0:
            heavy, term, sums, own, picks = call(
                back,
                (*given, rates, forward, mass, live),
                [picks_shape, *back_shapes],
                inner,
                cost=4_000_000,
            )
        else:
            term, sums, own, picks = call(back, (*given, heavy), back_shapes, inner, cost=4_000_000)
        terms.append(term)
    term, sums = call(
        functools.partial(last_stage, polars, 2),
        (own, order, inverse, across, beside, scale, sums, picks, blocks, edges, heavy),
        [terms_shape, sums_shape],
        (pltpu.VMEM((rows, 2 * rim), jnp.float32),),
    )
    terms.append(term)
    term = call(
        combine_stage,
        (gather_all(sums, "dom"), sums, *terms),
        shape(tall, LANES),
    )
    gradient = sum_over(term, "freq").reshape(1, slots)
    updated = sigma.reshape(1, slots) * jnp.exp(-0.5 * jnp.tanh(gradient))
    return gradient, updated


def solution(mesh):
    return jax.shard_map(
        local,
        mesh=mesh,
        in_specs=(
            P("freq"),
            P("dom", None, None),
            P("dom", None, None),
            P("dom", None),
            P("dom", None, None),
            P("dom", None),
            P("freq", None, "dom", None),
            P("freq", None, "dom", None),
            P("dom", None),
        ),
        out_specs=(P("dom", None), P("dom", None)),
        check_vma=False,
    )
```

```python
import functools

import jax
import jax.numpy as jnp
from jax import lax
from jax.experimental import pallas as pl
from jax.experimental.pallas import tpu as pltpu
from jax.sharding import PartitionSpec as P

LANES = 128
SUBLANES = 8
SIDE = 6
VMEM = pl.BlockSpec(memory_space=pltpu.VMEM)
HBM = pl.BlockSpec(memory_space=pltpu.HBM)

PICK_LANES = lax.GatherDimensionNumbers(
    offset_dims=(),
    collapsed_slice_dims=(1,),
    start_index_map=(1,),
    operand_batching_dims=(0,),
    start_indices_batching_dims=(0,),
)


def pick_lanes(block, lanes):
    return lax.gather(
        block,
        lanes[..., None],
        PICK_LANES,
        (1, 1),
        mode=lax.GatherScatterMode.PROMISE_IN_BOUNDS,
    )


def pick_wide(chunks, index):
    lanes = index & (LANES - 1)
    high = index >> 7
    level = [pick_lanes(chunk, lanes) for chunk in chunks]
    bit = 0
    while len(level) > 1:
        odd = (high >> bit) & 1 == 1
        level = [
            jnp.where(odd, level[t + 1], level[t]) if t + 1 < len(level) else level[t]
            for t in range(0, len(level), 2)
        ]
        bit += 1
    return level[0]


def row_ids(rows):
    return lax.broadcasted_iota(jnp.int32, (rows, LANES), 0)


def lane_ids(rows):
    return lax.broadcasted_iota(jnp.int32, (rows, LANES), 1)


def spread(row, rows):
    return jnp.broadcast_to(row, (rows, row.shape[-1]))


def cut(ref):
    return [ref[:, c : c + LANES] for c in range(0, ref.shape[-1], LANES)]


def swap_halves(block):
    return pltpu.roll(block, block.shape[0] // 2, 0)


def doubled(block):
    half = block.shape[0] // 2
    return jnp.where(row_ids(2 * half) < half, block, swap_halves(block))


def lane_sum(block):
    return jnp.broadcast_to(jnp.sum(block, axis=1, keepdims=True), block.shape)


def put_lane(block, lane, value):
    return jnp.where(lane_ids(block.shape[0]) == lane, value, block)


def put_chunks(ref, chunks):
    for c, chunk in enumerate(chunks):
        ref[:, c * LANES : (c + 1) * LANES] = chunk


def is_even():
    return lax.rem(lax.axis_index("dom"), 2) == 0


def put_rims(across_ref, beside_ref, lower, upper):
    even = is_even()
    for c, (low, high) in enumerate(zip(lower, upper)):
        here = slice(c * LANES, (c + 1) * LANES)
        across_ref[:, here] = jnp.where(even, low, high)
        beside_ref[:, here] = jnp.where(even, high, low)


def take_rims(across_ref, beside_ref):
    even = is_even()
    pairs = list(zip(cut(across_ref), cut(beside_ref)))
    prior = [jnp.where(even, a, b) for a, b in pairs]
    above = [jnp.where(even, b, a) for a, b in pairs]
    return prior, above


def picks_of(rows_of_group, edges):
    chunks = [spread(row, edges.shape[1]) for row in rows_of_group]
    return [pick_wide(chunks, edges[j]) for j in range(SIDE)]


def group_rows(ref, g):
    return [ref[g : g + 1, c : c + LANES] for c in range(0, ref.shape[-1], LANES)]


def times_block(entries, base, picked):
    out = []
    for i in range(SIDE):
        total = None
        for j in range(SIDE):
            one = entries[base + SIDE * i + j] * picked[j]
            total = one if total is None else total + one
        out.append(total)
    return out


def weighted_sum(left, right):
    total = None
    for a, b in zip(left, right):
        total = a * b if total is None else total + a * b
    return total


def scatter_side(pieces, edges, places, heights, i):
    depth = SIDE * edges.shape[1]
    rows = pieces.shape[0] // depth
    slots = edges.shape[1] * LANES
    columns = []
    for s in range(edges.shape[1]):
        both = pieces[pl.ds(i * edges.shape[1] + s, rows, stride=depth), :]
        high = spread(edges[i, s : s + 1, :] >> 7, rows)
        stacked = [jnp.where(high == h, both, 0.0) for h in heights]
        columns.append(jnp.concatenate(stacked, axis=0).astype(jnp.bfloat16))
    return lax.dot_general(
        jnp.concatenate(columns, axis=1),
        places[:, i * slots : (i + 1) * slots],
        (((1,), (1,)), ((), ())),
        preferred_element_type=jnp.float32,
    )


def add(total, part):
    return part if total is None else total + part


def parts_joined(total, count):
    rows = total.shape[0] // count
    out = []
    for n in range(count):
        piece = total[rows * n : rows * (n + 1)]
        out.append(piece + swap_halves(piece))
    return out


def scatter(pieces, edges, places, heights):
    total = None
    for i in range(SIDE):
        total = add(total, scatter_side(pieces, edges, places, heights, i))
    return parts_joined(total, len(heights))


def rim_heights(edge_count, rim):
    count = edge_count // LANES
    return [*range(rim), *range(count - rim, count)], list(range(rim, count - rim))


def corrections(from_prior, from_above, order, inverse):
    lower = [pick_wide(from_prior, index) for index in order]
    return lower + [pick_wide(from_above, index) for index in inverse]


def corrected(own, delta):
    rim = len(delta) // 2
    lower = [a + b for a, b in zip(own[:rim], delta[:rim])]
    upper = [a + b for a, b in zip(own[len(own) - rim :], delta[rim:])]
    return lower + own[rim : len(own) - rim] + upper


def squares(chunks, rim, has_prior):
    total = None
    for c, chunk in enumerate(chunks):
        term = chunk * chunk
        if c < rim:
            term = term * (1.0 - has_prior)
        total = term if total is None else total + term
    return total


def start_copies(routes, arrived):
    copies = [
        pltpu.make_async_copy(here, there, arrived.at[n])
        for n, (here, there) in enumerate(routes)
    ]
    for copy in copies:
        copy.start()
    return copies


def stacked_chunk(source, at):
    piece = [source[g, :, at : at + LANES] for g in range(source.shape[0])]
    return jnp.concatenate(piece + piece, axis=0)


def rims_stage(source_in, order_in, across_ref, beside_ref, source, order_ref, order, arrived):
    for copy in start_copies(((source_in, source), (order_in, order)), arrived):
        copy.wait()
    rows, rim = order_ref.shape
    first = row_ids(rows) < rows // 2
    order_ref[...] = spread(order[...], rows)
    numbers = [x.astype(jnp.float32) for x in cut(order_ref)]
    lower = [stacked_chunk(source, c) for c in range(0, rim, LANES)]
    start = source.shape[-1] - rim
    upper = [stacked_chunk(source, start + c) for c in range(0, rim, LANES)]
    lower = [jnp.where(first, x, o) for x, o in zip(lower, numbers)]
    upper = [jnp.where(first, x, 1.0) for x in upper]
    put_rims(across_ref, beside_ref, lower, upper)


def table_stage(
    angular_in,
    stiffness_in,
    mass_in,
    sigma_in,
    live_in,
    edges_in,
    forward_in,
    source,
    places_ref,
    blocks_ref,
    scale_ref,
    picks_ref,
    stacked_ref,
    rates,
    mass,
    sigma,
    live,
    edges,
    forward_ref,
    angular,
    stiffness,
    arrived,
):
    copies = start_copies(
        (
            (edges_in, edges),
            (angular_in, angular),
            (sigma_in, sigma),
            (live_in, live),
            (stiffness_in, stiffness),
            (mass_in, mass),
            (forward_in, forward_ref),
        ),
        arrived,
    )
    copies[0].wait()
    numbers = row_ids(LANES)
    rows = edges.shape[1]

    def body(i, carry):
        for s in range(rows):
            lanes = spread(edges[i, s : s + 1, :] & (LANES - 1), LANES)
            column = pl.ds(pl.multiple_of((i * rows + s) * LANES, LANES), LANES)
            places_ref[:, column] = jnp.where(lanes == numbers, 1.0, 0.0).astype(jnp.bfloat16)
        return carry

    lax.fori_loop(0, SIDE, body, 0)
    count = source.shape[-1]
    put_chunks(stacked_ref, [stacked_chunk(source, c) for c in range(0, count, LANES)])
    put_picks(picks_ref, stacked_ref, edges, source.shape[0])
    for copy in copies[1:]:
        copy.wait()
    for f in range(angular.shape[0]):
        rates[f] = jnp.full(rates.shape[1:], angular[f], jnp.float32)
    alive = live[...].astype(jnp.float32)
    weight = sigma[...]
    freqs = rates.shape[0]
    peak = None
    for i in range(SIDE):
        for f in range(freqs):
            entry = (SIDE + 1) * i
            size = stiffness[entry] + rates[f] * weight * mass[entry]
            peak = size if peak is None else jnp.maximum(peak, size)
    peak = jnp.max(peak * alive, axis=1, keepdims=True)
    scale = jnp.broadcast_to(jnp.max(peak, axis=0, keepdims=True), scale_ref.shape)
    scale_ref[...] = scale
    alive = alive / scale[:1, :1]
    for entry in range(SIDE * SIDE):
        stiff = stiffness[entry] * alive
        heavy = mass[entry] * (weight * alive)
        for f in range(freqs):
            blocks_ref[f * SIDE * SIDE + entry] = stiff + rates[f] * heavy


def put_picks(picks_ref, field, edges, groups):
    for g in range(groups):
        for j, value in enumerate(picks_of(group_rows(field, g), edges)):
            picks_ref[g * SIDE + j] = value


def pick_rims(rows, index, edge_count):
    rim = len(rows) // 2
    start = edge_count - rim * LANES
    lower = pick_wide([spread(row, index.shape[0]) for row in rows[:rim]], index)
    upper = pick_wide([spread(row, index.shape[0]) for row in rows[rim:]], index - start)
    lower = jnp.where(index < rim * LANES, lower, 0.0)
    return lower + jnp.where(index >= start, upper, 0.0)


def corrected_picks(delta_ref, own_picks, edges, edge_count):
    out = []
    for g in range(delta_ref.shape[0] // 2):
        delta = group_rows(delta_ref, g)
        out.append(
            [
                own_picks[g * SIDE + j] + pick_rims(delta, edges[j], edge_count)
                for j in range(SIDE)
            ]
        )
    return out


def products(blocks, picked, polars, i):
    out = []
    for g, mine in enumerate(picked):
        base = (g // polars) * SIDE * SIDE + SIDE * i
        out.append(weighted_sum([blocks[base + j] for j in range(SIDE)], mine))
    return out


def rows_of_forms(forms, rows):
    out = jnp.zeros((rows, LANES), jnp.float32)
    for g, form in enumerate(forms):
        row = jnp.sum(form, axis=0, keepdims=True)
        out = jnp.where(row_ids(rows) == g, spread(row, rows), out)
    return out


def invert(above, groups, rows):
    above_order = jnp.concatenate([x[groups : groups + 1] for x in above], axis=1)
    rim = above_order.shape[1]
    slot = lax.broadcasted_iota(jnp.int32, (rim, rim), 0).astype(jnp.float32)
    match = jnp.where(spread(above_order, rim) == slot, 1.0, 0.0).astype(jnp.bfloat16)
    numbers = lax.broadcasted_iota(jnp.int32, (2 * rows, rim), 1).astype(jnp.bfloat16)
    inverse = lax.dot_general(
        numbers, match, (((1,), (1,)), ((), ())), preferred_element_type=jnp.float32
    )
    return inverse[:rows].astype(jnp.int32)


def rescaled(block, inverse_scale, step):
    ratio = swap_halves(block) * inverse_scale
    for _ in range(step):
        block = block * ratio
    return doubled(block)


def front_stage(
    polars,
    step,
    edge_count,
    order_ref,
    across_in,
    beside_in,
    scale_in,
    own_picks,
    blocks,
    edges,
    places,
    *rest,
):
    if step == 0:
        inverse_ref, *rest = rest
    else:
        inverse_in, *rest = rest
    delta_ref, picks_ref, pieces, forms_ref, rims_ref, across_ref, beside_ref = rest
    rows = delta_ref.shape[0]
    groups = rows // 2
    first = row_ids(rows) < groups
    scale = scale_in[...]
    prior, above = take_rims(across_in, beside_in)
    if step == 0:
        inverse_ref[...] = invert(above, groups, rows)
        inverse = cut(inverse_ref)
        prior, above = [doubled(x) for x in prior], [doubled(x) for x in above]
    else:
        inverse = cut(inverse_in)
        inverse_scale = 1.0 / scale
        prior = [rescaled(x, inverse_scale, step) for x in prior]
        above = [rescaled(x, inverse_scale, step) for x in above]
    put_chunks(delta_ref, corrections(prior, above, cut(order_ref), inverse))

    picked = corrected_picks(delta_ref, own_picks, edges, edge_count)
    for g in range(groups):
        for j in range(SIDE):
            picks_ref[g * SIDE + j] = picked[g][j]
    rim = len(prior)
    heights = rim_heights(edge_count, rim)[0]
    tall = edges.shape[1]
    forms, total = [None] * groups, None
    for i in range(SIDE):
        for g, value in enumerate(products(blocks, picked, polars, i)):
            forms[g] = add(forms[g], picked[g][i] * value)
            coarse = value.astype(jnp.bfloat16).astype(jnp.float32)
            for part, piece in enumerate((coarse, value - coarse)):
                at = ((part * groups + g) * SIDE + i) * tall
                pieces[at : at + tall, :] = piece
        total = add(total, scatter_side(pieces, edges, places, heights, i))
    forms_ref[...] = rows_of_forms(forms, rows)
    chunks = parts_joined(total, len(heights))
    put_chunks(rims_ref, chunks)
    put_rims(
        across_ref,
        beside_ref,
        [jnp.where(first, x, scale) for x in chunks[:rim]],
        [jnp.where(first, x, scale) for x in chunks[rim:]],
    )


def inner_products(step, sums, own, delta, forms, across_in, beside_in):
    rows = sums.shape[0]
    first = row_ids(rows) < rows // 2
    prior, _ = take_rims(across_in, beside_in)
    has_prior = jnp.where(first, swap_halves(prior[0]), prior[0])
    has_prior = spread(jnp.where(has_prior[:1, :1] > 0.0, 1.0, 0.0), rows)
    field = corrected(own, delta)
    sums = put_lane(sums, 2 * step, lane_sum(squares(field, len(delta) // 2, has_prior)))
    return put_lane(sums, 2 * step + 1, lane_sum(forms))


def back_stage(
    polars,
    step,
    own,
    delta,
    forms,
    across_in,
    beside_in,
    sums_in,
    picks,
    pieces,
    rims,
    edges,
    places,
    *rest,
):
    if step == 0:
        rates, forward, mass, live, heavy, terms_ref, sums_ref, image_ref, picks_ref = rest
    else:
        heavy, terms_ref, sums_ref, image_ref, picks_ref = rest
    rows, edge_count = own.shape
    groups = rows // 2
    rim = rims.shape[-1] // LANES // 2
    outer = cut(rims)
    inner = scatter(pieces, edges, places, rim_heights(edge_count, rim)[1])
    put_chunks(image_ref, outer[:rim] + inner + outer[rim:])
    put_picks(picks_ref, image_ref, edges, groups)
    if step == 0:
        dead = -live[...].astype(jnp.float32)
        for g in range(groups):
            row = [forward[g, :, c : c + LANES] for c in range(0, edge_count, LANES)]
            values = times_block(mass, 0, picks_of(row, edges))
            factor = dead * rates[g // polars]
            for i in range(SIDE):
                heavy[g * SIDE + i] = factor * values[i]
    for g in range(groups):
        side = range(g * SIDE, (g + 1) * SIDE)
        terms_ref[g] = weighted_sum([picks[i] for i in side], [heavy[i] for i in side])
    sums_ref[...] = inner_products(
        step, sums_in[...], cut(own), cut(delta), forms[...], across_in, beside_in
    )


def last_stage(
    polars,
    step,
    own,
    order_ref,
    inverse_in,
    across_in,
    beside_in,
    scale_in,
    sums_in,
    own_picks,
    blocks,
    edges,
    heavy,
    terms_ref,
    sums_ref,
    delta_ref,
):
    rows, edge_count = own.shape
    first = row_ids(rows) < rows // 2
    scale = scale_in[...]
    inverse_scale = 1.0 / scale
    prior, above = take_rims(across_in, beside_in)
    prior = [rescaled(x, inverse_scale, step) for x in prior]
    above = [rescaled(x, inverse_scale, step) for x in above]
    put_chunks(delta_ref, corrections(prior, above, cut(order_ref), cut(inverse_in)))

    picked = corrected_picks(delta_ref, own_picks, edges, edge_count)
    forms = [None] * len(picked)
    for i in range(SIDE):
        for g, value in enumerate(products(blocks, picked, polars, i)):
            forms[g] = add(forms[g], picked[g][i] * value)
    for g, mine in enumerate(picked):
        terms_ref[g] = weighted_sum(mine, [heavy[g * SIDE + i] for i in range(SIDE)])
    forms = rows_of_forms(forms, rows)
    sums = inner_products(
        step, sums_in[...], cut(own), cut(delta_ref), forms, across_in, beside_in
    )
    sums_ref[...] = jnp.where(first, sums, scale)


def combine_stage(everyone, sums_in, terms0, terms1, terms2, out_ref):
    rows = sums_in.shape[0]
    groups = rows // 2
    first = row_ids(rows) < groups

    def scale_of(block):
        return jnp.where(first, swap_halves(block), block)

    parts = [everyone[q] for q in range(everyone.shape[0])]
    scales = [scale_of(block) for block in parts]
    top = functools.reduce(jnp.maximum, scales)
    lanes = lane_ids(rows)
    inverse_top = 1.0 / top
    total = None
    for block, scale in zip(parts, scales):
        ratio = scale * inverse_top
        power = jnp.ones_like(ratio)
        factor = jnp.ones_like(ratio)
        for k in range(1, 6):
            power = power * ratio
            factor = jnp.where(lanes == k, power, factor)
        term = block * factor
        total = term if total is None else total + term
    m = [jnp.broadcast_to(total[:, k : k + 1], (rows, LANES)) for k in range(6)]
    l1 = m[2] / m[1]
    l2 = m[3] / m[1]
    d2 = m[3] - l1 * m[2]
    cross = m[4] - l2 * m[2]
    l3 = cross / d2
    d3 = m[5] - l2 * m[3] - l3 * cross
    y1 = m[1] - l1 * m[0]
    y2 = m[2] - l2 * m[0] - l3 * y1
    c2 = y2 / d3
    c1 = y1 / d2 - l3 * c2
    c0 = m[0] / m[1] - l1 * c1 - l2 * c2
    mine = scale_of(sums_in[...]) * inverse_top
    c0 = c0 * inverse_top
    c1 = c1 * mine * inverse_top
    c2 = c2 * mine * mine * inverse_top
    out = None
    for terms, c in ((terms0, c0), (terms1, c1), (terms2, c2)):
        for g in range(groups):
            one = terms[g] * spread(c[g : g + 1], out_ref.shape[0])
            out = one if out is None else out + one
    out_ref[...] = out


def pinned(*arguments):
    return [pltpu.with_memory_space_constraint(x, pltpu.HBM) for x in arguments]


def call(kernel, arguments, outs, scratch=(), space=VMEM, cost=0):
    return pl.pallas_call(
        kernel,
        out_shape=outs,
        in_specs=space if isinstance(space, list) else [space] * len(arguments),
        out_specs=jax.tree.map(lambda _: VMEM, outs),
        scratch_shapes=list(scratch),
        cost_estimate=pl.CostEstimate(flops=cost, bytes_accessed=cost, transcendentals=0),
        compiler_params=pltpu.CompilerParams(vmem_limit_bytes=16 * 1024 * 1024),
    )(*arguments)


def swap(block, axis, offset):
    size = lax.axis_size(axis)
    route = []
    for low in range(offset, size - 1, 2):
        route += [(low, low + 1), (low + 1, low)]
    return lax.ppermute(block, axis, route)


def gather_all(block, axis):
    size = lax.axis_size(axis)
    copies = jnp.broadcast_to(block[None], (size, *block.shape))
    return lax.all_to_all(copies, axis, 0, 0)


def sum_over(block, axis):
    size = lax.axis_size(axis)
    if size & (size - 1):
        return jnp.sum(gather_all(block, axis), axis=0)
    step = size // 2
    while step > 0:
        block = block + lax.ppermute(block, axis, [(i, i ^ step) for i in range(size)])
        step //= 2
    return block


def local(
    angular,
    stiffness,
    mass_matrix,
    conductivity,
    element_edges,
    live_slots,
    adjoint_source,
    forward_field,
    neighbour_map,
):
    freqs = angular.shape[0]
    polars = adjoint_source.shape[1]
    groups = freqs * polars
    rows = 2 * groups
    edge_count = adjoint_source.shape[-1]
    rim = neighbour_map.shape[-1]
    slots = element_edges.shape[-1]
    tall = slots // LANES
    stiff = stiffness.reshape(SIDE * SIDE, tall, LANES)
    mass = mass_matrix.reshape(SIDE * SIDE, tall, LANES)
    edges = element_edges.reshape(SIDE, tall, LANES)
    sigma = conductivity.reshape(tall, LANES)
    live = live_slots.reshape(tall, LANES)
    source = adjoint_source.reshape(groups, 1, edge_count)
    forward = forward_field.reshape(groups, 1, edge_count)

    def shape(*dims, kind=jnp.float32):
        return jax.ShapeDtypeStruct(dims, kind)

    field_shape, rim_shape = shape(rows, edge_count), shape(rows, rim)
    sums_shape, terms_shape = shape(rows, LANES), shape(groups, tall, LANES)
    picks_shape = shape(groups * SIDE, tall, LANES)

    across, beside, source, order = call(
        rims_stage,
        pinned(source, neighbour_map),
        [rim_shape, rim_shape, shape(*source.shape), shape(rows, rim, kind=jnp.int32)],
        (
            pltpu.VMEM(neighbour_map.shape, neighbour_map.dtype),
            pltpu.SemaphoreType.DMA((2,)),
        ),
        space=HBM,
    )
    across, beside = swap(across, "dom", 1), swap(beside, "dom", 0)
    kept = [jax.ShapeDtypeStruct(x.shape, x.dtype) for x in (mass, sigma, live, edges, forward)]
    places, blocks, scale, picks, own, rates, mass, sigma, live, edges, forward = call(
        table_stage,
        [*pinned(angular, stiff, mass, sigma, live, edges, forward), source],
        [
            shape(LANES, SIDE * slots, kind=jnp.bfloat16),
            shape(freqs * SIDE * SIDE, tall, LANES),
            sums_shape,
            picks_shape,
            field_shape,
            shape(freqs, tall, LANES),
            *kept,
        ],
        (
            pltpu.SMEM(angular.shape, angular.dtype),
            pltpu.VMEM(stiff.shape, stiff.dtype),
            pltpu.SemaphoreType.DMA((7,)),
        ),
        space=[HBM] * 7 + [VMEM],
        cost=4_000_000,
    )
    front_shapes = [
        shape(rows, 2 * rim),
        picks_shape,
        shape(rows * SIDE * tall, LANES),
        sums_shape,
        shape(rows, 2 * rim),
        rim_shape,
        rim_shape,
    ]
    back_shapes = [terms_shape, sums_shape, field_shape, picks_shape]
    sums, terms = jnp.zeros((rows, LANES), jnp.float32), []
    for step in range(2):
        arrived = (across, beside)
        given = (order, *arrived, scale, picks, blocks, edges, places)
        front = functools.partial(front_stage, polars, step, edge_count)
        if step == 0:
            inverse, *outs = call(
                front, given, [shape(rows, rim, kind=jnp.int32), *front_shapes]
            )
        else:
            outs = call(front, (*given, inverse), front_shapes)
        delta, picks, pieces, forms, rims, across, beside = outs
        across, beside = swap(across, "dom", 1), swap(beside, "dom", 0)
        given = (own, delta, forms, *arrived, sums, picks, pieces, rims, edges, places)
        back = functools.partial(back_stage, polars, step)
        if step == 0:
            heavy, term, sums, own, picks = call(
                back,
                (*given, rates, forward, mass, live),
                [picks_shape, *back_shapes],
                cost=4_000_000,
            )
        else:
            term, sums, own, picks = call(back, (*given, heavy), back_shapes, cost=4_000_000)
        terms.append(term)
    term, sums = call(
        functools.partial(last_stage, polars, 2),
        (own, order, inverse, across, beside, scale, sums, picks, blocks, edges, heavy),
        [terms_shape, sums_shape],
        (pltpu.VMEM((rows, 2 * rim), jnp.float32),),
    )
    terms.append(term)
    term = call(
        combine_stage,
        (gather_all(sums, "dom"), sums, *terms),
        shape(tall, LANES),
    )
    gradient = sum_over(term, "freq").reshape(1, slots)
    updated = sigma.reshape(1, slots) * jnp.exp(-0.5 * jnp.tanh(gradient))
    return gradient, updated


def solution(mesh):
    return jax.shard_map(
        local,
        mesh=mesh,
        in_specs=(
            P("freq"),
            P("dom", None, None),
            P("dom", None, None),
            P("dom", None),
            P("dom", None, None),
            P("dom", None),
            P("freq", None, "dom", None),
            P("freq", None, "dom", None),
            P("dom", None),
        ),
        out_specs=(P("dom", None), P("dom", None)),
        check_vma=False,
    )
```

```python
import functools

import jax
import jax.numpy as jnp
from jax import lax
from jax.experimental import pallas as pl
from jax.experimental.pallas import tpu as pltpu
from jax.sharding import PartitionSpec as P

LANES = 128
SUBLANES = 8
SIDE = 6
VMEM = pl.BlockSpec(memory_space=pltpu.VMEM)
HBM = pl.BlockSpec(memory_space=pltpu.HBM)

PICK_LANES = lax.GatherDimensionNumbers(
    offset_dims=(),
    collapsed_slice_dims=(1,),
    start_index_map=(1,),
    operand_batching_dims=(0,),
    start_indices_batching_dims=(0,),
)


def pick_lanes(block, lanes):
    return lax.gather(
        block,
        lanes[..., None],
        PICK_LANES,
        (1, 1),
        mode=lax.GatherScatterMode.PROMISE_IN_BOUNDS,
    )


def pick_wide(chunks, index):
    lanes = index & (LANES - 1)
    high = index >> 7
    level = [pick_lanes(chunk, lanes) for chunk in chunks]
    bit = 0
    while len(level) > 1:
        odd = (high >> bit) & 1 == 1
        level = [
            jnp.where(odd, level[t + 1], level[t]) if t + 1 < len(level) else level[t]
            for t in range(0, len(level), 2)
        ]
        bit += 1
    return level[0]


def row_ids(rows):
    return lax.broadcasted_iota(jnp.int32, (rows, LANES), 0)


def lane_ids(rows):
    return lax.broadcasted_iota(jnp.int32, (rows, LANES), 1)


def spread(row, rows):
    return jnp.broadcast_to(row, (rows, row.shape[-1]))


def cut(ref):
    return [ref[:, c : c + LANES] for c in range(0, ref.shape[-1], LANES)]


def swap_halves(block):
    return pltpu.roll(block, block.shape[0] // 2, 0)


def doubled(block):
    half = block.shape[0] // 2
    return jnp.where(row_ids(2 * half) < half, block, swap_halves(block))


def lane_sum(block):
    return jnp.broadcast_to(jnp.sum(block, axis=1, keepdims=True), block.shape)


def put_lane(block, lane, value):
    return jnp.where(lane_ids(block.shape[0]) == lane, value, block)


def put_chunks(ref, chunks):
    for c, chunk in enumerate(chunks):
        ref[:, c * LANES : (c + 1) * LANES] = chunk


def is_even():
    return lax.rem(lax.axis_index("dom"), 2) == 0


def put_rims(across_ref, beside_ref, lower, upper):
    even = is_even()
    for c, (low, high) in enumerate(zip(lower, upper)):
        here = slice(c * LANES, (c + 1) * LANES)
        across_ref[:, here] = jnp.where(even, low, high)
        beside_ref[:, here] = jnp.where(even, high, low)


def take_rims(across_ref, beside_ref):
    even = is_even()
    pairs = list(zip(cut(across_ref), cut(beside_ref)))
    prior = [jnp.where(even, a, b) for a, b in pairs]
    above = [jnp.where(even, b, a) for a, b in pairs]
    return prior, above


def picks_of(rows_of_group, edges):
    chunks = [spread(row, edges.shape[1]) for row in rows_of_group]
    return [pick_wide(chunks, edges[j]) for j in range(SIDE)]


def group_rows(ref, g):
    return [ref[g : g + 1, c : c + LANES] for c in range(0, ref.shape[-1], LANES)]


def times_block(entries, base, picked):
    out = []
    for i in range(SIDE):
        total = None
        for j in range(SIDE):
            one = entries[base + SIDE * i + j] * picked[j]
            total = one if total is None else total + one
        out.append(total)
    return out


def weighted_sum(left, right):
    total = None
    for a, b in zip(left, right):
        total = a * b if total is None else total + a * b
    return total


def scatter_side(pieces, edges, places, heights, i):
    depth = SIDE * edges.shape[1]
    rows = pieces.shape[0] // depth
    slots = edges.shape[1] * LANES
    columns = []
    for s in range(edges.shape[1]):
        both = pieces[pl.ds(i * edges.shape[1] + s, rows, stride=depth), :]
        high = spread(edges[i, s : s + 1, :] >> 7, rows)
        stacked = [jnp.where(high == h, both, 0.0) for h in heights]
        columns.append(jnp.concatenate(stacked, axis=0).astype(jnp.bfloat16))
    return lax.dot_general(
        jnp.concatenate(columns, axis=1),
        places[:, i * slots : (i + 1) * slots],
        (((1,), (1,)), ((), ())),
        preferred_element_type=jnp.float32,
    )


def add(total, part):
    return part if total is None else total + part


def parts_joined(total, count):
    rows = total.shape[0] // count
    out = []
    for n in range(count):
        piece = total[rows * n : rows * (n + 1)]
        out.append(piece + swap_halves(piece))
    return out


def scatter(pieces, edges, places, heights):
    total = None
    for i in range(SIDE):
        total = add(total, scatter_side(pieces, edges, places, heights, i))
    return parts_joined(total, len(heights))


def rim_heights(edge_count, rim):
    count = edge_count // LANES
    return [*range(rim), *range(count - rim, count)], list(range(rim, count - rim))


def corrections(from_prior, from_above, order, inverse):
    lower = [pick_wide(from_prior, index) for index in order]
    return lower + [pick_wide(from_above, index) for index in inverse]


def corrected(own, delta):
    rim = len(delta) // 2
    lower = [a + b for a, b in zip(own[:rim], delta[:rim])]
    upper = [a + b for a, b in zip(own[len(own) - rim :], delta[rim:])]
    return lower + own[rim : len(own) - rim] + upper


def squares(chunks, rim, has_prior):
    total = None
    for c, chunk in enumerate(chunks):
        term = chunk * chunk
        if c < rim:
            term = term * (1.0 - has_prior)
        total = term if total is None else total + term
    return total


def start_copies(routes, arrived):
    copies = [
        pltpu.make_async_copy(here, there, arrived.at[n])
        for n, (here, there) in enumerate(routes)
    ]
    for copy in copies:
        copy.start()
    return copies


def stacked_chunk(source, at):
    piece = [source[g, :, at : at + LANES] for g in range(source.shape[0])]
    return jnp.concatenate(piece + piece, axis=0)


def rims_stage(source_in, order_in, across_ref, beside_ref, source, order_ref, order, arrived):
    for copy in start_copies(((source_in, source), (order_in, order)), arrived):
        copy.wait()
    rows, rim = order_ref.shape
    first = row_ids(rows) < rows // 2
    order_ref[...] = spread(order[...], rows)
    numbers = [x.astype(jnp.float32) for x in cut(order_ref)]
    lower = [stacked_chunk(source, c) for c in range(0, rim, LANES)]
    start = source.shape[-1] - rim
    upper = [stacked_chunk(source, start + c) for c in range(0, rim, LANES)]
    lower = [jnp.where(first, x, o) for x, o in zip(lower, numbers)]
    upper = [jnp.where(first, x, 1.0) for x in upper]
    put_rims(across_ref, beside_ref, lower, upper)


def table_stage(
    angular_in,
    stiffness_in,
    mass_in,
    sigma_in,
    live_in,
    edges_in,
    forward_in,
    source,
    places_ref,
    blocks_ref,
    scale_ref,
    picks_ref,
    stacked_ref,
    rates,
    mass,
    sigma,
    live,
    edges,
    forward_ref,
    angular,
    stiffness,
    arrived,
):
    copies = start_copies(
        (
            (edges_in, edges),
            (angular_in, angular),
            (sigma_in, sigma),
            (live_in, live),
            (stiffness_in, stiffness),
            (mass_in, mass),
            (forward_in, forward_ref),
        ),
        arrived,
    )
    copies[0].wait()
    numbers = row_ids(LANES)
    rows = edges.shape[1]

    def body(i, carry):
        for s in range(rows):
            lanes = spread(edges[i, s : s + 1, :] & (LANES - 1), LANES)
            column = pl.ds(pl.multiple_of((i * rows + s) * LANES, LANES), LANES)
            places_ref[:, column] = jnp.where(lanes == numbers, 1.0, 0.0).astype(jnp.bfloat16)
        return carry

    lax.fori_loop(0, SIDE, body, 0)
    count = source.shape[-1]
    put_chunks(stacked_ref, [stacked_chunk(source, c) for c in range(0, count, LANES)])
    put_picks(picks_ref, stacked_ref, edges, source.shape[0])
    for copy in copies[1:]:
        copy.wait()
    for f in range(angular.shape[0]):
        rates[f] = jnp.full(rates.shape[1:], angular[f], jnp.float32)
    alive = live[...].astype(jnp.float32)
    weight = sigma[...]
    freqs = rates.shape[0]
    peak = None
    for i in range(SIDE):
        for f in range(freqs):
            entry = (SIDE + 1) * i
            size = stiffness[entry] + rates[f] * weight * mass[entry]
            peak = size if peak is None else jnp.maximum(peak, size)
    peak = jnp.max(peak * alive, axis=1, keepdims=True)
    scale = jnp.broadcast_to(jnp.max(peak, axis=0, keepdims=True), scale_ref.shape)
    scale_ref[...] = scale
    alive = alive / scale[:1, :1]
    for entry in range(SIDE * SIDE):
        stiff = stiffness[entry] * alive
        heavy = mass[entry] * (weight * alive)
        for f in range(freqs):
            blocks_ref[f * SIDE * SIDE + entry] = stiff + rates[f] * heavy


def put_picks(picks_ref, field, edges, groups):
    for g in range(groups):
        for j, value in enumerate(picks_of(group_rows(field, g), edges)):
            picks_ref[g * SIDE + j] = value


def pick_rims(rows, index, edge_count):
    rim = len(rows) // 2
    start = edge_count - rim * LANES
    lower = pick_wide([spread(row, index.shape[0]) for row in rows[:rim]], index)
    upper = pick_wide([spread(row, index.shape[0]) for row in rows[rim:]], index - start)
    lower = jnp.where(index < rim * LANES, lower, 0.0)
    return lower + jnp.where(index >= start, upper, 0.0)


def corrected_picks(delta_ref, own_picks, edges, edge_count):
    out = []
    for g in range(delta_ref.shape[0] // 2):
        delta = group_rows(delta_ref, g)
        out.append(
            [
                own_picks[g * SIDE + j] + pick_rims(delta, edges[j], edge_count)
                for j in range(SIDE)
            ]
        )
    return out


def products(blocks, picked, polars, i):
    out = []
    for g, mine in enumerate(picked):
        base = (g // polars) * SIDE * SIDE + SIDE * i
        out.append(weighted_sum([blocks[base + j] for j in range(SIDE)], mine))
    return out


def rows_of_forms(forms, rows):
    out = jnp.zeros((rows, LANES), jnp.float32)
    for g, form in enumerate(forms):
        row = jnp.sum(form, axis=0, keepdims=True)
        out = jnp.where(row_ids(rows) == g, spread(row, rows), out)
    return out


def invert(above, groups, rows):
    above_order = jnp.concatenate([x[groups : groups + 1] for x in above], axis=1)
    rim = above_order.shape[1]
    slot = lax.broadcasted_iota(jnp.int32, (rim, rim), 0).astype(jnp.float32)
    match = jnp.where(spread(above_order, rim) == slot, 1.0, 0.0).astype(jnp.bfloat16)
    numbers = lax.broadcasted_iota(jnp.int32, (2 * rows, rim), 1).astype(jnp.bfloat16)
    inverse = lax.dot_general(
        numbers, match, (((1,), (1,)), ((), ())), preferred_element_type=jnp.float32
    )
    return inverse[:rows].astype(jnp.int32)


def rescaled(block, inverse_scale, step):
    ratio = swap_halves(block) * inverse_scale
    for _ in range(step):
        block = block * ratio
    return doubled(block)


def front_stage(
    polars,
    step,
    edge_count,
    order_ref,
    across_in,
    beside_in,
    scale_in,
    own_picks,
    blocks,
    edges,
    places,
    *rest,
):
    if step == 0:
        inverse_ref, *rest = rest
    else:
        inverse_in, *rest = rest
    delta_ref, picks_ref, pieces, forms_ref, rims_ref, across_ref, beside_ref = rest
    rows = delta_ref.shape[0]
    groups = rows // 2
    first = row_ids(rows) < groups
    scale = scale_in[...]
    prior, above = take_rims(across_in, beside_in)
    if step == 0:
        inverse_ref[...] = invert(above, groups, rows)
        inverse = cut(inverse_ref)
        prior, above = [doubled(x) for x in prior], [doubled(x) for x in above]
    else:
        inverse = cut(inverse_in)
        inverse_scale = 1.0 / scale
        prior = [rescaled(x, inverse_scale, step) for x in prior]
        above = [rescaled(x, inverse_scale, step) for x in above]
    put_chunks(delta_ref, corrections(prior, above, cut(order_ref), inverse))

    picked = corrected_picks(delta_ref, own_picks, edges, edge_count)
    for g in range(groups):
        for j in range(SIDE):
            picks_ref[g * SIDE + j] = picked[g][j]
    rim = len(prior)
    heights = rim_heights(edge_count, rim)[0]
    tall = edges.shape[1]
    forms, total = [None] * groups, None
    for i in range(SIDE):
        for g, value in enumerate(products(blocks, picked, polars, i)):
            forms[g] = add(forms[g], picked[g][i] * value)
            coarse = value.astype(jnp.bfloat16).astype(jnp.float32)
            for part, piece in enumerate((coarse, value - coarse)):
                at = ((part * groups + g) * SIDE + i) * tall
                pieces[at : at + tall, :] = piece
        total = add(total, scatter_side(pieces, edges, places, heights, i))
    forms_ref[...] = rows_of_forms(forms, rows)
    chunks = parts_joined(total, len(heights))
    put_chunks(rims_ref, chunks)
    put_rims(
        across_ref,
        beside_ref,
        [jnp.where(first, x, scale) for x in chunks[:rim]],
        [jnp.where(first, x, scale) for x in chunks[rim:]],
    )


def inner_products(step, sums, own, delta, forms, across_in, beside_in):
    rows = sums.shape[0]
    first = row_ids(rows) < rows // 2
    prior, _ = take_rims(across_in, beside_in)
    has_prior = jnp.where(first, swap_halves(prior[0]), prior[0])
    has_prior = spread(jnp.where(has_prior[:1, :1] > 0.0, 1.0, 0.0), rows)
    field = corrected(own, delta)
    sums = put_lane(sums, 2 * step, lane_sum(squares(field, len(delta) // 2, has_prior)))
    return put_lane(sums, 2 * step + 1, lane_sum(forms))


def back_stage(
    polars,
    step,
    own,
    delta,
    forms,
    across_in,
    beside_in,
    sums_in,
    picks,
    pieces,
    rims,
    edges,
    places,
    *rest,
):
    if step == 0:
        rates, forward, mass, live, heavy, terms_ref, sums_ref, image_ref, picks_ref = rest
    else:
        heavy, terms_ref, sums_ref, image_ref, picks_ref = rest
    rows, edge_count = own.shape
    groups = rows // 2
    rim = rims.shape[-1] // LANES // 2
    outer = cut(rims)
    inner = scatter(pieces, edges, places, rim_heights(edge_count, rim)[1])
    put_chunks(image_ref, outer[:rim] + inner + outer[rim:])
    put_picks(picks_ref, image_ref, edges, groups)
    if step == 0:
        dead = -live[...].astype(jnp.float32)
        for g in range(groups):
            row = [forward[g, :, c : c + LANES] for c in range(0, edge_count, LANES)]
            values = times_block(mass, 0, picks_of(row, edges))
            factor = dead * rates[g // polars]
            for i in range(SIDE):
                heavy[g * SIDE + i] = factor * values[i]
    for g in range(groups):
        side = range(g * SIDE, (g + 1) * SIDE)
        terms_ref[g] = weighted_sum([picks[i] for i in side], [heavy[i] for i in side])
    sums_ref[...] = inner_products(
        step, sums_in[...], cut(own), cut(delta), forms[...], across_in, beside_in
    )


def last_stage(
    polars,
    step,
    own,
    order_ref,
    inverse_in,
    across_in,
    beside_in,
    scale_in,
    sums_in,
    own_picks,
    blocks,
    edges,
    heavy,
    terms0,
    terms1,
    terms_ref,
    sums_ref,
    delta_ref,
):
    rows, edge_count = own.shape
    groups = rows // 2
    terms_ref[:groups] = terms0[...]
    terms_ref[groups : 2 * groups] = terms1[...]
    terms_ref[3 * groups] = jnp.broadcast_to(scale_in[:1, :1], terms_ref.shape[1:])
    first = row_ids(rows) < rows // 2
    scale = scale_in[...]
    inverse_scale = 1.0 / scale
    prior, above = take_rims(across_in, beside_in)
    prior = [rescaled(x, inverse_scale, step) for x in prior]
    above = [rescaled(x, inverse_scale, step) for x in above]
    put_chunks(delta_ref, corrections(prior, above, cut(order_ref), cut(inverse_in)))

    picked = corrected_picks(delta_ref, own_picks, edges, edge_count)
    forms = [None] * len(picked)
    for i in range(SIDE):
        for g, value in enumerate(products(blocks, picked, polars, i)):
            forms[g] = add(forms[g], picked[g][i] * value)
    for g, mine in enumerate(picked):
        terms_ref[2 * groups + g] = weighted_sum(
            mine, [heavy[g * SIDE + i] for i in range(SIDE)]
        )
    forms = rows_of_forms(forms, rows)
    sums = inner_products(
        step, sums_in[...], cut(own), cut(delta_ref), forms, across_in, beside_in
    )
    sums_ref[...] = jnp.where(first, sums, scale)


def combine_stage(everyone, own, other, out_ref):
    rows = everyone.shape[1]
    groups = rows // 2
    first = row_ids(rows) < groups

    def scale_of(block):
        return jnp.where(first, swap_halves(block), block)

    parts = [everyone[q] for q in range(everyone.shape[0])]
    scales = [scale_of(block) for block in parts]
    top = functools.reduce(jnp.maximum, scales)
    lanes = lane_ids(rows)
    inverse_top = 1.0 / top
    total = None
    for block, scale in zip(parts, scales):
        ratio = scale * inverse_top
        power = jnp.ones_like(ratio)
        factor = jnp.ones_like(ratio)
        for k in range(1, 6):
            power = power * ratio
            factor = jnp.where(lanes == k, power, factor)
        term = block * factor
        total = term if total is None else total + term
    m = [jnp.broadcast_to(total[:, k : k + 1], (rows, LANES)) for k in range(6)]
    l1 = m[2] / m[1]
    l2 = m[3] / m[1]
    d2 = m[3] - l1 * m[2]
    cross = m[4] - l2 * m[2]
    l3 = cross / d2
    d3 = m[5] - l2 * m[3] - l3 * cross
    y1 = m[1] - l1 * m[0]
    y2 = m[2] - l2 * m[0] - l3 * y1
    c2 = y2 / d3
    c1 = y1 / d2 - l3 * c2
    c0 = m[0] / m[1] - l1 * c1 - l2 * c2
    tall = out_ref.shape[1]
    for n, terms in enumerate((own, other)):
        mine = terms[3 * groups] * inverse_top[:1]
        weight = spread(inverse_top[:1], tall)
        out = None
        for place, c in enumerate((c0, c1, c2)):
            part = None
            for g in range(groups):
                part = add(part, terms[place * groups + g] * spread(c[g : g + 1], tall))
            out = add(out, part * weight)
            weight = weight * mine
        out_ref[n] = out


def pinned(*arguments):
    return [pltpu.with_memory_space_constraint(x, pltpu.HBM) for x in arguments]


def call(kernel, arguments, outs, scratch=(), space=VMEM, cost=0):
    return pl.pallas_call(
        kernel,
        out_shape=outs,
        in_specs=space if isinstance(space, list) else [space] * len(arguments),
        out_specs=jax.tree.map(lambda _: VMEM, outs),
        scratch_shapes=list(scratch),
        cost_estimate=pl.CostEstimate(flops=cost, bytes_accessed=cost, transcendentals=0),
        compiler_params=pltpu.CompilerParams(vmem_limit_bytes=16 * 1024 * 1024),
    )(*arguments)


def swap(block, axis, offset):
    size = lax.axis_size(axis)
    route = []
    for low in range(offset, size - 1, 2):
        route += [(low, low + 1), (low + 1, low)]
    return lax.ppermute(block, axis, route)


def gather_all(block, axis):
    size = lax.axis_size(axis)
    copies = jnp.broadcast_to(block[None], (size, *block.shape))
    return lax.all_to_all(copies, axis, 0, 0)


def sum_over_freq(block):
    size, width = lax.axis_size("freq"), lax.axis_size("dom")
    places = range(1, width, 2)
    step = size // 2
    while step > 0:
        route = [(f * width + p, (f ^ step) * width + p) for f in range(size) for p in places]
        block = block + lax.ppermute(block, ("freq", "dom"), route)
        step //= 2
    return block


def local(
    angular,
    stiffness,
    mass_matrix,
    conductivity,
    element_edges,
    live_slots,
    adjoint_source,
    forward_field,
    neighbour_map,
):
    freqs = angular.shape[0]
    polars = adjoint_source.shape[1]
    groups = freqs * polars
    rows = 2 * groups
    edge_count = adjoint_source.shape[-1]
    rim = neighbour_map.shape[-1]
    slots = element_edges.shape[-1]
    tall = slots // LANES
    stiff = stiffness.reshape(SIDE * SIDE, tall, LANES)
    mass = mass_matrix.reshape(SIDE * SIDE, tall, LANES)
    edges = element_edges.reshape(SIDE, tall, LANES)
    sigma = conductivity.reshape(tall, LANES)
    live = live_slots.reshape(tall, LANES)
    source = adjoint_source.reshape(groups, 1, edge_count)
    forward = forward_field.reshape(groups, 1, edge_count)

    def shape(*dims, kind=jnp.float32):
        return jax.ShapeDtypeStruct(dims, kind)

    field_shape, rim_shape = shape(rows, edge_count), shape(rows, rim)
    sums_shape, terms_shape = shape(rows, LANES), shape(groups, tall, LANES)
    picks_shape = shape(groups * SIDE, tall, LANES)

    across, beside, source, order = call(
        rims_stage,
        pinned(source, neighbour_map),
        [rim_shape, rim_shape, shape(*source.shape), shape(rows, rim, kind=jnp.int32)],
        (
            pltpu.VMEM(neighbour_map.shape, neighbour_map.dtype),
            pltpu.SemaphoreType.DMA((2,)),
        ),
        space=HBM,
    )
    across, beside = swap(across, "dom", 1), swap(beside, "dom", 0)
    kept = [jax.ShapeDtypeStruct(x.shape, x.dtype) for x in (mass, sigma, live, edges, forward)]
    places, blocks, scale, picks, own, rates, mass, sigma, live, edges, forward = call(
        table_stage,
        [*pinned(angular, stiff, mass, sigma, live, edges, forward), source],
        [
            shape(LANES, SIDE * slots, kind=jnp.bfloat16),
            shape(freqs * SIDE * SIDE, tall, LANES),
            sums_shape,
            picks_shape,
            field_shape,
            shape(freqs, tall, LANES),
            *kept,
        ],
        (
            pltpu.SMEM(angular.shape, angular.dtype),
            pltpu.VMEM(stiff.shape, stiff.dtype),
            pltpu.SemaphoreType.DMA((7,)),
        ),
        space=[HBM] * 7 + [VMEM],
        cost=4_000_000,
    )
    front_shapes = [
        shape(rows, 2 * rim),
        picks_shape,
        shape(rows * SIDE * tall, LANES),
        sums_shape,
        shape(rows, 2 * rim),
        rim_shape,
        rim_shape,
    ]
    back_shapes = [terms_shape, sums_shape, field_shape, picks_shape]
    sums, terms = jnp.zeros((rows, LANES), jnp.float32), []
    for step in range(2):
        arrived = (across, beside)
        given = (order, *arrived, scale, picks, blocks, edges, places)
        front = functools.partial(front_stage, polars, step, edge_count)
        if step == 0:
            inverse, *outs = call(
                front, given, [shape(rows, rim, kind=jnp.int32), *front_shapes]
            )
        else:
            outs = call(front, (*given, inverse), front_shapes)
        delta, picks, pieces, forms, rims, across, beside = outs
        across, beside = swap(across, "dom", 1), swap(beside, "dom", 0)
        given = (own, delta, forms, *arrived, sums, picks, pieces, rims, edges, places)
        back = functools.partial(back_stage, polars, step)
        if step == 0:
            heavy, term, sums, own, picks = call(
                back,
                (*given, rates, forward, mass, live),
                [picks_shape, *back_shapes],
                cost=4_000_000,
            )
        else:
            term, sums, own, picks = call(back, (*given, heavy), back_shapes, cost=4_000_000)
        terms.append(term)
    terms, sums = call(
        functools.partial(last_stage, polars, 2),
        (own, order, inverse, across, beside, scale, sums, picks, blocks, edges, heavy, *terms),
        [shape(3 * groups + 1, tall, LANES), sums_shape],
        (pltpu.VMEM((rows, 2 * rim), jnp.float32),),
    )
    both = call(
        combine_stage,
        (gather_all(sums, "dom"), terms, swap(terms, "dom", 0)),
        shape(2, tall, LANES),
    )
    both = sum_over_freq(both)
    returned = swap(both[1], "dom", 0)
    odd = lax.rem(lax.axis_index("dom"), 2) == 1
    gradient = jnp.where(odd, both[0], returned).reshape(1, slots)
    updated = sigma.reshape(1, slots) * jnp.exp(-0.5 * jnp.tanh(gradient))
    return gradient, updated


def solution(mesh):
    return jax.shard_map(
        local,
        mesh=mesh,
        in_specs=(
            P("freq"),
            P("dom", None, None),
            P("dom", None, None),
            P("dom", None),
            P("dom", None, None),
            P("dom", None),
            P("freq", None, "dom", None),
            P("freq", None, "dom", None),
            P("dom", None),
        ),
        out_specs=(P("dom", None), P("dom", None)),
        check_vma=False,
    )
```

```python
import functools

import jax
import jax.numpy as jnp
from jax import lax
from jax.experimental import pallas as pl
from jax.experimental.pallas import tpu as pltpu
from jax.sharding import PartitionSpec as P

LANES = 128
SUBLANES = 8
SIDE = 6
VMEM = pl.BlockSpec(memory_space=pltpu.VMEM)
HBM = pl.BlockSpec(memory_space=pltpu.HBM)

PICK_LANES = lax.GatherDimensionNumbers(
    offset_dims=(),
    collapsed_slice_dims=(1,),
    start_index_map=(1,),
    operand_batching_dims=(0,),
    start_indices_batching_dims=(0,),
)


def pick_lanes(block, lanes):
    return lax.gather(
        block,
        lanes[..., None],
        PICK_LANES,
        (1, 1),
        mode=lax.GatherScatterMode.PROMISE_IN_BOUNDS,
    )


def pick_wide(chunks, index):
    lanes = index & (LANES - 1)
    high = index >> 7
    level = [pick_lanes(chunk, lanes) for chunk in chunks]
    bit = 0
    while len(level) > 1:
        odd = (high >> bit) & 1 == 1
        level = [
            jnp.where(odd, level[t + 1], level[t]) if t + 1 < len(level) else level[t]
            for t in range(0, len(level), 2)
        ]
        bit += 1
    return level[0]


def row_ids(rows):
    return lax.broadcasted_iota(jnp.int32, (rows, LANES), 0)


def lane_ids(rows):
    return lax.broadcasted_iota(jnp.int32, (rows, LANES), 1)


def spread(row, rows):
    return jnp.broadcast_to(row, (rows, row.shape[-1]))


def cut(ref):
    return [ref[:, c : c + LANES] for c in range(0, ref.shape[-1], LANES)]


def swap_halves(block):
    return pltpu.roll(block, block.shape[0] // 2, 0)


def doubled(block):
    half = block.shape[0] // 2
    return jnp.where(row_ids(2 * half) < half, block, swap_halves(block))


def lane_sum(block):
    return jnp.broadcast_to(jnp.sum(block, axis=1, keepdims=True), block.shape)


def put_lane(block, lane, value):
    return jnp.where(lane_ids(block.shape[0]) == lane, value, block)


def put_chunks(ref, chunks):
    for c, chunk in enumerate(chunks):
        ref[:, c * LANES : (c + 1) * LANES] = chunk


def is_even():
    return lax.rem(lax.axis_index("dom"), 2) == 0


def put_rims(across_ref, beside_ref, lower, upper):
    even = is_even()
    for c, (low, high) in enumerate(zip(lower, upper)):
        here = slice(c * LANES, (c + 1) * LANES)
        across_ref[:, here] = jnp.where(even, low, high)
        beside_ref[:, here] = jnp.where(even, high, low)


def take_rims(across_ref, beside_ref):
    even = is_even()
    device = lax.axis_index("dom")
    outermost = (device == 0) | (device == lax.axis_size("dom") - 1)
    pairs = [
        (jnp.where(outermost, 0.0, a), b) for a, b in zip(cut(across_ref), cut(beside_ref))
    ]
    prior = [jnp.where(even, a, b) for a, b in pairs]
    above = [jnp.where(even, b, a) for a, b in pairs]
    return prior, above


def picks_of(rows_of_group, edges):
    chunks = [spread(row, edges.shape[1]) for row in rows_of_group]
    return [pick_wide(chunks, edges[j]) for j in range(SIDE)]


def group_rows(ref, g):
    return [ref[g : g + 1, c : c + LANES] for c in range(0, ref.shape[-1], LANES)]


def times_block(entries, base, picked):
    out = []
    for i in range(SIDE):
        total = None
        for j in range(SIDE):
            one = entries[base + SIDE * i + j] * picked[j]
            total = one if total is None else total + one
        out.append(total)
    return out


def weighted_sum(left, right):
    total = None
    for a, b in zip(left, right):
        total = a * b if total is None else total + a * b
    return total


def scatter_side(pieces, edges, places, heights, i):
    depth = SIDE * edges.shape[1]
    rows = pieces.shape[0] // depth
    slots = edges.shape[1] * LANES
    columns = []
    for s in range(edges.shape[1]):
        both = pieces[pl.ds(i * edges.shape[1] + s, rows, stride=depth), :]
        high = spread(edges[i, s : s + 1, :] >> 7, rows)
        stacked = [jnp.where(high == h, both, 0.0) for h in heights]
        columns.append(jnp.concatenate(stacked, axis=0).astype(jnp.bfloat16))
    return lax.dot_general(
        jnp.concatenate(columns, axis=1),
        places[:, i * slots : (i + 1) * slots],
        (((1,), (1,)), ((), ())),
        preferred_element_type=jnp.float32,
    )


def add(total, part):
    return part if total is None else total + part


def parts_joined(total, count):
    rows = total.shape[0] // count
    out = []
    for n in range(count):
        piece = total[rows * n : rows * (n + 1)]
        out.append(piece + swap_halves(piece))
    return out


def scatter(pieces, edges, places, heights):
    total = None
    for i in range(SIDE):
        total = add(total, scatter_side(pieces, edges, places, heights, i))
    return parts_joined(total, len(heights))


def rim_heights(edge_count, rim):
    count = edge_count // LANES
    return [*range(rim), *range(count - rim, count)], list(range(rim, count - rim))


def corrections(from_prior, from_above, order, inverse):
    lower = [pick_wide(from_prior, index) for index in order]
    return lower + [pick_wide(from_above, index) for index in inverse]


def corrected(own, delta):
    rim = len(delta) // 2
    lower = [a + b for a, b in zip(own[:rim], delta[:rim])]
    upper = [a + b for a, b in zip(own[len(own) - rim :], delta[rim:])]
    return lower + own[rim : len(own) - rim] + upper


def squares(chunks, rim, has_prior):
    total = None
    for c, chunk in enumerate(chunks):
        term = chunk * chunk
        if c < rim:
            term = term * (1.0 - has_prior)
        total = term if total is None else total + term
    return total


def start_copies(routes, arrived):
    copies = [
        pltpu.make_async_copy(here, there, arrived.at[n])
        for n, (here, there) in enumerate(routes)
    ]
    for copy in copies:
        copy.start()
    return copies


def stacked_chunk(source, at):
    piece = [source[g, :, at : at + LANES] for g in range(source.shape[0])]
    return jnp.concatenate(piece + piece, axis=0)


def rims_stage(source_in, order_in, across_ref, beside_ref, source, order_ref, order, arrived):
    for copy in start_copies(((source_in, source), (order_in, order)), arrived):
        copy.wait()
    rows, rim = order_ref.shape
    first = row_ids(rows) < rows // 2
    order_ref[...] = spread(order[...], rows)
    numbers = [x.astype(jnp.float32) for x in cut(order_ref)]
    lower = [stacked_chunk(source, c) for c in range(0, rim, LANES)]
    start = source.shape[-1] - rim
    upper = [stacked_chunk(source, start + c) for c in range(0, rim, LANES)]
    lower = [jnp.where(first, x, o) for x, o in zip(lower, numbers)]
    upper = [jnp.where(first, x, 1.0) for x in upper]
    put_rims(across_ref, beside_ref, lower, upper)


def table_stage(
    angular_in,
    stiffness_in,
    mass_in,
    sigma_in,
    live_in,
    edges_in,
    forward_in,
    source,
    places_ref,
    blocks_ref,
    scale_ref,
    picks_ref,
    stacked_ref,
    rates,
    mass,
    sigma,
    live,
    edges,
    forward_ref,
    angular,
    stiffness,
    arrived,
):
    copies = start_copies(
        (
            (edges_in, edges),
            (angular_in, angular),
            (sigma_in, sigma),
            (live_in, live),
            (stiffness_in, stiffness),
            (mass_in, mass),
            (forward_in, forward_ref),
        ),
        arrived,
    )
    copies[0].wait()
    numbers = row_ids(LANES)
    rows = edges.shape[1]

    def body(i, carry):
        for s in range(rows):
            lanes = spread(edges[i, s : s + 1, :] & (LANES - 1), LANES)
            column = pl.ds(pl.multiple_of((i * rows + s) * LANES, LANES), LANES)
            places_ref[:, column] = jnp.where(lanes == numbers, 1.0, 0.0).astype(jnp.bfloat16)
        return carry

    lax.fori_loop(0, SIDE, body, 0)
    count = source.shape[-1]
    put_chunks(stacked_ref, [stacked_chunk(source, c) for c in range(0, count, LANES)])
    put_picks(picks_ref, stacked_ref, edges, source.shape[0])
    for copy in copies[1:]:
        copy.wait()
    for f in range(angular.shape[0]):
        rates[f] = jnp.full(rates.shape[1:], angular[f], jnp.float32)
    alive = live[...].astype(jnp.float32)
    weight = sigma[...]
    freqs = rates.shape[0]
    peak = None
    for i in range(SIDE):
        for f in range(freqs):
            entry = (SIDE + 1) * i
            size = stiffness[entry] + rates[f] * weight * mass[entry]
            peak = size if peak is None else jnp.maximum(peak, size)
    peak = jnp.max(peak * alive, axis=1, keepdims=True)
    scale = jnp.broadcast_to(jnp.max(peak, axis=0, keepdims=True), scale_ref.shape)
    scale_ref[...] = scale
    alive = alive / scale[:1, :1]
    for entry in range(SIDE * SIDE):
        stiff = stiffness[entry] * alive
        heavy = mass[entry] * (weight * alive)
        for f in range(freqs):
            blocks_ref[f * SIDE * SIDE + entry] = stiff + rates[f] * heavy


def put_picks(picks_ref, field, edges, groups):
    for g in range(groups):
        for j, value in enumerate(picks_of(group_rows(field, g), edges)):
            picks_ref[g * SIDE + j] = value


def pick_rims(rows, index, edge_count):
    rim = len(rows) // 2
    start = edge_count - rim * LANES
    lower = pick_wide([spread(row, index.shape[0]) for row in rows[:rim]], index)
    upper = pick_wide([spread(row, index.shape[0]) for row in rows[rim:]], index - start)
    lower = jnp.where(index < rim * LANES, lower, 0.0)
    return lower + jnp.where(index >= start, upper, 0.0)


def corrected_picks(delta_ref, own_picks, edges, edge_count):
    out = []
    for g in range(delta_ref.shape[0] // 2):
        delta = group_rows(delta_ref, g)
        out.append(
            [
                own_picks[g * SIDE + j] + pick_rims(delta, edges[j], edge_count)
                for j in range(SIDE)
            ]
        )
    return out


def products(blocks, picked, polars, i):
    out = []
    for g, mine in enumerate(picked):
        base = (g // polars) * SIDE * SIDE + SIDE * i
        out.append(weighted_sum([blocks[base + j] for j in range(SIDE)], mine))
    return out


def rows_of_forms(forms, rows):
    out = jnp.zeros((rows, LANES), jnp.float32)
    for g, form in enumerate(forms):
        row = jnp.sum(form, axis=0, keepdims=True)
        out = jnp.where(row_ids(rows) == g, spread(row, rows), out)
    return out


def invert(above, groups, rows):
    above_order = jnp.concatenate([x[groups : groups + 1] for x in above], axis=1)
    rim = above_order.shape[1]
    slot = lax.broadcasted_iota(jnp.int32, (rim, rim), 0).astype(jnp.float32)
    match = jnp.where(spread(above_order, rim) == slot, 1.0, 0.0).astype(jnp.bfloat16)
    numbers = lax.broadcasted_iota(jnp.int32, (2 * rows, rim), 1).astype(jnp.bfloat16)
    inverse = lax.dot_general(
        numbers, match, (((1,), (1,)), ((), ())), preferred_element_type=jnp.float32
    )
    return inverse[:rows].astype(jnp.int32)


def rescaled(block, inverse_scale, step):
    ratio = swap_halves(block) * inverse_scale
    for _ in range(step):
        block = block * ratio
    return doubled(block)


def front_stage(
    polars,
    step,
    edge_count,
    order_ref,
    across_in,
    beside_in,
    scale_in,
    own_picks,
    blocks,
    edges,
    places,
    *rest,
):
    if step == 0:
        inverse_ref, *rest = rest
    else:
        inverse_in, *rest = rest
    delta_ref, picks_ref, pieces, forms_ref, rims_ref, across_ref, beside_ref = rest
    rows = delta_ref.shape[0]
    groups = rows // 2
    first = row_ids(rows) < groups
    scale = scale_in[...]
    prior, above = take_rims(across_in, beside_in)
    if step == 0:
        inverse_ref[...] = invert(above, groups, rows)
        inverse = cut(inverse_ref)
        prior, above = [doubled(x) for x in prior], [doubled(x) for x in above]
    else:
        inverse = cut(inverse_in)
        inverse_scale = 1.0 / scale
        prior = [rescaled(x, inverse_scale, step) for x in prior]
        above = [rescaled(x, inverse_scale, step) for x in above]
    put_chunks(delta_ref, corrections(prior, above, cut(order_ref), inverse))

    picked = corrected_picks(delta_ref, own_picks, edges, edge_count)
    for g in range(groups):
        for j in range(SIDE):
            picks_ref[g * SIDE + j] = picked[g][j]
    rim = len(prior)
    heights = rim_heights(edge_count, rim)[0]
    tall = edges.shape[1]
    forms, total = [None] * groups, None
    for i in range(SIDE):
        for g, value in enumerate(products(blocks, picked, polars, i)):
            forms[g] = add(forms[g], picked[g][i] * value)
            coarse = value.astype(jnp.bfloat16).astype(jnp.float32)
            for part, piece in enumerate((coarse, value - coarse)):
                at = ((part * groups + g) * SIDE + i) * tall
                pieces[at : at + tall, :] = piece
        total = add(total, scatter_side(pieces, edges, places, heights, i))
    forms_ref[...] = rows_of_forms(forms, rows)
    chunks = parts_joined(total, len(heights))
    put_chunks(rims_ref, chunks)
    put_rims(
        across_ref,
        beside_ref,
        [jnp.where(first, x, scale) for x in chunks[:rim]],
        [jnp.where(first, x, scale) for x in chunks[rim:]],
    )


def inner_products(step, sums, own, delta, forms, across_in, beside_in):
    rows = sums.shape[0]
    first = row_ids(rows) < rows // 2
    prior, _ = take_rims(across_in, beside_in)
    has_prior = jnp.where(first, swap_halves(prior[0]), prior[0])
    has_prior = spread(jnp.where(has_prior[:1, :1] > 0.0, 1.0, 0.0), rows)
    field = corrected(own, delta)
    sums = put_lane(sums, 2 * step, lane_sum(squares(field, len(delta) // 2, has_prior)))
    return put_lane(sums, 2 * step + 1, lane_sum(forms))


def back_stage(
    polars,
    step,
    own,
    delta,
    forms,
    across_in,
    beside_in,
    sums_in,
    picks,
    pieces,
    rims,
    edges,
    places,
    *rest,
):
    if step == 0:
        rates, forward, mass, live, heavy, terms_ref, sums_ref, image_ref, picks_ref = rest
    else:
        heavy, terms_ref, sums_ref, image_ref, picks_ref = rest
    rows, edge_count = own.shape
    groups = rows // 2
    rim = rims.shape[-1] // LANES // 2
    outer = cut(rims)
    inner = scatter(pieces, edges, places, rim_heights(edge_count, rim)[1])
    put_chunks(image_ref, outer[:rim] + inner + outer[rim:])
    put_picks(picks_ref, image_ref, edges, groups)
    if step == 0:
        dead = -live[...].astype(jnp.float32)
        for g in range(groups):
            row = [forward[g, :, c : c + LANES] for c in range(0, edge_count, LANES)]
            values = times_block(mass, 0, picks_of(row, edges))
            factor = dead * rates[g // polars]
            for i in range(SIDE):
                heavy[g * SIDE + i] = factor * values[i]
    for g in range(groups):
        side = range(g * SIDE, (g + 1) * SIDE)
        terms_ref[g] = weighted_sum([picks[i] for i in side], [heavy[i] for i in side])
    sums_ref[...] = inner_products(
        step, sums_in[...], cut(own), cut(delta), forms[...], across_in, beside_in
    )


def last_stage(
    polars,
    step,
    own,
    order_ref,
    inverse_in,
    across_in,
    beside_in,
    scale_in,
    sums_in,
    own_picks,
    blocks,
    edges,
    heavy,
    terms_ref,
    sums_ref,
    delta_ref,
):
    rows, edge_count = own.shape
    first = row_ids(rows) < rows // 2
    scale = scale_in[...]
    inverse_scale = 1.0 / scale
    prior, above = take_rims(across_in, beside_in)
    prior = [rescaled(x, inverse_scale, step) for x in prior]
    above = [rescaled(x, inverse_scale, step) for x in above]
    put_chunks(delta_ref, corrections(prior, above, cut(order_ref), cut(inverse_in)))

    picked = corrected_picks(delta_ref, own_picks, edges, edge_count)
    forms = [None] * len(picked)
    for i in range(SIDE):
        for g, value in enumerate(products(blocks, picked, polars, i)):
            forms[g] = add(forms[g], picked[g][i] * value)
    for g, mine in enumerate(picked):
        terms_ref[g] = weighted_sum(mine, [heavy[g * SIDE + i] for i in range(SIDE)])
    forms = rows_of_forms(forms, rows)
    sums = inner_products(
        step, sums_in[...], cut(own), cut(delta_ref), forms, across_in, beside_in
    )
    sums_ref[...] = jnp.where(first, sums, scale)


def combine_stage(everyone, sums_in, terms0, terms1, terms2, out_ref):
    rows = sums_in.shape[0]
    groups = rows // 2
    first = row_ids(rows) < groups

    def scale_of(block):
        return jnp.where(first, swap_halves(block), block)

    parts = [everyone[q] for q in range(everyone.shape[0])]
    scales = [scale_of(block) for block in parts]
    top = functools.reduce(jnp.maximum, scales)
    lanes = lane_ids(rows)
    inverse_top = 1.0 / top
    total = None
    for block, scale in zip(parts, scales):
        ratio = scale * inverse_top
        power = jnp.ones_like(ratio)
        factor = jnp.ones_like(ratio)
        for k in range(1, 6):
            power = power * ratio
            factor = jnp.where(lanes == k, power, factor)
        term = block * factor
        total = term if total is None else total + term
    m = [jnp.broadcast_to(total[:, k : k + 1], (rows, LANES)) for k in range(6)]
    l1 = m[2] / m[1]
    l2 = m[3] / m[1]
    d2 = m[3] - l1 * m[2]
    cross = m[4] - l2 * m[2]
    l3 = cross / d2
    d3 = m[5] - l2 * m[3] - l3 * cross
    y1 = m[1] - l1 * m[0]
    y2 = m[2] - l2 * m[0] - l3 * y1
    c2 = y2 / d3
    c1 = y1 / d2 - l3 * c2
    c0 = m[0] / m[1] - l1 * c1 - l2 * c2
    mine = scale_of(sums_in[...]) * inverse_top
    c0 = c0 * inverse_top
    c1 = c1 * mine * inverse_top
    c2 = c2 * mine * mine * inverse_top
    out = None
    for terms, c in ((terms0, c0), (terms1, c1), (terms2, c2)):
        for g in range(groups):
            one = terms[g] * spread(c[g : g + 1], out_ref.shape[0])
            out = one if out is None else out + one
    out_ref[...] = out


def pinned(*arguments):
    return [pltpu.with_memory_space_constraint(x, pltpu.HBM) for x in arguments]


def call(kernel, arguments, outs, scratch=(), space=VMEM, cost=0):
    return pl.pallas_call(
        kernel,
        out_shape=outs,
        in_specs=space if isinstance(space, list) else [space] * len(arguments),
        out_specs=jax.tree.map(lambda _: VMEM, outs),
        scratch_shapes=list(scratch),
        cost_estimate=pl.CostEstimate(flops=cost, bytes_accessed=cost, transcendentals=0),
        compiler_params=pltpu.CompilerParams(vmem_limit_bytes=16 * 1024 * 1024),
    )(*arguments)


def swap_across(block):
    size = lax.axis_size("dom")
    route = []
    for low in range(1, size, 2):
        high = (low + 1) % size
        route += [(low, high), (high, low)]
    return lax.ppermute(block, "dom", route)


def swap_beside(block):
    return lax.ppermute(block, "dom", [(i, i ^ 1) for i in range(lax.axis_size("dom"))])


def gather_all(block, axis):
    size = lax.axis_size(axis)
    copies = jnp.broadcast_to(block[None], (size, *block.shape))
    return lax.all_to_all(copies, axis, 0, 0)


def sum_over(block, axis):
    size = lax.axis_size(axis)
    if size & (size - 1):
        return jnp.sum(gather_all(block, axis), axis=0)
    step = size // 2
    while step > 0:
        block = block + lax.ppermute(block, axis, [(i, i ^ step) for i in range(size)])
        step //= 2
    return block


def local(
    angular,
    stiffness,
    mass_matrix,
    conductivity,
    element_edges,
    live_slots,
    adjoint_source,
    forward_field,
    neighbour_map,
):
    freqs = angular.shape[0]
    polars = adjoint_source.shape[1]
    groups = freqs * polars
    rows = 2 * groups
    edge_count = adjoint_source.shape[-1]
    rim = neighbour_map.shape[-1]
    slots = element_edges.shape[-1]
    tall = slots // LANES
    stiff = stiffness.reshape(SIDE * SIDE, tall, LANES)
    mass = mass_matrix.reshape(SIDE * SIDE, tall, LANES)
    edges = element_edges.reshape(SIDE, tall, LANES)
    sigma = conductivity.reshape(tall, LANES)
    live = live_slots.reshape(tall, LANES)
    source = adjoint_source.reshape(groups, 1, edge_count)
    forward = forward_field.reshape(groups, 1, edge_count)

    def shape(*dims, kind=jnp.float32):
        return jax.ShapeDtypeStruct(dims, kind)

    field_shape, rim_shape = shape(rows, edge_count), shape(rows, rim)
    sums_shape, terms_shape = shape(rows, LANES), shape(groups, tall, LANES)
    picks_shape = shape(groups * SIDE, tall, LANES)

    across, beside, source, order = call(
        rims_stage,
        pinned(source, neighbour_map),
        [rim_shape, rim_shape, shape(*source.shape), shape(rows, rim, kind=jnp.int32)],
        (
            pltpu.VMEM(neighbour_map.shape, neighbour_map.dtype),
            pltpu.SemaphoreType.DMA((2,)),
        ),
        space=HBM,
    )
    across, beside = swap_across(across), swap_beside(beside)
    kept = [jax.ShapeDtypeStruct(x.shape, x.dtype) for x in (mass, sigma, live, edges, forward)]
    places, blocks, scale, picks, own, rates, mass, sigma, live, edges, forward = call(
        table_stage,
        [*pinned(angular, stiff, mass, sigma, live, edges, forward), source],
        [
            shape(LANES, SIDE * slots, kind=jnp.bfloat16),
            shape(freqs * SIDE * SIDE, tall, LANES),
            sums_shape,
            picks_shape,
            field_shape,
            shape(freqs, tall, LANES),
            *kept,
        ],
        (
            pltpu.SMEM(angular.shape, angular.dtype),
            pltpu.VMEM(stiff.shape, stiff.dtype),
            pltpu.SemaphoreType.DMA((7,)),
        ),
        space=[HBM] * 7 + [VMEM],
        cost=4_000_000,
    )
    front_shapes = [
        shape(rows, 2 * rim),
        picks_shape,
        shape(rows * SIDE * tall, LANES),
        sums_shape,
        shape(rows, 2 * rim),
        rim_shape,
        rim_shape,
    ]
    back_shapes = [terms_shape, sums_shape, field_shape, picks_shape]
    sums, terms = jnp.zeros((rows, LANES), jnp.float32), []
    for step in range(2):
        arrived = (across, beside)
        given = (order, *arrived, scale, picks, blocks, edges, places)
        front = functools.partial(front_stage, polars, step, edge_count)
        if step == 0:
            inverse, *outs = call(
                front, given, [shape(rows, rim, kind=jnp.int32), *front_shapes]
            )
        else:
            outs = call(front, (*given, inverse), front_shapes)
        delta, picks, pieces, forms, rims, across, beside = outs
        across, beside = swap_across(across), swap_beside(beside)
        given = (own, delta, forms, *arrived, sums, picks, pieces, rims, edges, places)
        back = functools.partial(back_stage, polars, step)
        if step == 0:
            heavy, term, sums, own, picks = call(
                back,
                (*given, rates, forward, mass, live),
                [picks_shape, *back_shapes],
                cost=4_000_000,
            )
        else:
            term, sums, own, picks = call(back, (*given, heavy), back_shapes, cost=4_000_000)
        terms.append(term)
    term, sums = call(
        functools.partial(last_stage, polars, 2),
        (own, order, inverse, across, beside, scale, sums, picks, blocks, edges, heavy),
        [terms_shape, sums_shape],
        (pltpu.VMEM((rows, 2 * rim), jnp.float32),),
    )
    terms.append(term)
    term = call(
        combine_stage,
        (gather_all(sums, "dom"), sums, *terms),
        shape(tall, LANES),
    )
    gradient = sum_over(term, "freq").reshape(1, slots)
    updated = sigma.reshape(1, slots) * jnp.exp(-0.5 * jnp.tanh(gradient))
    return gradient, updated


def solution(mesh):
    return jax.shard_map(
        local,
        mesh=mesh,
        in_specs=(
            P("freq"),
            P("dom", None, None),
            P("dom", None, None),
            P("dom", None),
            P("dom", None, None),
            P("dom", None),
            P("freq", None, "dom", None),
            P("freq", None, "dom", None),
            P("dom", None),
        ),
        out_specs=(P("dom", None), P("dom", None)),
        check_vma=False,
    )
```

```python
import functools

import jax
import jax.numpy as jnp
from jax import lax
from jax.experimental import pallas as pl
from jax.experimental.pallas import tpu as pltpu
from jax.sharding import PartitionSpec as P

LANES = 128
SUBLANES = 8
SIDE = 6
VMEM = pl.BlockSpec(memory_space=pltpu.VMEM)
HBM = pl.BlockSpec(memory_space=pltpu.HBM)

PICK_LANES = lax.GatherDimensionNumbers(
    offset_dims=(),
    collapsed_slice_dims=(1,),
    start_index_map=(1,),
    operand_batching_dims=(0,),
    start_indices_batching_dims=(0,),
)


def pick_lanes(block, lanes):
    return lax.gather(
        block,
        lanes[..., None],
        PICK_LANES,
        (1, 1),
        mode=lax.GatherScatterMode.PROMISE_IN_BOUNDS,
    )


def pick_wide(chunks, index):
    lanes = index & (LANES - 1)
    high = index >> 7
    level = [pick_lanes(chunk, lanes) for chunk in chunks]
    bit = 0
    while len(level) > 1:
        odd = (high >> bit) & 1 == 1
        level = [
            jnp.where(odd, level[t + 1], level[t]) if t + 1 < len(level) else level[t]
            for t in range(0, len(level), 2)
        ]
        bit += 1
    return level[0]


def row_ids(rows):
    return lax.broadcasted_iota(jnp.int32, (rows, LANES), 0)


def lane_ids(rows):
    return lax.broadcasted_iota(jnp.int32, (rows, LANES), 1)


def spread(row, rows):
    return jnp.broadcast_to(row, (rows, row.shape[-1]))


def cut(ref):
    return [ref[:, c : c + LANES] for c in range(0, ref.shape[-1], LANES)]


def swap_halves(block):
    return pltpu.roll(block, block.shape[0] // 2, 0)


def doubled(block):
    half = block.shape[0] // 2
    return jnp.where(row_ids(2 * half) < half, block, swap_halves(block))


def lane_sum(block):
    return jnp.broadcast_to(jnp.sum(block, axis=1, keepdims=True), block.shape)


def put_lane(block, lane, value):
    return jnp.where(lane_ids(block.shape[0]) == lane, value, block)


def put_chunks(ref, chunks):
    for c, chunk in enumerate(chunks):
        ref[:, c * LANES : (c + 1) * LANES] = chunk


def is_even():
    return lax.rem(lax.axis_index("dom"), 2) == 0


def put_rims(across_ref, beside_ref, lower, upper):
    even = is_even()
    for c, (low, high) in enumerate(zip(lower, upper)):
        here = slice(c * LANES, (c + 1) * LANES)
        across_ref[:, here] = jnp.where(even, low, high)
        beside_ref[:, here] = jnp.where(even, high, low)


def take_rims(across_ref, beside_ref):
    even = is_even()
    device = lax.axis_index("dom")
    outermost = (device == 0) | (device == lax.axis_size("dom") - 1)
    pairs = [
        (jnp.where(outermost, 0.0, a), b) for a, b in zip(cut(across_ref), cut(beside_ref))
    ]
    prior = [jnp.where(even, a, b) for a, b in pairs]
    above = [jnp.where(even, b, a) for a, b in pairs]
    return prior, above


def picks_of(rows_of_group, edges):
    chunks = [spread(row, edges.shape[1]) for row in rows_of_group]
    return [pick_wide(chunks, edges[j]) for j in range(SIDE)]


def group_rows(ref, g):
    return [ref[g : g + 1, c : c + LANES] for c in range(0, ref.shape[-1], LANES)]


def times_block(entries, base, picked):
    out = []
    for i in range(SIDE):
        total = None
        for j in range(SIDE):
            one = entries[base + SIDE * i + j] * picked[j]
            total = one if total is None else total + one
        out.append(total)
    return out


def weighted_sum(left, right):
    total = None
    for a, b in zip(left, right):
        total = a * b if total is None else total + a * b
    return total


def scatter_side(pieces, edges, places, heights, i):
    depth = SIDE * edges.shape[1]
    rows = pieces.shape[0] // depth
    slots = edges.shape[1] * LANES
    columns = []
    for s in range(edges.shape[1]):
        both = pieces[pl.ds(i * edges.shape[1] + s, rows, stride=depth), :]
        high = spread(edges[i, s : s + 1, :] >> 7, rows)
        stacked = [jnp.where(high == h, both, 0.0) for h in heights]
        columns.append(jnp.concatenate(stacked, axis=0).astype(jnp.bfloat16))
    return lax.dot_general(
        jnp.concatenate(columns, axis=1),
        places[:, i * slots : (i + 1) * slots],
        (((1,), (1,)), ((), ())),
        preferred_element_type=jnp.float32,
    )


def add(total, part):
    return part if total is None else total + part


def parts_joined(total, count):
    rows = total.shape[0] // count
    out = []
    for n in range(count):
        piece = total[rows * n : rows * (n + 1)]
        out.append(piece + swap_halves(piece))
    return out


def scatter(pieces, edges, places, heights):
    total = None
    for i in range(SIDE):
        total = add(total, scatter_side(pieces, edges, places, heights, i))
    return parts_joined(total, len(heights))


def rim_heights(edge_count, rim):
    count = edge_count // LANES
    return [*range(rim), *range(count - rim, count)], list(range(rim, count - rim))


def corrections(from_prior, from_above, order, inverse):
    lower = [pick_wide(from_prior, index) for index in order]
    return lower + [pick_wide(from_above, index) for index in inverse]


def corrected(own, delta):
    rim = len(delta) // 2
    lower = [a + b for a, b in zip(own[:rim], delta[:rim])]
    upper = [a + b for a, b in zip(own[len(own) - rim :], delta[rim:])]
    return lower + own[rim : len(own) - rim] + upper


def squares(chunks, rim, has_prior):
    total = None
    for c, chunk in enumerate(chunks):
        term = chunk * chunk
        if c < rim:
            term = term * (1.0 - has_prior)
        total = term if total is None else total + term
    return total


def start_copies(routes, arrived):
    copies = [
        pltpu.make_async_copy(here, there, arrived.at[n])
        for n, (here, there) in enumerate(routes)
    ]
    for copy in copies:
        copy.start()
    return copies


def stacked_chunk(source, at):
    piece = [source[g, :, at : at + LANES] for g in range(source.shape[0])]
    return jnp.concatenate(piece + piece, axis=0)


def rims_stage(source_in, order_in, across_ref, beside_ref, source, order_ref, order, arrived):
    for copy in start_copies(((source_in, source), (order_in, order)), arrived):
        copy.wait()
    rows, rim = order_ref.shape
    first = row_ids(rows) < rows // 2
    order_ref[...] = spread(order[...], rows)
    numbers = [x.astype(jnp.float32) for x in cut(order_ref)]
    lower = [stacked_chunk(source, c) for c in range(0, rim, LANES)]
    start = source.shape[-1] - rim
    upper = [stacked_chunk(source, start + c) for c in range(0, rim, LANES)]
    lower = [jnp.where(first, x, o) for x, o in zip(lower, numbers)]
    upper = [jnp.where(first, x, 1.0) for x in upper]
    put_rims(across_ref, beside_ref, lower, upper)


def table_stage(
    angular_in,
    stiffness_in,
    mass_in,
    sigma_in,
    live_in,
    edges_in,
    forward_in,
    source,
    places_ref,
    blocks_ref,
    scale_ref,
    picks_ref,
    stacked_ref,
    rates,
    mass,
    sigma,
    live,
    edges,
    forward_ref,
    angular,
    stiffness,
    arrived,
):
    copies = start_copies(
        (
            (edges_in, edges),
            (angular_in, angular),
            (sigma_in, sigma),
            (live_in, live),
            (stiffness_in, stiffness),
            (mass_in, mass),
            (forward_in, forward_ref),
        ),
        arrived,
    )
    copies[0].wait()
    numbers = row_ids(LANES)
    rows = edges.shape[1]

    def body(i, carry):
        for s in range(rows):
            lanes = spread(edges[i, s : s + 1, :] & (LANES - 1), LANES)
            column = pl.ds(pl.multiple_of((i * rows + s) * LANES, LANES), LANES)
            places_ref[:, column] = jnp.where(lanes == numbers, 1.0, 0.0).astype(jnp.bfloat16)
        return carry

    lax.fori_loop(0, SIDE, body, 0)
    count = source.shape[-1]
    put_chunks(stacked_ref, [stacked_chunk(source, c) for c in range(0, count, LANES)])
    put_picks(picks_ref, stacked_ref, edges, source.shape[0])
    for copy in copies[1:]:
        copy.wait()
    for f in range(angular.shape[0]):
        rates[f] = jnp.full(rates.shape[1:], angular[f], jnp.float32)
    alive = live[...].astype(jnp.float32)
    weight = sigma[...]
    freqs = rates.shape[0]
    peak = None
    for i in range(SIDE):
        for f in range(freqs):
            entry = (SIDE + 1) * i
            size = stiffness[entry] + rates[f] * weight * mass[entry]
            peak = size if peak is None else jnp.maximum(peak, size)
    peak = jnp.max(peak * alive, axis=1, keepdims=True)
    scale = jnp.broadcast_to(jnp.max(peak, axis=0, keepdims=True), scale_ref.shape)
    scale_ref[...] = scale
    alive = alive / scale[:1, :1]
    for entry in range(SIDE * SIDE):
        stiff = stiffness[entry] * alive
        heavy = mass[entry] * (weight * alive)
        for f in range(freqs):
            blocks_ref[f * SIDE * SIDE + entry] = stiff + rates[f] * heavy


def put_picks(picks_ref, field, edges, groups):
    for g in range(groups):
        for j, value in enumerate(picks_of(group_rows(field, g), edges)):
            picks_ref[g * SIDE + j] = value


def pick_rims(rows, index, edge_count):
    rim = len(rows) // 2
    start = edge_count - rim * LANES
    lower = pick_wide([spread(row, index.shape[0]) for row in rows[:rim]], index)
    upper = pick_wide([spread(row, index.shape[0]) for row in rows[rim:]], index - start)
    lower = jnp.where(index < rim * LANES, lower, 0.0)
    return lower + jnp.where(index >= start, upper, 0.0)


def corrected_picks(delta_ref, own_picks, edges, edge_count):
    out = []
    for g in range(delta_ref.shape[0] // 2):
        delta = group_rows(delta_ref, g)
        out.append(
            [
                own_picks[g * SIDE + j] + pick_rims(delta, edges[j], edge_count)
                for j in range(SIDE)
            ]
        )
    return out


def products(blocks, picked, polars, i):
    out = []
    for g, mine in enumerate(picked):
        base = (g // polars) * SIDE * SIDE + SIDE * i
        out.append(weighted_sum([blocks[base + j] for j in range(SIDE)], mine))
    return out


def rows_of_forms(forms, rows):
    out = jnp.zeros((rows, LANES), jnp.float32)
    for g, form in enumerate(forms):
        row = jnp.sum(form, axis=0, keepdims=True)
        out = jnp.where(row_ids(rows) == g, spread(row, rows), out)
    return out


def invert(above, groups, rows):
    above_order = jnp.concatenate([x[groups : groups + 1] for x in above], axis=1)
    rim = above_order.shape[1]
    slot = lax.broadcasted_iota(jnp.int32, (rim, rim), 0).astype(jnp.float32)
    match = jnp.where(spread(above_order, rim) == slot, 1.0, 0.0).astype(jnp.bfloat16)
    numbers = lax.broadcasted_iota(jnp.int32, (2 * rows, rim), 1).astype(jnp.bfloat16)
    inverse = lax.dot_general(
        numbers, match, (((1,), (1,)), ((), ())), preferred_element_type=jnp.float32
    )
    return inverse[:rows].astype(jnp.int32)


def rescaled(block, inverse_scale, step):
    ratio = swap_halves(block) * inverse_scale
    for _ in range(step):
        block = block * ratio
    return doubled(block)


def front_stage(
    polars,
    step,
    edge_count,
    order_ref,
    across_in,
    beside_in,
    scale_in,
    own_picks,
    blocks,
    edges,
    places,
    *rest,
):
    if step == 0:
        inverse_ref, *rest = rest
    else:
        inverse_in, *rest = rest
    delta_ref, picks_ref, pieces, forms_ref, rims_ref, across_ref, beside_ref = rest
    rows = delta_ref.shape[0]
    groups = rows // 2
    first = row_ids(rows) < groups
    scale = scale_in[...]
    prior, above = take_rims(across_in, beside_in)
    if step == 0:
        inverse_ref[...] = invert(above, groups, rows)
        inverse = cut(inverse_ref)
        prior, above = [doubled(x) for x in prior], [doubled(x) for x in above]
    else:
        inverse = cut(inverse_in)
        inverse_scale = 1.0 / scale
        prior = [rescaled(x, inverse_scale, step) for x in prior]
        above = [rescaled(x, inverse_scale, step) for x in above]
    put_chunks(delta_ref, corrections(prior, above, cut(order_ref), inverse))

    picked = corrected_picks(delta_ref, own_picks, edges, edge_count)
    for g in range(groups):
        for j in range(SIDE):
            picks_ref[g * SIDE + j] = picked[g][j]
    rim = len(prior)
    heights = rim_heights(edge_count, rim)[0]
    tall = edges.shape[1]
    forms, total = [None] * groups, None
    for i in range(SIDE):
        for g, value in enumerate(products(blocks, picked, polars, i)):
            forms[g] = add(forms[g], picked[g][i] * value)
            coarse = value.astype(jnp.bfloat16).astype(jnp.float32)
            for part, piece in enumerate((coarse, value - coarse)):
                at = ((part * groups + g) * SIDE + i) * tall
                pieces[at : at + tall, :] = piece
        total = add(total, scatter_side(pieces, edges, places, heights, i))
    forms_ref[...] = rows_of_forms(forms, rows)
    chunks = parts_joined(total, len(heights))
    put_chunks(rims_ref, chunks)
    put_rims(
        across_ref,
        beside_ref,
        [jnp.where(first, x, scale) for x in chunks[:rim]],
        [jnp.where(first, x, scale) for x in chunks[rim:]],
    )


def inner_products(step, sums, own, delta, forms, across_in, beside_in):
    rows = sums.shape[0]
    first = row_ids(rows) < rows // 2
    prior, _ = take_rims(across_in, beside_in)
    has_prior = jnp.where(first, swap_halves(prior[0]), prior[0])
    has_prior = spread(jnp.where(has_prior[:1, :1] > 0.0, 1.0, 0.0), rows)
    field = corrected(own, delta)
    sums = put_lane(sums, 2 * step, lane_sum(squares(field, len(delta) // 2, has_prior)))
    return put_lane(sums, 2 * step + 1, lane_sum(forms))


def back_stage(
    polars,
    step,
    own,
    delta,
    forms,
    across_in,
    beside_in,
    sums_in,
    picks,
    pieces,
    rims,
    edges,
    places,
    *rest,
):
    if step == 0:
        rates, forward, mass, live, heavy, terms_ref, sums_ref, image_ref, picks_ref = rest
    else:
        heavy, terms_ref, sums_ref, image_ref, picks_ref = rest
    rows, edge_count = own.shape
    groups = rows // 2
    rim = rims.shape[-1] // LANES // 2
    outer = cut(rims)
    inner = scatter(pieces, edges, places, rim_heights(edge_count, rim)[1])
    put_chunks(image_ref, outer[:rim] + inner + outer[rim:])
    put_picks(picks_ref, image_ref, edges, groups)
    if step == 0:
        dead = -live[...].astype(jnp.float32)
        for g in range(groups):
            row = [forward[g, :, c : c + LANES] for c in range(0, edge_count, LANES)]
            values = times_block(mass, 0, picks_of(row, edges))
            factor = dead * rates[g // polars]
            for i in range(SIDE):
                heavy[g * SIDE + i] = factor * values[i]
    for g in range(groups):
        side = range(g * SIDE, (g + 1) * SIDE)
        terms_ref[g] = weighted_sum([picks[i] for i in side], [heavy[i] for i in side])
    sums_ref[...] = inner_products(
        step, sums_in[...], cut(own), cut(delta), forms[...], across_in, beside_in
    )


def last_stage(
    polars,
    step,
    own,
    order_ref,
    inverse_in,
    across_in,
    beside_in,
    scale_in,
    sums_in,
    own_picks,
    blocks,
    edges,
    heavy,
    terms_ref,
    sums_ref,
    delta_ref,
):
    rows, edge_count = own.shape
    first = row_ids(rows) < rows // 2
    scale = scale_in[...]
    inverse_scale = 1.0 / scale
    prior, above = take_rims(across_in, beside_in)
    prior = [rescaled(x, inverse_scale, step) for x in prior]
    above = [rescaled(x, inverse_scale, step) for x in above]
    put_chunks(delta_ref, corrections(prior, above, cut(order_ref), cut(inverse_in)))

    picked = corrected_picks(delta_ref, own_picks, edges, edge_count)
    forms = [None] * len(picked)
    for i in range(SIDE):
        for g, value in enumerate(products(blocks, picked, polars, i)):
            forms[g] = add(forms[g], picked[g][i] * value)
    for g, mine in enumerate(picked):
        terms_ref[g] = weighted_sum(mine, [heavy[g * SIDE + i] for i in range(SIDE)])
    forms = rows_of_forms(forms, rows)
    sums = inner_products(
        step, sums_in[...], cut(own), cut(delta_ref), forms, across_in, beside_in
    )
    sums_ref[...] = jnp.where(first, sums, scale)


def combine_stage(count, *refs):
    everyone, (sums_in, terms0, terms1, terms2, out_ref) = refs[:count], refs[count:]
    rows = sums_in.shape[0]
    groups = rows // 2
    first = row_ids(rows) < groups

    def scale_of(block):
        return jnp.where(first, swap_halves(block), block)

    parts = [
        ref[at : at + rows, :] for ref in everyone for at in range(0, ref.shape[0], rows)
    ]
    scales = [scale_of(block) for block in parts]
    top = functools.reduce(jnp.maximum, scales)
    lanes = lane_ids(rows)
    inverse_top = 1.0 / top
    total = None
    for block, scale in zip(parts, scales):
        ratio = scale * inverse_top
        power = jnp.ones_like(ratio)
        factor = jnp.ones_like(ratio)
        for k in range(1, 6):
            power = power * ratio
            factor = jnp.where(lanes == k, power, factor)
        term = block * factor
        total = term if total is None else total + term
    m = [jnp.broadcast_to(total[:, k : k + 1], (rows, LANES)) for k in range(6)]
    l1 = m[2] / m[1]
    l2 = m[3] / m[1]
    d2 = m[3] - l1 * m[2]
    cross = m[4] - l2 * m[2]
    l3 = cross / d2
    d3 = m[5] - l2 * m[3] - l3 * cross
    y1 = m[1] - l1 * m[0]
    y2 = m[2] - l2 * m[0] - l3 * y1
    c2 = y2 / d3
    c1 = y1 / d2 - l3 * c2
    c0 = m[0] / m[1] - l1 * c1 - l2 * c2
    mine = scale_of(sums_in[...]) * inverse_top
    c0 = c0 * inverse_top
    c1 = c1 * mine * inverse_top
    c2 = c2 * mine * mine * inverse_top
    out = None
    for terms, c in ((terms0, c0), (terms1, c1), (terms2, c2)):
        for g in range(groups):
            one = terms[g] * spread(c[g : g + 1], out_ref.shape[0])
            out = one if out is None else out + one
    out_ref[...] = out


def pinned(*arguments):
    return [pltpu.with_memory_space_constraint(x, pltpu.HBM) for x in arguments]


def call(kernel, arguments, outs, scratch=(), space=VMEM, cost=0):
    return pl.pallas_call(
        kernel,
        out_shape=outs,
        in_specs=space if isinstance(space, list) else [space] * len(arguments),
        out_specs=jax.tree.map(lambda _: VMEM, outs),
        scratch_shapes=list(scratch),
        cost_estimate=pl.CostEstimate(flops=cost, bytes_accessed=cost, transcendentals=0),
        compiler_params=pltpu.CompilerParams(vmem_limit_bytes=16 * 1024 * 1024),
    )(*arguments)


def swap_across(block):
    size = lax.axis_size("dom")
    route = [(0, 0), (size - 1, size - 1)]
    for low in range(1, size - 1, 2):
        route += [(low, low + 1), (low + 1, low)]
    return lax.ppermute(block, "dom", route)


def swap_beside(block):
    return lax.ppermute(block, "dom", [(i, i ^ 1) for i in range(lax.axis_size("dom"))])


def gather_all(block, axis):
    size = lax.axis_size(axis)
    copies = jnp.broadcast_to(block[None], (size, *block.shape))
    return lax.all_to_all(copies, axis, 0, 0)


def gather_sums(block):
    size = lax.axis_size("dom")
    if size > 8:
        return [gather_all(block, "dom").reshape(-1, block.shape[1])]
    pair = jnp.concatenate([block, swap_beside(block)], axis=0)
    return [pair] + [
        lax.ppermute(pair, "dom", [(i, i ^ step) for i in range(size)])
        for step in range(size - 2, 0, -2)
    ]


def sum_over(block, axis):
    size = lax.axis_size(axis)
    if size & (size - 1):
        return jnp.sum(gather_all(block, axis), axis=0)
    step = size // 2
    while step > 0:
        block = block + lax.ppermute(block, axis, [(i, i ^ step) for i in range(size)])
        step //= 2
    return block


def local(
    angular,
    stiffness,
    mass_matrix,
    conductivity,
    element_edges,
    live_slots,
    adjoint_source,
    forward_field,
    neighbour_map,
):
    freqs = angular.shape[0]
    polars = adjoint_source.shape[1]
    groups = freqs * polars
    rows = 2 * groups
    edge_count = adjoint_source.shape[-1]
    rim = neighbour_map.shape[-1]
    slots = element_edges.shape[-1]
    tall = slots // LANES
    stiff = stiffness.reshape(SIDE * SIDE, tall, LANES)
    mass = mass_matrix.reshape(SIDE * SIDE, tall, LANES)
    edges = element_edges.reshape(SIDE, tall, LANES)
    sigma = conductivity.reshape(tall, LANES)
    live = live_slots.reshape(tall, LANES)
    source = adjoint_source.reshape(groups, 1, edge_count)
    forward = forward_field.reshape(groups, 1, edge_count)

    def shape(*dims, kind=jnp.float32):
        return jax.ShapeDtypeStruct(dims, kind)

    field_shape, rim_shape = shape(rows, edge_count), shape(rows, rim)
    sums_shape, terms_shape = shape(rows, LANES), shape(groups, tall, LANES)
    picks_shape = shape(groups * SIDE, tall, LANES)

    across, beside, source, order = call(
        rims_stage,
        pinned(source, neighbour_map),
        [rim_shape, rim_shape, shape(*source.shape), shape(rows, rim, kind=jnp.int32)],
        (
            pltpu.VMEM(neighbour_map.shape, neighbour_map.dtype),
            pltpu.SemaphoreType.DMA((2,)),
        ),
        space=HBM,
    )
    across, beside = swap_across(across), swap_beside(beside)
    kept = [jax.ShapeDtypeStruct(x.shape, x.dtype) for x in (mass, sigma, live, edges, forward)]
    places, blocks, scale, picks, own, rates, mass, sigma, live, edges, forward = call(
        table_stage,
        [*pinned(angular, stiff, mass, sigma, live, edges, forward), source],
        [
            shape(LANES, SIDE * slots, kind=jnp.bfloat16),
            shape(freqs * SIDE * SIDE, tall, LANES),
            sums_shape,
            picks_shape,
            field_shape,
            shape(freqs, tall, LANES),
            *kept,
        ],
        (
            pltpu.SMEM(angular.shape, angular.dtype),
            pltpu.VMEM(stiff.shape, stiff.dtype),
            pltpu.SemaphoreType.DMA((7,)),
        ),
        space=[HBM] * 7 + [VMEM],
        cost=4_000_000,
    )
    front_shapes = [
        shape(rows, 2 * rim),
        picks_shape,
        shape(rows * SIDE * tall, LANES),
        sums_shape,
        shape(rows, 2 * rim),
        rim_shape,
        rim_shape,
    ]
    back_shapes = [terms_shape, sums_shape, field_shape, picks_shape]
    sums, terms = jnp.zeros((rows, LANES), jnp.float32), []
    for step in range(2):
        arrived = (across, beside)
        given = (order, *arrived, scale, picks, blocks, edges, places)
        front = functools.partial(front_stage, polars, step, edge_count)
        if step == 0:
            inverse, *outs = call(
                front, given, [shape(rows, rim, kind=jnp.int32), *front_shapes]
            )
        else:
            outs = call(front, (*given, inverse), front_shapes)
        delta, picks, pieces, forms, rims, across, beside = outs
        across, beside = swap_across(across), swap_beside(beside)
        given = (own, delta, forms, *arrived, sums, picks, pieces, rims, edges, places)
        back = functools.partial(back_stage, polars, step)
        if step == 0:
            heavy, term, sums, own, picks = call(
                back,
                (*given, rates, forward, mass, live),
                [picks_shape, *back_shapes],
                cost=4_000_000,
            )
        else:
            term, sums, own, picks = call(back, (*given, heavy), back_shapes, cost=4_000_000)
        terms.append(term)
    term, sums = call(
        functools.partial(last_stage, polars, 2),
        (own, order, inverse, across, beside, scale, sums, picks, blocks, edges, heavy),
        [terms_shape, sums_shape],
        (pltpu.VMEM((rows, 2 * rim), jnp.float32),),
    )
    terms.append(term)
    everyone = gather_sums(sums)
    term = call(
        functools.partial(combine_stage, len(everyone)),
        (*everyone, sums, *terms),
        shape(tall, LANES),
    )
    gradient = sum_over(term, "freq").reshape(1, slots)
    updated = sigma.reshape(1, slots) * jnp.exp(-0.5 * jnp.tanh(gradient))
    return gradient, updated


def solution(mesh):
    return jax.shard_map(
        local,
        mesh=mesh,
        in_specs=(
            P("freq"),
            P("dom", None, None),
            P("dom", None, None),
            P("dom", None),
            P("dom", None, None),
            P("dom", None),
            P("freq", None, "dom", None),
            P("freq", None, "dom", None),
            P("dom", None),
        ),
        out_specs=(P("dom", None), P("dom", None)),
        check_vma=False,
    )
```

```python
import functools

import jax
import jax.numpy as jnp
from jax import lax
from jax.experimental import pallas as pl
from jax.experimental.pallas import tpu as pltpu
from jax.sharding import PartitionSpec as P

LANES = 128
SUBLANES = 8
SIDE = 6
VMEM = pl.BlockSpec(memory_space=pltpu.VMEM)
HBM = pl.BlockSpec(memory_space=pltpu.HBM)

PICK_LANES = lax.GatherDimensionNumbers(
    offset_dims=(),
    collapsed_slice_dims=(1,),
    start_index_map=(1,),
    operand_batching_dims=(0,),
    start_indices_batching_dims=(0,),
)


def pick_lanes(block, lanes):
    return lax.gather(
        block,
        lanes[..., None],
        PICK_LANES,
        (1, 1),
        mode=lax.GatherScatterMode.PROMISE_IN_BOUNDS,
    )


def pick_wide(chunks, index):
    lanes = index & (LANES - 1)
    high = index >> 7
    level = [pick_lanes(chunk, lanes) for chunk in chunks]
    bit = 0
    while len(level) > 1:
        odd = (high >> bit) & 1 == 1
        level = [
            jnp.where(odd, level[t + 1], level[t]) if t + 1 < len(level) else level[t]
            for t in range(0, len(level), 2)
        ]
        bit += 1
    return level[0]


def row_ids(rows):
    return lax.broadcasted_iota(jnp.int32, (rows, LANES), 0)


def lane_ids(rows):
    return lax.broadcasted_iota(jnp.int32, (rows, LANES), 1)


def spread(row, rows):
    return jnp.broadcast_to(row, (rows, row.shape[-1]))


def cut(ref):
    return [ref[:, c : c + LANES] for c in range(0, ref.shape[-1], LANES)]


def swap_halves(block):
    return pltpu.roll(block, block.shape[0] // 2, 0)


def doubled(block):
    half = block.shape[0] // 2
    return jnp.where(row_ids(2 * half) < half, block, swap_halves(block))


def lane_sum(block):
    return jnp.broadcast_to(jnp.sum(block, axis=1, keepdims=True), block.shape)


def put_lane(block, lane, value):
    return jnp.where(lane_ids(block.shape[0]) == lane, value, block)


def put_chunks(ref, chunks):
    for c, chunk in enumerate(chunks):
        ref[:, c * LANES : (c + 1) * LANES] = chunk


def is_even():
    return lax.rem(lax.axis_index("dom"), 2) == 0


def put_rims(across_ref, beside_ref, lower, upper):
    even = is_even()
    for c, (low, high) in enumerate(zip(lower, upper)):
        here = slice(c * LANES, (c + 1) * LANES)
        across_ref[:, here] = jnp.where(even, low, high)
        beside_ref[:, here] = jnp.where(even, high, low)


def take_rims(across_ref, beside_ref):
    even = is_even()
    device = lax.axis_index("dom")
    outermost = (device == 0) | (device == lax.axis_size("dom") - 1)
    pairs = [
        (jnp.where(outermost, 0.0, a), b) for a, b in zip(cut(across_ref), cut(beside_ref))
    ]
    prior = [jnp.where(even, a, b) for a, b in pairs]
    above = [jnp.where(even, b, a) for a, b in pairs]
    return prior, above


def picks_of(rows_of_group, edges):
    chunks = [spread(row, edges.shape[1]) for row in rows_of_group]
    return [pick_wide(chunks, edges[j]) for j in range(SIDE)]


def group_rows(ref, g):
    return [ref[g : g + 1, c : c + LANES] for c in range(0, ref.shape[-1], LANES)]


def times_block(entries, base, picked):
    out = []
    for i in range(SIDE):
        total = None
        for j in range(SIDE):
            one = entries[base + SIDE * i + j] * picked[j]
            total = one if total is None else total + one
        out.append(total)
    return out


def weighted_sum(left, right):
    total = None
    for a, b in zip(left, right):
        total = a * b if total is None else total + a * b
    return total


def scatter_side(pieces, edges, places, heights, i):
    depth = SIDE * edges.shape[1]
    rows = pieces.shape[0] // depth
    slots = edges.shape[1] * LANES
    columns = []
    for s in range(edges.shape[1]):
        both = pieces[pl.ds(i * edges.shape[1] + s, rows, stride=depth), :]
        high = spread(edges[i, s : s + 1, :] >> 7, rows)
        stacked = [jnp.where(high == h, both, 0.0) for h in heights]
        columns.append(jnp.concatenate(stacked, axis=0).astype(jnp.bfloat16))
    return lax.dot_general(
        jnp.concatenate(columns, axis=1),
        places[:, i * slots : (i + 1) * slots],
        (((1,), (1,)), ((), ())),
        preferred_element_type=jnp.float32,
    )


def add(total, part):
    return part if total is None else total + part


def parts_joined(total, count):
    rows = total.shape[0] // count
    out = []
    for n in range(count):
        piece = total[rows * n : rows * (n + 1)]
        out.append(piece + swap_halves(piece))
    return out


def scatter(pieces, edges, places, heights):
    total = None
    for i in range(SIDE):
        total = add(total, scatter_side(pieces, edges, places, heights, i))
    return parts_joined(total, len(heights))


def rim_heights(edge_count, rim):
    count = edge_count // LANES
    return [*range(rim), *range(count - rim, count)], list(range(rim, count - rim))


def corrections(from_prior, from_above, order, inverse):
    lower = [pick_wide(from_prior, index) for index in order]
    return lower + [pick_wide(from_above, index) for index in inverse]


def corrected(own, delta):
    rim = len(delta) // 2
    lower = [a + b for a, b in zip(own[:rim], delta[:rim])]
    upper = [a + b for a, b in zip(own[len(own) - rim :], delta[rim:])]
    return lower + own[rim : len(own) - rim] + upper


def squares(chunks, rim, has_prior):
    total = None
    for c, chunk in enumerate(chunks):
        term = chunk * chunk
        if c < rim:
            term = term * (1.0 - has_prior)
        total = term if total is None else total + term
    return total


def start_copies(routes, arrived):
    copies = [
        pltpu.make_async_copy(here, there, arrived.at[n])
        for n, (here, there) in enumerate(routes)
    ]
    for copy in copies:
        copy.start()
    return copies


def stacked_chunk(source, at):
    piece = [source[g, :, at : at + LANES] for g in range(source.shape[0])]
    return jnp.concatenate(piece + piece, axis=0)


def rims_stage(source_in, order_in, across_ref, beside_ref, source, order_ref, order, arrived):
    for copy in start_copies(((source_in, source), (order_in, order)), arrived):
        copy.wait()
    rows, rim = order_ref.shape
    first = row_ids(rows) < rows // 2
    order_ref[...] = spread(order[...], rows)
    numbers = [x.astype(jnp.float32) for x in cut(order_ref)]
    lower = [stacked_chunk(source, c) for c in range(0, rim, LANES)]
    start = source.shape[-1] - rim
    upper = [stacked_chunk(source, start + c) for c in range(0, rim, LANES)]
    lower = [jnp.where(first, x, o) for x, o in zip(lower, numbers)]
    upper = [jnp.where(first, x, 1.0) for x in upper]
    put_rims(across_ref, beside_ref, lower, upper)


def table_stage(
    angular_in,
    stiffness_in,
    mass_in,
    sigma_in,
    live_in,
    edges_in,
    forward_in,
    source,
    places_ref,
    blocks_ref,
    scale_ref,
    picks_ref,
    stacked_ref,
    rates,
    mass,
    sigma,
    live,
    edges,
    forward_ref,
    angular,
    stiffness,
    arrived,
):
    copies = start_copies(
        (
            (edges_in, edges),
            (angular_in, angular),
            (sigma_in, sigma),
            (live_in, live),
            (stiffness_in, stiffness),
            (mass_in, mass),
            (forward_in, forward_ref),
        ),
        arrived,
    )
    copies[0].wait()
    numbers = row_ids(LANES)
    rows = edges.shape[1]

    def body(i, carry):
        for s in range(rows):
            lanes = spread(edges[i, s : s + 1, :] & (LANES - 1), LANES)
            column = pl.ds(pl.multiple_of((i * rows + s) * LANES, LANES), LANES)
            places_ref[:, column] = jnp.where(lanes == numbers, 1.0, 0.0).astype(jnp.bfloat16)
        return carry

    lax.fori_loop(0, SIDE, body, 0)
    count = source.shape[-1]
    put_chunks(stacked_ref, [stacked_chunk(source, c) for c in range(0, count, LANES)])
    put_picks(picks_ref, stacked_ref, edges, source.shape[0])
    for copy in copies[1:]:
        copy.wait()
    for f in range(angular.shape[0]):
        rates[f] = jnp.full(rates.shape[1:], angular[f], jnp.float32)
    alive = live[...].astype(jnp.float32)
    weight = sigma[...]
    freqs = rates.shape[0]
    peak = None
    for i in range(SIDE):
        for f in range(freqs):
            entry = (SIDE + 1) * i
            size = stiffness[entry] + rates[f] * weight * mass[entry]
            peak = size if peak is None else jnp.maximum(peak, size)
    peak = jnp.max(peak * alive, axis=1, keepdims=True)
    scale = jnp.broadcast_to(jnp.max(peak, axis=0, keepdims=True), scale_ref.shape)
    scale_ref[...] = scale
    alive = alive / scale[:1, :1]
    for entry in range(SIDE * SIDE):
        stiff = stiffness[entry] * alive
        heavy = mass[entry] * (weight * alive)
        for f in range(freqs):
            blocks_ref[f * SIDE * SIDE + entry] = stiff + rates[f] * heavy


def put_picks(picks_ref, field, edges, groups):
    for g in range(groups):
        for j, value in enumerate(picks_of(group_rows(field, g), edges)):
            picks_ref[g * SIDE + j] = value


def pick_rims(rows, index, edge_count):
    rim = len(rows) // 2
    start = edge_count - rim * LANES
    lower = pick_wide([spread(row, index.shape[0]) for row in rows[:rim]], index)
    upper = pick_wide([spread(row, index.shape[0]) for row in rows[rim:]], index - start)
    lower = jnp.where(index < rim * LANES, lower, 0.0)
    return lower + jnp.where(index >= start, upper, 0.0)


def corrected_picks(delta_ref, own_picks, edges, edge_count):
    out = []
    for g in range(delta_ref.shape[0] // 2):
        delta = group_rows(delta_ref, g)
        out.append(
            [
                own_picks[g * SIDE + j] + pick_rims(delta, edges[j], edge_count)
                for j in range(SIDE)
            ]
        )
    return out


def products(blocks, picked, polars, i):
    out = []
    for g, mine in enumerate(picked):
        base = (g // polars) * SIDE * SIDE + SIDE * i
        out.append(weighted_sum([blocks[base + j] for j in range(SIDE)], mine))
    return out


def rows_of_forms(forms, rows):
    out = jnp.zeros((rows, LANES), jnp.float32)
    for g, form in enumerate(forms):
        row = jnp.sum(form, axis=0, keepdims=True)
        out = jnp.where(row_ids(rows) == g, spread(row, rows), out)
    return out


def invert(above, groups, rows):
    above_order = jnp.concatenate([x[groups : groups + 1] for x in above], axis=1)
    rim = above_order.shape[1]
    slot = lax.broadcasted_iota(jnp.int32, (rim, rim), 0).astype(jnp.float32)
    match = jnp.where(spread(above_order, rim) == slot, 1.0, 0.0).astype(jnp.bfloat16)
    numbers = lax.broadcasted_iota(jnp.int32, (2 * rows, rim), 1).astype(jnp.bfloat16)
    inverse = lax.dot_general(
        numbers, match, (((1,), (1,)), ((), ())), preferred_element_type=jnp.float32
    )
    return inverse[:rows].astype(jnp.int32)


def rescaled(block, inverse_scale, step):
    ratio = swap_halves(block) * inverse_scale
    for _ in range(step):
        block = block * ratio
    return doubled(block)


def front_stage(
    polars,
    step,
    edge_count,
    order_ref,
    across_in,
    beside_in,
    scale_in,
    own_picks,
    blocks,
    edges,
    places,
    *rest,
):
    if step == 0:
        inverse_ref, *rest = rest
    else:
        inverse_in, *rest = rest
    delta_ref, picks_ref, pieces, forms_ref, rims_ref, across_ref, beside_ref = rest
    rows = delta_ref.shape[0]
    groups = rows // 2
    first = row_ids(rows) < groups
    scale = scale_in[...]
    prior, above = take_rims(across_in, beside_in)
    if step == 0:
        inverse_ref[...] = invert(above, groups, rows)
        inverse = cut(inverse_ref)
        prior, above = [doubled(x) for x in prior], [doubled(x) for x in above]
    else:
        inverse = cut(inverse_in)
        inverse_scale = 1.0 / scale
        prior = [rescaled(x, inverse_scale, step) for x in prior]
        above = [rescaled(x, inverse_scale, step) for x in above]
    put_chunks(delta_ref, corrections(prior, above, cut(order_ref), inverse))

    picked = corrected_picks(delta_ref, own_picks, edges, edge_count)
    for g in range(groups):
        for j in range(SIDE):
            picks_ref[g * SIDE + j] = picked[g][j]
    rim = len(prior)
    heights = rim_heights(edge_count, rim)[0]
    tall = edges.shape[1]
    forms, total = [None] * groups, None
    for i in range(SIDE):
        for g, value in enumerate(products(blocks, picked, polars, i)):
            forms[g] = add(forms[g], picked[g][i] * value)
            coarse = value.astype(jnp.bfloat16).astype(jnp.float32)
            for part, piece in enumerate((coarse, value - coarse)):
                at = ((part * groups + g) * SIDE + i) * tall
                pieces[at : at + tall, :] = piece
        total = add(total, scatter_side(pieces, edges, places, heights, i))
    forms_ref[...] = rows_of_forms(forms, rows)
    chunks = parts_joined(total, len(heights))
    put_chunks(rims_ref, chunks)
    put_rims(
        across_ref,
        beside_ref,
        [jnp.where(first, x, scale) for x in chunks[:rim]],
        [jnp.where(first, x, scale) for x in chunks[rim:]],
    )


def inner_products(step, sums, own, delta, forms, across_in, beside_in):
    rows = sums.shape[0]
    first = row_ids(rows) < rows // 2
    prior, _ = take_rims(across_in, beside_in)
    has_prior = jnp.where(first, swap_halves(prior[0]), prior[0])
    has_prior = spread(jnp.where(has_prior[:1, :1] > 0.0, 1.0, 0.0), rows)
    field = corrected(own, delta)
    sums = put_lane(sums, 2 * step, lane_sum(squares(field, len(delta) // 2, has_prior)))
    return put_lane(sums, 2 * step + 1, lane_sum(forms))


def back_stage(
    polars,
    step,
    own,
    delta,
    forms,
    across_in,
    beside_in,
    sums_in,
    picks,
    pieces,
    rims,
    edges,
    places,
    *rest,
):
    if step == 0:
        rates, forward, mass, live, heavy, terms_ref, sums_ref, image_ref, picks_ref = rest
    else:
        heavy, terms_ref, sums_ref, image_ref, picks_ref = rest
    rows, edge_count = own.shape
    groups = rows // 2
    rim = rims.shape[-1] // LANES // 2
    outer = cut(rims)
    inner = scatter(pieces, edges, places, rim_heights(edge_count, rim)[1])
    put_chunks(image_ref, outer[:rim] + inner + outer[rim:])
    put_picks(picks_ref, image_ref, edges, groups)
    if step == 0:
        dead = -live[...].astype(jnp.float32)
        for g in range(groups):
            row = [forward[g, :, c : c + LANES] for c in range(0, edge_count, LANES)]
            values = times_block(mass, 0, picks_of(row, edges))
            factor = dead * rates[g // polars]
            for i in range(SIDE):
                heavy[g * SIDE + i] = factor * values[i]
    for g in range(groups):
        side = range(g * SIDE, (g + 1) * SIDE)
        terms_ref[g] = weighted_sum([picks[i] for i in side], [heavy[i] for i in side])
    sums_ref[...] = inner_products(
        step, sums_in[...], cut(own), cut(delta), forms[...], across_in, beside_in
    )


def last_stage(
    polars,
    step,
    own,
    order_ref,
    inverse_in,
    across_in,
    beside_in,
    scale_in,
    sums_in,
    own_picks,
    blocks,
    edges,
    heavy,
    terms0,
    terms1,
    terms_ref,
    sums_ref,
    delta_ref,
):
    rows, edge_count = own.shape
    groups = rows // 2
    terms_ref[:groups] = terms0[...]
    terms_ref[groups : 2 * groups] = terms1[...]
    terms_ref[3 * groups] = jnp.broadcast_to(scale_in[:1, :1], terms_ref.shape[1:])
    first = row_ids(rows) < rows // 2
    scale = scale_in[...]
    inverse_scale = 1.0 / scale
    prior, above = take_rims(across_in, beside_in)
    prior = [rescaled(x, inverse_scale, step) for x in prior]
    above = [rescaled(x, inverse_scale, step) for x in above]
    put_chunks(delta_ref, corrections(prior, above, cut(order_ref), cut(inverse_in)))

    picked = corrected_picks(delta_ref, own_picks, edges, edge_count)
    forms = [None] * len(picked)
    for i in range(SIDE):
        for g, value in enumerate(products(blocks, picked, polars, i)):
            forms[g] = add(forms[g], picked[g][i] * value)
    for g, mine in enumerate(picked):
        terms_ref[2 * groups + g] = weighted_sum(
            mine, [heavy[g * SIDE + i] for i in range(SIDE)]
        )
    forms = rows_of_forms(forms, rows)
    sums = inner_products(
        step, sums_in[...], cut(own), cut(delta_ref), forms, across_in, beside_in
    )
    sums_ref[...] = jnp.where(first, sums, scale)


def combine_stage(everyone, own, other, out_ref):
    rows = everyone.shape[1]
    groups = rows // 2
    first = row_ids(rows) < groups

    def scale_of(block):
        return jnp.where(first, swap_halves(block), block)

    parts = [everyone[q] for q in range(everyone.shape[0])]
    scales = [scale_of(block) for block in parts]
    top = functools.reduce(jnp.maximum, scales)
    lanes = lane_ids(rows)
    inverse_top = 1.0 / top
    total = None
    for block, scale in zip(parts, scales):
        ratio = scale * inverse_top
        power = jnp.ones_like(ratio)
        factor = jnp.ones_like(ratio)
        for k in range(1, 6):
            power = power * ratio
            factor = jnp.where(lanes == k, power, factor)
        term = block * factor
        total = term if total is None else total + term
    m = [jnp.broadcast_to(total[:, k : k + 1], (rows, LANES)) for k in range(6)]
    l1 = m[2] / m[1]
    l2 = m[3] / m[1]
    d2 = m[3] - l1 * m[2]
    cross = m[4] - l2 * m[2]
    l3 = cross / d2
    d3 = m[5] - l2 * m[3] - l3 * cross
    y1 = m[1] - l1 * m[0]
    y2 = m[2] - l2 * m[0] - l3 * y1
    c2 = y2 / d3
    c1 = y1 / d2 - l3 * c2
    c0 = m[0] / m[1] - l1 * c1 - l2 * c2
    tall = out_ref.shape[1]
    for n, terms in enumerate((own, other)):
        mine = terms[3 * groups] * inverse_top[:1]
        weight = spread(inverse_top[:1], tall)
        out = None
        for place, c in enumerate((c0, c1, c2)):
            part = None
            for g in range(groups):
                part = add(part, terms[place * groups + g] * spread(c[g : g + 1], tall))
            out = add(out, part * weight)
            weight = weight * mine
        out_ref[n] = out


def pinned(*arguments):
    return [pltpu.with_memory_space_constraint(x, pltpu.HBM) for x in arguments]


def call(kernel, arguments, outs, scratch=(), space=VMEM, cost=0):
    return pl.pallas_call(
        kernel,
        out_shape=outs,
        in_specs=space if isinstance(space, list) else [space] * len(arguments),
        out_specs=jax.tree.map(lambda _: VMEM, outs),
        scratch_shapes=list(scratch),
        cost_estimate=pl.CostEstimate(flops=cost, bytes_accessed=cost, transcendentals=0),
        compiler_params=pltpu.CompilerParams(vmem_limit_bytes=16 * 1024 * 1024),
    )(*arguments)


def swap_across(block):
    size = lax.axis_size("dom")
    route = []
    for low in range(1, size, 2):
        high = (low + 1) % size
        route += [(low, high), (high, low)]
    return lax.ppermute(block, "dom", route)


def swap_beside(block):
    return lax.ppermute(block, "dom", [(i, i ^ 1) for i in range(lax.axis_size("dom"))])


def gather_all(block, axis):
    size = lax.axis_size(axis)
    copies = jnp.broadcast_to(block[None], (size, *block.shape))
    return lax.all_to_all(copies, axis, 0, 0)


def sum_over_freq(block):
    size, width = lax.axis_size("freq"), lax.axis_size("dom")
    step = size // 2
    while step > 0:
        route = []
        for f in range(size):
            for p in range(width):
                there = (f ^ step) * width + p if p % 2 else f * width + (p ^ 2)
                route.append((f * width + p, there))
        block = block + lax.ppermute(block, ("freq", "dom"), route)
        step //= 2
    return block


def local(
    angular,
    stiffness,
    mass_matrix,
    conductivity,
    element_edges,
    live_slots,
    adjoint_source,
    forward_field,
    neighbour_map,
):
    freqs = angular.shape[0]
    polars = adjoint_source.shape[1]
    groups = freqs * polars
    rows = 2 * groups
    edge_count = adjoint_source.shape[-1]
    rim = neighbour_map.shape[-1]
    slots = element_edges.shape[-1]
    tall = slots // LANES
    stiff = stiffness.reshape(SIDE * SIDE, tall, LANES)
    mass = mass_matrix.reshape(SIDE * SIDE, tall, LANES)
    edges = element_edges.reshape(SIDE, tall, LANES)
    sigma = conductivity.reshape(tall, LANES)
    live = live_slots.reshape(tall, LANES)
    source = adjoint_source.reshape(groups, 1, edge_count)
    forward = forward_field.reshape(groups, 1, edge_count)

    def shape(*dims, kind=jnp.float32):
        return jax.ShapeDtypeStruct(dims, kind)

    field_shape, rim_shape = shape(rows, edge_count), shape(rows, rim)
    sums_shape, terms_shape = shape(rows, LANES), shape(groups, tall, LANES)
    picks_shape = shape(groups * SIDE, tall, LANES)

    across, beside, source, order = call(
        rims_stage,
        pinned(source, neighbour_map),
        [rim_shape, rim_shape, shape(*source.shape), shape(rows, rim, kind=jnp.int32)],
        (
            pltpu.VMEM(neighbour_map.shape, neighbour_map.dtype),
            pltpu.SemaphoreType.DMA((2,)),
        ),
        space=HBM,
    )
    across, beside = swap_across(across), swap_beside(beside)
    kept = [jax.ShapeDtypeStruct(x.shape, x.dtype) for x in (mass, sigma, live, edges, forward)]
    places, blocks, scale, picks, own, rates, mass, sigma, live, edges, forward = call(
        table_stage,
        [*pinned(angular, stiff, mass, sigma, live, edges, forward), source],
        [
            shape(LANES, SIDE * slots, kind=jnp.bfloat16),
            shape(freqs * SIDE * SIDE, tall, LANES),
            sums_shape,
            picks_shape,
            field_shape,
            shape(freqs, tall, LANES),
            *kept,
        ],
        (
            pltpu.SMEM(angular.shape, angular.dtype),
            pltpu.VMEM(stiff.shape, stiff.dtype),
            pltpu.SemaphoreType.DMA((7,)),
        ),
        space=[HBM] * 7 + [VMEM],
        cost=4_000_000,
    )
    front_shapes = [
        shape(rows, 2 * rim),
        picks_shape,
        shape(rows * SIDE * tall, LANES),
        sums_shape,
        shape(rows, 2 * rim),
        rim_shape,
        rim_shape,
    ]
    back_shapes = [terms_shape, sums_shape, field_shape, picks_shape]
    sums, terms = jnp.zeros((rows, LANES), jnp.float32), []
    for step in range(2):
        arrived = (across, beside)
        given = (order, *arrived, scale, picks, blocks, edges, places)
        front = functools.partial(front_stage, polars, step, edge_count)
        if step == 0:
            inverse, *outs = call(
                front, given, [shape(rows, rim, kind=jnp.int32), *front_shapes]
            )
        else:
            outs = call(front, (*given, inverse), front_shapes)
        delta, picks, pieces, forms, rims, across, beside = outs
        across, beside = swap_across(across), swap_beside(beside)
        given = (own, delta, forms, *arrived, sums, picks, pieces, rims, edges, places)
        back = functools.partial(back_stage, polars, step)
        if step == 0:
            heavy, term, sums, own, picks = call(
                back,
                (*given, rates, forward, mass, live),
                [picks_shape, *back_shapes],
                cost=4_000_000,
            )
        else:
            term, sums, own, picks = call(back, (*given, heavy), back_shapes, cost=4_000_000)
        terms.append(term)
    terms, sums = call(
        functools.partial(last_stage, polars, 2),
        (own, order, inverse, across, beside, scale, sums, picks, blocks, edges, heavy, *terms),
        [shape(3 * groups + 1, tall, LANES), sums_shape],
        (pltpu.VMEM((rows, 2 * rim), jnp.float32),),
    )
    both = call(
        combine_stage,
        (gather_all(sums, "dom"), terms, swap_beside(terms)),
        shape(2, tall, LANES),
    )
    both = sum_over_freq(both)
    returned = swap_beside(both[1])
    odd = lax.rem(lax.axis_index("dom"), 2) == 1
    gradient = jnp.where(odd, both[0], returned).reshape(1, slots)
    updated = sigma.reshape(1, slots) * jnp.exp(-0.5 * jnp.tanh(gradient))
    return gradient, updated


def solution(mesh):
    return jax.shard_map(
        local,
        mesh=mesh,
        in_specs=(
            P("freq"),
            P("dom", None, None),
            P("dom", None, None),
            P("dom", None),
            P("dom", None, None),
            P("dom", None),
            P("freq", None, "dom", None),
            P("freq", None, "dom", None),
            P("dom", None),
        ),
        out_specs=(P("dom", None), P("dom", None)),
        check_vma=False,
    )
```

```python
import functools

import jax
import jax.numpy as jnp
from jax import lax
from jax.experimental import pallas as pl
from jax.experimental.pallas import tpu as pltpu
from jax.sharding import PartitionSpec as P

LANES = 128
SUBLANES = 8
SIDE = 6
VMEM = pl.BlockSpec(memory_space=pltpu.VMEM)
HBM = pl.BlockSpec(memory_space=pltpu.HBM)

PICK_LANES = lax.GatherDimensionNumbers(
    offset_dims=(),
    collapsed_slice_dims=(1,),
    start_index_map=(1,),
    operand_batching_dims=(0,),
    start_indices_batching_dims=(0,),
)


def pick_lanes(block, lanes):
    return lax.gather(
        block,
        lanes[..., None],
        PICK_LANES,
        (1, 1),
        mode=lax.GatherScatterMode.PROMISE_IN_BOUNDS,
    )


def pick_wide(chunks, index):
    lanes = index & (LANES - 1)
    high = index >> 7
    level = [pick_lanes(chunk, lanes) for chunk in chunks]
    bit = 0
    while len(level) > 1:
        odd = (high >> bit) & 1 == 1
        level = [
            jnp.where(odd, level[t + 1], level[t]) if t + 1 < len(level) else level[t]
            for t in range(0, len(level), 2)
        ]
        bit += 1
    return level[0]


def row_ids(rows):
    return lax.broadcasted_iota(jnp.int32, (rows, LANES), 0)


def lane_ids(rows):
    return lax.broadcasted_iota(jnp.int32, (rows, LANES), 1)


def spread(row, rows):
    return jnp.broadcast_to(row, (rows, row.shape[-1]))


def cut(ref):
    return [ref[:, c : c + LANES] for c in range(0, ref.shape[-1], LANES)]


def swap_halves(block):
    return pltpu.roll(block, block.shape[0] // 2, 0)


def doubled(block):
    half = block.shape[0] // 2
    return jnp.where(row_ids(2 * half) < half, block, swap_halves(block))


def lane_sum(block):
    return jnp.broadcast_to(jnp.sum(block, axis=1, keepdims=True), block.shape)


def put_lane(block, lane, value):
    return jnp.where(lane_ids(block.shape[0]) == lane, value, block)


def put_chunks(ref, chunks):
    for c, chunk in enumerate(chunks):
        ref[:, c * LANES : (c + 1) * LANES] = chunk


def is_even():
    return lax.rem(lax.axis_index("dom"), 2) == 0


def put_rims(across_ref, beside_ref, lower, upper):
    even = is_even()
    for c, (low, high) in enumerate(zip(lower, upper)):
        here = slice(c * LANES, (c + 1) * LANES)
        across_ref[:, here] = jnp.where(even, low, high)
        beside_ref[:, here] = jnp.where(even, high, low)


def take_rims(across_ref, beside_ref):
    even = is_even()
    device = lax.axis_index("dom")
    outermost = (device == 0) | (device == lax.axis_size("dom") - 1)
    pairs = [
        (jnp.where(outermost, 0.0, a), b) for a, b in zip(cut(across_ref), cut(beside_ref))
    ]
    prior = [jnp.where(even, a, b) for a, b in pairs]
    above = [jnp.where(even, b, a) for a, b in pairs]
    return prior, above


def picks_of(rows_of_group, edges):
    chunks = [spread(row, edges.shape[1]) for row in rows_of_group]
    return [pick_wide(chunks, edges[j]) for j in range(SIDE)]


def group_rows(ref, g):
    return [ref[g : g + 1, c : c + LANES] for c in range(0, ref.shape[-1], LANES)]


def times_block(entries, base, picked):
    out = []
    for i in range(SIDE):
        total = None
        for j in range(SIDE):
            one = entries[base + SIDE * i + j] * picked[j]
            total = one if total is None else total + one
        out.append(total)
    return out


def weighted_sum(left, right):
    total = None
    for a, b in zip(left, right):
        total = a * b if total is None else total + a * b
    return total


def scatter_side(pieces, edges, places, heights, i):
    depth = SIDE * edges.shape[1]
    rows = pieces.shape[0] // depth
    slots = edges.shape[1] * LANES
    columns = []
    for s in range(edges.shape[1]):
        both = pieces[pl.ds(i * edges.shape[1] + s, rows, stride=depth), :]
        high = spread(edges[i, s : s + 1, :] >> 7, rows)
        stacked = [jnp.where(high == h, both, 0.0) for h in heights]
        columns.append(jnp.concatenate(stacked, axis=0).astype(jnp.bfloat16))
    return lax.dot_general(
        jnp.concatenate(columns, axis=1),
        places[:, i * slots : (i + 1) * slots],
        (((1,), (1,)), ((), ())),
        preferred_element_type=jnp.float32,
    )


def add(total, part):
    return part if total is None else total + part


def parts_joined(total, count):
    rows = total.shape[0] // count
    out = []
    for n in range(count):
        piece = total[rows * n : rows * (n + 1)]
        out.append(piece + swap_halves(piece))
    return out


def scatter(pieces, edges, places, heights):
    total = None
    for i in range(SIDE):
        total = add(total, scatter_side(pieces, edges, places, heights, i))
    return parts_joined(total, len(heights))


def rim_heights(edge_count, rim):
    count = edge_count // LANES
    return [*range(rim), *range(count - rim, count)], list(range(rim, count - rim))


def corrections(from_prior, from_above, order, inverse):
    lower = [pick_wide(from_prior, index) for index in order]
    return lower + [pick_wide(from_above, index) for index in inverse]


def corrected(own, delta):
    rim = len(delta) // 2
    lower = [a + b for a, b in zip(own[:rim], delta[:rim])]
    upper = [a + b for a, b in zip(own[len(own) - rim :], delta[rim:])]
    return lower + own[rim : len(own) - rim] + upper


def squares(chunks, rim, has_prior):
    total = None
    for c, chunk in enumerate(chunks):
        term = chunk * chunk
        if c < rim:
            term = term * (1.0 - has_prior)
        total = term if total is None else total + term
    return total


def start_copies(routes, arrived):
    copies = [
        pltpu.make_async_copy(here, there, arrived.at[n])
        for n, (here, there) in enumerate(routes)
    ]
    for copy in copies:
        copy.start()
    return copies


def stacked_chunk(source, at):
    piece = [source[g, :, at : at + LANES] for g in range(source.shape[0])]
    return jnp.concatenate(piece + piece, axis=0)


def rims_stage(source_in, order_in, across_ref, beside_ref, source, order_ref, order, arrived):
    for copy in start_copies(((source_in, source), (order_in, order)), arrived):
        copy.wait()
    rows, rim = order_ref.shape
    first = row_ids(rows) < rows // 2
    order_ref[...] = spread(order[...], rows)
    numbers = [x.astype(jnp.float32) for x in cut(order_ref)]
    lower = [stacked_chunk(source, c) for c in range(0, rim, LANES)]
    start = source.shape[-1] - rim
    upper = [stacked_chunk(source, start + c) for c in range(0, rim, LANES)]
    lower = [jnp.where(first, x, o) for x, o in zip(lower, numbers)]
    upper = [jnp.where(first, x, 1.0) for x in upper]
    put_rims(across_ref, beside_ref, lower, upper)


def table_stage(
    angular_in,
    stiffness_in,
    mass_in,
    sigma_in,
    live_in,
    edges_in,
    forward_in,
    source,
    places_ref,
    blocks_ref,
    scale_ref,
    picks_ref,
    stacked_ref,
    rates,
    mass,
    sigma,
    live,
    edges,
    forward_ref,
    angular,
    stiffness,
    arrived,
):
    copies = start_copies(
        (
            (edges_in, edges),
            (angular_in, angular),
            (sigma_in, sigma),
            (live_in, live),
            (stiffness_in, stiffness),
            (mass_in, mass),
            (forward_in, forward_ref),
        ),
        arrived,
    )
    copies[0].wait()
    numbers = row_ids(LANES)
    rows = edges.shape[1]

    def body(i, carry):
        for s in range(rows):
            lanes = spread(edges[i, s : s + 1, :] & (LANES - 1), LANES)
            column = pl.ds(pl.multiple_of((i * rows + s) * LANES, LANES), LANES)
            places_ref[:, column] = jnp.where(lanes == numbers, 1.0, 0.0).astype(jnp.bfloat16)
        return carry

    lax.fori_loop(0, SIDE, body, 0)
    count = source.shape[-1]
    put_chunks(stacked_ref, [stacked_chunk(source, c) for c in range(0, count, LANES)])
    put_picks(picks_ref, stacked_ref, edges, source.shape[0])
    for copy in copies[1:]:
        copy.wait()
    for f in range(angular.shape[0]):
        rates[f] = jnp.full(rates.shape[1:], angular[f], jnp.float32)
    alive = live[...].astype(jnp.float32)
    weight = sigma[...]
    freqs = rates.shape[0]
    peak = None
    for i in range(SIDE):
        for f in range(freqs):
            entry = (SIDE + 1) * i
            size = stiffness[entry] + rates[f] * weight * mass[entry]
            peak = size if peak is None else jnp.maximum(peak, size)
    peak = jnp.max(peak * alive, axis=1, keepdims=True)
    scale = jnp.broadcast_to(jnp.max(peak, axis=0, keepdims=True), scale_ref.shape)
    scale_ref[...] = scale
    alive = alive / scale[:1, :1]
    for entry in range(SIDE * SIDE):
        stiff = stiffness[entry] * alive
        heavy = mass[entry] * (weight * alive)
        for f in range(freqs):
            blocks_ref[f * SIDE * SIDE + entry] = stiff + rates[f] * heavy


def put_picks(picks_ref, field, edges, groups):
    for g in range(groups):
        for j, value in enumerate(picks_of(group_rows(field, g), edges)):
            picks_ref[g * SIDE + j] = value


def pick_rims(rows, index, edge_count):
    rim = len(rows) // 2
    start = edge_count - rim * LANES
    lower = pick_wide([spread(row, index.shape[0]) for row in rows[:rim]], index)
    upper = pick_wide([spread(row, index.shape[0]) for row in rows[rim:]], index - start)
    lower = jnp.where(index < rim * LANES, lower, 0.0)
    return lower + jnp.where(index >= start, upper, 0.0)


def corrected_picks(delta_ref, own_picks, edges, edge_count):
    out = []
    for g in range(delta_ref.shape[0] // 2):
        delta = group_rows(delta_ref, g)
        out.append(
            [
                own_picks[g * SIDE + j] + pick_rims(delta, edges[j], edge_count)
                for j in range(SIDE)
            ]
        )
    return out


def products(blocks, picked, polars, i):
    out = []
    for g, mine in enumerate(picked):
        base = (g // polars) * SIDE * SIDE + SIDE * i
        out.append(weighted_sum([blocks[base + j] for j in range(SIDE)], mine))
    return out


def rows_of_forms(forms, rows):
    out = jnp.zeros((rows, LANES), jnp.float32)
    for g, form in enumerate(forms):
        row = jnp.sum(form, axis=0, keepdims=True)
        out = jnp.where(row_ids(rows) == g, spread(row, rows), out)
    return out


def invert(above, groups, rows):
    above_order = jnp.concatenate([x[groups : groups + 1] for x in above], axis=1)
    rim = above_order.shape[1]
    slot = lax.broadcasted_iota(jnp.int32, (rim, rim), 0).astype(jnp.float32)
    match = jnp.where(spread(above_order, rim) == slot, 1.0, 0.0).astype(jnp.bfloat16)
    numbers = lax.broadcasted_iota(jnp.int32, (2 * rows, rim), 1).astype(jnp.bfloat16)
    inverse = lax.dot_general(
        numbers, match, (((1,), (1,)), ((), ())), preferred_element_type=jnp.float32
    )
    return inverse[:rows].astype(jnp.int32)


def rescaled(block, inverse_scale, step):
    ratio = swap_halves(block) * inverse_scale
    for _ in range(step):
        block = block * ratio
    return doubled(block)


def front_stage(
    polars,
    step,
    edge_count,
    order_ref,
    across_in,
    beside_in,
    scale_in,
    own_picks,
    blocks,
    edges,
    places,
    *rest,
):
    if step == 0:
        inverse_ref, *rest = rest
    else:
        inverse_in, *rest = rest
    delta_ref, picks_ref, pieces, forms_ref, rims_ref, across_ref, beside_ref = rest
    rows = delta_ref.shape[0]
    groups = rows // 2
    first = row_ids(rows) < groups
    scale = scale_in[...]
    prior, above = take_rims(across_in, beside_in)
    if step == 0:
        inverse_ref[...] = invert(above, groups, rows)
        inverse = cut(inverse_ref)
        prior, above = [doubled(x) for x in prior], [doubled(x) for x in above]
    else:
        inverse = cut(inverse_in)
        inverse_scale = 1.0 / scale
        prior = [rescaled(x, inverse_scale, step) for x in prior]
        above = [rescaled(x, inverse_scale, step) for x in above]
    put_chunks(delta_ref, corrections(prior, above, cut(order_ref), inverse))

    picked = corrected_picks(delta_ref, own_picks, edges, edge_count)
    for g in range(groups):
        for j in range(SIDE):
            picks_ref[g * SIDE + j] = picked[g][j]
    rim = len(prior)
    heights = rim_heights(edge_count, rim)[0]
    tall = edges.shape[1]
    forms, total = [None] * groups, None
    for i in range(SIDE):
        for g, value in enumerate(products(blocks, picked, polars, i)):
            forms[g] = add(forms[g], picked[g][i] * value)
            coarse = value.astype(jnp.bfloat16).astype(jnp.float32)
            for part, piece in enumerate((coarse, value - coarse)):
                at = ((part * groups + g) * SIDE + i) * tall
                pieces[at : at + tall, :] = piece
        total = add(total, scatter_side(pieces, edges, places, heights, i))
    forms_ref[...] = rows_of_forms(forms, rows)
    chunks = parts_joined(total, len(heights))
    put_chunks(rims_ref, chunks)
    put_rims(
        across_ref,
        beside_ref,
        [jnp.where(first, x, scale) for x in chunks[:rim]],
        [jnp.where(first, x, scale) for x in chunks[rim:]],
    )


def inner_products(step, sums, own, delta, forms, across_in, beside_in):
    rows = sums.shape[0]
    first = row_ids(rows) < rows // 2
    prior, _ = take_rims(across_in, beside_in)
    has_prior = jnp.where(first, swap_halves(prior[0]), prior[0])
    has_prior = spread(jnp.where(has_prior[:1, :1] > 0.0, 1.0, 0.0), rows)
    field = corrected(own, delta)
    sums = put_lane(sums, 2 * step, lane_sum(squares(field, len(delta) // 2, has_prior)))
    return put_lane(sums, 2 * step + 1, lane_sum(forms))


def back_stage(
    polars,
    step,
    own,
    delta,
    forms,
    across_in,
    beside_in,
    sums_in,
    picks,
    pieces,
    rims,
    edges,
    places,
    *rest,
):
    if step == 0:
        rates, forward, mass, live, heavy, terms_ref, sums_ref, image_ref, picks_ref = rest
    else:
        heavy, terms_ref, sums_ref, image_ref, picks_ref = rest
    rows, edge_count = own.shape
    groups = rows // 2
    rim = rims.shape[-1] // LANES // 2
    outer = cut(rims)
    inner = scatter(pieces, edges, places, rim_heights(edge_count, rim)[1])
    put_chunks(image_ref, outer[:rim] + inner + outer[rim:])
    put_picks(picks_ref, image_ref, edges, groups)
    if step == 0:
        dead = -live[...].astype(jnp.float32)
        for g in range(groups):
            row = [forward[g, :, c : c + LANES] for c in range(0, edge_count, LANES)]
            values = times_block(mass, 0, picks_of(row, edges))
            factor = dead * rates[g // polars]
            for i in range(SIDE):
                heavy[g * SIDE + i] = factor * values[i]
    for g in range(groups):
        side = range(g * SIDE, (g + 1) * SIDE)
        terms_ref[g] = weighted_sum([picks[i] for i in side], [heavy[i] for i in side])
    sums_ref[...] = inner_products(
        step, sums_in[...], cut(own), cut(delta), forms[...], across_in, beside_in
    )


def last_stage(
    polars,
    step,
    own,
    order_ref,
    inverse_in,
    across_in,
    beside_in,
    scale_in,
    sums_in,
    own_picks,
    blocks,
    edges,
    heavy,
    terms_ref,
    sums_ref,
    delta_ref,
):
    rows, edge_count = own.shape
    first = row_ids(rows) < rows // 2
    scale = scale_in[...]
    inverse_scale = 1.0 / scale
    prior, above = take_rims(across_in, beside_in)
    prior = [rescaled(x, inverse_scale, step) for x in prior]
    above = [rescaled(x, inverse_scale, step) for x in above]
    put_chunks(delta_ref, corrections(prior, above, cut(order_ref), cut(inverse_in)))

    picked = corrected_picks(delta_ref, own_picks, edges, edge_count)
    forms = [None] * len(picked)
    for i in range(SIDE):
        for g, value in enumerate(products(blocks, picked, polars, i)):
            forms[g] = add(forms[g], picked[g][i] * value)
    for g, mine in enumerate(picked):
        terms_ref[g] = weighted_sum(mine, [heavy[g * SIDE + i] for i in range(SIDE)])
    forms = rows_of_forms(forms, rows)
    sums = inner_products(
        step, sums_in[...], cut(own), cut(delta_ref), forms, across_in, beside_in
    )
    sums_ref[...] = jnp.where(first, sums, scale)


def combine_stage(everyone, sums_in, terms0, terms1, terms2, out_ref):
    rows = sums_in.shape[0]
    groups = rows // 2
    first = row_ids(rows) < groups

    def scale_of(block):
        return jnp.where(first, swap_halves(block), block)

    parts = [everyone[q] for q in range(everyone.shape[0])]
    scales = [scale_of(block) for block in parts]
    top = functools.reduce(jnp.maximum, scales)
    lanes = lane_ids(rows)
    inverse_top = 1.0 / top
    total = None
    for block, scale in zip(parts, scales):
        ratio = scale * inverse_top
        power = jnp.ones_like(ratio)
        factor = jnp.ones_like(ratio)
        for k in range(1, 6):
            power = power * ratio
            factor = jnp.where(lanes == k, power, factor)
        term = block * factor
        total = term if total is None else total + term
    m = [jnp.broadcast_to(total[:, k : k + 1], (rows, LANES)) for k in range(6)]
    l1 = m[2] / m[1]
    l2 = m[3] / m[1]
    d2 = m[3] - l1 * m[2]
    cross = m[4] - l2 * m[2]
    l3 = cross / d2
    d3 = m[5] - l2 * m[3] - l3 * cross
    y1 = m[1] - l1 * m[0]
    y2 = m[2] - l2 * m[0] - l3 * y1
    c2 = y2 / d3
    c1 = y1 / d2 - l3 * c2
    c0 = m[0] / m[1] - l1 * c1 - l2 * c2
    mine = scale_of(sums_in[...]) * inverse_top
    c0 = c0 * inverse_top
    c1 = c1 * mine * inverse_top
    c2 = c2 * mine * mine * inverse_top
    out = None
    for terms, c in ((terms0, c0), (terms1, c1), (terms2, c2)):
        for g in range(groups):
            one = terms[g] * spread(c[g : g + 1], out_ref.shape[0])
            out = one if out is None else out + one
    out_ref[...] = out


def pinned(*arguments):
    return [pltpu.with_memory_space_constraint(x, pltpu.HBM) for x in arguments]


def call(kernel, arguments, outs, scratch=(), space=VMEM, cost=0):
    return pl.pallas_call(
        kernel,
        out_shape=outs,
        in_specs=space if isinstance(space, list) else [space] * len(arguments),
        out_specs=jax.tree.map(lambda _: VMEM, outs),
        scratch_shapes=list(scratch),
        cost_estimate=pl.CostEstimate(flops=cost, bytes_accessed=cost, transcendentals=0),
        compiler_params=pltpu.CompilerParams(vmem_limit_bytes=16 * 1024 * 1024),
    )(*arguments)


def swap_across(block):
    size, planes = lax.axis_size("dom"), lax.axis_size("freq")
    route = []
    for f in range(planes):
        for p in range(size):
            if p in (0, size - 1) and planes % 2 == 0:
                there = (f ^ 1) * size + p
            elif p % 2:
                there = f * size + (p + 1) % size
            else:
                there = f * size + (p - 1) % size
            route.append((f * size + p, there))
    return lax.ppermute(block, ("freq", "dom"), route)


def swap_beside(block):
    return lax.ppermute(block, "dom", [(i, i ^ 1) for i in range(lax.axis_size("dom"))])


def gather_all(block, axis):
    size = lax.axis_size(axis)
    copies = jnp.broadcast_to(block[None], (size, *block.shape))
    return lax.all_to_all(copies, axis, 0, 0)


def sum_over(block, axis):
    size = lax.axis_size(axis)
    if size & (size - 1):
        return jnp.sum(gather_all(block, axis), axis=0)
    step = size // 2
    while step > 0:
        block = block + lax.ppermute(block, axis, [(i, i ^ step) for i in range(size)])
        step //= 2
    return block


def local(
    angular,
    stiffness,
    mass_matrix,
    conductivity,
    element_edges,
    live_slots,
    adjoint_source,
    forward_field,
    neighbour_map,
):
    freqs = angular.shape[0]
    polars = adjoint_source.shape[1]
    groups = freqs * polars
    rows = 2 * groups
    edge_count = adjoint_source.shape[-1]
    rim = neighbour_map.shape[-1]
    slots = element_edges.shape[-1]
    tall = slots // LANES
    stiff = stiffness.reshape(SIDE * SIDE, tall, LANES)
    mass = mass_matrix.reshape(SIDE * SIDE, tall, LANES)
    edges = element_edges.reshape(SIDE, tall, LANES)
    sigma = conductivity.reshape(tall, LANES)
    live = live_slots.reshape(tall, LANES)
    source = adjoint_source.reshape(groups, 1, edge_count)
    forward = forward_field.reshape(groups, 1, edge_count)

    def shape(*dims, kind=jnp.float32):
        return jax.ShapeDtypeStruct(dims, kind)

    field_shape, rim_shape = shape(rows, edge_count), shape(rows, rim)
    sums_shape, terms_shape = shape(rows, LANES), shape(groups, tall, LANES)
    picks_shape = shape(groups * SIDE, tall, LANES)

    across, beside, source, order = call(
        rims_stage,
        pinned(source, neighbour_map),
        [rim_shape, rim_shape, shape(*source.shape), shape(rows, rim, kind=jnp.int32)],
        (
            pltpu.VMEM(neighbour_map.shape, neighbour_map.dtype),
            pltpu.SemaphoreType.DMA((2,)),
        ),
        space=HBM,
    )
    across, beside = swap_across(across), swap_beside(beside)
    kept = [jax.ShapeDtypeStruct(x.shape, x.dtype) for x in (mass, sigma, live, edges, forward)]
    places, blocks, scale, picks, own, rates, mass, sigma, live, edges, forward = call(
        table_stage,
        [*pinned(angular, stiff, mass, sigma, live, edges, forward), source],
        [
            shape(LANES, SIDE * slots, kind=jnp.bfloat16),
            shape(freqs * SIDE * SIDE, tall, LANES),
            sums_shape,
            picks_shape,
            field_shape,
            shape(freqs, tall, LANES),
            *kept,
        ],
        (
            pltpu.SMEM(angular.shape, angular.dtype),
            pltpu.VMEM(stiff.shape, stiff.dtype),
            pltpu.SemaphoreType.DMA((7,)),
        ),
        space=[HBM] * 7 + [VMEM],
        cost=4_000_000,
    )
    front_shapes = [
        shape(rows, 2 * rim),
        picks_shape,
        shape(rows * SIDE * tall, LANES),
        sums_shape,
        shape(rows, 2 * rim),
        rim_shape,
        rim_shape,
    ]
    back_shapes = [terms_shape, sums_shape, field_shape, picks_shape]
    sums, terms = jnp.zeros((rows, LANES), jnp.float32), []
    for step in range(2):
        arrived = (across, beside)
        given = (order, *arrived, scale, picks, blocks, edges, places)
        front = functools.partial(front_stage, polars, step, edge_count)
        if step == 0:
            inverse, *outs = call(
                front, given, [shape(rows, rim, kind=jnp.int32), *front_shapes]
            )
        else:
            outs = call(front, (*given, inverse), front_shapes)
        delta, picks, pieces, forms, rims, across, beside = outs
        across, beside = swap_across(across), swap_beside(beside)
        given = (own, delta, forms, *arrived, sums, picks, pieces, rims, edges, places)
        back = functools.partial(back_stage, polars, step)
        if step == 0:
            heavy, term, sums, own, picks = call(
                back,
                (*given, rates, forward, mass, live),
                [picks_shape, *back_shapes],
                cost=4_000_000,
            )
        else:
            term, sums, own, picks = call(back, (*given, heavy), back_shapes, cost=4_000_000)
        terms.append(term)
    term, sums = call(
        functools.partial(last_stage, polars, 2),
        (own, order, inverse, across, beside, scale, sums, picks, blocks, edges, heavy),
        [terms_shape, sums_shape],
        (pltpu.VMEM((rows, 2 * rim), jnp.float32),),
    )
    terms.append(term)
    term = call(
        combine_stage,
        (gather_all(sums, "dom"), sums, *terms),
        shape(tall, LANES),
    )
    gradient = sum_over(term, "freq").reshape(1, slots)
    updated = sigma.reshape(1, slots) * jnp.exp(-0.5 * jnp.tanh(gradient))
    return gradient, updated


def solution(mesh):
    return jax.shard_map(
        local,
        mesh=mesh,
        in_specs=(
            P("freq"),
            P("dom", None, None),
            P("dom", None, None),
            P("dom", None),
            P("dom", None, None),
            P("dom", None),
            P("freq", None, "dom", None),
            P("freq", None, "dom", None),
            P("dom", None),
        ),
        out_specs=(P("dom", None), P("dom", None)),
        check_vma=False,
    )
```

```python
import functools

import jax
import jax.numpy as jnp
from jax import lax
from jax.experimental import pallas as pl
from jax.experimental.pallas import tpu as pltpu
from jax.sharding import PartitionSpec as P

LANES = 128
SUBLANES = 8
SIDE = 6
VMEM = pl.BlockSpec(memory_space=pltpu.VMEM)
HBM = pl.BlockSpec(memory_space=pltpu.HBM)

PICK_LANES = lax.GatherDimensionNumbers(
    offset_dims=(),
    collapsed_slice_dims=(1,),
    start_index_map=(1,),
    operand_batching_dims=(0,),
    start_indices_batching_dims=(0,),
)


def pick_lanes(block, lanes):
    return lax.gather(
        block,
        lanes[..., None],
        PICK_LANES,
        (1, 1),
        mode=lax.GatherScatterMode.PROMISE_IN_BOUNDS,
    )


def pick_wide(chunks, index):
    lanes = index & (LANES - 1)
    high = index >> 7
    level = [pick_lanes(chunk, lanes) for chunk in chunks]
    bit = 0
    while len(level) > 1:
        odd = (high >> bit) & 1 == 1
        level = [
            jnp.where(odd, level[t + 1], level[t]) if t + 1 < len(level) else level[t]
            for t in range(0, len(level), 2)
        ]
        bit += 1
    return level[0]


def row_ids(rows):
    return lax.broadcasted_iota(jnp.int32, (rows, LANES), 0)


def lane_ids(rows):
    return lax.broadcasted_iota(jnp.int32, (rows, LANES), 1)


def spread(row, rows):
    return jnp.broadcast_to(row, (rows, row.shape[-1]))


def cut(ref):
    return [ref[:, c : c + LANES] for c in range(0, ref.shape[-1], LANES)]


def swap_halves(block):
    return pltpu.roll(block, block.shape[0] // 2, 0)


def doubled(block):
    half = block.shape[0] // 2
    return jnp.where(row_ids(2 * half) < half, block, swap_halves(block))


def lane_sum(block):
    return jnp.broadcast_to(jnp.sum(block, axis=1, keepdims=True), block.shape)


def put_lane(block, lane, value):
    return jnp.where(lane_ids(block.shape[0]) == lane, value, block)


def put_chunks(ref, chunks):
    for c, chunk in enumerate(chunks):
        ref[:, c * LANES : (c + 1) * LANES] = chunk


def is_even():
    return lax.rem(lax.axis_index("dom"), 2) == 0


def put_rims(across_ref, beside_ref, lower, upper):
    even = is_even()
    for c, (low, high) in enumerate(zip(lower, upper)):
        here = slice(c * LANES, (c + 1) * LANES)
        across_ref[:, here] = jnp.where(even, low, high)
        beside_ref[:, here] = jnp.where(even, high, low)


def take_rims(across_ref, beside_ref):
    even = is_even()
    device = lax.axis_index("dom")
    outermost = (device == 0) | (device == lax.axis_size("dom") - 1)
    pairs = [
        (jnp.where(outermost, 0.0, a), b) for a, b in zip(cut(across_ref), cut(beside_ref))
    ]
    prior = [jnp.where(even, a, b) for a, b in pairs]
    above = [jnp.where(even, b, a) for a, b in pairs]
    return prior, above


def picks_of(rows_of_group, edges):
    chunks = [spread(row, edges.shape[1]) for row in rows_of_group]
    return [pick_wide(chunks, edges[j]) for j in range(SIDE)]


def group_rows(ref, g):
    return [ref[g : g + 1, c : c + LANES] for c in range(0, ref.shape[-1], LANES)]


def times_block(entries, base, picked):
    out = []
    for i in range(SIDE):
        total = None
        for j in range(SIDE):
            one = entries[base + SIDE * i + j] * picked[j]
            total = one if total is None else total + one
        out.append(total)
    return out


def weighted_sum(left, right):
    total = None
    for a, b in zip(left, right):
        total = a * b if total is None else total + a * b
    return total


def scatter_side(pieces, edges, places, heights, i):
    depth = SIDE * edges.shape[1]
    rows = pieces.shape[0] // depth
    slots = edges.shape[1] * LANES
    columns = []
    for s in range(edges.shape[1]):
        both = pieces[pl.ds(i * edges.shape[1] + s, rows, stride=depth), :]
        high = spread(edges[i, s : s + 1, :] >> 7, rows)
        stacked = [jnp.where(high == h, both, 0.0) for h in heights]
        columns.append(jnp.concatenate(stacked, axis=0).astype(jnp.bfloat16))
    return lax.dot_general(
        jnp.concatenate(columns, axis=1),
        places[:, i * slots : (i + 1) * slots],
        (((1,), (1,)), ((), ())),
        preferred_element_type=jnp.float32,
    )


def add(total, part):
    return part if total is None else total + part


def parts_joined(total, count):
    rows = total.shape[0] // count
    out = []
    for n in range(count):
        piece = total[rows * n : rows * (n + 1)]
        out.append(piece + swap_halves(piece))
    return out


def scatter(pieces, edges, places, heights):
    total = None
    for i in range(SIDE):
        total = add(total, scatter_side(pieces, edges, places, heights, i))
    return parts_joined(total, len(heights))


def rim_heights(edge_count, rim):
    count = edge_count // LANES
    return [*range(rim), *range(count - rim, count)], list(range(rim, count - rim))


def corrections(from_prior, from_above, order, inverse):
    lower = [pick_wide(from_prior, index) for index in order]
    return lower + [pick_wide(from_above, index) for index in inverse]


def corrected(own, delta):
    rim = len(delta) // 2
    lower = [a + b for a, b in zip(own[:rim], delta[:rim])]
    upper = [a + b for a, b in zip(own[len(own) - rim :], delta[rim:])]
    return lower + own[rim : len(own) - rim] + upper


def squares(chunks, rim, has_prior):
    total = None
    for c, chunk in enumerate(chunks):
        term = chunk * chunk
        if c < rim:
            term = term * (1.0 - has_prior)
        total = term if total is None else total + term
    return total


def start_copies(routes, arrived):
    copies = [
        pltpu.make_async_copy(here, there, arrived.at[n])
        for n, (here, there) in enumerate(routes)
    ]
    for copy in copies:
        copy.start()
    return copies


def stacked_chunk(source, at):
    piece = [source[g, :, at : at + LANES] for g in range(source.shape[0])]
    return jnp.concatenate(piece + piece, axis=0)


def rims_stage(source_in, order_in, across_ref, beside_ref, source, order_ref, order, arrived):
    for copy in start_copies(((source_in, source), (order_in, order)), arrived):
        copy.wait()
    rows, rim = order_ref.shape
    first = row_ids(rows) < rows // 2
    order_ref[...] = spread(order[...], rows)
    numbers = [x.astype(jnp.float32) for x in cut(order_ref)]
    lower = [stacked_chunk(source, c) for c in range(0, rim, LANES)]
    start = source.shape[-1] - rim
    upper = [stacked_chunk(source, start + c) for c in range(0, rim, LANES)]
    lower = [jnp.where(first, x, o) for x, o in zip(lower, numbers)]
    upper = [jnp.where(first, x, 1.0) for x in upper]
    put_rims(across_ref, beside_ref, lower, upper)


def table_stage(
    angular_in,
    stiffness_in,
    mass_in,
    sigma_in,
    live_in,
    edges_in,
    forward_in,
    source,
    places_ref,
    blocks_ref,
    scale_ref,
    picks_ref,
    stacked_ref,
    rates,
    mass,
    sigma,
    live,
    edges,
    forward_ref,
    angular,
    stiffness,
    arrived,
):
    copies = start_copies(
        (
            (edges_in, edges),
            (angular_in, angular),
            (sigma_in, sigma),
            (live_in, live),
            (stiffness_in, stiffness),
            (mass_in, mass),
            (forward_in, forward_ref),
        ),
        arrived,
    )
    copies[0].wait()
    numbers = row_ids(LANES)
    rows = edges.shape[1]

    def body(i, carry):
        for s in range(rows):
            lanes = spread(edges[i, s : s + 1, :] & (LANES - 1), LANES)
            column = pl.ds(pl.multiple_of((i * rows + s) * LANES, LANES), LANES)
            places_ref[:, column] = jnp.where(lanes == numbers, 1.0, 0.0).astype(jnp.bfloat16)
        return carry

    lax.fori_loop(0, SIDE, body, 0)
    count = source.shape[-1]
    put_chunks(stacked_ref, [stacked_chunk(source, c) for c in range(0, count, LANES)])
    put_picks(picks_ref, stacked_ref, edges, source.shape[0])
    for copy in copies[1:]:
        copy.wait()
    for f in range(angular.shape[0]):
        rates[f] = jnp.full(rates.shape[1:], angular[f], jnp.float32)
    alive = live[...].astype(jnp.float32)
    weight = sigma[...]
    freqs = rates.shape[0]
    peak = None
    for i in range(SIDE):
        for f in range(freqs):
            entry = (SIDE + 1) * i
            size = stiffness[entry] + rates[f] * weight * mass[entry]
            peak = size if peak is None else jnp.maximum(peak, size)
    peak = jnp.max(peak * alive, axis=1, keepdims=True)
    scale = jnp.broadcast_to(jnp.max(peak, axis=0, keepdims=True), scale_ref.shape)
    scale_ref[...] = scale
    alive = alive / scale[:1, :1]
    for entry in range(SIDE * SIDE):
        stiff = stiffness[entry] * alive
        heavy = mass[entry] * (weight * alive)
        for f in range(freqs):
            blocks_ref[f * SIDE * SIDE + entry] = stiff + rates[f] * heavy


def put_picks(picks_ref, field, edges, groups):
    for g in range(groups):
        for j, value in enumerate(picks_of(group_rows(field, g), edges)):
            picks_ref[g * SIDE + j] = value


def pick_rims(rows, index, edge_count):
    rim = len(rows) // 2
    start = edge_count - rim * LANES
    lower = pick_wide([spread(row, index.shape[0]) for row in rows[:rim]], index)
    upper = pick_wide([spread(row, index.shape[0]) for row in rows[rim:]], index - start)
    lower = jnp.where(index < rim * LANES, lower, 0.0)
    return lower + jnp.where(index >= start, upper, 0.0)


def corrected_picks(delta_ref, own_picks, edges, edge_count):
    out = []
    for g in range(delta_ref.shape[0] // 2):
        delta = group_rows(delta_ref, g)
        out.append(
            [
                own_picks[g * SIDE + j] + pick_rims(delta, edges[j], edge_count)
                for j in range(SIDE)
            ]
        )
    return out


def products(blocks, picked, polars, i):
    out = []
    for g, mine in enumerate(picked):
        base = (g // polars) * SIDE * SIDE + SIDE * i
        out.append(weighted_sum([blocks[base + j] for j in range(SIDE)], mine))
    return out


def rows_of_forms(forms, rows):
    out = jnp.zeros((rows, LANES), jnp.float32)
    for g, form in enumerate(forms):
        row = jnp.sum(form, axis=0, keepdims=True)
        out = jnp.where(row_ids(rows) == g, spread(row, rows), out)
    return out


def invert(above, groups, rows):
    above_order = jnp.concatenate([x[groups : groups + 1] for x in above], axis=1)
    rim = above_order.shape[1]
    slot = lax.broadcasted_iota(jnp.int32, (rim, rim), 0).astype(jnp.float32)
    match = jnp.where(spread(above_order, rim) == slot, 1.0, 0.0).astype(jnp.bfloat16)
    numbers = lax.broadcasted_iota(jnp.int32, (2 * rows, rim), 1).astype(jnp.bfloat16)
    inverse = lax.dot_general(
        numbers, match, (((1,), (1,)), ((), ())), preferred_element_type=jnp.float32
    )
    return inverse[:rows].astype(jnp.int32)


def rescaled(block, inverse_scale, step):
    ratio = swap_halves(block) * inverse_scale
    for _ in range(step):
        block = block * ratio
    return doubled(block)


def unpacked(blocks, with_scale, inverse_scale, step):
    ratio = doubled(swap_halves(with_scale)) * inverse_scale
    out = []
    for block in blocks:
        for _ in range(step):
            block = block * ratio
        out += [doubled(block), doubled(swap_halves(block))]
    return out


def front_stage(
    polars,
    step,
    edge_count,
    order_ref,
    across_in,
    beside_in,
    scale_in,
    own_picks,
    blocks,
    edges,
    places,
    *rest,
):
    if step == 0:
        inverse_ref, *rest = rest
    else:
        inverse_in, *rest = rest
    delta_ref, picks_ref, pieces, forms_ref, rims_ref, across_ref, beside_ref = rest
    rows = delta_ref.shape[0]
    groups = rows // 2
    first = row_ids(rows) < groups
    scale = scale_in[...]
    prior, above = take_rims(across_in, beside_in)
    if step == 0:
        inverse_ref[...] = invert(above, groups, rows)
        inverse = cut(inverse_ref)
        prior, above = [doubled(x) for x in prior], [doubled(x) for x in above]
    else:
        inverse = cut(inverse_in)
        inverse_scale = 1.0 / scale
        prior = [rescaled(x, inverse_scale, step) for x in prior]
        above = [rescaled(x, inverse_scale, step) for x in above]
    put_chunks(delta_ref, corrections(prior, above, cut(order_ref), inverse))

    picked = corrected_picks(delta_ref, own_picks, edges, edge_count)
    for g in range(groups):
        for j in range(SIDE):
            picks_ref[g * SIDE + j] = picked[g][j]
    rim = len(prior)
    heights = rim_heights(edge_count, rim)[0]
    tall = edges.shape[1]
    forms, total = [None] * groups, None
    for i in range(SIDE):
        for g, value in enumerate(products(blocks, picked, polars, i)):
            forms[g] = add(forms[g], picked[g][i] * value)
            coarse = value.astype(jnp.bfloat16).astype(jnp.float32)
            for part, piece in enumerate((coarse, value - coarse)):
                at = ((part * groups + g) * SIDE + i) * tall
                pieces[at : at + tall, :] = piece
        total = add(total, scatter_side(pieces, edges, places, heights, i))
    forms_ref[...] = rows_of_forms(forms, rows)
    chunks = parts_joined(total, len(heights))
    put_chunks(rims_ref, chunks)
    lower, upper = chunks[:rim], chunks[rim:]
    if step == 0:
        lower = [jnp.where(first, x, scale) for x in lower]
        upper = [jnp.where(first, x, scale) for x in upper]
    else:
        lower = [jnp.where(first, a, b) for a, b in zip(lower[::2], lower[1::2])]
        upper = [jnp.where(first, a, b) for a, b in zip(upper[::2], upper[1::2])]
    put_rims(across_ref, beside_ref, lower, upper)


def inner_products(step, sums, own, delta, forms, across_in, beside_in):
    rows = sums.shape[0]
    first = row_ids(rows) < rows // 2
    prior, _ = take_rims(across_in, beside_in)
    has_prior = jnp.where(first, swap_halves(prior[0]), prior[0])
    has_prior = spread(jnp.where(has_prior[:1, :1] > 0.0, 1.0, 0.0), rows)
    field = corrected(own, delta)
    sums = put_lane(sums, 2 * step, lane_sum(squares(field, len(delta) // 2, has_prior)))
    return put_lane(sums, 2 * step + 1, lane_sum(forms))


def back_stage(
    polars,
    step,
    own,
    delta,
    forms,
    across_in,
    beside_in,
    sums_in,
    picks,
    pieces,
    rims,
    edges,
    places,
    *rest,
):
    if step == 0:
        rates, forward, mass, live, heavy, terms_ref, sums_ref, image_ref, picks_ref = rest
    else:
        heavy, terms_ref, sums_ref, image_ref, picks_ref = rest
    rows, edge_count = own.shape
    groups = rows // 2
    rim = rims.shape[-1] // LANES // 2
    outer = cut(rims)
    inner = scatter(pieces, edges, places, rim_heights(edge_count, rim)[1])
    put_chunks(image_ref, outer[:rim] + inner + outer[rim:])
    put_picks(picks_ref, image_ref, edges, groups)
    if step == 0:
        dead = -live[...].astype(jnp.float32)
        for g in range(groups):
            row = [forward[g, :, c : c + LANES] for c in range(0, edge_count, LANES)]
            values = times_block(mass, 0, picks_of(row, edges))
            factor = dead * rates[g // polars]
            for i in range(SIDE):
                heavy[g * SIDE + i] = factor * values[i]
    for g in range(groups):
        side = range(g * SIDE, (g + 1) * SIDE)
        terms_ref[g] = weighted_sum([picks[i] for i in side], [heavy[i] for i in side])
    sums_ref[...] = inner_products(
        step, sums_in[...], cut(own), cut(delta), forms[...], across_in, beside_in
    )


def last_stage(
    polars,
    step,
    own,
    order_ref,
    inverse_in,
    across_in,
    beside_in,
    across_before,
    beside_before,
    scale_in,
    sums_in,
    own_picks,
    blocks,
    edges,
    heavy,
    terms_ref,
    sums_ref,
    delta_ref,
):
    rows, edge_count = own.shape
    first = row_ids(rows) < rows // 2
    scale = scale_in[...]
    inverse_scale = 1.0 / scale
    prior, above = (
        unpacked(now, before[0], inverse_scale, step)
        for now, before in zip(
            take_rims(across_in, beside_in), take_rims(across_before, beside_before)
        )
    )
    put_chunks(delta_ref, corrections(prior, above, cut(order_ref), cut(inverse_in)))

    picked = corrected_picks(delta_ref, own_picks, edges, edge_count)
    forms = [None] * len(picked)
    for i in range(SIDE):
        for g, value in enumerate(products(blocks, picked, polars, i)):
            forms[g] = add(forms[g], picked[g][i] * value)
    for g, mine in enumerate(picked):
        terms_ref[g] = weighted_sum(mine, [heavy[g * SIDE + i] for i in range(SIDE)])
    forms = rows_of_forms(forms, rows)
    sums = inner_products(
        step, sums_in[...], cut(own), cut(delta_ref), forms, across_before, beside_before
    )
    sums_ref[...] = jnp.where(first, sums, scale)


def combine_stage(everyone, sums_in, terms0, terms1, terms2, out_ref):
    rows = sums_in.shape[0]
    groups = rows // 2
    first = row_ids(rows) < groups

    def scale_of(block):
        return jnp.where(first, swap_halves(block), block)

    parts = [everyone[q] for q in range(everyone.shape[0])]
    scales = [scale_of(block) for block in parts]
    top = functools.reduce(jnp.maximum, scales)
    lanes = lane_ids(rows)
    inverse_top = 1.0 / top
    total = None
    for block, scale in zip(parts, scales):
        ratio = scale * inverse_top
        power = jnp.ones_like(ratio)
        factor = jnp.ones_like(ratio)
        for k in range(1, 6):
            power = power * ratio
            factor = jnp.where(lanes == k, power, factor)
        term = block * factor
        total = term if total is None else total + term
    m = [jnp.broadcast_to(total[:, k : k + 1], (rows, LANES)) for k in range(6)]
    l1 = m[2] / m[1]
    l2 = m[3] / m[1]
    d2 = m[3] - l1 * m[2]
    cross = m[4] - l2 * m[2]
    l3 = cross / d2
    d3 = m[5] - l2 * m[3] - l3 * cross
    y1 = m[1] - l1 * m[0]
    y2 = m[2] - l2 * m[0] - l3 * y1
    c2 = y2 / d3
    c1 = y1 / d2 - l3 * c2
    c0 = m[0] / m[1] - l1 * c1 - l2 * c2
    mine = scale_of(sums_in[...]) * inverse_top
    c0 = c0 * inverse_top
    c1 = c1 * mine * inverse_top
    c2 = c2 * mine * mine * inverse_top
    out = None
    for terms, c in ((terms0, c0), (terms1, c1), (terms2, c2)):
        for g in range(groups):
            one = terms[g] * spread(c[g : g + 1], out_ref.shape[0])
            out = one if out is None else out + one
    out_ref[...] = out


def pinned(*arguments):
    return [pltpu.with_memory_space_constraint(x, pltpu.HBM) for x in arguments]


def call(kernel, arguments, outs, scratch=(), space=VMEM, cost=0):
    return pl.pallas_call(
        kernel,
        out_shape=outs,
        in_specs=space if isinstance(space, list) else [space] * len(arguments),
        out_specs=jax.tree.map(lambda _: VMEM, outs),
        scratch_shapes=list(scratch),
        cost_estimate=pl.CostEstimate(flops=cost, bytes_accessed=cost, transcendentals=0),
        compiler_params=pltpu.CompilerParams(vmem_limit_bytes=16 * 1024 * 1024),
    )(*arguments)


def swap_across(block):
    size, planes = lax.axis_size("dom"), lax.axis_size("freq")
    route = []
    for f in range(planes):
        for p in range(size):
            if p in (0, size - 1) and planes % 2 == 0:
                there = (f ^ 1) * size + p
            elif p % 2:
                there = f * size + (p + 1) % size
            else:
                there = f * size + (p - 1) % size
            route.append((f * size + p, there))
    return lax.ppermute(block, ("freq", "dom"), route)


def swap_beside(block):
    return lax.ppermute(block, "dom", [(i, i ^ 1) for i in range(lax.axis_size("dom"))])


def gather_all(block, axis):
    size = lax.axis_size(axis)
    copies = jnp.broadcast_to(block[None], (size, *block.shape))
    return lax.all_to_all(copies, axis, 0, 0)


def sum_over(block, axis):
    size = lax.axis_size(axis)
    if size & (size - 1):
        return jnp.sum(gather_all(block, axis), axis=0)
    step = size // 2
    while step > 0:
        block = block + lax.ppermute(block, axis, [(i, i ^ step) for i in range(size)])
        step //= 2
    return block


def local(
    angular,
    stiffness,
    mass_matrix,
    conductivity,
    element_edges,
    live_slots,
    adjoint_source,
    forward_field,
    neighbour_map,
):
    freqs = angular.shape[0]
    polars = adjoint_source.shape[1]
    groups = freqs * polars
    rows = 2 * groups
    edge_count = adjoint_source.shape[-1]
    rim = neighbour_map.shape[-1]
    slots = element_edges.shape[-1]
    tall = slots // LANES
    stiff = stiffness.reshape(SIDE * SIDE, tall, LANES)
    mass = mass_matrix.reshape(SIDE * SIDE, tall, LANES)
    edges = element_edges.reshape(SIDE, tall, LANES)
    sigma = conductivity.reshape(tall, LANES)
    live = live_slots.reshape(tall, LANES)
    source = adjoint_source.reshape(groups, 1, edge_count)
    forward = forward_field.reshape(groups, 1, edge_count)

    def shape(*dims, kind=jnp.float32):
        return jax.ShapeDtypeStruct(dims, kind)

    field_shape, rim_shape = shape(rows, edge_count), shape(rows, rim)
    sums_shape, terms_shape = shape(rows, LANES), shape(groups, tall, LANES)
    picks_shape = shape(groups * SIDE, tall, LANES)

    across, beside, source, order = call(
        rims_stage,
        pinned(source, neighbour_map),
        [rim_shape, rim_shape, shape(*source.shape), shape(rows, rim, kind=jnp.int32)],
        (
            pltpu.VMEM(neighbour_map.shape, neighbour_map.dtype),
            pltpu.SemaphoreType.DMA((2,)),
        ),
        space=HBM,
    )
    across, beside = swap_across(across), swap_beside(beside)
    kept = [jax.ShapeDtypeStruct(x.shape, x.dtype) for x in (mass, sigma, live, edges, forward)]
    places, blocks, scale, picks, own, rates, mass, sigma, live, edges, forward = call(
        table_stage,
        [*pinned(angular, stiff, mass, sigma, live, edges, forward), source],
        [
            shape(LANES, SIDE * slots, kind=jnp.bfloat16),
            shape(freqs * SIDE * SIDE, tall, LANES),
            sums_shape,
            picks_shape,
            field_shape,
            shape(freqs, tall, LANES),
            *kept,
        ],
        (
            pltpu.SMEM(angular.shape, angular.dtype),
            pltpu.VMEM(stiff.shape, stiff.dtype),
            pltpu.SemaphoreType.DMA((7,)),
        ),
        space=[HBM] * 7 + [VMEM],
        cost=4_000_000,
    )
    front_shapes = [
        shape(rows, 2 * rim),
        picks_shape,
        shape(rows * SIDE * tall, LANES),
        sums_shape,
        shape(rows, 2 * rim),
        rim_shape,
        rim_shape,
    ]
    back_shapes = [terms_shape, sums_shape, field_shape, picks_shape]
    sums, terms = jnp.zeros((rows, LANES), jnp.float32), []
    for step in range(2):
        arrived = (across, beside)
        given = (order, *arrived, scale, picks, blocks, edges, places)
        front = functools.partial(front_stage, polars, step, edge_count)
        if step == 0:
            inverse, *outs = call(
                front, given, [shape(rows, rim, kind=jnp.int32), *front_shapes]
            )
        else:
            outs = call(
                front, (*given, inverse), [*front_shapes[:-2], *[shape(rows, rim // 2)] * 2]
            )
        delta, picks, pieces, forms, rims, across, beside = outs
        across, beside = swap_across(across), swap_beside(beside)
        given = (own, delta, forms, *arrived, sums, picks, pieces, rims, edges, places)
        back = functools.partial(back_stage, polars, step)
        if step == 0:
            heavy, term, sums, own, picks = call(
                back,
                (*given, rates, forward, mass, live),
                [picks_shape, *back_shapes],
                cost=4_000_000,
            )
        else:
            term, sums, own, picks = call(back, (*given, heavy), back_shapes, cost=4_000_000)
        terms.append(term)
    term, sums = call(
        functools.partial(last_stage, polars, 2),
        (
            own,
            order,
            inverse,
            across,
            beside,
            *arrived,
            scale,
            sums,
            picks,
            blocks,
            edges,
            heavy,
        ),
        [terms_shape, sums_shape],
        (pltpu.VMEM((rows, 2 * rim), jnp.float32),),
    )
    terms.append(term)
    term = call(
        combine_stage,
        (gather_all(sums, "dom"), sums, *terms),
        shape(tall, LANES),
    )
    gradient = sum_over(term, "freq").reshape(1, slots)
    updated = sigma.reshape(1, slots) * jnp.exp(-0.5 * jnp.tanh(gradient))
    return gradient, updated


def solution(mesh):
    return jax.shard_map(
        local,
        mesh=mesh,
        in_specs=(
            P("freq"),
            P("dom", None, None),
            P("dom", None, None),
            P("dom", None),
            P("dom", None, None),
            P("dom", None),
            P("freq", None, "dom", None),
            P("freq", None, "dom", None),
            P("dom", None),
        ),
        out_specs=(P("dom", None), P("dom", None)),
        check_vma=False,
    )
```

```python
import functools

import jax
import jax.numpy as jnp
from jax import lax
from jax.experimental import pallas as pl
from jax.experimental.pallas import tpu as pltpu
from jax.sharding import PartitionSpec as P

LANES = 128
SUBLANES = 8
SIDE = 6
VMEM = pl.BlockSpec(memory_space=pltpu.VMEM)
HBM = pl.BlockSpec(memory_space=pltpu.HBM)

PICK_LANES = lax.GatherDimensionNumbers(
    offset_dims=(),
    collapsed_slice_dims=(1,),
    start_index_map=(1,),
    operand_batching_dims=(0,),
    start_indices_batching_dims=(0,),
)


def pick_lanes(block, lanes):
    return lax.gather(
        block,
        lanes[..., None],
        PICK_LANES,
        (1, 1),
        mode=lax.GatherScatterMode.PROMISE_IN_BOUNDS,
    )


def pick_wide(chunks, index):
    lanes = index & (LANES - 1)
    high = index >> 7
    level = [pick_lanes(chunk, lanes) for chunk in chunks]
    bit = 0
    while len(level) > 1:
        odd = (high >> bit) & 1 == 1
        level = [
            jnp.where(odd, level[t + 1], level[t]) if t + 1 < len(level) else level[t]
            for t in range(0, len(level), 2)
        ]
        bit += 1
    return level[0]


def row_ids(rows):
    return lax.broadcasted_iota(jnp.int32, (rows, LANES), 0)


def lane_ids(rows):
    return lax.broadcasted_iota(jnp.int32, (rows, LANES), 1)


def spread(row, rows):
    return jnp.broadcast_to(row, (rows, row.shape[-1]))


def cut(ref):
    return [ref[:, c : c + LANES] for c in range(0, ref.shape[-1], LANES)]


def swap_halves(block):
    return pltpu.roll(block, block.shape[0] // 2, 0)


def doubled(block):
    half = block.shape[0] // 2
    return jnp.where(row_ids(2 * half) < half, block, swap_halves(block))


def lane_sum(block):
    return jnp.broadcast_to(jnp.sum(block, axis=1, keepdims=True), block.shape)


def put_lane(block, lane, value):
    return jnp.where(lane_ids(block.shape[0]) == lane, value, block)


def put_chunks(ref, chunks):
    for c, chunk in enumerate(chunks):
        ref[:, c * LANES : (c + 1) * LANES] = chunk


def is_even():
    return lax.rem(lax.axis_index("dom"), 2) == 0


def put_rims(across_ref, beside_ref, lower, upper):
    even = is_even()
    for c, (low, high) in enumerate(zip(lower, upper)):
        here = slice(c * LANES, (c + 1) * LANES)
        across_ref[:, here] = jnp.where(even, low, high)
        beside_ref[:, here] = jnp.where(even, high, low)


def take_rims(across_ref, beside_ref):
    even = is_even()
    device = lax.axis_index("dom")
    outermost = (device == 0) | (device == lax.axis_size("dom") - 1)
    pairs = [
        (jnp.where(outermost, 0.0, a), b) for a, b in zip(cut(across_ref), cut(beside_ref))
    ]
    prior = [jnp.where(even, a, b) for a, b in pairs]
    above = [jnp.where(even, b, a) for a, b in pairs]
    return prior, above


def picks_of(rows_of_group, edges):
    chunks = [spread(row, edges.shape[1]) for row in rows_of_group]
    return [pick_wide(chunks, edges[j]) for j in range(SIDE)]


def group_rows(ref, g):
    return [ref[g : g + 1, c : c + LANES] for c in range(0, ref.shape[-1], LANES)]


def times_block(entries, base, picked):
    out = []
    for i in range(SIDE):
        total = None
        for j in range(SIDE):
            one = entries[base + SIDE * i + j] * picked[j]
            total = one if total is None else total + one
        out.append(total)
    return out


def weighted_sum(left, right):
    total = None
    for a, b in zip(left, right):
        total = a * b if total is None else total + a * b
    return total


def scatter_side(pieces, edges, places, heights, i):
    depth = SIDE * edges.shape[1]
    rows = pieces.shape[0] // depth
    slots = edges.shape[1] * LANES
    columns = []
    for s in range(edges.shape[1]):
        both = pieces[pl.ds(i * edges.shape[1] + s, rows, stride=depth), :]
        high = spread(edges[i, s : s + 1, :] >> 7, rows)
        stacked = [jnp.where(high == h, both, 0.0) for h in heights]
        columns.append(jnp.concatenate(stacked, axis=0).astype(jnp.bfloat16))
    return lax.dot_general(
        jnp.concatenate(columns, axis=1),
        places[:, i * slots : (i + 1) * slots],
        (((1,), (1,)), ((), ())),
        preferred_element_type=jnp.float32,
    )


def add(total, part):
    return part if total is None else total + part


def parts_joined(total, count):
    rows = total.shape[0] // count
    out = []
    for n in range(count):
        piece = total[rows * n : rows * (n + 1)]
        out.append(piece + swap_halves(piece))
    return out


def scatter(pieces, edges, places, heights):
    total = None
    for i in range(SIDE):
        total = add(total, scatter_side(pieces, edges, places, heights, i))
    return parts_joined(total, len(heights))


def rim_heights(edge_count, rim):
    count = edge_count // LANES
    return [*range(rim), *range(count - rim, count)], list(range(rim, count - rim))


def corrections(from_prior, from_above, order, inverse):
    lower = [pick_wide(from_prior, index) for index in order]
    return lower + [pick_wide(from_above, index) for index in inverse]


def corrected(own, delta):
    rim = len(delta) // 2
    lower = [a + b for a, b in zip(own[:rim], delta[:rim])]
    upper = [a + b for a, b in zip(own[len(own) - rim :], delta[rim:])]
    return lower + own[rim : len(own) - rim] + upper


def squares(chunks, rim, has_prior):
    total = None
    for c, chunk in enumerate(chunks):
        term = chunk * chunk
        if c < rim:
            term = term * (1.0 - has_prior)
        total = term if total is None else total + term
    return total


def start_copies(routes, arrived):
    copies = [
        pltpu.make_async_copy(here, there, arrived.at[n])
        for n, (here, there) in enumerate(routes)
    ]
    for copy in copies:
        copy.start()
    return copies


def stacked_chunk(source, at):
    piece = [source[g, :, at : at + LANES] for g in range(source.shape[0])]
    return jnp.concatenate(piece + piece, axis=0)


def rims_stage(source_in, order_in, across_ref, beside_ref, source, order_ref, order, arrived):
    for copy in start_copies(((source_in, source), (order_in, order)), arrived):
        copy.wait()
    rows, rim = order_ref.shape
    first = row_ids(rows) < rows // 2
    order_ref[...] = spread(order[...], rows)
    numbers = [x.astype(jnp.float32) for x in cut(order_ref)]
    lower = [stacked_chunk(source, c) for c in range(0, rim, LANES)]
    start = source.shape[-1] - rim
    upper = [stacked_chunk(source, start + c) for c in range(0, rim, LANES)]
    lower = [jnp.where(first, x, o) for x, o in zip(lower, numbers)]
    upper = [jnp.where(first, x, 1.0) for x in upper]
    put_rims(across_ref, beside_ref, lower, upper)


def table_stage(
    angular_in,
    stiffness_in,
    mass_in,
    sigma_in,
    live_in,
    edges_in,
    forward_in,
    source,
    places_ref,
    blocks_ref,
    scale_ref,
    picks_ref,
    stacked_ref,
    rates,
    mass,
    sigma,
    live,
    edges,
    forward_ref,
    angular,
    stiffness,
    arrived,
):
    copies = start_copies(
        (
            (edges_in, edges),
            (angular_in, angular),
            (sigma_in, sigma),
            (live_in, live),
            (stiffness_in, stiffness),
            (mass_in, mass),
            (forward_in, forward_ref),
        ),
        arrived,
    )
    copies[0].wait()
    numbers = row_ids(LANES)
    rows = edges.shape[1]

    def body(i, carry):
        for s in range(rows):
            lanes = spread(edges[i, s : s + 1, :] & (LANES - 1), LANES)
            column = pl.ds(pl.multiple_of((i * rows + s) * LANES, LANES), LANES)
            places_ref[:, column] = jnp.where(lanes == numbers, 1.0, 0.0).astype(jnp.bfloat16)
        return carry

    lax.fori_loop(0, SIDE, body, 0)
    count = source.shape[-1]
    put_chunks(stacked_ref, [stacked_chunk(source, c) for c in range(0, count, LANES)])
    put_picks(picks_ref, stacked_ref, edges, source.shape[0])
    for copy in copies[1:]:
        copy.wait()
    for f in range(angular.shape[0]):
        rates[f] = jnp.full(rates.shape[1:], angular[f], jnp.float32)
    alive = live[...].astype(jnp.float32)
    weight = sigma[...]
    freqs = rates.shape[0]
    peak = None
    for i in range(SIDE):
        for f in range(freqs):
            entry = (SIDE + 1) * i
            size = stiffness[entry] + rates[f] * weight * mass[entry]
            peak = size if peak is None else jnp.maximum(peak, size)
    peak = jnp.max(peak * alive, axis=1, keepdims=True)
    scale = jnp.broadcast_to(jnp.max(peak, axis=0, keepdims=True), scale_ref.shape)
    scale_ref[...] = scale
    alive = alive / scale[:1, :1]
    for entry in range(SIDE * SIDE):
        stiff = stiffness[entry] * alive
        heavy = mass[entry] * (weight * alive)
        for f in range(freqs):
            blocks_ref[f * SIDE * SIDE + entry] = stiff + rates[f] * heavy


def put_picks(picks_ref, field, edges, groups):
    for g in range(groups):
        for j, value in enumerate(picks_of(group_rows(field, g), edges)):
            picks_ref[g * SIDE + j] = value


def pick_rims(rows, index, edge_count):
    rim = len(rows) // 2
    start = edge_count - rim * LANES
    lower = pick_wide([spread(row, index.shape[0]) for row in rows[:rim]], index)
    upper = pick_wide([spread(row, index.shape[0]) for row in rows[rim:]], index - start)
    lower = jnp.where(index < rim * LANES, lower, 0.0)
    return lower + jnp.where(index >= start, upper, 0.0)


def corrected_picks(delta_ref, own_picks, edges, edge_count):
    out = []
    for g in range(delta_ref.shape[0] // 2):
        delta = group_rows(delta_ref, g)
        out.append(
            [
                own_picks[g * SIDE + j] + pick_rims(delta, edges[j], edge_count)
                for j in range(SIDE)
            ]
        )
    return out


def products(blocks, picked, polars, i):
    out = []
    for g, mine in enumerate(picked):
        base = (g // polars) * SIDE * SIDE + SIDE * i
        out.append(weighted_sum([blocks[base + j] for j in range(SIDE)], mine))
    return out


def rows_of_forms(forms, rows):
    out = jnp.zeros((rows, LANES), jnp.float32)
    for g, form in enumerate(forms):
        row = jnp.sum(form, axis=0, keepdims=True)
        out = jnp.where(row_ids(rows) == g, spread(row, rows), out)
    return out


def invert(above, groups, rows):
    above_order = jnp.concatenate([x[groups : groups + 1] for x in above], axis=1)
    rim = above_order.shape[1]
    slot = lax.broadcasted_iota(jnp.int32, (rim, rim), 0).astype(jnp.float32)
    match = jnp.where(spread(above_order, rim) == slot, 1.0, 0.0).astype(jnp.bfloat16)
    numbers = lax.broadcasted_iota(jnp.int32, (2 * rows, rim), 1).astype(jnp.bfloat16)
    inverse = lax.dot_general(
        numbers, match, (((1,), (1,)), ((), ())), preferred_element_type=jnp.float32
    )
    return inverse[:rows].astype(jnp.int32)


def rescaled(block, inverse_scale, step):
    ratio = swap_halves(block) * inverse_scale
    for _ in range(step):
        block = block * ratio
    return doubled(block)


def unpacked(blocks, with_scale, inverse_scale, step):
    ratio = doubled(swap_halves(with_scale)) * inverse_scale
    out = []
    for block in blocks:
        for _ in range(step):
            block = block * ratio
        out += [doubled(block), doubled(swap_halves(block))]
    return out


def front_stage(
    polars,
    step,
    edge_count,
    order_ref,
    across_in,
    beside_in,
    scale_in,
    own_picks,
    blocks,
    edges,
    places,
    *rest,
):
    if step == 0:
        inverse_ref, *rest = rest
    else:
        inverse_in, *rest = rest
    delta_ref, picks_ref, pieces, forms_ref, rims_ref, across_ref, beside_ref = rest
    rows = delta_ref.shape[0]
    groups = rows // 2
    first = row_ids(rows) < groups
    scale = scale_in[...]
    prior, above = take_rims(across_in, beside_in)
    if step == 0:
        inverse_ref[...] = invert(above, groups, rows)
        inverse = cut(inverse_ref)
        prior, above = [doubled(x) for x in prior], [doubled(x) for x in above]
    else:
        inverse = cut(inverse_in)
        inverse_scale = 1.0 / scale
        prior = [rescaled(x, inverse_scale, step) for x in prior]
        above = [rescaled(x, inverse_scale, step) for x in above]
    put_chunks(delta_ref, corrections(prior, above, cut(order_ref), inverse))

    picked = corrected_picks(delta_ref, own_picks, edges, edge_count)
    for g in range(groups):
        for j in range(SIDE):
            picks_ref[g * SIDE + j] = picked[g][j]
    rim = len(prior)
    heights = rim_heights(edge_count, rim)[0]
    tall = edges.shape[1]
    forms, total = [None] * groups, None
    for i in range(SIDE):
        for g, value in enumerate(products(blocks, picked, polars, i)):
            forms[g] = add(forms[g], picked[g][i] * value)
            coarse = value.astype(jnp.bfloat16).astype(jnp.float32)
            for part, piece in enumerate((coarse, value - coarse)):
                at = ((part * groups + g) * SIDE + i) * tall
                pieces[at : at + tall, :] = piece
        total = add(total, scatter_side(pieces, edges, places, heights, i))
    forms_ref[...] = rows_of_forms(forms, rows)
    chunks = parts_joined(total, len(heights))
    put_chunks(rims_ref, chunks)
    lower, upper = chunks[:rim], chunks[rim:]
    if step == 0:
        lower = [jnp.where(first, x, scale) for x in lower]
        upper = [jnp.where(first, x, scale) for x in upper]
    else:
        lower = [jnp.where(first, a, b) for a, b in zip(lower[::2], lower[1::2])]
        upper = [jnp.where(first, a, b) for a, b in zip(upper[::2], upper[1::2])]
    put_rims(across_ref, beside_ref, lower, upper)


def inner_products(step, sums, own, delta, forms, across_in, beside_in):
    rows = sums.shape[0]
    first = row_ids(rows) < rows // 2
    prior, _ = take_rims(across_in, beside_in)
    has_prior = jnp.where(first, swap_halves(prior[0]), prior[0])
    has_prior = spread(jnp.where(has_prior[:1, :1] > 0.0, 1.0, 0.0), rows)
    field = corrected(own, delta)
    sums = put_lane(sums, 2 * step, lane_sum(squares(field, len(delta) // 2, has_prior)))
    return put_lane(sums, 2 * step + 1, lane_sum(forms))


def back_stage(
    polars,
    step,
    own,
    delta,
    forms,
    across_in,
    beside_in,
    sums_in,
    picks,
    pieces,
    rims,
    edges,
    places,
    *rest,
):
    if step == 0:
        rates, forward, mass, live, heavy, terms_ref, sums_ref, image_ref, picks_ref = rest
    else:
        heavy, terms_ref, sums_ref, image_ref, picks_ref = rest
    rows, edge_count = own.shape
    groups = rows // 2
    rim = rims.shape[-1] // LANES // 2
    outer = cut(rims)
    inner = scatter(pieces, edges, places, rim_heights(edge_count, rim)[1])
    put_chunks(image_ref, outer[:rim] + inner + outer[rim:])
    put_picks(picks_ref, image_ref, edges, groups)
    if step == 0:
        dead = -live[...].astype(jnp.float32)
        for g in range(groups):
            row = [forward[g, :, c : c + LANES] for c in range(0, edge_count, LANES)]
            values = times_block(mass, 0, picks_of(row, edges))
            factor = dead * rates[g // polars]
            for i in range(SIDE):
                heavy[g * SIDE + i] = factor * values[i]
    for g in range(groups):
        side = range(g * SIDE, (g + 1) * SIDE)
        terms_ref[g] = weighted_sum([picks[i] for i in side], [heavy[i] for i in side])
    sums_ref[...] = inner_products(
        step, sums_in[...], cut(own), cut(delta), forms[...], across_in, beside_in
    )


def last_stage(
    polars,
    step,
    own,
    order_ref,
    inverse_in,
    across_in,
    beside_in,
    across_before,
    beside_before,
    scale_in,
    sums_in,
    own_picks,
    blocks,
    edges,
    heavy,
    terms_ref,
    sums_ref,
    delta_ref,
):
    rows, edge_count = own.shape
    first = row_ids(rows) < rows // 2
    scale = scale_in[...]
    inverse_scale = 1.0 / scale
    prior, above = (
        unpacked(now, before[0], inverse_scale, step)
        for now, before in zip(
            take_rims(across_in, beside_in), take_rims(across_before, beside_before)
        )
    )
    put_chunks(delta_ref, corrections(prior, above, cut(order_ref), cut(inverse_in)))

    picked = corrected_picks(delta_ref, own_picks, edges, edge_count)
    forms = [None] * len(picked)
    for i in range(SIDE):
        for g, value in enumerate(products(blocks, picked, polars, i)):
            forms[g] = add(forms[g], picked[g][i] * value)
    for g, mine in enumerate(picked):
        terms_ref[g] = weighted_sum(mine, [heavy[g * SIDE + i] for i in range(SIDE)])
    forms = rows_of_forms(forms, rows)
    sums = inner_products(
        step, sums_in[...], cut(own), cut(delta_ref), forms, across_before, beside_before
    )
    sums_ref[...] = jnp.where(first, sums, scale)


def combine_stage(everyone, sums_in, terms0, terms1, terms2, out_ref):
    rows = sums_in.shape[0]
    groups = rows // 2
    first = row_ids(rows) < groups

    def scale_of(block):
        return jnp.where(first, swap_halves(block), block)

    parts = [everyone[q] for q in range(everyone.shape[0])]
    scales = [scale_of(block) for block in parts]
    top = functools.reduce(jnp.maximum, scales)
    lanes = lane_ids(rows)
    inverse_top = 1.0 / top
    total = None
    for block, scale in zip(parts, scales):
        ratio = scale * inverse_top
        power = jnp.ones_like(ratio)
        factor = jnp.ones_like(ratio)
        for k in range(1, 6):
            power = power * ratio
            factor = jnp.where(lanes == k, power, factor)
        term = block * factor
        total = term if total is None else total + term
    m = [jnp.broadcast_to(total[:, k : k + 1], (rows, LANES)) for k in range(6)]
    l1 = m[2] / m[1]
    l2 = m[3] / m[1]
    d2 = m[3] - l1 * m[2]
    cross = m[4] - l2 * m[2]
    l3 = cross / d2
    d3 = m[5] - l2 * m[3] - l3 * cross
    y1 = m[1] - l1 * m[0]
    y2 = m[2] - l2 * m[0] - l3 * y1
    c2 = y2 / d3
    c1 = y1 / d2 - l3 * c2
    c0 = m[0] / m[1] - l1 * c1 - l2 * c2
    mine = scale_of(sums_in[...]) * inverse_top
    c0 = c0 * inverse_top
    c1 = c1 * mine * inverse_top
    c2 = c2 * mine * mine * inverse_top
    out = None
    for terms, c in ((terms0, c0), (terms1, c1), (terms2, c2)):
        for g in range(groups):
            one = terms[g] * spread(c[g : g + 1], out_ref.shape[0])
            out = one if out is None else out + one
    out_ref[...] = out


def pinned(*arguments):
    return [pltpu.with_memory_space_constraint(x, pltpu.HBM) for x in arguments]


def call(kernel, arguments, outs, scratch=(), space=VMEM, cost=0):
    return pl.pallas_call(
        kernel,
        out_shape=outs,
        in_specs=space if isinstance(space, list) else [space] * len(arguments),
        out_specs=jax.tree.map(lambda _: VMEM, outs),
        scratch_shapes=list(scratch),
        cost_estimate=pl.CostEstimate(flops=cost, bytes_accessed=cost, transcendentals=0),
        compiler_params=pltpu.CompilerParams(vmem_limit_bytes=16 * 1024 * 1024),
    )(*arguments)


def swap_across(block):
    size, planes = lax.axis_size("dom"), lax.axis_size("freq")
    route = []
    for f in range(planes):
        for p in range(size):
            if p in (0, size - 1) and planes % 2 == 0:
                there = (f ^ 1) * size + p
            elif p % 2:
                there = f * size + (p + 1) % size
            else:
                there = f * size + (p - 1) % size
            route.append((f * size + p, there))
    return lax.ppermute(block, ("freq", "dom"), route)


def swap_beside(block):
    return lax.ppermute(block, "dom", [(i, i ^ 1) for i in range(lax.axis_size("dom"))])


def gather_all(block, axis):
    size = lax.axis_size(axis)
    copies = jnp.broadcast_to(block[None], (size, *block.shape))
    return lax.all_to_all(copies, axis, 0, 0)


def sum_over(block, axis):
    size = lax.axis_size(axis)
    if size & (size - 1):
        return jnp.sum(gather_all(block, axis), axis=0)
    near = min(size, 4)
    parts = [block] + [None] * (near - 1)
    for step in [*range(near // 2, near), *range(1, near // 2)]:
        parts[step] = lax.ppermute(block, axis, [(i, i ^ step) for i in range(size)])
    while len(parts) > 1:
        parts = [a + b for a, b in zip(parts[::2], parts[1::2])]
    block = parts[0]
    step = near
    while step < size:
        block = block + lax.ppermute(block, axis, [(i, i ^ step) for i in range(size)])
        step *= 2
    return block


def local(
    angular,
    stiffness,
    mass_matrix,
    conductivity,
    element_edges,
    live_slots,
    adjoint_source,
    forward_field,
    neighbour_map,
):
    freqs = angular.shape[0]
    polars = adjoint_source.shape[1]
    groups = freqs * polars
    rows = 2 * groups
    edge_count = adjoint_source.shape[-1]
    rim = neighbour_map.shape[-1]
    slots = element_edges.shape[-1]
    tall = slots // LANES
    stiff = stiffness.reshape(SIDE * SIDE, tall, LANES)
    mass = mass_matrix.reshape(SIDE * SIDE, tall, LANES)
    edges = element_edges.reshape(SIDE, tall, LANES)
    sigma = conductivity.reshape(tall, LANES)
    live = live_slots.reshape(tall, LANES)
    source = adjoint_source.reshape(groups, 1, edge_count)
    forward = forward_field.reshape(groups, 1, edge_count)

    def shape(*dims, kind=jnp.float32):
        return jax.ShapeDtypeStruct(dims, kind)

    field_shape, rim_shape = shape(rows, edge_count), shape(rows, rim)
    sums_shape, terms_shape = shape(rows, LANES), shape(groups, tall, LANES)
    picks_shape = shape(groups * SIDE, tall, LANES)

    across, beside, source, order = call(
        rims_stage,
        pinned(source, neighbour_map),
        [rim_shape, rim_shape, shape(*source.shape), shape(rows, rim, kind=jnp.int32)],
        (
            pltpu.VMEM(neighbour_map.shape, neighbour_map.dtype),
            pltpu.SemaphoreType.DMA((2,)),
        ),
        space=HBM,
    )
    across, beside = swap_across(across), swap_beside(beside)
    kept = [jax.ShapeDtypeStruct(x.shape, x.dtype) for x in (mass, sigma, live, edges, forward)]
    places, blocks, scale, picks, own, rates, mass, sigma, live, edges, forward = call(
        table_stage,
        [*pinned(angular, stiff, mass, sigma, live, edges, forward), source],
        [
            shape(LANES, SIDE * slots, kind=jnp.bfloat16),
            shape(freqs * SIDE * SIDE, tall, LANES),
            sums_shape,
            picks_shape,
            field_shape,
            shape(freqs, tall, LANES),
            *kept,
        ],
        (
            pltpu.SMEM(angular.shape, angular.dtype),
            pltpu.VMEM(stiff.shape, stiff.dtype),
            pltpu.SemaphoreType.DMA((7,)),
        ),
        space=[HBM] * 7 + [VMEM],
        cost=4_000_000,
    )
    front_shapes = [
        shape(rows, 2 * rim),
        picks_shape,
        shape(rows * SIDE * tall, LANES),
        sums_shape,
        shape(rows, 2 * rim),
        rim_shape,
        rim_shape,
    ]
    back_shapes = [terms_shape, sums_shape, field_shape, picks_shape]
    sums, terms = jnp.zeros((rows, LANES), jnp.float32), []
    for step in range(2):
        arrived = (across, beside)
        given = (order, *arrived, scale, picks, blocks, edges, places)
        front = functools.partial(front_stage, polars, step, edge_count)
        if step == 0:
            inverse, *outs = call(
                front, given, [shape(rows, rim, kind=jnp.int32), *front_shapes]
            )
        else:
            outs = call(
                front, (*given, inverse), [*front_shapes[:-2], *[shape(rows, rim // 2)] * 2]
            )
        delta, picks, pieces, forms, rims, across, beside = outs
        across, beside = swap_across(across), swap_beside(beside)
        given = (own, delta, forms, *arrived, sums, picks, pieces, rims, edges, places)
        back = functools.partial(back_stage, polars, step)
        if step == 0:
            heavy, term, sums, own, picks = call(
                back,
                (*given, rates, forward, mass, live),
                [picks_shape, *back_shapes],
                cost=4_000_000,
            )
        else:
            term, sums, own, picks = call(back, (*given, heavy), back_shapes, cost=4_000_000)
        terms.append(term)
    term, sums = call(
        functools.partial(last_stage, polars, 2),
        (
            own,
            order,
            inverse,
            across,
            beside,
            *arrived,
            scale,
            sums,
            picks,
            blocks,
            edges,
            heavy,
        ),
        [terms_shape, sums_shape],
        (pltpu.VMEM((rows, 2 * rim), jnp.float32),),
    )
    terms.append(term)
    term = call(
        combine_stage,
        (gather_all(sums, "dom"), sums, *terms),
        shape(tall, LANES),
    )
    gradient = sum_over(term, "freq").reshape(1, slots)
    updated = sigma.reshape(1, slots) * jnp.exp(-0.5 * jnp.tanh(gradient))
    return gradient, updated


def solution(mesh):
    return jax.shard_map(
        local,
        mesh=mesh,
        in_specs=(
            P("freq"),
            P("dom", None, None),
            P("dom", None, None),
            P("dom", None),
            P("dom", None, None),
            P("dom", None),
            P("freq", None, "dom", None),
            P("freq", None, "dom", None),
            P("dom", None),
        ),
        out_specs=(P("dom", None), P("dom", None)),
        check_vma=False,
    )
```

```python
import functools

import jax
import jax.numpy as jnp
from jax import lax
from jax.experimental import pallas as pl
from jax.experimental.pallas import tpu as pltpu
from jax.sharding import PartitionSpec as P

LANES = 128
SUBLANES = 8
SIDE = 6
VMEM = pl.BlockSpec(memory_space=pltpu.VMEM)
HBM = pl.BlockSpec(memory_space=pltpu.HBM)

PICK_LANES = lax.GatherDimensionNumbers(
    offset_dims=(),
    collapsed_slice_dims=(1,),
    start_index_map=(1,),
    operand_batching_dims=(0,),
    start_indices_batching_dims=(0,),
)


def pick_lanes(block, lanes):
    return lax.gather(
        block,
        lanes[..., None],
        PICK_LANES,
        (1, 1),
        mode=lax.GatherScatterMode.PROMISE_IN_BOUNDS,
    )


def pick_wide(chunks, index):
    lanes = index & (LANES - 1)
    high = index >> 7
    level = [pick_lanes(chunk, lanes) for chunk in chunks]
    bit = 0
    while len(level) > 1:
        odd = (high >> bit) & 1 == 1
        level = [
            jnp.where(odd, level[t + 1], level[t]) if t + 1 < len(level) else level[t]
            for t in range(0, len(level), 2)
        ]
        bit += 1
    return level[0]


def row_ids(rows):
    return lax.broadcasted_iota(jnp.int32, (rows, LANES), 0)


def lane_ids(rows):
    return lax.broadcasted_iota(jnp.int32, (rows, LANES), 1)


def spread(row, rows):
    return jnp.broadcast_to(row, (rows, row.shape[-1]))


def cut(ref):
    return [ref[:, c : c + LANES] for c in range(0, ref.shape[-1], LANES)]


def swap_halves(block):
    return pltpu.roll(block, block.shape[0] // 2, 0)


def doubled(block):
    half = block.shape[0] // 2
    return jnp.where(row_ids(2 * half) < half, block, swap_halves(block))


def lane_sum(block):
    return jnp.broadcast_to(jnp.sum(block, axis=1, keepdims=True), block.shape)


def put_lane(block, lane, value):
    return jnp.where(lane_ids(block.shape[0]) == lane, value, block)


def put_chunks(ref, chunks):
    for c, chunk in enumerate(chunks):
        ref[:, c * LANES : (c + 1) * LANES] = chunk


def is_even():
    return lax.rem(lax.axis_index("dom"), 2) == 0


def put_rims(across_ref, beside_ref, lower, upper):
    even = is_even()
    for c, (low, high) in enumerate(zip(lower, upper)):
        here = slice(c * LANES, (c + 1) * LANES)
        across_ref[:, here] = jnp.where(even, low, high)
        beside_ref[:, here] = jnp.where(even, high, low)


def take_rims(across_ref, beside_ref):
    even = is_even()
    device = lax.axis_index("dom")
    outermost = (device == 0) | (device == lax.axis_size("dom") - 1)
    pairs = [
        (jnp.where(outermost, 0.0, a), b) for a, b in zip(cut(across_ref), cut(beside_ref))
    ]
    prior = [jnp.where(even, a, b) for a, b in pairs]
    above = [jnp.where(even, b, a) for a, b in pairs]
    return prior, above


def picks_of(rows_of_group, edges):
    chunks = [spread(row, edges.shape[1]) for row in rows_of_group]
    return [pick_wide(chunks, edges[j]) for j in range(SIDE)]


def group_rows(ref, g):
    return [ref[g : g + 1, c : c + LANES] for c in range(0, ref.shape[-1], LANES)]


def times_block(entries, base, picked):
    out = []
    for i in range(SIDE):
        total = None
        for j in range(SIDE):
            one = entries[base + SIDE * i + j] * picked[j]
            total = one if total is None else total + one
        out.append(total)
    return out


def weighted_sum(left, right):
    total = None
    for a, b in zip(left, right):
        total = a * b if total is None else total + a * b
    return total


def scatter_side(pieces, edges, places, heights, i):
    depth = SIDE * edges.shape[1]
    rows = pieces.shape[0] // depth
    slots = edges.shape[1] * LANES
    columns = []
    for s in range(edges.shape[1]):
        both = pieces[pl.ds(i * edges.shape[1] + s, rows, stride=depth), :]
        high = spread(edges[i, s : s + 1, :] >> 7, rows)
        stacked = [jnp.where(high == h, both, 0.0) for h in heights]
        columns.append(jnp.concatenate(stacked, axis=0).astype(jnp.bfloat16))
    return lax.dot_general(
        jnp.concatenate(columns, axis=1),
        places[:, i * slots : (i + 1) * slots],
        (((1,), (1,)), ((), ())),
        preferred_element_type=jnp.float32,
    )


def add(total, part):
    return part if total is None else total + part


def parts_joined(total, count):
    rows = total.shape[0] // count
    out = []
    for n in range(count):
        piece = total[rows * n : rows * (n + 1)]
        out.append(piece + swap_halves(piece))
    return out


def scatter(pieces, edges, places, heights):
    total = None
    for i in range(SIDE):
        total = add(total, scatter_side(pieces, edges, places, heights, i))
    return parts_joined(total, len(heights))


def rim_heights(edge_count, rim):
    count = edge_count // LANES
    return [*range(rim), *range(count - rim, count)], list(range(rim, count - rim))


def corrections(from_prior, from_above, order, inverse):
    lower = [pick_wide(from_prior, index) for index in order]
    return lower + [pick_wide(from_above, index) for index in inverse]


def corrected(own, delta):
    rim = len(delta) // 2
    lower = [a + b for a, b in zip(own[:rim], delta[:rim])]
    upper = [a + b for a, b in zip(own[len(own) - rim :], delta[rim:])]
    return lower + own[rim : len(own) - rim] + upper


def squares(chunks, rim, has_prior):
    total = None
    for c, chunk in enumerate(chunks):
        term = chunk * chunk
        if c < rim:
            term = term * (1.0 - has_prior)
        total = term if total is None else total + term
    return total


def start_copies(routes, arrived):
    copies = [
        pltpu.make_async_copy(here, there, arrived.at[n])
        for n, (here, there) in enumerate(routes)
    ]
    for copy in copies:
        copy.start()
    return copies


def stacked_chunk(source, at):
    piece = [source[g, :, at : at + LANES] for g in range(source.shape[0])]
    return jnp.concatenate(piece + piece, axis=0)


def rims_stage(source_in, order_in, across_ref, beside_ref, source, order_ref, order, arrived):
    for copy in start_copies(((source_in, source), (order_in, order)), arrived):
        copy.wait()
    rows, rim = order_ref.shape
    first = row_ids(rows) < rows // 2
    order_ref[...] = spread(order[...], rows)
    numbers = [x.astype(jnp.float32) for x in cut(order_ref)]
    lower = [stacked_chunk(source, c) for c in range(0, rim, LANES)]
    start = source.shape[-1] - rim
    upper = [stacked_chunk(source, start + c) for c in range(0, rim, LANES)]
    lower = [jnp.where(first, x, o) for x, o in zip(lower, numbers)]
    upper = [jnp.where(first, x, 1.0) for x in upper]
    put_rims(across_ref, beside_ref, lower, upper)


def table_stage(
    angular_in,
    stiffness_in,
    mass_in,
    sigma_in,
    live_in,
    edges_in,
    forward_in,
    source,
    places_ref,
    blocks_ref,
    scale_ref,
    picks_ref,
    stacked_ref,
    rates,
    mass,
    sigma,
    live,
    edges,
    forward_ref,
    angular,
    stiffness,
    arrived,
):
    copies = start_copies(
        (
            (edges_in, edges),
            (angular_in, angular),
            (sigma_in, sigma),
            (live_in, live),
            (stiffness_in, stiffness),
            (mass_in, mass),
            (forward_in, forward_ref),
        ),
        arrived,
    )
    copies[0].wait()
    numbers = row_ids(LANES)
    rows = edges.shape[1]

    def body(i, carry):
        for s in range(rows):
            lanes = spread(edges[i, s : s + 1, :] & (LANES - 1), LANES)
            column = pl.ds(pl.multiple_of((i * rows + s) * LANES, LANES), LANES)
            places_ref[:, column] = jnp.where(lanes == numbers, 1.0, 0.0).astype(jnp.bfloat16)
        return carry

    lax.fori_loop(0, SIDE, body, 0)
    count = source.shape[-1]
    put_chunks(stacked_ref, [stacked_chunk(source, c) for c in range(0, count, LANES)])
    put_picks(picks_ref, stacked_ref, edges, source.shape[0])
    for copy in copies[1:]:
        copy.wait()
    for f in range(angular.shape[0]):
        rates[f] = jnp.full(rates.shape[1:], angular[f], jnp.float32)
    alive = live[...].astype(jnp.float32)
    weight = sigma[...]
    freqs = rates.shape[0]
    peak = None
    for i in range(SIDE):
        for f in range(freqs):
            entry = (SIDE + 1) * i
            size = stiffness[entry] + rates[f] * weight * mass[entry]
            peak = size if peak is None else jnp.maximum(peak, size)
    peak = jnp.max(peak * alive, axis=1, keepdims=True)
    scale = jnp.broadcast_to(jnp.max(peak, axis=0, keepdims=True), scale_ref.shape)
    scale_ref[...] = scale
    alive = alive / scale[:1, :1]
    for entry in range(SIDE * SIDE):
        stiff = stiffness[entry] * alive
        heavy = mass[entry] * (weight * alive)
        for f in range(freqs):
            blocks_ref[f * SIDE * SIDE + entry] = stiff + rates[f] * heavy


def put_picks(picks_ref, field, edges, groups):
    for g in range(groups):
        for j, value in enumerate(picks_of(group_rows(field, g), edges)):
            picks_ref[g * SIDE + j] = value


def pick_rims(rows, index, edge_count):
    rim = len(rows) // 2
    start = edge_count - rim * LANES
    lower = pick_wide([spread(row, index.shape[0]) for row in rows[:rim]], index)
    upper = pick_wide([spread(row, index.shape[0]) for row in rows[rim:]], index - start)
    lower = jnp.where(index < rim * LANES, lower, 0.0)
    return lower + jnp.where(index >= start, upper, 0.0)


def corrected_picks(delta_ref, own_picks, edges, edge_count):
    out = []
    for g in range(delta_ref.shape[0] // 2):
        delta = group_rows(delta_ref, g)
        out.append(
            [
                own_picks[g * SIDE + j] + pick_rims(delta, edges[j], edge_count)
                for j in range(SIDE)
            ]
        )
    return out


def products(blocks, picked, polars, i):
    out = []
    for g, mine in enumerate(picked):
        base = (g // polars) * SIDE * SIDE + SIDE * i
        out.append(weighted_sum([blocks[base + j] for j in range(SIDE)], mine))
    return out


def rows_of_forms(forms, rows):
    out = jnp.zeros((rows, LANES), jnp.float32)
    for g, form in enumerate(forms):
        row = jnp.sum(form, axis=0, keepdims=True)
        out = jnp.where(row_ids(rows) == g, spread(row, rows), out)
    return out


def invert(above, groups, rows):
    above_order = jnp.concatenate([x[groups : groups + 1] for x in above], axis=1)
    rim = above_order.shape[1]
    slot = lax.broadcasted_iota(jnp.int32, (rim, rim), 0).astype(jnp.float32)
    match = jnp.where(spread(above_order, rim) == slot, 1.0, 0.0).astype(jnp.bfloat16)
    numbers = lax.broadcasted_iota(jnp.int32, (2 * rows, rim), 1).astype(jnp.bfloat16)
    inverse = lax.dot_general(
        numbers, match, (((1,), (1,)), ((), ())), preferred_element_type=jnp.float32
    )
    return inverse[:rows].astype(jnp.int32)


def rescaled(block, inverse_scale, step):
    ratio = swap_halves(block) * inverse_scale
    for _ in range(step):
        block = block * ratio
    return doubled(block)


def unpacked(blocks, with_scale, inverse_scale, step):
    ratio = doubled(swap_halves(with_scale)) * inverse_scale
    out = []
    for block in blocks:
        for _ in range(step):
            block = block * ratio
        out += [doubled(block), doubled(swap_halves(block))]
    return out


def front_stage(
    polars,
    step,
    edge_count,
    order_ref,
    across_in,
    beside_in,
    scale_in,
    own_picks,
    blocks,
    edges,
    places,
    *rest,
):
    if step == 0:
        inverse_ref, *rest = rest
    else:
        inverse_in, *rest = rest
    delta_ref, picks_ref, pieces, forms_ref, rims_ref, across_ref, beside_ref = rest
    rows = delta_ref.shape[0]
    groups = rows // 2
    first = row_ids(rows) < groups
    scale = scale_in[...]
    prior, above = take_rims(across_in, beside_in)
    if step == 0:
        inverse_ref[...] = invert(above, groups, rows)
        inverse = cut(inverse_ref)
        prior, above = [doubled(x) for x in prior], [doubled(x) for x in above]
    else:
        inverse = cut(inverse_in)
        inverse_scale = 1.0 / scale
        prior = [rescaled(x, inverse_scale, step) for x in prior]
        above = [rescaled(x, inverse_scale, step) for x in above]
    put_chunks(delta_ref, corrections(prior, above, cut(order_ref), inverse))

    picked = corrected_picks(delta_ref, own_picks, edges, edge_count)
    for g in range(groups):
        for j in range(SIDE):
            picks_ref[g * SIDE + j] = picked[g][j]
    rim = len(prior)
    heights = rim_heights(edge_count, rim)[0]
    tall = edges.shape[1]
    forms, total = [None] * groups, None
    for i in range(SIDE):
        for g, value in enumerate(products(blocks, picked, polars, i)):
            forms[g] = add(forms[g], picked[g][i] * value)
            coarse = value.astype(jnp.bfloat16).astype(jnp.float32)
            for part, piece in enumerate((coarse, value - coarse)):
                at = ((part * groups + g) * SIDE + i) * tall
                pieces[at : at + tall, :] = piece
        total = add(total, scatter_side(pieces, edges, places, heights, i))
    forms_ref[...] = rows_of_forms(forms, rows)
    chunks = parts_joined(total, len(heights))
    put_chunks(rims_ref, chunks)
    lower, upper = chunks[:rim], chunks[rim:]
    if step == 0:
        lower = [jnp.where(first, x, scale) for x in lower]
        upper = [jnp.where(first, x, scale) for x in upper]
    else:
        lower = [jnp.where(first, a, b) for a, b in zip(lower[::2], lower[1::2])]
        upper = [jnp.where(first, a, b) for a, b in zip(upper[::2], upper[1::2])]
    put_rims(across_ref, beside_ref, lower, upper)


def inner_products(step, sums, own, delta, forms, across_in, beside_in):
    rows = sums.shape[0]
    first = row_ids(rows) < rows // 2
    prior, _ = take_rims(across_in, beside_in)
    has_prior = jnp.where(first, swap_halves(prior[0]), prior[0])
    has_prior = spread(jnp.where(has_prior[:1, :1] > 0.0, 1.0, 0.0), rows)
    field = corrected(own, delta)
    sums = put_lane(sums, 2 * step, lane_sum(squares(field, len(delta) // 2, has_prior)))
    return put_lane(sums, 2 * step + 1, lane_sum(forms))


def back_stage(
    polars,
    step,
    own,
    delta,
    forms,
    across_in,
    beside_in,
    sums_in,
    picks,
    pieces,
    rims,
    edges,
    places,
    *rest,
):
    if step == 0:
        rates, forward, mass, live, heavy, terms_ref, sums_ref, image_ref, picks_ref = rest
    else:
        heavy, terms_ref, sums_ref, image_ref, picks_ref = rest
    rows, edge_count = own.shape
    groups = rows // 2
    rim = rims.shape[-1] // LANES // 2
    outer = cut(rims)
    inner = scatter(pieces, edges, places, rim_heights(edge_count, rim)[1])
    put_chunks(image_ref, outer[:rim] + inner + outer[rim:])
    put_picks(picks_ref, image_ref, edges, groups)
    if step == 0:
        dead = -live[...].astype(jnp.float32)
        for g in range(groups):
            row = [forward[g, :, c : c + LANES] for c in range(0, edge_count, LANES)]
            values = times_block(mass, 0, picks_of(row, edges))
            factor = dead * rates[g // polars]
            for i in range(SIDE):
                heavy[g * SIDE + i] = factor * values[i]
    for g in range(groups):
        side = range(g * SIDE, (g + 1) * SIDE)
        terms_ref[g] = weighted_sum([picks[i] for i in side], [heavy[i] for i in side])
    sums_ref[...] = inner_products(
        step, sums_in[...], cut(own), cut(delta), forms[...], across_in, beside_in
    )


def last_stage(
    polars,
    step,
    own,
    order_ref,
    inverse_in,
    across_in,
    beside_in,
    across_before,
    beside_before,
    scale_in,
    sums_in,
    own_picks,
    blocks,
    edges,
    heavy,
    terms_ref,
    sums_ref,
    delta_ref,
):
    rows, edge_count = own.shape
    first = row_ids(rows) < rows // 2
    scale = scale_in[...]
    inverse_scale = 1.0 / scale
    prior, above = (
        unpacked(now, before[0], inverse_scale, step)
        for now, before in zip(
            take_rims(across_in, beside_in), take_rims(across_before, beside_before)
        )
    )
    put_chunks(delta_ref, corrections(prior, above, cut(order_ref), cut(inverse_in)))

    picked = corrected_picks(delta_ref, own_picks, edges, edge_count)
    forms = [None] * len(picked)
    for i in range(SIDE):
        for g, value in enumerate(products(blocks, picked, polars, i)):
            forms[g] = add(forms[g], picked[g][i] * value)
    for g, mine in enumerate(picked):
        terms_ref[g] = weighted_sum(mine, [heavy[g * SIDE + i] for i in range(SIDE)])
    forms = rows_of_forms(forms, rows)
    sums = inner_products(
        step, sums_in[...], cut(own), cut(delta_ref), forms, across_before, beside_before
    )
    sums_ref[...] = jnp.where(first, sums, scale)


def combine_stage(everyone, sums_in, terms0, terms1, terms2, out_ref):
    rows = sums_in.shape[0]
    groups = rows // 2
    first = row_ids(rows) < groups

    def scale_of(block):
        return jnp.where(first, swap_halves(block), block)

    parts = [everyone[q] for q in range(everyone.shape[0])]
    scales = [scale_of(block) for block in parts]
    top = functools.reduce(jnp.maximum, scales)
    lanes = lane_ids(rows)
    inverse_top = 1.0 / top
    total = None
    for block, scale in zip(parts, scales):
        ratio = scale * inverse_top
        power = jnp.ones_like(ratio)
        factor = jnp.ones_like(ratio)
        for k in range(1, 6):
            power = power * ratio
            factor = jnp.where(lanes == k, power, factor)
        term = block * factor
        total = term if total is None else total + term
    m = [jnp.broadcast_to(total[:, k : k + 1], (rows, LANES)) for k in range(6)]
    l1 = m[2] / m[1]
    l2 = m[3] / m[1]
    d2 = m[3] - l1 * m[2]
    cross = m[4] - l2 * m[2]
    l3 = cross / d2
    d3 = m[5] - l2 * m[3] - l3 * cross
    y1 = m[1] - l1 * m[0]
    y2 = m[2] - l2 * m[0] - l3 * y1
    c2 = y2 / d3
    c1 = y1 / d2 - l3 * c2
    c0 = m[0] / m[1] - l1 * c1 - l2 * c2
    mine = scale_of(sums_in[...]) * inverse_top
    c0 = c0 * inverse_top
    c1 = c1 * mine * inverse_top
    c2 = c2 * mine * mine * inverse_top
    out = None
    for terms, c in ((terms0, c0), (terms1, c1), (terms2, c2)):
        for g in range(groups):
            one = terms[g] * spread(c[g : g + 1], out_ref.shape[0])
            out = one if out is None else out + one
    out_ref[...] = out


def pinned(*arguments):
    return [pltpu.with_memory_space_constraint(x, pltpu.HBM) for x in arguments]


def call(kernel, arguments, outs, scratch=(), space=VMEM, cost=0):
    return pl.pallas_call(
        kernel,
        out_shape=outs,
        in_specs=space if isinstance(space, list) else [space] * len(arguments),
        out_specs=jax.tree.map(lambda _: VMEM, outs),
        scratch_shapes=list(scratch),
        cost_estimate=pl.CostEstimate(flops=cost, bytes_accessed=cost, transcendentals=0),
        compiler_params=pltpu.CompilerParams(vmem_limit_bytes=16 * 1024 * 1024),
    )(*arguments)


def swap_across(block):
    size, planes = lax.axis_size("dom"), lax.axis_size("freq")
    route = []
    for f in range(planes):
        for p in range(size):
            if p in (0, size - 1) and planes % 2 == 0:
                there = (f ^ 1) * size + p
            elif p % 2:
                there = f * size + (p + 1) % size
            else:
                there = f * size + (p - 1) % size
            route.append((f * size + p, there))
    return lax.ppermute(block, ("freq", "dom"), route)


def swap_beside(block):
    return lax.ppermute(block, "dom", [(i, i ^ 1) for i in range(lax.axis_size("dom"))])


def gather_all(block, axis):
    size = lax.axis_size(axis)
    copies = jnp.broadcast_to(block[None], (size, *block.shape))
    return lax.all_to_all(copies, axis, 0, 0)


def sum_over(block, axis):
    size = lax.axis_size(axis)
    if size & (size - 1):
        return jnp.sum(gather_all(block, axis), axis=0)
    near = min(size, 4)
    parts = [block] + [None] * (near - 1)
    for step in [*range(near // 2, near), *range(1, near // 2)]:
        parts[step] = lax.ppermute(block, axis, [(i, i ^ step) for i in range(size)])
    if near == 4:
        block = (parts[0] + parts[1]) + (parts[3] + parts[2])
    else:
        block = sum(parts[1:], parts[0])
    step = near
    while step < size:
        block = block + lax.ppermute(block, axis, [(i, i ^ step) for i in range(size)])
        step *= 2
    return block


def local(
    angular,
    stiffness,
    mass_matrix,
    conductivity,
    element_edges,
    live_slots,
    adjoint_source,
    forward_field,
    neighbour_map,
):
    freqs = angular.shape[0]
    polars = adjoint_source.shape[1]
    groups = freqs * polars
    rows = 2 * groups
    edge_count = adjoint_source.shape[-1]
    rim = neighbour_map.shape[-1]
    slots = element_edges.shape[-1]
    tall = slots // LANES
    stiff = stiffness.reshape(SIDE * SIDE, tall, LANES)
    mass = mass_matrix.reshape(SIDE * SIDE, tall, LANES)
    edges = element_edges.reshape(SIDE, tall, LANES)
    sigma = conductivity.reshape(tall, LANES)
    live = live_slots.reshape(tall, LANES)
    source = adjoint_source.reshape(groups, 1, edge_count)
    forward = forward_field.reshape(groups, 1, edge_count)

    def shape(*dims, kind=jnp.float32):
        return jax.ShapeDtypeStruct(dims, kind)

    field_shape, rim_shape = shape(rows, edge_count), shape(rows, rim)
    sums_shape, terms_shape = shape(rows, LANES), shape(groups, tall, LANES)
    picks_shape = shape(groups * SIDE, tall, LANES)

    across, beside, source, order = call(
        rims_stage,
        pinned(source, neighbour_map),
        [rim_shape, rim_shape, shape(*source.shape), shape(rows, rim, kind=jnp.int32)],
        (
            pltpu.VMEM(neighbour_map.shape, neighbour_map.dtype),
            pltpu.SemaphoreType.DMA((2,)),
        ),
        space=HBM,
    )
    across, beside = swap_across(across), swap_beside(beside)
    kept = [jax.ShapeDtypeStruct(x.shape, x.dtype) for x in (mass, sigma, live, edges, forward)]
    places, blocks, scale, picks, own, rates, mass, sigma, live, edges, forward = call(
        table_stage,
        [*pinned(angular, stiff, mass, sigma, live, edges, forward), source],
        [
            shape(LANES, SIDE * slots, kind=jnp.bfloat16),
            shape(freqs * SIDE * SIDE, tall, LANES),
            sums_shape,
            picks_shape,
            field_shape,
            shape(freqs, tall, LANES),
            *kept,
        ],
        (
            pltpu.SMEM(angular.shape, angular.dtype),
            pltpu.VMEM(stiff.shape, stiff.dtype),
            pltpu.SemaphoreType.DMA((7,)),
        ),
        space=[HBM] * 7 + [VMEM],
        cost=4_000_000,
    )
    front_shapes = [
        shape(rows, 2 * rim),
        picks_shape,
        shape(rows * SIDE * tall, LANES),
        sums_shape,
        shape(rows, 2 * rim),
        rim_shape,
        rim_shape,
    ]
    back_shapes = [terms_shape, sums_shape, field_shape, picks_shape]
    sums, terms = jnp.zeros((rows, LANES), jnp.float32), []
    for step in range(2):
        arrived = (across, beside)
        given = (order, *arrived, scale, picks, blocks, edges, places)
        front = functools.partial(front_stage, polars, step, edge_count)
        if step == 0:
            inverse, *outs = call(
                front, given, [shape(rows, rim, kind=jnp.int32), *front_shapes]
            )
        else:
            outs = call(
                front, (*given, inverse), [*front_shapes[:-2], *[shape(rows, rim // 2)] * 2]
            )
        delta, picks, pieces, forms, rims, across, beside = outs
        across, beside = swap_across(across), swap_beside(beside)
        given = (own, delta, forms, *arrived, sums, picks, pieces, rims, edges, places)
        back = functools.partial(back_stage, polars, step)
        if step == 0:
            heavy, term, sums, own, picks = call(
                back,
                (*given, rates, forward, mass, live),
                [picks_shape, *back_shapes],
                cost=4_000_000,
            )
        else:
            term, sums, own, picks = call(back, (*given, heavy), back_shapes, cost=4_000_000)
        terms.append(term)
    term, sums = call(
        functools.partial(last_stage, polars, 2),
        (
            own,
            order,
            inverse,
            across,
            beside,
            *arrived,
            scale,
            sums,
            picks,
            blocks,
            edges,
            heavy,
        ),
        [terms_shape, sums_shape],
        (pltpu.VMEM((rows, 2 * rim), jnp.float32),),
    )
    terms.append(term)
    term = call(
        combine_stage,
        (gather_all(sums, "dom"), sums, *terms),
        shape(tall, LANES),
    )
    gradient = sum_over(term, "freq").reshape(1, slots)
    updated = sigma.reshape(1, slots) * jnp.exp(-0.5 * jnp.tanh(gradient))
    return gradient, updated


def solution(mesh):
    return jax.shard_map(
        local,
        mesh=mesh,
        in_specs=(
            P("freq"),
            P("dom", None, None),
            P("dom", None, None),
            P("dom", None),
            P("dom", None, None),
            P("dom", None),
            P("freq", None, "dom", None),
            P("freq", None, "dom", None),
            P("dom", None),
        ),
        out_specs=(P("dom", None), P("dom", None)),
        check_vma=False,
    )
```
